32 devices in a mesh: groups: 2 (over y), gx: 4 (over x, core), gy: 4 (over z).
Axes of the slice: x: 2, y: 2, z: 4, core: 2. Of those that a mesh axis runs over, the one named last changes fastest.
Arguments:
- fine_features: bfloat16 [8, 4, 32, 4096], P(('groups', 'gx'), 'gy'), parts along dimension 0, may hold values from -6 to 6
- coarse_items: bfloat16 [8, 4, 64, 1024], P(('groups', 'gx'), 'gy'), parts along dimension 0, may hold values from -6 to 6
- conv_weight: bfloat16 [27, 64, 64], replicated, may hold values from -0.15625 to 0.15625
- up_weight: bfloat16 [8, 128, 64], replicated, may hold values from -0.5 to 0.5
- neighbours: int32 [8, 4, 32, 27], P(('groups', 'gx'), 'gy'), parts along dimension 0, may hold values from 0 to 64, as said below
- side_sends: int32 [8, 4, 2, 8], P(('groups', 'gx'), 'gy'), parts along dimension 0, may hold values from 0 to 31
- cross_sends: int32 [8, 4, 2, 8], P(('groups', 'gx'), 'gy'), parts along dimension 0, may hold values from 0 to 47
- parent_slots: int32 [8, 4, 32], P(('groups', 'gx'), 'gy'), parts along dimension 0, may hold values from 0 to 63, as said below
- coarse_sends: int32 [8, 4, 16, 4], P(('groups', 'gx'), 'gy'), parts along dimension 0, may hold values from 0 to 64, as said below
- cotangent: bfloat16 [8, 4, 32, 4096], P(('groups', 'gx'), 'gy'), parts along dimension 0, may hold values from -6 to 6
Outputs:
- conv_out: bfloat16 [8, 4, 32, 4096], P(('groups', 'gx'), 'gy'), parts along dimension 0
- grad_fine: bfloat16 [8, 4, 32, 4096], P(('groups', 'gx'), 'gy'), parts along dimension 0
- grad_coarse: bfloat16 [8, 4, 64, 1024], P(('groups', 'gx'), 'gy'), parts along dimension 0
- grad_conv: float32 [54, 64, 64], P('groups'), parts along dimension 0
- grad_up: float32 [16, 128, 64], P('groups'), parts along dimension 0
The draws below stay inside these ranges and needn't reach their ends.
There are 2 independent parts, one for each index of `groups`. The reference program is written for one: setup_inputs(seed, part) draws one part's arguments, and reference() takes and returns one part's arrays. A program takes and returns all parts, laid end to end along the dimension named above; an argument that names none is the same for every part. Nothing has to cross between parts.
Inputs may be any that keep to these rules, and one draw needn't show every extreme that they name: `neighbours`: entry 13 of brick b's row is b itself; the value 65 - 1 names the zero row (an empty neighbour brick). `parent_slots`: the 32 values of one device are distinct and each names a slot that its owner fills; some pair of devices fills all 4 slots. `coarse_sends`: each owned item is named at most once over all destinations; 64 marks an empty slot.
All inputs are finite; a program needn't handle non-finite values.
Results may differ from the reference program's by a relative error of at most 0.0052.
Values may be sent and summed in bfloat16 or wider, within the bound.
No kernel may reach another device: no remote copies, remote signals or barrier semaphores. Data moves between devices by JAX's collectives and lax.ppermute only.
A program may use at most 192 MiB of HBM per device.

```python
import math
import jax
import jax.numpy as jnp
from jax import lax

C = 64
CC = 128
NB = 32
FACE = 8
CAP = 4
NCI = 64
TAB = 65
VOXELS = 32768
N_GX = 4
N_GY = 4


def draw_neighbours(key, part):
    key = jax.random.fold_in(key, 11)
    key_rows, key_vacant = jax.random.split(key)
    full_shape = (N_GX, N_GY, NB, 27)
    chosen = jax.random.randint(key_rows, full_shape, 0, TAB - 1)
    vacant = jax.random.randint(key_vacant, full_shape, 0, 4) == 0
    chosen = jnp.where(vacant, TAB - 1, chosen)
    center = jnp.broadcast_to(jnp.arange(NB, dtype=jnp.int32)[:, None], full_shape)
    column = jnp.arange(27, dtype=jnp.int32)[None, None, None, :] == 13
    return jnp.where(column, center, chosen).astype(jnp.int32)


def coarse_plan(key):
    key = jax.random.fold_in(key, 5)
    device_count = N_GX * N_GY
    slot_count = device_count * CAP
    key_slots, key_favored, key_items = jax.random.split(key, 3)
    scores = jax.vmap(lambda subkey: jax.random.permutation(subkey, slot_count))(jax.random.split(key_slots, device_count)).astype(jnp.int32)
    favored = jax.random.randint(key_favored, (device_count,), 0, device_count).astype(jnp.int32)
    favored = favored.at[0].set(device_count - 1).at[1].set(0)
    slot_ids = jnp.arange(slot_count, dtype=jnp.int32)
    inside = slot_ids[None, :] // CAP == favored[:, None]
    scores = jnp.where(inside, slot_ids[None, :] % CAP, scores + CAP)
    ranking = jnp.argsort(scores, axis=1)
    chosen = ranking[:, :NB].astype(jnp.int32)
    taken_slot = jnp.zeros((device_count, slot_count), jnp.int32).at[jnp.arange(device_count, dtype=jnp.int32)[:, None], chosen].set(1)
    owner_items = jax.vmap(lambda subkey: jax.random.permutation(subkey, slot_count))(jax.random.split(key_items, device_count)).astype(jnp.int32)
    taken_owner = taken_slot.reshape(device_count, device_count, CAP).transpose(1, 0, 2)
    item_table = owner_items.reshape(device_count, device_count, CAP)
    sends = jnp.where(taken_owner == 1, item_table, NCI)
    return (chosen.reshape(N_GX, N_GY, NB), sends.reshape(N_GX, N_GY, device_count, CAP).astype(jnp.int32))


def draw_parent_slots(key, part):
    return coarse_plan(key)[0]


def draw_coarse_sends(key, part):
    return coarse_plan(key)[1]


def place_ends(values, own_key, least, top_value):
    dims = values.shape
    spot = [jax.random.randint(jax.random.fold_in(own_key, axis), (), 0, dims[axis]) for axis in range(len(dims))]
    values = values.at[tuple(spot)].set(least)
    longest = dims.index(max(dims))
    spot[longest] = (spot[longest] + 1) % dims[longest]
    return values.at[tuple(spot)].set(top_value)


def levels(own_key, shape, shards, least, largest):
    gain, own = 1.0, jax.random.fold_in(own_key, 6)
    for axis_at, blocks in shards:
        heights = jnp.exp(jax.random.uniform(jax.random.fold_in(own, axis_at), (blocks,), jnp.float32, least / len(shards), largest / len(shards)))
        gain = gain * jnp.repeat(heights, shape[axis_at] // blocks).reshape([-1 if axis == axis_at else 1 for axis in range(len(shape))])
    return gain


def normal_values(own_key, shape, deviation, bound, pieces=(), kind=jnp.bfloat16):
    result = deviation * jax.random.normal(own_key, shape, jnp.float32)
    if pieces:
        result = result * levels(own_key, shape, pieces, -0.22, 0.18)
    return jnp.clip(result, -bound, bound).astype(kind)


def setup_inputs(seed: int = 0, part: int = 0) -> dict:
    splits = jax.random.split(jax.random.key(seed), 11)
    own_keys = jax.random.split(jax.random.fold_in(splits[10], part), 11)
    fine_features = normal_values(own_keys[0], (N_GX, N_GY, NB, 64 * C), 1.0, 6.0, ((0, 4), (1, 4)))
    coarse_items = normal_values(own_keys[1], (N_GX, N_GY, NCI, 8 * CC), 1.0, 6.0, ((0, 4), (1, 4)))
    conv_weight = normal_values(splits[2], (27, C, C), (27 * C) ** -0.5, 0.15625)
    up_weight = normal_values(splits[3], (8, CC, C), CC ** -0.5, 0.5)
    neighbours = draw_neighbours(jax.random.fold_in(jax.random.fold_in(splits[10], part), 71), part)
    side_sends = place_ends(jax.random.randint(own_keys[5], (N_GX, N_GY, 2, FACE), 0, NB), jax.random.fold_in(own_keys[5], 1), 0, NB - 1).astype(jnp.int32)
    cross_sends = place_ends(jax.random.randint(own_keys[6], (N_GX, N_GY, 2, FACE), 0, NB + 2 * FACE), jax.random.fold_in(own_keys[6], 1), 0, (NB + 2 * FACE) - 1).astype(jnp.int32)
    parent_slots = draw_parent_slots(jax.random.fold_in(jax.random.fold_in(splits[10], part), 71), part)
    coarse_sends = draw_coarse_sends(jax.random.fold_in(jax.random.fold_in(splits[10], part), 71), part)
    cotangent = normal_values(own_keys[9], (N_GX, N_GY, NB, 64 * C), 1.0, 6.0, ((0, 4), (1, 4)))
    return dict(fine_features=fine_features, coarse_items=coarse_items, conv_weight=conv_weight, up_weight=up_weight, neighbours=neighbours, side_sends=side_sends, cross_sends=cross_sends, parent_slots=parent_slots, coarse_sends=coarse_sends, cotangent=cotangent)


def fold_side(blocks, along):
    lower = lax.slice_in_dim(lax.index_in_dim(blocks, 0, along, keepdims=False), 3, 4, axis=along)
    middle = lax.index_in_dim(blocks, 1, along, keepdims=False)
    upper = lax.slice_in_dim(lax.index_in_dim(blocks, 2, along, keepdims=False), 0, 1, axis=along)
    return jnp.concatenate([lower, middle, upper], axis=along)

def unfold_side(padded, along):
    before = [(0, 0)] * padded.ndim
    after = [(0, 0)] * padded.ndim
    before[along] = (3, 0)
    after[along] = (0, 3)
    lower = jnp.pad(lax.slice_in_dim(padded, 0, 1, axis=along), before)
    middle = lax.slice_in_dim(padded, 1, 5, axis=along)
    upper = jnp.pad(lax.slice_in_dim(padded, 5, 6, axis=along), after)
    return jnp.stack([lower, middle, upper], axis=along)

def gather_patches(brick_table, near_index):
    bricks = near_index.shape[0]
    channels = brick_table.shape[1] // 64
    blocks = jnp.take(brick_table, near_index.reshape(-1), axis=0)
    blocks = blocks.reshape(bricks, 3, 3, 3, 4, 4, 4, channels).transpose(0, 1, 4, 2, 5, 3, 6, 7)
    padded = fold_side(fold_side(fold_side(blocks, 1), 2), 3)
    columns = []
    for offset in range(27):
        along_x, along_y, along_z = (offset // 9, offset // 3 % 3, offset % 3)
        window = padded[:, along_x:along_x + 4, along_y:along_y + 4, along_z:along_z + 4, :]
        columns.append(window.reshape(bricks * 64, channels))
    return jnp.concatenate(columns, axis=1)

def scatter_patches(patch_grads, near_index, row_count):
    bricks = near_index.shape[0]
    channels = patch_grads.shape[1] // 27
    padded = jnp.zeros((bricks, 6, 6, 6, channels), jnp.float32)
    for offset in range(27):
        along_x, along_y, along_z = (offset // 9, offset // 3 % 3, offset % 3)
        piece = patch_grads[:, offset * channels:(offset + 1) * channels].reshape(bricks, 4, 4, 4, channels)
        padded = padded.at[:, along_x:along_x + 4, along_y:along_y + 4, along_z:along_z + 4, :].add(piece)
    blocks = unfold_side(unfold_side(unfold_side(padded, 3), 2), 1)
    blocks = blocks.transpose(0, 1, 3, 5, 2, 4, 6, 7).reshape(bricks * 27, 64 * channels)
    return jnp.zeros((row_count, 64 * channels), jnp.float32).at[near_index.reshape(-1)].add(blocks)

def wide_weight(up_weight):
    return up_weight.transpose(1, 0, 2).reshape(up_weight.shape[1], 8 * up_weight.shape[2])

def upsample(parents, up_weight):
    bricks = parents.shape[0]
    coarse_channels = up_weight.shape[1]
    channels = up_weight.shape[2]
    spread = jnp.dot(parents.reshape(bricks * 8, coarse_channels), wide_weight(up_weight), preferred_element_type=jnp.float32)
    spread = spread.reshape(bricks, 2, 2, 2, 2, 2, 2, channels).transpose(0, 1, 4, 2, 5, 3, 6, 7)
    return spread.reshape(bricks, 64 * channels)

def parity_rows(grads):
    bricks = grads.shape[0]
    channels = grads.shape[1] // 64
    shaped = grads.reshape(bricks, 2, 2, 2, 2, 2, 2, channels).transpose(0, 1, 3, 5, 2, 4, 6, 7)
    return shaped.reshape(bricks * 8, 8 * channels)

def from_lower(values, along):
    extent = values.shape[along]
    zeros_part = jnp.zeros_like(lax.slice_in_dim(values, 0, 1, axis=along))
    return jnp.concatenate([zeros_part, lax.slice_in_dim(values, 0, extent - 1, axis=along)], axis=along)

def from_upper(values, along):
    extent = values.shape[along]
    zeros_part = jnp.zeros_like(lax.slice_in_dim(values, 0, 1, axis=along))
    return jnp.concatenate([lax.slice_in_dim(values, 1, extent, axis=along), zeros_part], axis=along)

def pick_rows(base_rows, row_index):
    return jnp.take(base_rows, row_index, axis=0)

def add_rows(base_rows, row_index, values):
    return base_rows.at[row_index].add(values)

def reference(fine_features, coarse_items, conv_weight, up_weight, neighbours, side_sends, cross_sends, parent_slots, coarse_sends, cotangent):
    device_count = N_GX * N_GY
    grid_pick = jax.vmap(jax.vmap(pick_rows))
    grid_add = jax.vmap(jax.vmap(add_rows))
    flat_sends = coarse_sends.reshape(device_count, device_count, CAP)
    flat_parent = parent_slots.reshape(device_count, NB)
    source = flat_parent // CAP
    slot_place = flat_parent % CAP
    dest_ids = jnp.arange(device_count, dtype=jnp.int32)[:, None]
    item_index = flat_sends[source, dest_ids, slot_place]
    coarse_flat = coarse_items.reshape(device_count, NCI, 8 * CC)
    parents = coarse_flat[source, item_index].reshape(device_count * NB, 8 * CC)
    fine_rows = fine_features.reshape(device_count * NB, 64 * C)
    lifted = upsample(parents, up_weight)
    merged = (fine_rows.astype(jnp.float32) + lifted).astype(jnp.bfloat16).reshape(N_GX, N_GY, NB, 64 * C)
    lower_side = from_lower(grid_pick(merged, side_sends[:, :, 0]), 1)
    upper_side = from_upper(grid_pick(merged, side_sends[:, :, 1]), 1)
    extended = jnp.concatenate([merged, lower_side, upper_side], axis=2)
    lower_cross = from_lower(grid_pick(extended, cross_sends[:, :, 0]), 0)
    upper_cross = from_upper(grid_pick(extended, cross_sends[:, :, 1]), 0)
    zero_row = jnp.zeros((N_GX, N_GY, 1, 64 * C), jnp.bfloat16)
    tables = jnp.concatenate([extended, lower_cross, upper_cross, zero_row], axis=2)
    flat_weight = conv_weight.reshape(27 * C, C)

    def local_pass(operands):
        brick_table, near_index, cot_bricks = operands
        patches = gather_patches(brick_table, near_index)
        output = jnp.dot(patches, flat_weight, preferred_element_type=jnp.float32).astype(jnp.bfloat16)
        cot_rows = cot_bricks.reshape(NB * 64, C)
        weight_term = jnp.dot(patches.T, cot_rows, preferred_element_type=jnp.float32)
        patch_grads = jnp.dot(cot_rows, flat_weight.T, preferred_element_type=jnp.float32)
        table_grads = scatter_patches(patch_grads, near_index, TAB)
        return (output, table_grads, weight_term)
    outputs, table_grads, weight_terms = lax.map(local_pass, (tables.reshape(device_count, TAB, 64 * C), neighbours.reshape(device_count, NB, 27), cotangent.reshape(device_count, NB, 64 * C)))
    table_grads = table_grads.reshape(N_GX, N_GY, TAB, 64 * C)
    start_cross = NB + 2 * FACE
    lower_cross_grad = table_grads[:, :, start_cross:start_cross + FACE].astype(jnp.bfloat16)
    upper_cross_grad = table_grads[:, :, start_cross + FACE:start_cross + 2 * FACE].astype(jnp.bfloat16)
    extended_grad = table_grads[:, :, :start_cross]
    extended_grad = grid_add(extended_grad, cross_sends[:, :, 0], from_upper(lower_cross_grad, 0).astype(jnp.float32))
    extended_grad = grid_add(extended_grad, cross_sends[:, :, 1], from_lower(upper_cross_grad, 0).astype(jnp.float32))
    lower_side_grad = extended_grad[:, :, NB:NB + FACE].astype(jnp.bfloat16)
    upper_side_grad = extended_grad[:, :, NB + FACE:NB + 2 * FACE].astype(jnp.bfloat16)
    fine_grad = extended_grad[:, :, :NB]
    fine_grad = grid_add(fine_grad, side_sends[:, :, 0], from_upper(lower_side_grad, 1).astype(jnp.float32))
    fine_grad = grid_add(fine_grad, side_sends[:, :, 1], from_lower(upper_side_grad, 1).astype(jnp.float32))
    grad_fine = fine_grad.astype(jnp.bfloat16)
    rows_grad = parity_rows(grad_fine.reshape(device_count * NB, 64 * C))
    item_grads = jnp.dot(rows_grad, wide_weight(up_weight).T, preferred_element_type=jnp.float32).astype(jnp.bfloat16)
    item_grads = item_grads.reshape(device_count, NB, 8 * CC)
    up_term = jnp.dot(parents.reshape(device_count * NB * 8, CC).T, rows_grad, preferred_element_type=jnp.float32)
    coarse_grad = jnp.zeros((device_count, NCI + 1, 8 * CC), jnp.bfloat16).at[source, item_index].set(item_grads)[:, :NCI]
    grad_scale = 1.0 / math.sqrt(VOXELS)
    grad_conv = (lax.optimization_barrier(jnp.sum(weight_terms, axis=0)) * grad_scale).reshape(27, C, C)
    grad_up = (up_term * grad_scale).reshape(CC, 8, C).transpose(1, 0, 2)
    return (outputs.reshape(N_GX, N_GY, NB, 64 * C), grad_fine, coarse_grad.reshape(N_GX, N_GY, NCI, 8 * CC), grad_conv, grad_up)
```

```python
import functools
import math

import jax
import jax.numpy as jnp
from jax import lax
from jax.experimental import pallas as pl
from jax.experimental.pallas import tpu as pltpu
from jax.sharding import PartitionSpec as P

BF = jnp.bfloat16
F32 = jnp.float32
I32 = jnp.int32

C = 64
RUN = 4 * C
WIDE = RUN + 2 * C


def iota(shape, axis):
    return lax.broadcasted_iota(I32, shape, axis)


def ones_where(mask):
    return jnp.where(mask, 1.0, 0.0).astype(BF)


def dot(a, b):
    return jnp.dot(a, b, preferred_element_type=F32)


def dot_tn(a, b):
    return lax.dot_general(a, b, (((0,), (0,)), ((), ())), preferred_element_type=F32)


def dot_nt(a, b):
    return lax.dot_general(a, b, (((1,), (1,)), ((), ())), preferred_element_type=F32)


def column_of(row):
    size = row.shape[1]
    diagonal = iota((size, size), 0) == iota((size, size), 1)
    spread = jnp.broadcast_to(row.astype(F32), (size, size))
    return jnp.sum(jnp.where(diagonal, spread, 0.0), axis=1, keepdims=True).astype(I32)


def call(body, outs, *args, scratch=(), flops=0):
    moved = sum(a.size * a.dtype.itemsize for a in list(args) + list(outs))
    return pl.pallas_call(
        body,
        out_shape=tuple(outs),
        scratch_shapes=tuple(scratch),
        cost_estimate=pl.CostEstimate(flops=flops, bytes_accessed=moved, transcendentals=0),
        compiler_params=pltpu.CompilerParams(vmem_limit_bytes=28 * 2**20),
    )(*args)


def shape(dims, dtype=BF):
    return jax.ShapeDtypeStruct(dims, dtype)


def send_index(sends, group):
    capacity, devices = sends.shape
    lanes = devices * group
    spread = ones_where(iota((devices, lanes), 1) // group == iota((devices, lanes), 0))
    rows = dot(sends.astype(F32).astype(BF), spread)
    slot = iota((capacity, lanes), 1) % group
    picked = jnp.where(slot // 2 == iota((capacity, lanes), 0), rows, 0.0)
    return jnp.sum(picked, axis=0, keepdims=True).astype(I32)


def items_out_body(sends_ref, items_ref, out_ref):
    capacity, devices = sends_ref.shape
    count, width = items_ref.shape
    half = width // 2
    index = send_index(sends_ref[...], 2 * capacity)
    lanes = index.shape[1]
    odd = iota((count, lanes), 1) % 2
    named = iota((count, lanes), 0) == index
    total = dot_tn(ones_where(named & (odd == 0)), items_ref[:, :half])
    total += dot_tn(ones_where(named & (odd == 1)), items_ref[:, half:])
    out_ref[...] = total.astype(BF)


def merge_body(received_ref, slots_ref, up_ref, fine_ref, sides_ref, merged_ref, parents_ref, a_ref, b_ref):
    bricks = fine_ref.shape[0]
    lanes, half = received_ref.shape
    slot = column_of(slots_ref[...])
    place = iota((bricks, lanes), 1)
    named = place // 2 == slot
    received = received_ref[...]
    parents = jnp.concatenate(
        [dot(ones_where(named & (place % 2 == h)), received) for h in (0, 1)], axis=1
    ).astype(BF)
    coarse = 2 * half // 8
    stacked = jnp.concatenate([parents[:, v * coarse : (v + 1) * coarse] for v in range(8)], axis=0)
    parents_ref[...] = stacked
    lifted = dot_nt(stacked, up_ref[...])
    for v in range(8):
        cx, cy, cz = (v // 4, v // 2 % 2, v % 2)
        for parity in range(4):
            vx, vy = (2 * cx + parity // 2, 2 * cy + parity % 2)
            at = (vx * 4 + vy) * RUN + cz * 2 * C
            add = lifted[v * bricks : (v + 1) * bricks, parity * 2 * C : (parity + 1) * 2 * C]
            merged_ref[:, at : at + 2 * C] = (fine_ref[:, at : at + 2 * C].astype(F32) + add).astype(BF)
    pick_rows(sides_ref[...], merged_ref[...], a_ref, b_ref)


def pick_rows(lists, rows, a_ref, b_ref):
    count = rows.shape[0]
    for which, out_ref in ((0, a_ref), (1, b_ref)):
        face = lists.shape[1]
        chosen = ones_where(iota((count, face), 0) == lists[which : which + 1])
        out_ref[...] = dot_tn(chosen, rows).astype(BF)


def stack_rows(*refs):
    return jnp.concatenate([r[...].astype(F32) for r in refs], axis=0).astype(BF)


def cross_body(merged_ref, low_ref, high_ref, crosses_ref, a_ref, b_ref):
    rows = jnp.concatenate([merged_ref[...], stack_rows(low_ref, high_ref)], axis=0)
    pick_rows(crosses_ref[...], rows, a_ref, b_ref)


def build_bands(weight_ref, band_ref):
    zero = jnp.zeros((C, C), BF)
    blank = jnp.zeros((C, 2 * C), BF)

    def pair(a, b):
        return jnp.concatenate([a, b], axis=1)

    for e in range(9):
        low, mid, high = (weight_ref[3 * e + z] for z in range(3))
        first, second = (pair(mid, low), pair(high, mid))
        left, right = (pair(low, zero), pair(zero, high))
        rows = (
            (first, blank),
            (second, left),
            (right, first),
            (blank, second),
            (blank, right),
            (left, blank),
        )
        for z, halves in enumerate(rows):
            for s in range(2):
                band_ref[e, z * C : (z + 1) * C, s * 2 * C : (s + 1) * 2 * C] = halves[s]


def options(at):
    return [(at + 1, 0)] + ([(5, 1)] if at == 0 else []) + ([(0, -1)] if at == 3 else [])


def offset_of(dx, dy, dz):
    return (dx + 1) * 9 + (dy + 1) * 3 + dz + 1


def stack_runs(ref):
    return jnp.concatenate([ref[:, p * RUN : (p + 1) * RUN] for p in range(16)], axis=0)


def split_two(value):
    head = value.astype(BF)
    return head, (value - head.astype(F32)).astype(BF)


def table_grad_body(cot_ref, weight_ref, near_ref, ext_ref, low_ref, high_ref, band_ref, pad_ref):
    bricks = cot_ref.shape[0]
    face = low_ref.shape[0]
    start = ext_ref.shape[0]
    rows = start + 2 * face
    build_bands(weight_ref, band_ref)
    cot = stack_runs(cot_ref)
    pad_ref[...] = jnp.zeros(pad_ref.shape, F32)
    for e in range(9):
        ex, ey = (e // 3, e % 3)
        part = dot_nt(cot, band_ref[e]).reshape(4, 4, bricks, WIDE)
        pad_ref[ex : ex + 4, ey : ey + 4] += part
    near = [near_ref[o] for o in range(27)]

    def chooser(which):
        index = jnp.concatenate([near[o] for o in which], axis=1)
        return ones_where(iota((rows, index.shape[1]), 0) == index)

    lower_half = iota((rows, 2 * C), 1) < C
    cache = {}
    for x in range(4):
        for y in range(4):
            places = [(X, Y, dx, dy) for X, dx in options(x) for Y, dy in options(y)]
            key = tuple((dx, dy) for _, _, dx, dy in places)
            if key not in cache:
                moved = [d for d in key if d != (0, 0)]
                main = chooser([offset_of(*d, 0) for d in moved] * 2) if moved else None
                up = chooser([offset_of(*d, 1) for d in key] * 2)
                down = chooser([offset_of(*d, -1) for d in key] * 2)
                cache[key] = (main, jnp.concatenate([up, down], axis=0))
            main, ends = cache[key]
            own = pad_ref[x + 1, y + 1, :, :RUN]
            own = jnp.concatenate([own, jnp.zeros((rows - bricks, RUN), F32)], axis=0)
            if main is not None:
                parts = [split_two(pad_ref[X, Y, :, :RUN]) for X, Y, dx, dy in places if (dx, dy) != (0, 0)]
                value = jnp.concatenate([p[0] for p in parts] + [p[1] for p in parts], axis=0)
                own += dot(main, value)
            parts = [split_two(pad_ref[X, Y, :, RUN:]) for X, Y, _, _ in places]
            value = jnp.concatenate([p[0] for p in parts] + [p[1] for p in parts], axis=0)
            halo = dot(ends, value)
            first = own[:, : 2 * C] + jnp.where(lower_half, halo[:rows], 0.0)
            second = own[:, 2 * C :] + jnp.where(lower_half, 0.0, halo[rows:])
            total = jnp.concatenate([first, second], axis=1)
            at = (x * 4 + y) * RUN
            ext_ref[:, at : at + RUN] = total[:start]
            low_ref[:, at : at + RUN] = total[start : start + face].astype(BF)
            high_ref[:, at : at + RUN] = total[start + face :].astype(BF)


def conv_body(
    merged_ref, low_ref, high_ref, below_ref, above_ref, cot_ref, weight_ref, near_ref,
    out_ref, grad_ref, band_ref, pad_ref, table_ref,
):
    bricks = merged_ref.shape[0]
    rows = bricks + 4 * low_ref.shape[0]
    build_bands(weight_ref, band_ref)
    table_ref[:bricks] = merged_ref[...]
    table_ref[bricks:] = stack_rows(low_ref, high_ref, below_ref, above_ref)
    near = jnp.concatenate([near_ref[o] for o in range(27)] + [jnp.zeros((5, bricks), I32)], axis=0)
    near = near.astype(F32).T.astype(I32)

    def one_of(dx, dy, dz):
        o = offset_of(dx, dy, dz)
        return near[:, o : o + 1]

    place = iota((bricks, rows), 1)
    pair_place = iota((bricks, 2 * rows), 1)
    lower_half = iota((rows, 2 * C), 1) < C
    zero = jnp.zeros((rows, 2 * C), BF)
    cache = {}
    for x in range(4):
        for y in range(4):
            places = [(X, Y, dx, dy) for X, dx in options(x) for Y, dy in options(y)]
            for _, _, dx, dy in places:
                if (dx, dy) not in cache:
                    main = ones_where(place == one_of(dx, dy, 0))
                    ends = jnp.where(pair_place < rows, one_of(dx, dy, 1), one_of(dx, dy, -1) + rows)
                    cache[dx, dy] = (main, ones_where(pair_place == ends))
            at = (x * 4 + y) * RUN
            columns = table_ref[:, at : at + RUN]
            first = jnp.where(lower_half, columns[:, : 2 * C], zero)
            second = jnp.where(lower_half, zero, columns[:, 2 * C :])
            ends = jnp.concatenate([cache[dx, dy][1] for _, _, dx, dy in places], axis=0)
            halo = dot(ends, jnp.concatenate([first, second], axis=0)).astype(BF)
            for i, (X, Y, _, _) in enumerate(places):
                pad_ref[X, Y, :, RUN:] = halo[i * bricks : (i + 1) * bricks]
            pad_ref[x + 1, y + 1, :, :RUN] = columns[:bricks]
            moved = [p for p in places if p[2:] != (0, 0)]
            if moved:
                main = jnp.concatenate([cache[dx, dy][0] for _, _, dx, dy in moved], axis=0)
                got = dot(main, columns).astype(BF)
                for i, (X, Y, _, _) in enumerate(moved):
                    pad_ref[X, Y, :, :RUN] = got[i * bricks : (i + 1) * bricks]

    turned = stack_runs(cot_ref).T
    total = None
    lanes_low = iota((C, 2 * C), 1) < C
    sums = []
    for e in range(9):
        ex, ey = (e // 3, e % 3)
        inputs = pad_ref[ex : ex + 4, ey : ey + 4].reshape(16 * bricks, WIDE)
        part = dot(inputs, band_ref[e])
        total = part if total is None else total + part
        wide = dot(turned, inputs)

        def block(z, s):
            return wide[z * C : (z + 1) * C, s * 2 * C : (s + 1) * 2 * C]

        low = jnp.where(lanes_low, block(1, 0) + block(3, 1), block(0, 2) + block(2, 0))
        mid = jnp.where(lanes_low, block(0, 0) + block(2, 1), block(1, 0) + block(3, 1))
        high = jnp.where(lanes_low, block(1, 1) + block(3, 2), block(0, 0) + block(2, 1))
        for value in (low, mid, high):
            sums.append(value + pltpu.roll(value, C, 1))
    sums.append(jnp.zeros((C, 2 * C), F32))
    for p in range(16):
        out_ref[:, p * RUN : (p + 1) * RUN] = total[p * bricks : (p + 1) * bricks].astype(BF)
    for pair in range(7):
        both = [jnp.where(lanes_low, sums[14 * h + 2 * pair], sums[14 * h + 2 * pair + 1]) for h in range(2)]
        grad_ref[:, pair * 2 * C : (pair + 1) * 2 * C] = jnp.concatenate(both, axis=0).astype(BF)


def add_rows(base, lists, first_ref, second_ref):
    count, face = (base.shape[0], lists.shape[1])
    index = jnp.concatenate([lists[0:1], lists[1:2]], axis=1)
    chosen = ones_where(iota((count, 2 * face), 0) == index)
    return base + dot(chosen, stack_rows(first_ref, second_ref))


def side_grad_body(ext_ref, crosses_ref, next_ref, prev_ref, fine_ref, low_ref, high_ref):
    bricks, face = (fine_ref.shape[0], low_ref.shape[0])
    total = add_rows(ext_ref[...], crosses_ref[...], next_ref, prev_ref)
    fine_ref[...] = total[:bricks]
    low_ref[...] = total[bricks : bricks + face].astype(BF)
    high_ref[...] = total[bricks + face :].astype(BF)


def fine_grad_body(
    fine_ref, sides_ref, next_ref, prev_ref, up_ref, parents_ref, slots_ref, grad_ref, replies_ref, devices
):
    bricks = fine_ref.shape[0]
    grad_ref[...] = add_rows(fine_ref[...], sides_ref[...], next_ref, prev_ref).astype(BF)
    stacked = []
    for v in range(8):
        cx, cy, cz = (v // 4, v // 2 % 2, v % 2)
        lanes = []
        for parity in range(4):
            at = ((2 * cx + parity // 2) * 4 + 2 * cy + parity % 2) * RUN + cz * 2 * C
            lanes.append(grad_ref[:, at : at + 2 * C])
        stacked.append(jnp.concatenate(lanes, axis=1))
    stacked = jnp.concatenate(stacked, axis=0)
    items = dot(stacked, up_ref[...]).astype(BF)
    items = jnp.concatenate([items[v * bricks : (v + 1) * bricks] for v in range(8)], axis=1)
    up_sum = dot_tn(stacked, parents_ref[...]).astype(BF)
    coarse = up_sum.shape[1]
    quarter = up_sum.shape[0] // 4
    up_sum = jnp.concatenate([up_sum[q * quarter : (q + 1) * quarter] for q in range(4)], axis=1)
    half = items.shape[1] // 2
    count = replies_ref.shape[0]
    share = quarter // devices
    group = count // devices
    item_rows = group - share
    row = iota((count, bricks), 0)
    inside = row % group
    place = row // group * item_rows + inside
    named = (place // 2 == slots_ref[...]) & (inside < item_rows)
    row = iota((count, quarter), 0)
    inside = row % group
    chosen = (inside >= item_rows) & (row // group * share + inside - item_rows == iota((count, quarter), 1))
    replies = dot(ones_where(named & (place % 2 == 0)), items[:, :half])
    replies += dot(ones_where(named & (place % 2 == 1)), items[:, half:])
    replies += dot(ones_where(chosen), up_sum)
    replies_ref[...] = replies.astype(BF)


def coarse_grad_body(returned_ref, sends_ref, out_ref, share_ref):
    capacity, devices = sends_ref.shape
    count = out_ref.shape[0]
    lanes, half = returned_ref.shape
    group = lanes // devices
    share = share_ref.shape[0]
    item_rows = group - share
    index = send_index(sends_ref[...], group)
    inside = iota((count, lanes), 1) % group
    named = (iota((count, lanes), 0) == index) & (inside < item_rows)
    returned = returned_ref[...]
    for h in range(2):
        chosen = ones_where(named & (inside % 2 == h))
        out_ref[:, h * half : (h + 1) * half] = dot(chosen, returned).astype(BF)
    inside = iota((share, lanes), 1) % group
    share_ref[...] = dot(ones_where(inside - item_rows == iota((share, lanes), 0)), returned).astype(BF)


def share_body(arrived_ref, up_ref, out_ref):
    lanes, width = arrived_ref.shape
    share = up_ref.shape[0]
    chosen = ones_where(iota((share, lanes), 1) % share == iota((share, lanes), 0))
    out_ref[:, :width] = dot(chosen, arrived_ref[...]).astype(BF)
    out_ref[:, width:] = up_ref[...]


def final_body(totals_ref, conv_ref, up_ref, scale):
    width = 14 * C
    for pair in range(7):
        turned = totals_ref[:, pair * 2 * C : (pair + 1) * 2 * C].astype(F32).T * scale
        for h in range(2):
            for s in range(2):
                o = 14 * h + 2 * pair + s
                if o < 27:
                    conv_ref[o] = turned[s * C : (s + 1) * C, h * C : (h + 1) * C]
    quarter = totals_ref.shape[0]
    coarse = up_ref.shape[1]
    for q in range(4):
        up_ref[q * quarter : (q + 1) * quarter] = (
            totals_ref[:, width + q * coarse : width + (q + 1) * coarse].astype(F32) * scale
        )


def passed_along(value, axis, steps):
    count = lax.axis_size(axis)
    initial, last = (max(0, -steps), min(count, count - steps))
    return lax.ppermute(value, axis, [(source, source + steps) for source in range(initial, last)])


def trade_rows(values, devices):
    rows, width = values.shape
    grid_view = values.reshape(devices, rows // devices, width)
    return lax.all_to_all(grid_view, ("gx", "gy"), split_axis=0, concat_axis=0, tiled=True).reshape(rows, width)


def on_device(
    fine_features, coarse_items, conv_weight, up_weight, neighbours,
    side_sends, cross_sends, parent_slots, coarse_sends, cotangent,
):
    fine = fine_features[0, 0]
    items = coarse_items[0, 0]
    cot = cotangent[0, 0]
    bricks, width = fine.shape
    face = side_sends.shape[-1]
    across_x, across_y = (lax.axis_size("gx"), lax.axis_size("gy"))
    devices = across_x * across_y
    capacity = coarse_sends.shape[-1]
    item_count, item_width = items.shape
    coarse = up_weight.shape[1]
    start = bricks + 2 * face
    sends = coarse_sends[0, 0].T
    slots = parent_slots[0]
    sides = side_sends[0, 0]
    crosses = cross_sends[0, 0]
    near = neighbours[0, 0].T.reshape(27, 1, bricks)
    up_turned = up_weight.transpose(0, 2, 1).reshape(8 * C, coarse)
    half = item_width // 2
    share = 2 * C // devices
    band = pltpu.VMEM((9, WIDE, RUN), BF)
    face_rows = shape((face, width))
    conv_flops = 2 * 9 * 16 * bricks * WIDE * RUN

    (outgoing,) = call(items_out_body, [shape((2 * capacity * devices, half))], sends, items)
    received = trade_rows(outgoing, devices)
    ext_grad, low_cross, high_cross = call(
        table_grad_body, [shape((start, width), F32), face_rows, face_rows], cot, conv_weight, near,
        scratch=[band, pltpu.VMEM((6, 6, bricks, WIDE), F32)], flops=2 * conv_flops,
    )
    merged, parents, to_next, to_prev = call(
        merge_body, [shape((bricks, width)), shape((8 * bricks, coarse)), face_rows, face_rows],
        received, slots, up_turned, fine, sides,
    )
    low_side = passed_along(to_next, "gy", 1)
    high_side = passed_along(to_prev, "gy", -1)
    grad_prev = passed_along(high_cross, "gx", 1)
    grad_next = passed_along(low_cross, "gx", -1)
    to_next, to_prev = call(cross_body, [face_rows, face_rows], merged, low_side, high_side, crosses)
    below = passed_along(to_next, "gx", 1)
    above = passed_along(to_prev, "gx", -1)
    fine_part, low_grad, high_grad = call(
        side_grad_body, [shape((bricks, width), F32), face_rows, face_rows], ext_grad, crosses, grad_next, grad_prev
    )
    grad_prev = passed_along(high_grad, "gy", 1)
    grad_next = passed_along(low_grad, "gy", -1)
    grad_fine, replies = call(
        functools.partial(fine_grad_body, devices=devices),
        [shape((bricks, width)), shape((devices * (2 * capacity + share), half))],
        fine_part, sides, grad_next, grad_prev, up_turned, parents, slots,
    )
    returned = trade_rows(replies, devices)
    output, conv_sum = call(
        conv_body, [shape((bricks, width)), shape((2 * C, 14 * C))],
        merged, low_side, high_side, below, above, cot, conv_weight, near,
        scratch=[band, pltpu.VMEM((6, 6, bricks, WIDE), BF), pltpu.VMEM((bricks + 4 * face, width), BF)],
        flops=2 * conv_flops,
    )
    coarse_grad, up_share = call(
        coarse_grad_body, [shape((item_count, item_width)), shape((share, half))], returned, sends
    )
    arrived = trade_rows(conv_sum, devices)
    (own_share,) = call(share_body, [shape((share, 14 * C + half))], arrived, up_share)
    totals = lax.all_gather(own_share, ("gx", "gy"), axis=0, tiled=True)
    scale = 1.0 / math.sqrt(64 * bricks * devices)
    grad_conv, grad_up = call(
        functools.partial(final_body, scale=scale),
        [shape((27, C, C), F32), shape((8 * C, coarse), F32)], totals,
    )
    return (
        output.reshape(1, 1, bricks, width),
        grad_fine.reshape(1, 1, bricks, width),
        coarse_grad.reshape(1, 1, item_count, item_width),
        grad_conv,
        grad_up.reshape(8, C, coarse).transpose(0, 2, 1),
    )


def solution(mesh):
    split = P(("groups", "gx"), "gy", None, None)
    placed = (split, split, P(), P(), split, split, split, P(("groups", "gx"), "gy", None), split, split)
    return jax.shard_map(
        on_device,
        mesh=mesh,
        in_specs=placed,
        out_specs=(split, split, split, P("groups", None, None), P("groups", None, None)),
        check_vma=False,
    )
```

```python
import functools
import math

import jax
import jax.numpy as jnp
from jax import lax
from jax.experimental import pallas as pl
from jax.experimental.pallas import tpu as pltpu
from jax.sharding import PartitionSpec as P

BF = jnp.bfloat16
F32 = jnp.float32
I32 = jnp.int32

C = 64
RUN = 4 * C
WIDE = RUN + 2 * C


def iota(shape, axis):
    return lax.broadcasted_iota(I32, shape, axis)


def ones_where(mask):
    return jnp.where(mask, 1.0, 0.0).astype(BF)


def dot(a, b):
    return jnp.dot(a, b, preferred_element_type=F32)


def dot_tn(a, b):
    return lax.dot_general(a, b, (((0,), (0,)), ((), ())), preferred_element_type=F32)


def dot_nt(a, b):
    return lax.dot_general(a, b, (((1,), (1,)), ((), ())), preferred_element_type=F32)


def column_of(row):
    size = row.shape[1]
    diagonal = iota((size, size), 0) == iota((size, size), 1)
    spread = jnp.broadcast_to(row.astype(F32), (size, size))
    return jnp.sum(jnp.where(diagonal, spread, 0.0), axis=1, keepdims=True).astype(I32)


def call(body, outs, *args, scratch=(), flops=0):
    moved = sum(a.size * a.dtype.itemsize for a in list(args) + list(outs))
    return pl.pallas_call(
        body,
        out_shape=tuple(outs),
        scratch_shapes=tuple(scratch),
        cost_estimate=pl.CostEstimate(flops=flops, bytes_accessed=moved, transcendentals=0),
        compiler_params=pltpu.CompilerParams(vmem_limit_bytes=28 * 2**20),
    )(*args)


def shape(dims, dtype=BF):
    return jax.ShapeDtypeStruct(dims, dtype)


def send_index(sends, group, pieces=1, j=0):
    capacity, devices = sends.shape
    lanes = devices * group
    spread = ones_where(iota((devices, lanes), 1) // group == iota((devices, lanes), 0))
    rows = dot(sends.astype(F32).astype(BF), spread)
    slot = (iota((capacity, lanes), 1) % group * pieces + j) // 2
    picked = jnp.where(slot == iota((capacity, lanes), 0), rows, 0.0)
    return jnp.sum(picked, axis=0, keepdims=True).astype(I32)


def items_out_body(sends_ref, items_ref, out_ref):
    capacity, devices = sends_ref.shape
    count, width = items_ref.shape
    half = width // 2
    index = send_index(sends_ref[...], 2 * capacity)
    lanes = index.shape[1]
    odd = iota((count, lanes), 1) % 2
    named = iota((count, lanes), 0) == index
    total = dot_tn(ones_where(named & (odd == 0)), items_ref[:, :half])
    total += dot_tn(ones_where(named & (odd == 1)), items_ref[:, half:])
    out_ref[...] = total.astype(BF)


def merge_body(received_ref, slots_ref, up_ref, fine_ref, sides_ref, merged_ref, parents_ref, a_ref, b_ref):
    bricks = fine_ref.shape[0]
    lanes, half = received_ref.shape
    slot = column_of(slots_ref[...])
    place = iota((bricks, lanes), 1)
    named = place // 2 == slot
    received = received_ref[...]
    parents = jnp.concatenate(
        [dot(ones_where(named & (place % 2 == h)), received) for h in (0, 1)], axis=1
    ).astype(BF)
    coarse = 2 * half // 8
    stacked = jnp.concatenate([parents[:, v * coarse : (v + 1) * coarse] for v in range(8)], axis=0)
    parents_ref[...] = stacked
    lifted = dot_nt(stacked, up_ref[...])
    for v in range(8):
        cx, cy, cz = (v // 4, v // 2 % 2, v % 2)
        for parity in range(4):
            vx, vy = (2 * cx + parity // 2, 2 * cy + parity % 2)
            at = (vx * 4 + vy) * RUN + cz * 2 * C
            add = lifted[v * bricks : (v + 1) * bricks, parity * 2 * C : (parity + 1) * 2 * C]
            merged_ref[:, at : at + 2 * C] = (fine_ref[:, at : at + 2 * C].astype(F32) + add).astype(BF)
    pick_rows(sides_ref[...], merged_ref[...], a_ref, b_ref)


def pick_rows(lists, rows, a_ref, b_ref):
    count = rows.shape[0]
    for which, out_ref in ((0, a_ref), (1, b_ref)):
        face = lists.shape[1]
        chosen = ones_where(iota((count, face), 0) == lists[which : which + 1])
        out_ref[...] = dot_tn(chosen, rows).astype(BF)


def stack_rows(*refs):
    return jnp.concatenate([r[...].astype(F32) for r in refs], axis=0).astype(BF)


def cross_body(merged_ref, low_ref, high_ref, crosses_ref, a_ref, b_ref):
    rows = jnp.concatenate([merged_ref[...], stack_rows(low_ref, high_ref)], axis=0)
    pick_rows(crosses_ref[...], rows, a_ref, b_ref)


def build_bands(weight_ref, band_ref):
    zero = jnp.zeros((C, C), BF)
    blank = jnp.zeros((C, 2 * C), BF)

    def pair(a, b):
        return jnp.concatenate([a, b], axis=1)

    for e in range(9):
        low, mid, high = (weight_ref[3 * e + z] for z in range(3))
        first, second = (pair(mid, low), pair(high, mid))
        left, right = (pair(low, zero), pair(zero, high))
        rows = (
            (first, blank),
            (second, left),
            (right, first),
            (blank, second),
            (blank, right),
            (left, blank),
        )
        for z, halves in enumerate(rows):
            for s in range(2):
                band_ref[e, z * C : (z + 1) * C, s * 2 * C : (s + 1) * 2 * C] = halves[s]


def options(at):
    return [(at + 1, 0)] + ([(5, 1)] if at == 0 else []) + ([(0, -1)] if at == 3 else [])


def offset_of(dx, dy, dz):
    return (dx + 1) * 9 + (dy + 1) * 3 + dz + 1


def stack_runs(ref):
    return jnp.concatenate([ref[:, p * RUN : (p + 1) * RUN] for p in range(16)], axis=0)


def split_two(value):
    head = value.astype(BF)
    return head, (value - head.astype(F32)).astype(BF)


def table_grad_body(cot_ref, weight_ref, near_ref, ext_ref, low_ref, high_ref, band_ref, pad_ref):
    bricks = cot_ref.shape[0]
    face = low_ref.shape[0]
    start = ext_ref.shape[0]
    rows = start + 2 * face
    build_bands(weight_ref, band_ref)
    cot = stack_runs(cot_ref)
    pad_ref[...] = jnp.zeros(pad_ref.shape, F32)
    for e in range(9):
        ex, ey = (e // 3, e % 3)
        part = dot_nt(cot, band_ref[e]).reshape(4, 4, bricks, WIDE)
        pad_ref[ex : ex + 4, ey : ey + 4] += part
    near = [near_ref[o] for o in range(27)]

    def chooser(which):
        index = jnp.concatenate([near[o] for o in which], axis=1)
        return ones_where(iota((rows, index.shape[1]), 0) == index)

    lower_half = iota((rows, 2 * C), 1) < C
    cache = {}
    for x in range(4):
        for y in range(4):
            places = [(X, Y, dx, dy) for X, dx in options(x) for Y, dy in options(y)]
            key = tuple((dx, dy) for _, _, dx, dy in places)
            if key not in cache:
                moved = [d for d in key if d != (0, 0)]
                main = chooser([offset_of(*d, 0) for d in moved] * 2) if moved else None
                up = chooser([offset_of(*d, 1) for d in key] * 2)
                down = chooser([offset_of(*d, -1) for d in key] * 2)
                cache[key] = (main, jnp.concatenate([up, down], axis=0))
            main, ends = cache[key]
            own = pad_ref[x + 1, y + 1, :, :RUN]
            own = jnp.concatenate([own, jnp.zeros((rows - bricks, RUN), F32)], axis=0)
            if main is not None:
                parts = [split_two(pad_ref[X, Y, :, :RUN]) for X, Y, dx, dy in places if (dx, dy) != (0, 0)]
                value = jnp.concatenate([p[0] for p in parts] + [p[1] for p in parts], axis=0)
                own += dot(main, value)
            parts = [split_two(pad_ref[X, Y, :, RUN:]) for X, Y, _, _ in places]
            value = jnp.concatenate([p[0] for p in parts] + [p[1] for p in parts], axis=0)
            halo = dot(ends, value)
            first = own[:, : 2 * C] + jnp.where(lower_half, halo[:rows], 0.0)
            second = own[:, 2 * C :] + jnp.where(lower_half, 0.0, halo[rows:])
            total = jnp.concatenate([first, second], axis=1)
            at = (x * 4 + y) * RUN
            ext_ref[:, at : at + RUN] = total[:start]
            low_ref[:, at : at + RUN] = total[start : start + face].astype(BF)
            high_ref[:, at : at + RUN] = total[start + face :].astype(BF)


def conv_body(
    merged_ref, low_ref, high_ref, below_ref, above_ref, cot_ref, weight_ref, near_ref,
    out_ref, back_ref, band_ref, pad_ref, table_ref,
):
    bricks = merged_ref.shape[0]
    rows = bricks + 4 * low_ref.shape[0]
    build_bands(weight_ref, band_ref)
    table_ref[:bricks] = merged_ref[...]
    table_ref[bricks:] = stack_rows(low_ref, high_ref, below_ref, above_ref)
    near = jnp.concatenate([near_ref[o] for o in range(27)] + [jnp.zeros((5, bricks), I32)], axis=0)
    near = near.astype(F32).T.astype(I32)

    def one_of(dx, dy, dz):
        o = offset_of(dx, dy, dz)
        return near[:, o : o + 1]

    place = iota((bricks, rows), 1)
    pair_place = iota((bricks, 2 * rows), 1)
    lower_half = iota((rows, 2 * C), 1) < C
    zero = jnp.zeros((rows, 2 * C), BF)
    cache = {}
    for x in range(4):
        for y in range(4):
            places = [(X, Y, dx, dy) for X, dx in options(x) for Y, dy in options(y)]
            for _, _, dx, dy in places:
                if (dx, dy) not in cache:
                    main = ones_where(place == one_of(dx, dy, 0))
                    ends = jnp.where(pair_place < rows, one_of(dx, dy, 1), one_of(dx, dy, -1) + rows)
                    cache[dx, dy] = (main, ones_where(pair_place == ends))
            at = (x * 4 + y) * RUN
            columns = table_ref[:, at : at + RUN]
            first = jnp.where(lower_half, columns[:, : 2 * C], zero)
            second = jnp.where(lower_half, zero, columns[:, 2 * C :])
            ends = jnp.concatenate([cache[dx, dy][1] for _, _, dx, dy in places], axis=0)
            halo = dot(ends, jnp.concatenate([first, second], axis=0)).astype(BF)
            for i, (X, Y, _, _) in enumerate(places):
                pad_ref[X, Y, :, RUN:] = halo[i * bricks : (i + 1) * bricks]
            pad_ref[x + 1, y + 1, :, :RUN] = columns[:bricks]
            moved = [p for p in places if p[2:] != (0, 0)]
            if moved:
                main = jnp.concatenate([cache[dx, dy][0] for _, _, dx, dy in moved], axis=0)
                got = dot(main, columns).astype(BF)
                for i, (X, Y, _, _) in enumerate(moved):
                    pad_ref[X, Y, :, :RUN] = got[i * bricks : (i + 1) * bricks]

    turned = stack_runs(cot_ref).T
    total = None
    lanes_low = iota((C, 2 * C), 1) < C
    sums = []
    for e in range(9):
        ex, ey = (e // 3, e % 3)
        inputs = pad_ref[ex : ex + 4, ey : ey + 4].reshape(16 * bricks, WIDE)
        part = dot(inputs, band_ref[e])
        total = part if total is None else total + part
        wide = dot(turned, inputs)

        def block(z, s):
            return wide[z * C : (z + 1) * C, s * 2 * C : (s + 1) * 2 * C]

        low = jnp.where(lanes_low, block(1, 0) + block(3, 1), block(0, 2) + block(2, 0))
        mid = jnp.where(lanes_low, block(0, 0) + block(2, 1), block(1, 0) + block(3, 1))
        high = jnp.where(lanes_low, block(1, 1) + block(3, 2), block(0, 0) + block(2, 1))
        for value in (low, mid, high):
            sums.append(value + pltpu.roll(value, C, 1))
    sums.append(jnp.zeros((C, 2 * C), F32))
    for p in range(16):
        out_ref[:, p * RUN : (p + 1) * RUN] = total[p * bricks : (p + 1) * bricks].astype(BF)
    for pair in range(7):
        both = [jnp.where(lanes_low, sums[14 * h + 2 * pair], sums[14 * h + 2 * pair + 1]) for h in range(2)]
        at = back_ref.shape[1] - 14 * C + pair * 2 * C
        back_ref[:, at : at + 2 * C] = jnp.concatenate(both, axis=0).astype(BF)


def add_rows(base, lists, first_ref, second_ref):
    count, face = (base.shape[0], lists.shape[1])
    index = jnp.concatenate([lists[0:1], lists[1:2]], axis=1)
    chosen = ones_where(iota((count, 2 * face), 0) == index)
    return base + dot(chosen, stack_rows(first_ref, second_ref))


def side_grad_body(ext_ref, crosses_ref, next_ref, prev_ref, fine_ref, low_ref, high_ref):
    bricks, face = (fine_ref.shape[0], low_ref.shape[0])
    total = add_rows(ext_ref[...], crosses_ref[...], next_ref, prev_ref)
    fine_ref[...] = total[:bricks]
    low_ref[...] = total[bricks : bricks + face].astype(BF)
    high_ref[...] = total[bricks + face :].astype(BF)


def fine_grad_body(fine_ref, sides_ref, next_ref, prev_ref, up_ref, parents_ref, slots_ref, grad_ref, back_ref, devices):
    bricks = fine_ref.shape[0]
    grad_ref[...] = add_rows(fine_ref[...], sides_ref[...], next_ref, prev_ref).astype(BF)
    stacked = []
    for v in range(8):
        cx, cy, cz = (v // 4, v // 2 % 2, v % 2)
        lanes = []
        for parity in range(4):
            at = ((2 * cx + parity // 2) * 4 + 2 * cy + parity % 2) * RUN + cz * 2 * C
            lanes.append(grad_ref[:, at : at + 2 * C])
        stacked.append(jnp.concatenate(lanes, axis=1))
    stacked = jnp.concatenate(stacked, axis=0)
    items = dot(stacked, up_ref[...]).astype(BF)
    items = jnp.concatenate([items[v * bricks : (v + 1) * bricks] for v in range(8)], axis=1)
    half = items.shape[1] // 2
    count = back_ref.shape[0]
    up_sum = dot_tn(stacked, parents_ref[...]).astype(BF)
    coarse = up_sum.shape[1]
    parts = up_sum.shape[0] // count
    item_lanes = back_ref.shape[1] - 14 * C - parts * coarse
    for q in range(parts):
        at = item_lanes + q * coarse
        back_ref[:, at : at + coarse] = up_sum[q * count : (q + 1) * count]
    for j in range(item_lanes // half):
        piece = iota((count, bricks), 0) * (item_lanes // half) + j
        named = piece // 2 == slots_ref[...]
        rows = dot(ones_where(named & (piece % 2 == 0)), items[:, :half])
        rows += dot(ones_where(named & (piece % 2 == 1)), items[:, half:])
        back_ref[:, j * half : (j + 1) * half] = rows.astype(BF)


def last_body(
    merged_ref, low_ref, high_ref, below_ref, above_ref, cot_ref, weight_ref, near_ref,
    fine_ref, sides_ref, next_ref, prev_ref, up_ref, parents_ref, slots_ref,
    out_ref, grad_ref, back_ref, band_ref, pad_ref, table_ref, devices,
):
    conv_body(
        merged_ref, low_ref, high_ref, below_ref, above_ref, cot_ref, weight_ref, near_ref,
        out_ref, back_ref, band_ref, pad_ref, table_ref,
    )
    fine_grad_body(
        fine_ref, sides_ref, next_ref, prev_ref, up_ref, parents_ref, slots_ref, grad_ref, back_ref, devices
    )


def share_body(back_ref, out_ref, devices):
    count, width = out_ref.shape
    share = count // devices
    same = iota((count, count), 0) % share == iota((count, count), 1) % share
    out_ref[...] = dot(ones_where(same), back_ref[:, back_ref.shape[1] - width :]).astype(BF)


def coarse_grad_body(back_ref, sends_ref, out_ref):
    capacity, devices = sends_ref.shape
    count, item_width = out_ref.shape
    half = item_width // 2
    lanes = back_ref.shape[0]
    pieces = 2 * capacity * devices // lanes
    group = lanes // devices
    for h in range(2):
        total = None
        for j in range(pieces):
            index = send_index(sends_ref[...], group, pieces, j)
            place = iota((count, lanes), 1) % group * pieces + j
            chosen = (iota((count, lanes), 0) == index) & (place % 2 == h)
            part = dot(ones_where(chosen), back_ref[:, j * half : (j + 1) * half])
            total = part if total is None else total + part
        out_ref[:, h * half : (h + 1) * half] = total.astype(BF)


def final_body(totals_ref, conv_ref, up_ref, scale):
    count = totals_ref.shape[0]
    coarse = up_ref.shape[1]
    parts = up_ref.shape[0] // count
    for q in range(parts):
        up_ref[q * count : (q + 1) * count] = totals_ref[:, q * coarse : (q + 1) * coarse].astype(F32) * scale
    for pair in range(7):
        at = parts * coarse + pair * 2 * C
        turned = totals_ref[:, at : at + 2 * C].astype(F32).T * scale
        for h in range(2):
            for s in range(2):
                o = 14 * h + 2 * pair + s
                if o < 27:
                    conv_ref[o] = turned[s * C : (s + 1) * C, h * C : (h + 1) * C]


def passed_along(value, axis, steps):
    count = lax.axis_size(axis)
    initial, last = (max(0, -steps), min(count, count - steps))
    return lax.ppermute(value, axis, [(source, source + steps) for source in range(initial, last)])


def trade_rows(values, devices):
    rows, width = values.shape
    grid_view = values.reshape(devices, rows // devices, width)
    return lax.all_to_all(grid_view, ("gx", "gy"), split_axis=0, concat_axis=0, tiled=True).reshape(rows, width)


def on_device(
    fine_features, coarse_items, conv_weight, up_weight, neighbours,
    side_sends, cross_sends, parent_slots, coarse_sends, cotangent,
):
    fine = fine_features[0, 0]
    items = coarse_items[0, 0]
    cot = cotangent[0, 0]
    bricks, width = fine.shape
    face = side_sends.shape[-1]
    across_x, across_y = (lax.axis_size("gx"), lax.axis_size("gy"))
    devices = across_x * across_y
    capacity = coarse_sends.shape[-1]
    item_count, item_width = items.shape
    coarse = up_weight.shape[1]
    start = bricks + 2 * face
    sends = coarse_sends[0, 0].T
    slots = parent_slots[0]
    sides = side_sends[0, 0]
    crosses = cross_sends[0, 0]
    near = neighbours[0, 0].T.reshape(27, 1, bricks)
    up_turned = up_weight.transpose(0, 2, 1).reshape(8 * C, coarse)
    half = item_width // 2
    count = 2 * C
    sums_width = 14 * C + 8 * C * coarse // count
    back_width = capacity * devices * item_width // count + sums_width
    band = pltpu.VMEM((9, WIDE, RUN), BF)
    face_rows = shape((face, width))
    conv_flops = 2 * 9 * 16 * bricks * WIDE * RUN

    (outgoing,) = call(items_out_body, [shape((2 * capacity * devices, half))], sends, items)
    received = trade_rows(outgoing, devices)
    ext_grad, low_cross, high_cross = call(
        table_grad_body, [shape((start, width), F32), face_rows, face_rows], cot, conv_weight, near,
        scratch=[band, pltpu.VMEM((6, 6, bricks, WIDE), F32)], flops=2 * conv_flops,
    )
    merged, parents, to_next, to_prev = call(
        merge_body, [shape((bricks, width)), shape((8 * bricks, coarse)), face_rows, face_rows],
        received, slots, up_turned, fine, sides,
    )
    low_side = passed_along(to_next, "gy", 1)
    high_side = passed_along(to_prev, "gy", -1)
    grad_prev = passed_along(high_cross, "gx", 1)
    grad_next = passed_along(low_cross, "gx", -1)
    to_next, to_prev = call(cross_body, [face_rows, face_rows], merged, low_side, high_side, crosses)
    below = passed_along(to_next, "gx", 1)
    above = passed_along(to_prev, "gx", -1)
    fine_part, low_grad, high_grad = call(
        side_grad_body, [shape((bricks, width), F32), face_rows, face_rows], ext_grad, crosses, grad_next, grad_prev
    )
    grad_prev = passed_along(high_grad, "gy", 1)
    grad_next = passed_along(low_grad, "gy", -1)
    output, grad_fine, back = call(
        functools.partial(last_body, devices=devices),
        [shape((bricks, width)), shape((bricks, width)), shape((count, back_width))],
        merged, low_side, high_side, below, above, cot, conv_weight, near,
        fine_part, sides, grad_next, grad_prev, up_turned, parents, slots,
        scratch=[band, pltpu.VMEM((6, 6, bricks, WIDE), BF), pltpu.VMEM((bricks + 4 * face, width), BF)],
        flops=2 * conv_flops,
    )
    back = trade_rows(back, devices)
    (sums,) = call(functools.partial(share_body, devices=devices), [shape((count, sums_width))], back)
    totals = trade_rows(sums, devices)
    (coarse_grad,) = call(coarse_grad_body, [shape((item_count, item_width))], back, sends)
    scale = 1.0 / math.sqrt(64 * bricks * devices)
    grad_conv, grad_up = call(
        functools.partial(final_body, scale=scale),
        [shape((27, C, C), F32), shape((8 * C, coarse), F32)], totals,
    )
    return (
        output.reshape(1, 1, bricks, width),
        grad_fine.reshape(1, 1, bricks, width),
        coarse_grad.reshape(1, 1, item_count, item_width),
        grad_conv,
        grad_up.reshape(8, C, coarse).transpose(0, 2, 1),
    )


def solution(mesh):
    split = P(("groups", "gx"), "gy", None, None)
    placed = (split, split, P(), P(), split, split, split, P(("groups", "gx"), "gy", None), split, split)
    return jax.shard_map(
        on_device,
        mesh=mesh,
        in_specs=placed,
        out_specs=(split, split, split, P("groups", None, None), P("groups", None, None)),
        check_vma=False,
    )
```

```python
import functools
import math

import jax
import jax.numpy as jnp
from jax import lax
from jax.experimental import pallas as pl
from jax.experimental.pallas import tpu as pltpu
from jax.sharding import PartitionSpec as P

BF = jnp.bfloat16
F32 = jnp.float32
I32 = jnp.int32

C = 64
RUN = 4 * C
WIDE = RUN + 2 * C


def iota(shape, axis):
    return lax.broadcasted_iota(I32, shape, axis)


def ones_where(mask):
    return jnp.where(mask, 1.0, 0.0).astype(BF)


def dot(a, b):
    return jnp.dot(a, b, preferred_element_type=F32)


def dot_tn(a, b):
    return lax.dot_general(a, b, (((0,), (0,)), ((), ())), preferred_element_type=F32)


def dot_nt(a, b):
    return lax.dot_general(a, b, (((1,), (1,)), ((), ())), preferred_element_type=F32)


def column_of(row):
    size = row.shape[1]
    diagonal = iota((size, size), 0) == iota((size, size), 1)
    spread = jnp.broadcast_to(row.astype(F32), (size, size))
    return jnp.sum(jnp.where(diagonal, spread, 0.0), axis=1, keepdims=True).astype(I32)


def call(body, outs, *args, scratch=(), flops=0, in_hbm=False):
    moved = sum(a.size * a.dtype.itemsize for a in list(args) + list(outs))
    return pl.pallas_call(
        body,
        out_shape=tuple(outs),
        in_specs=[pl.BlockSpec(memory_space=pl.ANY) if in_hbm else pl.BlockSpec() for _ in args],
        scratch_shapes=tuple(scratch),
        cost_estimate=pl.CostEstimate(flops=flops, bytes_accessed=moved, transcendentals=0),
        compiler_params=pltpu.CompilerParams(vmem_limit_bytes=28 * 2**20),
    )(*args)


def shape(dims, dtype=BF):
    return jax.ShapeDtypeStruct(dims, dtype)


def send_index(sends, group, pieces=1, j=0):
    capacity, devices = sends.shape
    lanes = devices * group
    spread = ones_where(iota((devices, lanes), 1) // group == iota((devices, lanes), 0))
    rows = dot(sends.astype(F32).astype(BF), spread)
    slot = (iota((capacity, lanes), 1) % group * pieces + j) // 2
    picked = jnp.where(slot == iota((capacity, lanes), 0), rows, 0.0)
    return jnp.sum(picked, axis=0, keepdims=True).astype(I32)


def items_out(sends_ref, items_ref, out_ref):
    capacity, devices = sends_ref.shape
    count, width = items_ref.shape
    half = width // 2
    index = send_index(sends_ref[...], 2 * capacity)
    lanes = index.shape[1]
    odd = iota((count, lanes), 1) % 2
    named = iota((count, lanes), 0) == index
    total = dot_tn(ones_where(named & (odd == 0)), items_ref[:, :half])
    total += dot_tn(ones_where(named & (odd == 1)), items_ref[:, half:])
    out_ref[...] = total.astype(BF)


def merge(received_ref, slots, up_ref, fine_ref, merged_ref, parents_ref):
    bricks = fine_ref.shape[0]
    lanes, half = received_ref.shape
    slot = column_of(slots)
    place = iota((bricks, lanes), 1)
    named = place // 2 == slot
    received = received_ref[...]
    parents = jnp.concatenate(
        [dot(ones_where(named & (place % 2 == h)), received) for h in (0, 1)], axis=1
    ).astype(BF)
    coarse = 2 * half // 8
    stacked = jnp.concatenate([parents[:, v * coarse : (v + 1) * coarse] for v in range(8)], axis=0)
    parents_ref[...] = stacked
    lifted = dot_nt(stacked, up_ref[...])
    for v in range(8):
        cx, cy, cz = (v // 4, v // 2 % 2, v % 2)
        for parity in range(4):
            vx, vy = (2 * cx + parity // 2, 2 * cy + parity % 2)
            at = (vx * 4 + vy) * RUN + cz * 2 * C
            add = lifted[v * bricks : (v + 1) * bricks, parity * 2 * C : (parity + 1) * 2 * C]
            merged_ref[:, at : at + 2 * C] = (fine_ref[:, at : at + 2 * C].astype(F32) + add).astype(BF)


def pick_rows(lists, rows):
    place = iota((rows.shape[0], lists.shape[1]), 0)
    return [dot_tn(ones_where(place == lists[w : w + 1]), rows) for w in (0, 1)]


def stack_rows(*parts):
    return jnp.concatenate([p.astype(F32) for p in parts], axis=0).astype(BF)


def sides_of(lists_ref, face):
    return lists_ref[0:2, :face]


def crosses_of(lists_ref, face):
    return lists_ref[2:4, :face]


def slots_of(lists_ref, bricks):
    return lists_ref[4:5, :bricks]


def cross_body(merged_ref, low_ref, high_ref, lists_ref, a_ref, b_ref):
    face = a_ref.shape[0]
    sides = stack_rows(low_ref[...].astype(F32)[:face], high_ref[...].astype(F32)[:face])
    rows = jnp.concatenate([merged_ref[...], sides], axis=0)
    first, second = pick_rows(crosses_of(lists_ref, face), rows)
    a_ref[...] = first.astype(BF)
    b_ref[...] = second.astype(BF)


def build_bands(weight_ref, band_ref):
    zero = jnp.zeros((C, C), BF)
    blank = jnp.zeros((C, 2 * C), BF)

    def pair(a, b):
        return jnp.concatenate([a, b], axis=1)

    for e in range(9):
        low, mid, high = (weight_ref[3 * e + z] for z in range(3))
        first, second = (pair(mid, low), pair(high, mid))
        left, right = (pair(low, zero), pair(zero, high))
        rows = (
            (first, blank),
            (second, left),
            (right, first),
            (blank, second),
            (blank, right),
            (left, blank),
        )
        for z, halves in enumerate(rows):
            for s in range(2):
                band_ref[e, z * C : (z + 1) * C, s * 2 * C : (s + 1) * 2 * C] = halves[s]


def options(at):
    return [(at + 1, 0)] + ([(5, 1)] if at == 0 else []) + ([(0, -1)] if at == 3 else [])


def offset_of(dx, dy, dz):
    return (dx + 1) * 9 + (dy + 1) * 3 + dz + 1


def stack_runs(ref):
    return jnp.concatenate([ref[:, p * RUN : (p + 1) * RUN] for p in range(16)], axis=0)


def split_two(value):
    head = value.astype(BF)
    return head, (value - head.astype(F32)).astype(BF)


def table_grad(cot_ref, weight_ref, near_ref, ext_ref, low_ref, high_ref, band_ref, pad_ref):
    bricks = cot_ref.shape[0]
    face = low_ref.shape[0]
    start = ext_ref.shape[0]
    rows = start + 2 * face
    build_bands(weight_ref, band_ref)
    cot = stack_runs(cot_ref)
    pad_ref[...] = jnp.zeros(pad_ref.shape, F32)
    for e in range(9):
        ex, ey = (e // 3, e % 3)
        part = dot_nt(cot, band_ref[e]).reshape(4, 4, bricks, WIDE)
        pad_ref[ex : ex + 4, ey : ey + 4] += part
    near = [near_ref[o] for o in range(27)]

    def chooser(which):
        index = jnp.concatenate([near[o] for o in which], axis=1)
        return ones_where(iota((rows, index.shape[1]), 0) == index)

    lower_half = iota((rows, 2 * C), 1) < C
    cache = {}
    for x in range(4):
        for y in range(4):
            places = [(X, Y, dx, dy) for X, dx in options(x) for Y, dy in options(y)]
            key = tuple((dx, dy) for _, _, dx, dy in places)
            if key not in cache:
                moved = [d for d in key if d != (0, 0)]
                main = chooser([offset_of(*d, 0) for d in moved] * 2) if moved else None
                up = chooser([offset_of(*d, 1) for d in key] * 2)
                down = chooser([offset_of(*d, -1) for d in key] * 2)
                cache[key] = (main, jnp.concatenate([up, down], axis=0))
            main, ends = cache[key]
            own = pad_ref[x + 1, y + 1, :, :RUN]
            own = jnp.concatenate([own, jnp.zeros((rows - bricks, RUN), F32)], axis=0)
            if main is not None:
                parts = [split_two(pad_ref[X, Y, :, :RUN]) for X, Y, dx, dy in places if (dx, dy) != (0, 0)]
                value = jnp.concatenate([p[0] for p in parts] + [p[1] for p in parts], axis=0)
                own += dot(main, value)
            parts = [split_two(pad_ref[X, Y, :, RUN:]) for X, Y, _, _ in places]
            value = jnp.concatenate([p[0] for p in parts] + [p[1] for p in parts], axis=0)
            halo = dot(ends, value)
            first = own[:, : 2 * C] + jnp.where(lower_half, halo[:rows], 0.0)
            second = own[:, 2 * C :] + jnp.where(lower_half, 0.0, halo[rows:])
            total = jnp.concatenate([first, second], axis=1)
            at = (x * 4 + y) * RUN
            ext_ref[:, at : at + RUN] = total[:start]
            low_ref[:, at : at + RUN] = total[start : start + face].astype(BF)
            high_ref[:, at : at + RUN] = total[start + face :].astype(BF)


def first_body(
    sends_hbm, items_hbm, weight_hbm, cot_hbm, near_hbm, sides_hbm, crosses_hbm, slots_hbm,
    out_ref, ext_ref, low_ref, high_ref, lists_ref,
    sends_ref, items_ref, weight_ref, cot_ref, near_ref, sides_ref, crosses_ref, slots_ref, band_ref, pad_ref, arrived,
):
    sources = (sends_hbm, items_hbm, weight_hbm, cot_hbm, near_hbm, sides_hbm, crosses_hbm, slots_hbm)
    places = (sends_ref, items_ref, weight_ref, cot_ref, near_ref, sides_ref, crosses_ref, slots_ref)
    copies = [pltpu.make_async_copy(s, p, arrived.at[i]) for i, (s, p) in enumerate(zip(sources, places))]
    for copy in copies:
        copy.start()
    copies[0].wait()
    copies[1].wait()
    items_out(sends_ref, items_ref, out_ref)
    for copy in copies[2:]:
        copy.wait()
    face, bricks = (sides_ref.shape[1], slots_ref.shape[1])
    lists_ref[...] = jnp.zeros(lists_ref.shape, I32)
    lists_ref[0:2, :face] = sides_ref[...]
    lists_ref[2:4, :face] = crosses_ref[...]
    lists_ref[4:5, :bricks] = slots_ref[...]
    table_grad(cot_ref, weight_ref, near_ref, ext_ref, low_ref, high_ref, band_ref, pad_ref)


def conv_body(
    merged_ref, low_ref, high_ref, below_ref, above_ref, cot_ref, weight_ref, near_ref,
    out_ref, back_ref, band_ref, pad_ref, table_ref,
):
    bricks = merged_ref.shape[0]
    face = below_ref.shape[0]
    rows = bricks + 4 * face
    build_bands(weight_ref, band_ref)
    table_ref[:bricks] = merged_ref[...]
    table_ref[bricks:] = stack_rows(
        low_ref[...].astype(F32)[:face], high_ref[...].astype(F32)[:face], below_ref[...], above_ref[...]
    )
    near = jnp.concatenate([near_ref[o] for o in range(27)] + [jnp.zeros((5, bricks), I32)], axis=0)
    near = near.astype(F32).T.astype(I32)

    def one_of(dx, dy, dz):
        o = offset_of(dx, dy, dz)
        return near[:, o : o + 1]

    place = iota((bricks, rows), 1)
    pair_place = iota((bricks, 2 * rows), 1)
    lower_half = iota((rows, 2 * C), 1) < C
    zero = jnp.zeros((rows, 2 * C), BF)
    cache = {}
    for x in range(4):
        for y in range(4):
            places = [(X, Y, dx, dy) for X, dx in options(x) for Y, dy in options(y)]
            for _, _, dx, dy in places:
                if (dx, dy) not in cache:
                    main = ones_where(place == one_of(dx, dy, 0))
                    ends = jnp.where(pair_place < rows, one_of(dx, dy, 1), one_of(dx, dy, -1) + rows)
                    cache[dx, dy] = (main, ones_where(pair_place == ends))
            at = (x * 4 + y) * RUN
            columns = table_ref[:, at : at + RUN]
            first = jnp.where(lower_half, columns[:, : 2 * C], zero)
            second = jnp.where(lower_half, zero, columns[:, 2 * C :])
            ends = jnp.concatenate([cache[dx, dy][1] for _, _, dx, dy in places], axis=0)
            halo = dot(ends, jnp.concatenate([first, second], axis=0)).astype(BF)
            for i, (X, Y, _, _) in enumerate(places):
                pad_ref[X, Y, :, RUN:] = halo[i * bricks : (i + 1) * bricks]
            pad_ref[x + 1, y + 1, :, :RUN] = columns[:bricks]
            moved = [p for p in places if p[2:] != (0, 0)]
            if moved:
                main = jnp.concatenate([cache[dx, dy][0] for _, _, dx, dy in moved], axis=0)
                got = dot(main, columns).astype(BF)
                for i, (X, Y, _, _) in enumerate(moved):
                    pad_ref[X, Y, :, :RUN] = got[i * bricks : (i + 1) * bricks]

    turned = stack_runs(cot_ref).T
    total = None
    lanes_low = iota((C, 2 * C), 1) < C
    sums = []
    for e in range(9):
        ex, ey = (e // 3, e % 3)
        inputs = pad_ref[ex : ex + 4, ey : ey + 4].reshape(16 * bricks, WIDE)
        part = dot(inputs, band_ref[e])
        total = part if total is None else total + part
        wide = dot(turned, inputs)

        def block(z, s):
            return wide[z * C : (z + 1) * C, s * 2 * C : (s + 1) * 2 * C]

        low = jnp.where(lanes_low, block(1, 0) + block(3, 1), block(0, 2) + block(2, 0))
        mid = jnp.where(lanes_low, block(0, 0) + block(2, 1), block(1, 0) + block(3, 1))
        high = jnp.where(lanes_low, block(1, 1) + block(3, 2), block(0, 0) + block(2, 1))
        for value in (low, mid, high):
            sums.append(value + pltpu.roll(value, C, 1))
    sums.append(jnp.zeros((C, 2 * C), F32))
    for p in range(16):
        out_ref[:, p * RUN : (p + 1) * RUN] = total[p * bricks : (p + 1) * bricks].astype(BF)
    for pair in range(7):
        both = [jnp.where(lanes_low, sums[14 * h + 2 * pair], sums[14 * h + 2 * pair + 1]) for h in range(2)]
        at = pair * 2 * C
        back_ref[:, at : at + 2 * C] = jnp.concatenate(both, axis=0).astype(BF)


def add_rows(base, lists, first, second):
    count, face = (base.shape[0], lists.shape[1])
    index = jnp.concatenate([lists[0:1], lists[1:2]], axis=1)
    chosen = ones_where(iota((count, 2 * face), 0) == index)
    return base + dot(chosen, stack_rows(first, second))


def merge_body(
    received_ref, up_ref, fine_ref, lists_ref, ext_ref, next_ref, prev_ref,
    merged_ref, parents_ref, part_ref, a_ref, b_ref,
):
    bricks, face = (fine_ref.shape[0], next_ref.shape[0])
    total = add_rows(ext_ref[...], crosses_of(lists_ref, face), next_ref[...], prev_ref[...])
    part_ref[...] = total[:bricks]
    merge(received_ref, slots_of(lists_ref, bricks), up_ref, fine_ref, merged_ref, parents_ref)
    first, second = pick_rows(sides_of(lists_ref, face), merged_ref[...])
    a_ref[...] = stack_rows(first, total[bricks + face :])
    b_ref[...] = stack_rows(second, total[bricks : bricks + face])


def fine_grad_body(part_ref, lists_ref, next_ref, prev_ref, up_ref, parents_ref, grad_ref, back_ref):
    bricks = part_ref.shape[0]
    face = next_ref.shape[0] // 2
    grad_ref[...] = add_rows(
        part_ref[...], sides_of(lists_ref, face), next_ref[...].astype(F32)[face:], prev_ref[...].astype(F32)[face:]
    ).astype(BF)
    stacked = []
    for v in range(8):
        cx, cy, cz = (v // 4, v // 2 % 2, v % 2)
        lanes = []
        for parity in range(4):
            at = ((2 * cx + parity // 2) * 4 + 2 * cy + parity % 2) * RUN + cz * 2 * C
            lanes.append(grad_ref[:, at : at + 2 * C])
        stacked.append(jnp.concatenate(lanes, axis=1))
    stacked = jnp.concatenate(stacked, axis=0)
    items = dot(stacked, up_ref[...]).astype(BF)
    items = jnp.concatenate([items[v * bricks : (v + 1) * bricks] for v in range(8)], axis=1)
    half = items.shape[1] // 2
    count = back_ref.shape[0]
    up_sum = dot_tn(stacked, parents_ref[...]).astype(BF)
    coarse = up_sum.shape[1]
    parts = up_sum.shape[0] // count
    item_lanes = back_ref.shape[1] - parts * coarse
    for q in range(parts):
        at = item_lanes + q * coarse
        back_ref[:, at : at + coarse] = up_sum[q * count : (q + 1) * count]
    slots = slots_of(lists_ref, bricks)
    for j in range(item_lanes // half):
        piece = iota((count, bricks), 0) * (item_lanes // half) + j
        named = piece // 2 == slots
        rows = dot(ones_where(named & (piece % 2 == 0)), items[:, :half])
        rows += dot(ones_where(named & (piece % 2 == 1)), items[:, half:])
        back_ref[:, j * half : (j + 1) * half] = rows.astype(BF)


def share_body(back_ref, conv_ref, out_ref, devices):
    count, width = out_ref.shape
    conv_width = conv_ref.shape[1]
    up_width = width - conv_width
    share = count // devices
    same = ones_where(iota((count, count), 0) % share == iota((count, count), 1) % share)
    out_ref[:, :up_width] = dot(same, back_ref[:, back_ref.shape[1] - up_width :]).astype(BF)
    out_ref[:, up_width:] = dot(same, conv_ref[...]).astype(BF)


def coarse_grad_body(back_ref, sends_ref, out_ref):
    capacity, devices = sends_ref.shape
    count, item_width = out_ref.shape
    half = item_width // 2
    lanes = back_ref.shape[0]
    pieces = 2 * capacity * devices // lanes
    group = lanes // devices
    for h in range(2):
        total = None
        for j in range(pieces):
            index = send_index(sends_ref[...], group, pieces, j)
            place = iota((count, lanes), 1) % group * pieces + j
            chosen = (iota((count, lanes), 0) == index) & (place % 2 == h)
            part = dot(ones_where(chosen), back_ref[:, j * half : (j + 1) * half])
            total = part if total is None else total + part
        out_ref[:, h * half : (h + 1) * half] = total.astype(BF)


def final_body(totals_ref, conv_ref, up_ref, scale):
    count = totals_ref.shape[0]
    coarse = up_ref.shape[1]
    parts = up_ref.shape[0] // count
    for q in range(parts):
        up_ref[q * count : (q + 1) * count] = totals_ref[:, q * coarse : (q + 1) * coarse].astype(F32) * scale
    for pair in range(7):
        at = parts * coarse + pair * 2 * C
        turned = totals_ref[:, at : at + 2 * C].astype(F32).T * scale
        for h in range(2):
            for s in range(2):
                o = 14 * h + 2 * pair + s
                if o < 27:
                    conv_ref[o] = turned[s * C : (s + 1) * C, h * C : (h + 1) * C]


def passed_along(value, axis, steps):
    count = lax.axis_size(axis)
    initial, last = (max(0, -steps), min(count, count - steps))
    return lax.ppermute(value, axis, [(source, source + steps) for source in range(initial, last)])


def trade_rows(values, devices):
    rows, width = values.shape
    grid_view = values.reshape(devices, rows // devices, width)
    return lax.all_to_all(grid_view, ("gx", "gy"), split_axis=0, concat_axis=0, tiled=True).reshape(rows, width)


def on_device(
    fine_features, coarse_items, conv_weight, up_weight, neighbours,
    side_sends, cross_sends, parent_slots, coarse_sends, cotangent,
):
    fine = fine_features[0, 0]
    items = coarse_items[0, 0]
    cot = cotangent[0, 0]
    bricks, width = fine.shape
    face = side_sends.shape[-1]
    across_x, across_y = (lax.axis_size("gx"), lax.axis_size("gy"))
    devices = across_x * across_y
    capacity = coarse_sends.shape[-1]
    item_count, item_width = items.shape
    coarse = up_weight.shape[1]
    start = bricks + 2 * face
    sends = coarse_sends.transpose(0, 1, 3, 2)[0, 0]
    slots = parent_slots[0]
    sides = side_sends[0, 0]
    crosses = cross_sends[0, 0]
    near = neighbours.transpose(0, 3, 1, 2)[0]
    up_turned = up_weight.transpose(0, 2, 1).reshape(8 * C, coarse)
    half = item_width // 2
    count = 2 * C
    up_width = 8 * C * coarse // count
    back_width = capacity * devices * item_width // count + up_width
    band = pltpu.VMEM((9, WIDE, RUN), BF)
    face_rows = shape((face, width))
    two_faces = shape((2 * face, width))
    conv_flops = 2 * 9 * 16 * bricks * WIDE * RUN

    loaded = (sends, items, conv_weight, cot, near, sides, crosses, slots)
    outgoing, ext_grad, low_cross, high_cross, lists = call(
        first_body,
        [shape((2 * capacity * devices, half)), shape((start, width), F32), face_rows, face_rows, shape((8, 128), I32)],
        *loaded,
        scratch=[pltpu.VMEM(a.shape, a.dtype) for a in loaded]
        + [band, pltpu.VMEM((6, 6, bricks, WIDE), F32), pltpu.SemaphoreType.DMA((len(loaded),))],
        flops=2 * conv_flops,
        in_hbm=True,
    )
    received = trade_rows(outgoing, devices)
    grad_prev = passed_along(high_cross, "gx", 1)
    grad_next = passed_along(low_cross, "gx", -1)
    merged, parents, fine_part, to_next, to_prev = call(
        merge_body,
        [shape((bricks, width)), shape((8 * bricks, coarse)), shape((bricks, width), F32), two_faces, two_faces],
        received, up_turned, fine, lists, ext_grad, grad_next, grad_prev,
    )
    low_side = passed_along(to_next, "gy", 1)
    high_side = passed_along(to_prev, "gy", -1)
    to_next, to_prev = call(cross_body, [face_rows, face_rows], merged, low_side, high_side, lists)
    below = passed_along(to_next, "gx", 1)
    above = passed_along(to_prev, "gx", -1)
    grad_fine, back = call(
        fine_grad_body, [shape((bricks, width)), shape((count, back_width))],
        fine_part, lists, high_side, low_side, up_turned, parents,
    )
    back = trade_rows(back, devices)
    output, conv_sum = call(
        conv_body, [shape((bricks, width)), shape((count, 14 * C))],
        merged, low_side, high_side, below, above, cot, conv_weight, near,
        scratch=[band, pltpu.VMEM((6, 6, bricks, WIDE), BF), pltpu.VMEM((bricks + 4 * face, width), BF)],
        flops=2 * conv_flops,
    )
    conv_sum = trade_rows(conv_sum, devices)
    (sums,) = call(
        functools.partial(share_body, devices=devices), [shape((count, up_width + 14 * C))], back, conv_sum
    )
    totals = trade_rows(sums, devices)
    (coarse_grad,) = call(coarse_grad_body, [shape((item_count, item_width))], back, sends)
    scale = 1.0 / math.sqrt(64 * bricks * devices)
    grad_conv, grad_up = call(
        functools.partial(final_body, scale=scale),
        [shape((27, C, C), F32), shape((8 * C, coarse), F32)], totals,
    )
    return (
        output.reshape(1, 1, bricks, width),
        grad_fine.reshape(1, 1, bricks, width),
        coarse_grad.reshape(1, 1, item_count, item_width),
        grad_conv,
        grad_up.reshape(8, C, coarse).transpose(0, 2, 1),
    )


def solution(mesh):
    split = P(("groups", "gx"), "gy", None, None)
    placed = (split, split, P(), P(), split, split, split, P(("groups", "gx"), "gy", None), split, split)
    return jax.shard_map(
        on_device,
        mesh=mesh,
        in_specs=placed,
        out_specs=(split, split, split, P("groups", None, None), P("groups", None, None)),
        check_vma=False,
    )
```

```python
import functools
import math

import jax
import jax.numpy as jnp
from jax import lax
from jax.experimental import pallas as pl
from jax.experimental.pallas import tpu as pltpu
from jax.sharding import PartitionSpec as P

BF = jnp.bfloat16
F32 = jnp.float32
I32 = jnp.int32

C = 64
RUN = 4 * C
WIDE = RUN + 2 * C


def iota(shape, axis):
    return lax.broadcasted_iota(I32, shape, axis)


def ones_where(mask):
    return jnp.where(mask, 1.0, 0.0).astype(BF)


def dot(a, b):
    return jnp.dot(a, b, preferred_element_type=F32)


def dot_tn(a, b):
    return lax.dot_general(a, b, (((0,), (0,)), ((), ())), preferred_element_type=F32)


def dot_nt(a, b):
    return lax.dot_general(a, b, (((1,), (1,)), ((), ())), preferred_element_type=F32)


def column_of(row):
    size = row.shape[1]
    diagonal = iota((size, size), 0) == iota((size, size), 1)
    spread = jnp.broadcast_to(row.astype(F32), (size, size))
    return jnp.sum(jnp.where(diagonal, spread, 0.0), axis=1, keepdims=True).astype(I32)


def call(body, outs, *args, scratch=(), flops=0, in_hbm=False):
    moved = sum(a.size * a.dtype.itemsize for a in list(args) + list(outs))
    return pl.pallas_call(
        body,
        out_shape=tuple(outs),
        in_specs=[pl.BlockSpec(memory_space=pltpu.HBM) if in_hbm else pl.BlockSpec() for _ in args],
        scratch_shapes=tuple(scratch),
        cost_estimate=pl.CostEstimate(flops=flops, bytes_accessed=moved, transcendentals=0),
        compiler_params=pltpu.CompilerParams(vmem_limit_bytes=28 * 2**20),
    )(*args)


def shape(dims, dtype=BF):
    return jax.ShapeDtypeStruct(dims, dtype)


def send_index(sends, group, pieces=1, j=0):
    capacity, devices = sends.shape
    lanes = devices * group
    spread = ones_where(iota((devices, lanes), 1) // group == iota((devices, lanes), 0))
    rows = dot(sends.astype(F32).astype(BF), spread)
    slot = (iota((capacity, lanes), 1) % group * pieces + j) // 2
    picked = jnp.where(slot == iota((capacity, lanes), 0), rows, 0.0)
    return jnp.sum(picked, axis=0, keepdims=True).astype(I32)


def items_out(sends_ref, items_ref, out_ref):
    capacity, devices = sends_ref.shape
    count, width = items_ref.shape
    half = width // 2
    index = send_index(sends_ref[...], 2 * capacity)
    lanes = index.shape[1]
    odd = iota((count, lanes), 1) % 2
    named = iota((count, lanes), 0) == index
    total = dot_tn(ones_where(named & (odd == 0)), items_ref[:, :half])
    total += dot_tn(ones_where(named & (odd == 1)), items_ref[:, half:])
    out_ref[...] = total.astype(BF)


def merge(received_ref, slots, up_ref, fine_ref, merged_ref, parents_ref):
    bricks = fine_ref.shape[0]
    lanes, half = received_ref.shape
    slot = column_of(slots)
    place = iota((bricks, lanes), 1)
    named = place // 2 == slot
    received = received_ref[...]
    parents = jnp.concatenate(
        [dot(ones_where(named & (place % 2 == h)), received) for h in (0, 1)], axis=1
    ).astype(BF)
    coarse = 2 * half // 8
    stacked = jnp.concatenate([parents[:, v * coarse : (v + 1) * coarse] for v in range(8)], axis=0)
    parents_ref[...] = stacked
    lifted = dot_nt(stacked, up_ref[...])
    for v in range(8):
        cx, cy, cz = (v // 4, v // 2 % 2, v % 2)
        for parity in range(4):
            vx, vy = (2 * cx + parity // 2, 2 * cy + parity % 2)
            at = (vx * 4 + vy) * RUN + cz * 2 * C
            add = lifted[v * bricks : (v + 1) * bricks, parity * 2 * C : (parity + 1) * 2 * C]
            merged_ref[:, at : at + 2 * C] = (fine_ref[:, at : at + 2 * C].astype(F32) + add).astype(BF)


def pick_rows(lists, rows):
    place = iota((rows.shape[0], lists.shape[1]), 0)
    return [dot_tn(ones_where(place == lists[w : w + 1]), rows) for w in (0, 1)]


def stack_rows(*parts):
    return jnp.concatenate([p.astype(F32) for p in parts], axis=0).astype(BF)


def sides_of(lists_ref, face):
    return lists_ref[0:2, :face]


def crosses_of(lists_ref, face):
    return lists_ref[2:4, :face]


def slots_of(lists_ref, bricks):
    return lists_ref[4:5, :bricks]


def cross_body(merged_ref, low_ref, high_ref, lists_ref, a_ref, b_ref, again_ref):
    again_ref[...] = lists_ref[...]
    face = a_ref.shape[0]
    sides = stack_rows(low_ref[...].astype(F32)[:face], high_ref[...].astype(F32)[:face])
    rows = jnp.concatenate([merged_ref[...], sides], axis=0)
    first, second = pick_rows(crosses_of(lists_ref, face), rows)
    a_ref[...] = first.astype(BF)
    b_ref[...] = second.astype(BF)


def build_bands(weight_ref, band_ref):
    zero = jnp.zeros((C, C), BF)
    blank = jnp.zeros((C, 2 * C), BF)

    def pair(a, b):
        return jnp.concatenate([a, b], axis=1)

    for e in range(9):
        low, mid, high = (weight_ref[3 * e + z] for z in range(3))
        first, second = (pair(mid, low), pair(high, mid))
        left, right = (pair(low, zero), pair(zero, high))
        rows = (
            (first, blank),
            (second, left),
            (right, first),
            (blank, second),
            (blank, right),
            (left, blank),
        )
        for z, halves in enumerate(rows):
            for s in range(2):
                band_ref[e, z * C : (z + 1) * C, s * 2 * C : (s + 1) * 2 * C] = halves[s]


def options(at):
    return [(at + 1, 0)] + ([(5, 1)] if at == 0 else []) + ([(0, -1)] if at == 3 else [])


def offset_of(dx, dy, dz):
    return (dx + 1) * 9 + (dy + 1) * 3 + dz + 1


def stack_runs(ref):
    return jnp.concatenate([ref[:, p * RUN : (p + 1) * RUN] for p in range(16)], axis=0)


def split_two(value):
    head = value.astype(BF)
    return head, (value - head.astype(F32)).astype(BF)


def table_grad_body(cot_ref, weight_ref, near_ref, ext_ref, low_ref, high_ref, band_ref, pad_ref):
    bricks = cot_ref.shape[0]
    face = low_ref.shape[0]
    start = ext_ref.shape[0]
    rows = start + 2 * face
    build_bands(weight_ref, band_ref)
    cot = stack_runs(cot_ref)
    pad_ref[...] = jnp.zeros(pad_ref.shape, F32)
    for e in range(9):
        ex, ey = (e // 3, e % 3)
        part = dot_nt(cot, band_ref[e]).reshape(4, 4, bricks, WIDE)
        pad_ref[ex : ex + 4, ey : ey + 4] += part
    near = [near_ref[o] for o in range(27)]

    def chooser(which):
        index = jnp.concatenate([near[o] for o in which], axis=1)
        return ones_where(iota((rows, index.shape[1]), 0) == index)

    lower_half = iota((rows, 2 * C), 1) < C
    cache = {}
    for x in range(4):
        for y in range(4):
            places = [(X, Y, dx, dy) for X, dx in options(x) for Y, dy in options(y)]
            key = tuple((dx, dy) for _, _, dx, dy in places)
            if key not in cache:
                moved = [d for d in key if d != (0, 0)]
                main = chooser([offset_of(*d, 0) for d in moved] * 2) if moved else None
                up = chooser([offset_of(*d, 1) for d in key] * 2)
                down = chooser([offset_of(*d, -1) for d in key] * 2)
                cache[key] = (main, jnp.concatenate([up, down], axis=0))
            main, ends = cache[key]
            own = pad_ref[x + 1, y + 1, :, :RUN]
            own = jnp.concatenate([own, jnp.zeros((rows - bricks, RUN), F32)], axis=0)
            if main is not None:
                parts = [split_two(pad_ref[X, Y, :, :RUN]) for X, Y, dx, dy in places if (dx, dy) != (0, 0)]
                value = jnp.concatenate([p[0] for p in parts] + [p[1] for p in parts], axis=0)
                own += dot(main, value)
            parts = [split_two(pad_ref[X, Y, :, RUN:]) for X, Y, _, _ in places]
            value = jnp.concatenate([p[0] for p in parts] + [p[1] for p in parts], axis=0)
            halo = dot(ends, value)
            first = own[:, : 2 * C] + jnp.where(lower_half, halo[:rows], 0.0)
            second = own[:, 2 * C :] + jnp.where(lower_half, 0.0, halo[rows:])
            total = jnp.concatenate([first, second], axis=1)
            at = (x * 4 + y) * RUN
            ext_ref[:, at : at + RUN] = total[:start]
            low_ref[:, at : at + RUN] = total[start : start + face].astype(BF)
            high_ref[:, at : at + RUN] = total[start + face :].astype(BF)


def first_body(
    sends_hbm, items_hbm, sides_hbm, crosses_hbm, slots_hbm, weight_hbm, cot_hbm, near_hbm, fine_hbm, up_hbm,
    out_ref, lists_ref, weight_ref, cot_ref, near_ref, fine_ref, up_ref,
    sends_ref, items_ref, sides_ref, crosses_ref, slots_ref, arrived,
):
    sources = (
        sends_hbm, items_hbm, sides_hbm, crosses_hbm, slots_hbm, weight_hbm, cot_hbm, near_hbm, fine_hbm, up_hbm,
    )
    places = (sends_ref, items_ref, sides_ref, crosses_ref, slots_ref, weight_ref, cot_ref, near_ref, fine_ref, up_ref)
    copies = [pltpu.make_async_copy(s, p, arrived.at[i]) for i, (s, p) in enumerate(zip(sources, places))]
    for copy in copies:
        copy.start()
    copies[0].wait()
    copies[1].wait()
    items_out(sends_ref, items_ref, out_ref)
    for copy in copies[2:]:
        copy.wait()
    face, bricks = (sides_ref.shape[1], slots_ref.shape[1])
    lists_ref[...] = jnp.zeros(lists_ref.shape, I32)
    lists_ref[0:2, :face] = sides_ref[...]
    lists_ref[2:4, :face] = crosses_ref[...]
    lists_ref[4:5, :bricks] = slots_ref[...]


def weight_grad_body(
    merged_ref, low_ref, high_ref, below_ref, above_ref, turned_ref, near_ref, part_ref, back_ref, pad_ref, table_ref
):
    bricks = merged_ref.shape[0]
    face = below_ref.shape[0]
    rows = bricks + 4 * face
    table_ref[:bricks] = merged_ref[...]
    table_ref[bricks:] = stack_rows(
        low_ref[...].astype(F32)[:face], high_ref[...].astype(F32)[:face], below_ref[...], above_ref[...]
    )
    back_ref[:, : part_ref.shape[1]] = part_ref[...]
    near = jnp.concatenate([near_ref[o] for o in range(27)] + [jnp.zeros((5, bricks), I32)], axis=0)
    near = near.astype(F32).T.astype(I32)

    def one_of(dx, dy, dz):
        o = offset_of(dx, dy, dz)
        return near[:, o : o + 1]

    place = iota((bricks, rows), 1)
    pair_place = iota((bricks, 2 * rows), 1)
    lower_half = iota((rows, 2 * C), 1) < C
    zero = jnp.zeros((rows, 2 * C), BF)
    cache = {}
    for x in range(4):
        for y in range(4):
            places = [(X, Y, dx, dy) for X, dx in options(x) for Y, dy in options(y)]
            for _, _, dx, dy in places:
                if (dx, dy) not in cache:
                    main = ones_where(place == one_of(dx, dy, 0))
                    ends = jnp.where(pair_place < rows, one_of(dx, dy, 1), one_of(dx, dy, -1) + rows)
                    cache[dx, dy] = (main, ones_where(pair_place == ends))
            at = (x * 4 + y) * RUN
            columns = table_ref[:, at : at + RUN]
            first = jnp.where(lower_half, columns[:, : 2 * C], zero)
            second = jnp.where(lower_half, zero, columns[:, 2 * C :])
            ends = jnp.concatenate([cache[dx, dy][1] for _, _, dx, dy in places], axis=0)
            halo = dot(ends, jnp.concatenate([first, second], axis=0)).astype(BF)
            for i, (X, Y, _, _) in enumerate(places):
                pad_ref[X, Y, :, RUN:] = halo[i * bricks : (i + 1) * bricks]
            pad_ref[x + 1, y + 1, :, :RUN] = columns[:bricks]
            moved = [p for p in places if p[2:] != (0, 0)]
            if moved:
                main = jnp.concatenate([cache[dx, dy][0] for _, _, dx, dy in moved], axis=0)
                got = dot(main, columns).astype(BF)
                for i, (X, Y, _, _) in enumerate(moved):
                    pad_ref[X, Y, :, :RUN] = got[i * bricks : (i + 1) * bricks]

    turned = turned_ref[...]
    lanes_low = iota((C, 2 * C), 1) < C
    sums = []
    for e in range(9):
        wide = dot(turned, inputs_at(pad_ref, e))

        def block(z, s):
            return wide[z * C : (z + 1) * C, s * 2 * C : (s + 1) * 2 * C]

        low = jnp.where(lanes_low, block(1, 0) + block(3, 1), block(0, 2) + block(2, 0))
        mid = jnp.where(lanes_low, block(0, 0) + block(2, 1), block(1, 0) + block(3, 1))
        high = jnp.where(lanes_low, block(1, 1) + block(3, 2), block(0, 0) + block(2, 1))
        for value in (low, mid, high):
            sums.append(value + pltpu.roll(value, C, 1))
    sums.append(jnp.zeros((C, 2 * C), F32))
    for pair in range(7):
        both = [jnp.where(lanes_low, sums[14 * h + 2 * pair], sums[14 * h + 2 * pair + 1]) for h in range(2)]
        at = part_ref.shape[1] + pair * 2 * C
        back_ref[:, at : at + 2 * C] = jnp.concatenate(both, axis=0).astype(BF)


def inputs_at(pad_ref, e):
    bricks = pad_ref.shape[2]
    ex, ey = (e // 3, e % 3)
    return pad_ref[ex : ex + 4, ey : ey + 4].reshape(16 * bricks, WIDE)


def conv_body(pad_ref, band_ref, out_ref):
    bricks = pad_ref.shape[2]
    total = None
    for e in range(9):
        part = dot(inputs_at(pad_ref, e), band_ref[e])
        total = part if total is None else total + part
    for p in range(16):
        out_ref[:, p * RUN : (p + 1) * RUN] = total[p * bricks : (p + 1) * bricks].astype(BF)


def add_rows(base, lists, first, second):
    count, face = (base.shape[0], lists.shape[1])
    index = jnp.concatenate([lists[0:1], lists[1:2]], axis=1)
    chosen = ones_where(iota((count, 2 * face), 0) == index)
    return base + dot(chosen, stack_rows(first, second))


def merge_body(
    received_ref, up_ref, fine_ref, lists_ref, ext_ref, next_ref, prev_ref,
    merged_ref, parents_ref, part_ref, a_ref, b_ref,
):
    bricks, face = (fine_ref.shape[0], next_ref.shape[0])
    total = add_rows(ext_ref[...], crosses_of(lists_ref, face), next_ref[...], prev_ref[...])
    part_ref[...] = total[:bricks]
    merge(received_ref, slots_of(lists_ref, bricks), up_ref, fine_ref, merged_ref, parents_ref)
    first, second = pick_rows(sides_of(lists_ref, face), merged_ref[...])
    a_ref[...] = stack_rows(first, total[bricks + face :])
    b_ref[...] = stack_rows(second, total[bricks : bricks + face])


def fine_grad_body(
    part_ref, lists_ref, next_ref, prev_ref, up_ref, parents_ref, cot_ref, grad_ref, back_ref, turned_ref
):
    turned_ref[...] = stack_runs(cot_ref).T
    bricks = part_ref.shape[0]
    face = next_ref.shape[0] // 2
    grad_ref[...] = add_rows(
        part_ref[...], sides_of(lists_ref, face), next_ref[...].astype(F32)[face:], prev_ref[...].astype(F32)[face:]
    ).astype(BF)
    stacked = []
    for v in range(8):
        cx, cy, cz = (v // 4, v // 2 % 2, v % 2)
        lanes = []
        for parity in range(4):
            at = ((2 * cx + parity // 2) * 4 + 2 * cy + parity % 2) * RUN + cz * 2 * C
            lanes.append(grad_ref[:, at : at + 2 * C])
        stacked.append(jnp.concatenate(lanes, axis=1))
    stacked = jnp.concatenate(stacked, axis=0)
    items = dot(stacked, up_ref[...]).astype(BF)
    items = jnp.concatenate([items[v * bricks : (v + 1) * bricks] for v in range(8)], axis=1)
    half = items.shape[1] // 2
    count = back_ref.shape[0]
    up_sum = dot_tn(stacked, parents_ref[...]).astype(BF)
    coarse = up_sum.shape[1]
    parts = up_sum.shape[0] // count
    item_lanes = back_ref.shape[1] - parts * coarse
    for q in range(parts):
        at = item_lanes + q * coarse
        back_ref[:, at : at + coarse] = up_sum[q * count : (q + 1) * count]
    slots = slots_of(lists_ref, bricks)
    for j in range(item_lanes // half):
        piece = iota((count, bricks), 0) * (item_lanes // half) + j
        named = piece // 2 == slots
        rows = dot(ones_where(named & (piece % 2 == 0)), items[:, :half])
        rows += dot(ones_where(named & (piece % 2 == 1)), items[:, half:])
        back_ref[:, j * half : (j + 1) * half] = rows.astype(BF)


def share_body(back_ref, out_ref, devices):
    count, width = out_ref.shape
    share = count // devices
    same = ones_where(iota((count, count), 0) % share == iota((count, count), 1) % share)
    out_ref[...] = dot(same, back_ref[:, back_ref.shape[1] - width :]).astype(BF)


def coarse_grad_body(back_ref, sends_ref, out_ref):
    capacity, devices = sends_ref.shape
    count, item_width = out_ref.shape
    half = item_width // 2
    lanes = back_ref.shape[0]
    pieces = 2 * capacity * devices // lanes
    group = lanes // devices
    for h in range(2):
        total = None
        for j in range(pieces):
            index = send_index(sends_ref[...], group, pieces, j)
            place = iota((count, lanes), 1) % group * pieces + j
            chosen = (iota((count, lanes), 0) == index) & (place % 2 == h)
            part = dot(ones_where(chosen), back_ref[:, j * half : (j + 1) * half])
            total = part if total is None else total + part
        out_ref[:, h * half : (h + 1) * half] = total.astype(BF)


def final_body(totals_ref, conv_ref, up_ref, scale):
    count = totals_ref.shape[0]
    coarse = up_ref.shape[1]
    parts = up_ref.shape[0] // count
    for q in range(parts):
        up_ref[q * count : (q + 1) * count] = totals_ref[:, q * coarse : (q + 1) * coarse].astype(F32) * scale
    for pair in range(7):
        at = parts * coarse + pair * 2 * C
        turned = totals_ref[:, at : at + 2 * C].astype(F32).T * scale
        for h in range(2):
            for s in range(2):
                o = 14 * h + 2 * pair + s
                if o < 27:
                    conv_ref[o] = turned[s * C : (s + 1) * C, h * C : (h + 1) * C]


def passed_along(value, axis, steps):
    count = lax.axis_size(axis)
    initial, last = (max(0, -steps), min(count, count - steps))
    return lax.ppermute(value, axis, [(source, source + steps) for source in range(initial, last)])


def trade_rows(values, devices):
    rows, width = values.shape
    grid_view = values.reshape(devices, rows // devices, width)
    return lax.all_to_all(grid_view, ("gx", "gy"), split_axis=0, concat_axis=0, tiled=True).reshape(rows, width)


def on_device(
    fine_features, coarse_items, conv_weight, up_weight, neighbours,
    side_sends, cross_sends, parent_slots, coarse_sends, cotangent,
):
    fine = fine_features[0, 0]
    items = coarse_items[0, 0]
    cot = cotangent[0, 0]
    bricks, width = fine.shape
    face = side_sends.shape[-1]
    across_x, across_y = (lax.axis_size("gx"), lax.axis_size("gy"))
    devices = across_x * across_y
    capacity = coarse_sends.shape[-1]
    item_count, item_width = items.shape
    coarse = up_weight.shape[1]
    start = bricks + 2 * face
    sends = coarse_sends.transpose(0, 1, 3, 2)[0, 0]
    slots = parent_slots[0]
    sides = side_sends[0, 0]
    crosses = cross_sends[0, 0]
    near = neighbours.transpose(0, 3, 1, 2)[0]
    up_turned = up_weight.transpose(0, 2, 1).reshape(8 * C, coarse)
    half = item_width // 2
    count = 2 * C
    up_width = 8 * C * coarse // count
    back_width = capacity * devices * item_width // count + up_width
    face_rows = shape((face, width))
    two_faces = shape((2 * face, width))
    conv_flops = 2 * 9 * 16 * bricks * WIDE * RUN

    listed = (sends, items, sides, crosses, slots)
    kept = (conv_weight, cot, near, fine, up_turned)
    outgoing, lists, weight, cot, near, fine, up_turned = call(
        first_body,
        [shape((2 * capacity * devices, half)), shape((8, 128), I32)] + [shape(a.shape, a.dtype) for a in kept],
        *listed, *kept,
        scratch=[pltpu.VMEM(a.shape, a.dtype) for a in listed]
        + [pltpu.SemaphoreType.DMA((len(listed) + len(kept),))],
        in_hbm=True,
    )
    received = trade_rows(outgoing, devices)
    ext_grad, low_cross, high_cross, band = call(
        table_grad_body,
        [shape((start, width), F32), face_rows, face_rows, shape((9, WIDE, RUN))],
        cot, weight, near, scratch=[pltpu.VMEM((6, 6, bricks, WIDE), F32)], flops=2 * conv_flops,
    )
    grad_prev = passed_along(high_cross, "gx", 1)
    grad_next = passed_along(low_cross, "gx", -1)
    merged, parents, fine_part, to_next, to_prev = call(
        merge_body,
        [shape((bricks, width)), shape((8 * bricks, coarse)), shape((bricks, width), F32), two_faces, two_faces],
        received, up_turned, fine, lists, ext_grad, grad_next, grad_prev,
    )
    low_side = passed_along(to_next, "gy", 1)
    high_side = passed_along(to_prev, "gy", -1)
    to_next, to_prev, lists = call(
        cross_body, [face_rows, face_rows, shape((8, 128), I32)], merged, low_side, high_side, lists
    )
    below = passed_along(to_next, "gx", 1)
    above = passed_along(to_prev, "gx", -1)
    grad_fine, part, turned = call(
        fine_grad_body,
        [shape((bricks, width)), shape((count, back_width)), shape((RUN, 16 * bricks))],
        fine_part, lists, high_side, low_side, up_turned, parents, cot,
    )
    back, pad = call(
        weight_grad_body, [shape((count, back_width + 14 * C)), shape((6, 6, bricks, WIDE))],
        merged, low_side, high_side, below, above, turned, near, part,
        scratch=[pltpu.VMEM((bricks + 4 * face, width), BF)], flops=conv_flops,
    )
    back = trade_rows(back, devices)
    (output,) = call(conv_body, [shape((bricks, width))], pad, band, flops=conv_flops)
    (sums,) = call(
        functools.partial(share_body, devices=devices), [shape((count, up_width + 14 * C))], back
    )
    totals = trade_rows(sums, devices)
    (coarse_grad,) = call(coarse_grad_body, [shape((item_count, item_width))], back, sends)
    scale = 1.0 / math.sqrt(64 * bricks * devices)
    grad_conv, grad_up = call(
        functools.partial(final_body, scale=scale),
        [shape((27, C, C), F32), shape((8 * C, coarse), F32)], totals,
    )
    return (
        output.reshape(1, 1, bricks, width),
        grad_fine.reshape(1, 1, bricks, width),
        coarse_grad.reshape(1, 1, item_count, item_width),
        grad_conv,
        grad_up.reshape(8, C, coarse).transpose(0, 2, 1),
    )


def solution(mesh):
    split = P(("groups", "gx"), "gy", None, None)
    placed = (split, split, P(), P(), split, split, split, P(("groups", "gx"), "gy", None), split, split)
    return jax.shard_map(
        on_device,
        mesh=mesh,
        in_specs=placed,
        out_specs=(split, split, split, P("groups", None, None), P("groups", None, None)),
        check_vma=False,
    )
```

```python
import functools
import math

import jax
import jax.numpy as jnp
from jax import lax
from jax.experimental import pallas as pl
from jax.experimental.pallas import tpu as pltpu
from jax.sharding import PartitionSpec as P

BF = jnp.bfloat16
F32 = jnp.float32
I32 = jnp.int32

C = 64
RUN = 4 * C
WIDE = RUN + 2 * C


def iota(shape, axis):
    return lax.broadcasted_iota(I32, shape, axis)


def ones_where(mask):
    return jnp.where(mask, 1.0, 0.0).astype(BF)


def dot(a, b):
    return jnp.dot(a, b, preferred_element_type=F32)


def dot_tn(a, b):
    return lax.dot_general(a, b, (((0,), (0,)), ((), ())), preferred_element_type=F32)


def dot_nt(a, b):
    return lax.dot_general(a, b, (((1,), (1,)), ((), ())), preferred_element_type=F32)


def column_of(row):
    size = row.shape[1]
    diagonal = iota((size, size), 0) == iota((size, size), 1)
    spread = jnp.broadcast_to(row.astype(F32), (size, size))
    return jnp.sum(jnp.where(diagonal, spread, 0.0), axis=1, keepdims=True).astype(I32)


def call(body, outs, *args, scratch=(), flops=0, in_hbm=False):
    moved = sum(a.size * a.dtype.itemsize for a in list(args) + list(outs))
    return pl.pallas_call(
        body,
        out_shape=tuple(outs),
        in_specs=[pl.BlockSpec(memory_space=pltpu.HBM) if in_hbm else pl.BlockSpec() for _ in args],
        scratch_shapes=tuple(scratch),
        cost_estimate=pl.CostEstimate(flops=flops, bytes_accessed=moved, transcendentals=0),
        compiler_params=pltpu.CompilerParams(vmem_limit_bytes=None if in_hbm else 28 * 2**20),
    )(*args)


def shape(dims, dtype=BF):
    return jax.ShapeDtypeStruct(dims, dtype)


def send_index(sends, group, pieces=1, j=0):
    capacity, devices = sends.shape
    lanes = devices * group
    spread = ones_where(iota((devices, lanes), 1) // group == iota((devices, lanes), 0))
    rows = dot(sends.astype(F32).astype(BF), spread)
    slot = (iota((capacity, lanes), 1) % group * pieces + j) // 2
    picked = jnp.where(slot == iota((capacity, lanes), 0), rows, 0.0)
    return jnp.sum(picked, axis=0, keepdims=True).astype(I32)


def items_out(sends_ref, items_ref, out_ref):
    capacity, devices = sends_ref.shape
    count, width = items_ref.shape
    half = width // 2
    index = send_index(sends_ref[...], 2 * capacity)
    lanes = index.shape[1]
    odd = iota((count, lanes), 1) % 2
    named = iota((count, lanes), 0) == index
    total = dot_tn(ones_where(named & (odd == 0)), items_ref[:, :half])
    total += dot_tn(ones_where(named & (odd == 1)), items_ref[:, half:])
    out_ref[...] = total.astype(BF)


def merge(received_ref, slots, up_ref, fine_ref, merged_ref, parents_ref):
    bricks = fine_ref.shape[0]
    lanes, half = received_ref.shape
    slot = column_of(slots)
    place = iota((bricks, lanes), 1)
    named = place // 2 == slot
    received = received_ref[...]
    parents = jnp.concatenate(
        [dot(ones_where(named & (place % 2 == h)), received) for h in (0, 1)], axis=1
    ).astype(BF)
    coarse = 2 * half // 8
    stacked = jnp.concatenate([parents[:, v * coarse : (v + 1) * coarse] for v in range(8)], axis=0)
    parents_ref[...] = stacked
    lifted = dot_nt(stacked, up_ref[...])
    for v in range(8):
        cx, cy, cz = (v // 4, v // 2 % 2, v % 2)
        for parity in range(4):
            vx, vy = (2 * cx + parity // 2, 2 * cy + parity % 2)
            at = (vx * 4 + vy) * RUN + cz * 2 * C
            add = lifted[v * bricks : (v + 1) * bricks, parity * 2 * C : (parity + 1) * 2 * C]
            merged_ref[:, at : at + 2 * C] = (fine_ref[:, at : at + 2 * C].astype(F32) + add).astype(BF)
    return parents


def pick_rows(lists, rows):
    place = iota((rows.shape[0], lists.shape[1]), 0)
    return [dot_tn(ones_where(place == lists[w : w + 1]), rows) for w in (0, 1)]


def stack_rows(*parts):
    return jnp.concatenate([p.astype(F32) for p in parts], axis=0).astype(BF)


def sides_of(lists_ref, face):
    return lists_ref[0:2, :face]


def crosses_of(lists_ref, face):
    return lists_ref[2:4, :face]


def slots_of(lists_ref, bricks):
    return lists_ref[4:5, :bricks]


def cross_body(merged_ref, low_ref, high_ref, lists_ref, low_grad_ref, high_grad_ref, a_ref, b_ref):
    face, width = low_grad_ref.shape
    rows = jnp.concatenate([merged_ref[...], stack_rows(low_ref[:, :width], high_ref[:, :width])], axis=0)
    first, second = pick_rows(crosses_of(lists_ref, face), rows)
    a_ref[...] = stack_rows(first, high_grad_ref[...])
    b_ref[...] = stack_rows(second, low_grad_ref[...])


def build_bands(weight_ref, band_ref):
    zero = jnp.zeros((C, C), BF)
    blank = jnp.zeros((C, 2 * C), BF)

    def pair(a, b):
        return jnp.concatenate([a, b], axis=1)

    for e in range(9):
        low, mid, high = (weight_ref[3 * e + z] for z in range(3))
        first, second = (pair(mid, low), pair(high, mid))
        left, right = (pair(low, zero), pair(zero, high))
        rows = (
            (first, blank),
            (second, left),
            (right, first),
            (blank, second),
            (blank, right),
            (left, blank),
        )
        for z, halves in enumerate(rows):
            for s in range(2):
                band_ref[e, z * C : (z + 1) * C, s * 2 * C : (s + 1) * 2 * C] = halves[s]


def options(at):
    return [(at + 1, 0)] + ([(5, 1)] if at == 0 else []) + ([(0, -1)] if at == 3 else [])


def offset_of(dx, dy, dz):
    return (dx + 1) * 9 + (dy + 1) * 3 + dz + 1


def stack_lanes(value, lanes):
    return jnp.concatenate([value[:, p * lanes : (p + 1) * lanes] for p in range(value.shape[1] // lanes)], axis=0)


def stack_parities(value):
    stacked = []
    for v in range(8):
        cx, cy, cz = (v // 4, v // 2 % 2, v % 2)
        lanes = []
        for parity in range(4):
            at = ((2 * cx + parity // 2) * 4 + 2 * cy + parity % 2) * RUN + cz * 2 * C
            lanes.append(value[:, at : at + 2 * C])
        stacked.append(jnp.concatenate(lanes, axis=1))
    return jnp.concatenate(stacked, axis=0)


def stack_runs(ref):
    return jnp.concatenate([ref[:, p * RUN : (p + 1) * RUN] for p in range(16)], axis=0)


def split_two(value):
    head = value.astype(BF)
    return head, (value - head.astype(F32)).astype(BF)


def table_grad_body(
    cot_ref, weight_ref, near_ref, lists_ref, ext_ref, low_ref, high_ref, turned_ref, again_ref, band_ref, pad_ref
):
    again_ref[...] = lists_ref[...]
    bricks = cot_ref.shape[0]
    face = low_ref.shape[0]
    start = ext_ref.shape[0]
    rows = start + 2 * face
    build_bands(weight_ref, band_ref)
    cot = stack_runs(cot_ref)
    turned_ref[...] = cot.T
    pad_ref[...] = jnp.zeros(pad_ref.shape, F32)
    for e in range(9):
        ex, ey = (e // 3, e % 3)
        part = dot_nt(cot, band_ref[e]).reshape(4, 4, bricks, WIDE)
        pad_ref[ex : ex + 4, ey : ey + 4] += part
    near = [near_ref[o] for o in range(27)]

    def chooser(which):
        index = jnp.concatenate([near[o] for o in which], axis=1)
        return ones_where(iota((rows, index.shape[1]), 0) == index)

    lower_half = iota((rows, 2 * C), 1) < C
    cache = {}
    for x in range(4):
        for y in range(4):
            places = [(X, Y, dx, dy) for X, dx in options(x) for Y, dy in options(y)]
            key = tuple((dx, dy) for _, _, dx, dy in places)
            if key not in cache:
                moved = [d for d in key if d != (0, 0)]
                main = chooser([offset_of(*d, 0) for d in moved] * 2) if moved else None
                up = chooser([offset_of(*d, 1) for d in key] * 2)
                down = chooser([offset_of(*d, -1) for d in key] * 2)
                cache[key] = (main, jnp.concatenate([up, down], axis=0))
            main, ends = cache[key]
            own = pad_ref[x + 1, y + 1, :, :RUN]
            own = jnp.concatenate([own, jnp.zeros((rows - bricks, RUN), F32)], axis=0)
            if main is not None:
                parts = [split_two(pad_ref[X, Y, :, :RUN]) for X, Y, dx, dy in places if (dx, dy) != (0, 0)]
                value = jnp.concatenate([p[0] for p in parts] + [p[1] for p in parts], axis=0)
                own += dot(main, value)
            parts = [split_two(pad_ref[X, Y, :, RUN:]) for X, Y, _, _ in places]
            value = jnp.concatenate([p[0] for p in parts] + [p[1] for p in parts], axis=0)
            halo = dot(ends, value)
            first = own[:, : 2 * C] + jnp.where(lower_half, halo[:rows], 0.0)
            second = own[:, 2 * C :] + jnp.where(lower_half, 0.0, halo[rows:])
            total = jnp.concatenate([first, second], axis=1)
            at = (x * 4 + y) * RUN
            ext_ref[:, at : at + RUN] = total[:start]
            low_ref[:, at : at + RUN] = total[start : start + face].astype(BF)
            high_ref[:, at : at + RUN] = total[start + face :].astype(BF)


def first_body(
    sends_hbm, items_hbm, sides_hbm, crosses_hbm, slots_hbm, out_ref, lists_ref,
    sends_ref, items_ref, sides_ref, crosses_ref, slots_ref, arrived,
):
    sources = (sends_hbm, items_hbm, sides_hbm, crosses_hbm, slots_hbm)
    places = (sends_ref, items_ref, sides_ref, crosses_ref, slots_ref)
    copies = [pltpu.make_async_copy(s, p, arrived.at[i]) for i, (s, p) in enumerate(zip(sources, places))]
    for copy in copies:
        copy.start()
    for copy in copies:
        copy.wait()
    face, bricks = (sides_ref.shape[1], slots_ref.shape[1])
    lists_ref[...] = jnp.zeros(lists_ref.shape, I32)
    lists_ref[0:2, :face] = sides_ref[...]
    lists_ref[2:4, :face] = crosses_ref[...]
    lists_ref[4:5, :bricks] = slots_ref[...]
    items_out(sends_ref, items_ref, out_ref)


def weight_grad_body(
    merged_ref, low_ref, high_ref, below_ref, above_ref, turned_ref, near_ref, lists_ref, ext_ref, parents_ref,
    sums_ref, pad_ref, part_ref, to_next_ref, to_prev_ref, table_ref,
):
    bricks, width = merged_ref.shape
    face = low_ref.shape[0]
    rows = bricks + 4 * face
    below = below_ref[...].astype(F32)
    above = above_ref[...].astype(F32)
    table_ref[:bricks] = merged_ref[...]
    table_ref[bricks:] = stack_rows(low_ref[:, :width], high_ref[:, :width], below[:face], above[:face])
    total = add_rows(ext_ref[...], crosses_of(lists_ref, face), above[face:], below[face:])
    part_ref[...] = total[:bricks]
    to_prev_ref[...] = total[bricks : bricks + face].astype(BF)
    to_next_ref[...] = total[bricks + face :].astype(BF)
    side_parents = stack_lanes(stack_rows(low_ref[:, width:], high_ref[:, width:]), parents_ref.shape[1])
    grads = [stack_parities(total[:bricks].astype(BF)), stack_parities(total[bricks:].astype(BF))]
    up_sum = dot_tn(jnp.concatenate(grads, axis=0), jnp.concatenate([parents_ref[...], side_parents], axis=0))
    coarse = up_sum.shape[1]
    count = sums_ref.shape[0]
    parts = up_sum.shape[0] // count
    for q in range(parts):
        sums_ref[:, q * coarse : (q + 1) * coarse] = up_sum[q * count : (q + 1) * count].astype(BF)
    near = jnp.concatenate([near_ref[o] for o in range(27)] + [jnp.zeros((5, bricks), I32)], axis=0)
    near = near.astype(F32).T.astype(I32)

    def one_of(dx, dy, dz):
        o = offset_of(dx, dy, dz)
        return near[:, o : o + 1]

    place = iota((bricks, rows), 1)
    pair_place = iota((bricks, 2 * rows), 1)
    lower_half = iota((rows, 2 * C), 1) < C
    zero = jnp.zeros((rows, 2 * C), BF)
    cache = {}
    for x in range(4):
        for y in range(4):
            places = [(X, Y, dx, dy) for X, dx in options(x) for Y, dy in options(y)]
            for _, _, dx, dy in places:
                if (dx, dy) not in cache:
                    main = ones_where(place == one_of(dx, dy, 0))
                    ends = jnp.where(pair_place < rows, one_of(dx, dy, 1), one_of(dx, dy, -1) + rows)
                    cache[dx, dy] = (main, ones_where(pair_place == ends))
            at = (x * 4 + y) * RUN
            columns = table_ref[:, at : at + RUN]
            first = jnp.where(lower_half, columns[:, : 2 * C], zero)
            second = jnp.where(lower_half, zero, columns[:, 2 * C :])
            ends = jnp.concatenate([cache[dx, dy][1] for _, _, dx, dy in places], axis=0)
            halo = dot(ends, jnp.concatenate([first, second], axis=0)).astype(BF)
            for i, (X, Y, _, _) in enumerate(places):
                pad_ref[X, Y, :, RUN:] = halo[i * bricks : (i + 1) * bricks]
            pad_ref[x + 1, y + 1, :, :RUN] = columns[:bricks]
            moved = [p for p in places if p[2:] != (0, 0)]
            if moved:
                main = jnp.concatenate([cache[dx, dy][0] for _, _, dx, dy in moved], axis=0)
                got = dot(main, columns).astype(BF)
                for i, (X, Y, _, _) in enumerate(moved):
                    pad_ref[X, Y, :, :RUN] = got[i * bricks : (i + 1) * bricks]

    turned = turned_ref[...]
    lanes_low = iota((C, 2 * C), 1) < C
    sums = []
    for e in range(9):
        wide = dot(turned, inputs_at(pad_ref, e))

        def block(z, s):
            return wide[z * C : (z + 1) * C, s * 2 * C : (s + 1) * 2 * C]

        low = jnp.where(lanes_low, block(1, 0) + block(3, 1), block(0, 2) + block(2, 0))
        mid = jnp.where(lanes_low, block(0, 0) + block(2, 1), block(1, 0) + block(3, 1))
        high = jnp.where(lanes_low, block(1, 1) + block(3, 2), block(0, 0) + block(2, 1))
        for value in (low, mid, high):
            sums.append(value + pltpu.roll(value, C, 1))
    sums.append(jnp.zeros((C, 2 * C), F32))
    for pair in range(7):
        both = [jnp.where(lanes_low, sums[14 * h + 2 * pair], sums[14 * h + 2 * pair + 1]) for h in range(2)]
        at = parts * coarse + pair * 2 * C
        sums_ref[:, at : at + 2 * C] = jnp.concatenate(both, axis=0).astype(BF)


def inputs_at(pad_ref, e):
    bricks = pad_ref.shape[2]
    ex, ey = (e // 3, e % 3)
    return pad_ref[ex : ex + 4, ey : ey + 4].reshape(16 * bricks, WIDE)


def conv_body(pad_ref, weight_ref, out_ref, band_ref):
    bricks = pad_ref.shape[2]
    build_bands(weight_ref, band_ref)
    total = None
    for e in range(9):
        part = dot(inputs_at(pad_ref, e), band_ref[e])
        total = part if total is None else total + part
    for p in range(16):
        out_ref[:, p * RUN : (p + 1) * RUN] = total[p * bricks : (p + 1) * bricks].astype(BF)


def add_rows(base, lists, first, second):
    count, face = (base.shape[0], lists.shape[1])
    index = jnp.concatenate([lists[0:1], lists[1:2]], axis=1)
    chosen = ones_where(iota((count, 2 * face), 0) == index)
    return base + dot(chosen, stack_rows(first, second))


def merge_body(received_ref, up_ref, fine_ref, lists_ref, merged_ref, parents_ref, a_ref, b_ref):
    bricks, width = fine_ref.shape
    face = a_ref.shape[0]
    parents = merge(received_ref, slots_of(lists_ref, bricks), up_ref, fine_ref, merged_ref, parents_ref)
    lists = sides_of(lists_ref, face)
    for out_ref, rows, owners in zip((a_ref, b_ref), pick_rows(lists, merged_ref[...]), pick_rows(lists, parents)):
        out_ref[:, :width] = rows.astype(BF)
        out_ref[:, width:] = owners.astype(BF)


def fine_grad_body(part_ref, lists_ref, next_ref, prev_ref, up_ref, grad_ref, replies_ref):
    bricks = part_ref.shape[0]
    face = next_ref.shape[0]
    total = add_rows(part_ref[...], sides_of(lists_ref, face), next_ref[...], prev_ref[...])
    grad_ref[...] = total.astype(BF)
    items = dot(stack_parities(grad_ref[...]), up_ref[...]).astype(BF)
    items = jnp.concatenate([items[v * bricks : (v + 1) * bricks] for v in range(8)], axis=1)
    half = items.shape[1] // 2
    count, item_lanes = replies_ref.shape
    slots = slots_of(lists_ref, bricks)
    for j in range(item_lanes // half):
        piece = iota((count, bricks), 0) * (item_lanes // half) + j
        named = piece // 2 == slots
        rows = dot(ones_where(named & (piece % 2 == 0)), items[:, :half])
        rows += dot(ones_where(named & (piece % 2 == 1)), items[:, half:])
        replies_ref[:, j * half : (j + 1) * half] = rows.astype(BF)


def share_body(sums_ref, replies_ref, out_ref, devices):
    count, item_lanes = replies_ref.shape
    share = count // devices
    same = iota((count, count), 0) % share == iota((count, count), 1) % share
    out_ref[:, :item_lanes] = replies_ref[...]
    out_ref[:, item_lanes:] = dot(ones_where(same), sums_ref[...]).astype(BF)


def coarse_grad(back_ref, sends_ref, out_ref):
    capacity, devices = sends_ref.shape
    count, item_width = out_ref.shape
    half = item_width // 2
    lanes = back_ref.shape[0]
    pieces = 2 * capacity * devices // lanes
    group = lanes // devices
    for h in range(2):
        total = None
        for j in range(pieces):
            index = send_index(sends_ref[...], group, pieces, j)
            place = iota((count, lanes), 1) % group * pieces + j
            chosen = (iota((count, lanes), 0) == index) & (place % 2 == h)
            part = dot(ones_where(chosen), back_ref[:, j * half : (j + 1) * half])
            total = part if total is None else total + part
        out_ref[:, h * half : (h + 1) * half] = total.astype(BF)


def last_body(back_ref, sends_ref, conv_ref, up_ref, out_ref, scale):
    coarse_grad(back_ref, sends_ref, out_ref)
    count, width = back_ref.shape
    coarse = up_ref.shape[1]
    parts = up_ref.shape[0] // count
    at = width - 14 * C - parts * coarse
    for q in range(parts):
        up_ref[q * count : (q + 1) * count] = back_ref[:, at : at + coarse].astype(F32) * scale
        at += coarse
    for pair in range(7):
        turned = back_ref[:, at : at + 2 * C].astype(F32).T * scale
        at += 2 * C
        for h in range(2):
            for s in range(2):
                o = 14 * h + 2 * pair + s
                if o < 27:
                    conv_ref[o] = turned[s * C : (s + 1) * C, h * C : (h + 1) * C]


def passed_along(value, axis, steps):
    count = lax.axis_size(axis)
    initial, last = (max(0, -steps), min(count, count - steps))
    return lax.ppermute(value, axis, [(source, source + steps) for source in range(initial, last)])


def trade_rows(values, devices):
    rows, width = values.shape
    grid_view = values.reshape(devices, rows // devices, width)
    return lax.all_to_all(grid_view, ("gx", "gy"), split_axis=0, concat_axis=0, tiled=True).reshape(rows, width)


def on_device(
    fine_features, coarse_items, conv_weight, up_weight, neighbours,
    side_sends, cross_sends, parent_slots, coarse_sends, cotangent,
):
    fine = fine_features[0, 0]
    items = coarse_items[0, 0]
    cot = cotangent[0, 0]
    bricks, width = fine.shape
    face = side_sends.shape[-1]
    across_x, across_y = (lax.axis_size("gx"), lax.axis_size("gy"))
    devices = across_x * across_y
    capacity = coarse_sends.shape[-1]
    item_count, item_width = items.shape
    coarse = up_weight.shape[1]
    start = bricks + 2 * face
    sends = coarse_sends.transpose(0, 1, 3, 2)[0, 0]
    slots = parent_slots[0]
    sides = side_sends[0, 0]
    crosses = cross_sends[0, 0]
    near = neighbours.transpose(0, 3, 1, 2)[0]
    up_turned = up_weight.transpose(0, 2, 1).reshape(8 * C, coarse)
    half = item_width // 2
    count = 2 * C
    item_lanes = capacity * devices * item_width // count
    sums_width = 8 * C * coarse // count + 14 * C
    rows = shape((bricks, width))
    face_rows = shape((face, width))
    faces_and_parents = shape((face, width + item_width))
    two_faces = shape((2 * face, width))
    lists_shape = shape((8, 128), I32)
    band = pltpu.VMEM((9, WIDE, RUN), BF)
    conv_flops = 2 * 9 * 16 * bricks * WIDE * RUN

    listed = (sends, items, sides, crosses, slots)
    outgoing, lists = call(
        first_body, [shape((2 * capacity * devices, half)), lists_shape], *listed,
        scratch=[pltpu.VMEM(a.shape, a.dtype) for a in listed] + [pltpu.SemaphoreType.DMA((len(listed),))],
        in_hbm=True,
    )
    received = trade_rows(outgoing, devices)
    ext_grad, low_cross, high_cross, turned, lists = call(
        table_grad_body,
        [shape((start, width), F32), face_rows, face_rows, shape((RUN, 16 * bricks)), lists_shape],
        cot, conv_weight, near, lists,
        scratch=[band, pltpu.VMEM((6, 6, bricks, WIDE), F32)], flops=2 * conv_flops,
    )
    merged, parents, to_next, to_prev = call(
        merge_body, [rows, shape((8 * bricks, coarse)), faces_and_parents, faces_and_parents],
        received, up_turned, fine, lists,
    )
    low_side = passed_along(to_next, "gy", 1)
    high_side = passed_along(to_prev, "gy", -1)
    to_next, to_prev = call(
        cross_body, [two_faces, two_faces], merged, low_side, high_side, lists, low_cross, high_cross
    )
    below = passed_along(to_next, "gx", 1)
    above = passed_along(to_prev, "gx", -1)
    sums, pad, fine_part, to_next, to_prev = call(
        weight_grad_body,
        [shape((count, sums_width)), shape((6, 6, bricks, WIDE)), shape((bricks, width), F32), face_rows, face_rows],
        merged, low_side, high_side, below, above, turned, near, lists, ext_grad, parents,
        scratch=[pltpu.VMEM((bricks + 4 * face, width), BF)], flops=conv_flops,
    )
    sums = trade_rows(sums, devices)
    grad_prev = passed_along(to_next, "gy", 1)
    grad_next = passed_along(to_prev, "gy", -1)
    grad_fine, replies = call(
        fine_grad_body, [rows, shape((count, item_lanes))], fine_part, lists, grad_next, grad_prev, up_turned
    )
    (output,) = call(conv_body, [rows], pad, conv_weight, scratch=[band], flops=conv_flops)
    (back,) = call(
        functools.partial(share_body, devices=devices), [shape((count, item_lanes + sums_width))], sums, replies
    )
    back = trade_rows(back, devices)
    scale = 1.0 / math.sqrt(64 * bricks * devices)
    grad_conv, grad_up, coarse_grad = call(
        functools.partial(last_body, scale=scale),
        [shape((27, C, C), F32), shape((8 * C, coarse), F32), shape((item_count, item_width))], back, sends,
    )
    return (
        output.reshape(1, 1, bricks, width),
        grad_fine.reshape(1, 1, bricks, width),
        coarse_grad.reshape(1, 1, item_count, item_width),
        grad_conv,
        grad_up.reshape(8, C, coarse).transpose(0, 2, 1),
    )


def solution(mesh):
    split = P(("groups", "gx"), "gy", None, None)
    placed = (split, split, P(), P(), split, split, split, P(("groups", "gx"), "gy", None), split, split)
    return jax.shard_map(
        on_device,
        mesh=mesh,
        in_specs=placed,
        out_specs=(split, split, split, P("groups", None, None), P("groups", None, None)),
        check_vma=False,
    )
```

```python
import functools
import math

import jax
import jax.numpy as jnp
from jax import lax
from jax.experimental import pallas as pl
from jax.experimental.pallas import tpu as pltpu
from jax.sharding import PartitionSpec as P

BF = jnp.bfloat16
F32 = jnp.float32
I32 = jnp.int32

C = 64
RUN = 4 * C
WIDE = RUN + 2 * C


def iota(shape, axis):
    return lax.broadcasted_iota(I32, shape, axis)


def ones_where(mask):
    return jnp.where(mask, 1.0, 0.0).astype(BF)


def dot(a, b):
    return jnp.dot(a, b, preferred_element_type=F32)


def dot_tn(a, b):
    return lax.dot_general(a, b, (((0,), (0,)), ((), ())), preferred_element_type=F32)


def dot_nt(a, b):
    return lax.dot_general(a, b, (((1,), (1,)), ((), ())), preferred_element_type=F32)


def column_of(row):
    size = row.shape[1]
    diagonal = iota((size, size), 0) == iota((size, size), 1)
    spread = jnp.broadcast_to(row.astype(F32), (size, size))
    return jnp.sum(jnp.where(diagonal, spread, 0.0), axis=1, keepdims=True).astype(I32)


def call(body, outs, *args, scratch=(), flops=0, in_hbm=False):
    moved = sum(a.size * a.dtype.itemsize for a in list(args) + list(outs))
    return pl.pallas_call(
        body,
        out_shape=tuple(outs),
        in_specs=[pl.BlockSpec(memory_space=pltpu.HBM) if in_hbm else pl.BlockSpec() for _ in args],
        scratch_shapes=tuple(scratch),
        cost_estimate=pl.CostEstimate(flops=flops, bytes_accessed=moved, transcendentals=0),
        compiler_params=pltpu.CompilerParams(vmem_limit_bytes=None if in_hbm else 28 * 2**20),
    )(*args)


def shape(dims, dtype=BF):
    return jax.ShapeDtypeStruct(dims, dtype)


def send_index(sends, group, pieces=1, j=0):
    capacity, devices = sends.shape
    lanes = devices * group
    spread = ones_where(iota((devices, lanes), 1) // group == iota((devices, lanes), 0))
    rows = dot(sends.astype(F32).astype(BF), spread)
    slot = (iota((capacity, lanes), 1) % group * pieces + j) // 2
    picked = jnp.where(slot == iota((capacity, lanes), 0), rows, 0.0)
    return jnp.sum(picked, axis=0, keepdims=True).astype(I32)


def items_out(sends_ref, items_ref, out_ref):
    capacity, devices = sends_ref.shape
    count, width = items_ref.shape
    half = width // 2
    group = 2 * capacity
    lanes = devices * group
    spread = ones_where(iota((lanes, devices), 0) // group == iota((lanes, devices), 1))
    slot = iota((lanes, capacity), 0) % group // 2
    values = dot_nt(spread, sends_ref[...].astype(F32).astype(BF))
    item = jnp.sum(jnp.where(slot == iota((lanes, capacity), 1), values, 0.0), axis=1, keepdims=True).astype(I32)
    place = jnp.where(item < count, item + iota((lanes, 1), 0) % 2 * count, -1)
    chosen = ones_where(iota((lanes, 2 * count), 1) == place)
    out_ref[...] = dot(chosen, jnp.concatenate([items_ref[:, :half], items_ref[:, half:]], axis=0)).astype(BF)


def merge(received_ref, slots, up_ref, fine_ref, merged_ref, parents_ref):
    bricks = fine_ref.shape[0]
    lanes, half = received_ref.shape
    slot = column_of(slots)
    place = iota((bricks, lanes), 1)
    named = place // 2 == slot
    received = received_ref[...]
    parents = jnp.concatenate(
        [dot(ones_where(named & (place % 2 == h)), received) for h in (0, 1)], axis=1
    ).astype(BF)
    coarse = 2 * half // 8
    stacked = jnp.concatenate([parents[:, v * coarse : (v + 1) * coarse] for v in range(8)], axis=0)
    parents_ref[...] = stacked
    lifted = dot_nt(stacked, up_ref[...])
    for v in range(8):
        cx, cy, cz = (v // 4, v // 2 % 2, v % 2)
        for parity in range(4):
            vx, vy = (2 * cx + parity // 2, 2 * cy + parity % 2)
            at = (vx * 4 + vy) * RUN + cz * 2 * C
            add = lifted[v * bricks : (v + 1) * bricks, parity * 2 * C : (parity + 1) * 2 * C]
            merged_ref[:, at : at + 2 * C] = (fine_ref[:, at : at + 2 * C].astype(F32) + add).astype(BF)
    return parents


def pick_rows(lists, rows):
    return [dot_tn(ones_where(iota((rows.shape[0], one.shape[1]), 0) == one), rows) for one in lists]


GX, GY = (0, 1)


def by_pair(lists_ref, axis, of_next, of_prev):
    odd = jnp.broadcast_to(lists_ref[5:6, axis : axis + 1], of_next.shape) == 1
    return jnp.where(odd, of_prev, of_next), jnp.where(odd, of_next, of_prev)


def from_pairs(lists_ref, axis, even_ref, odd_ref):
    return by_pair(lists_ref, axis, even_ref[...].astype(F32), odd_ref[...].astype(F32))


def stack_rows(*parts):
    return jnp.concatenate([p.astype(F32) for p in parts], axis=0).astype(BF)


def sides_of(lists_ref, face):
    return lists_ref[0:2, :face]


def crosses_of(lists_ref, face):
    return lists_ref[2:4, :face]


def slots_of(lists_ref, bricks):
    return lists_ref[4:5, :bricks]


def cross_body(merged_ref, even_ref, odd_ref, lists_ref, low_grad_ref, high_grad_ref, a_ref, b_ref):
    face, width = low_grad_ref.shape
    high, low = from_pairs(lists_ref, GY, even_ref, odd_ref)
    rows = jnp.concatenate([merged_ref[...], stack_rows(low[:, :width], high[:, :width])], axis=0)
    lists = crosses_of(lists_ref, face)
    picked = pick_rows(by_pair(lists_ref, GX, lists[0:1], lists[1:2]), rows)
    grads = from_pairs(lists_ref, GX, high_grad_ref, low_grad_ref)
    a_ref[...] = stack_rows(picked[0], grads[0])
    b_ref[...] = stack_rows(picked[1], grads[1])


def build_bands(weight_ref, band_ref):
    zero = jnp.zeros((C, C), BF)
    blank = jnp.zeros((C, 2 * C), BF)

    def pair(a, b):
        return jnp.concatenate([a, b], axis=1)

    for e in range(9):
        low, mid, high = (weight_ref[3 * e + z] for z in range(3))
        first, second = (pair(mid, low), pair(high, mid))
        left, right = (pair(low, zero), pair(zero, high))
        rows = (
            (first, blank),
            (second, left),
            (right, first),
            (blank, second),
            (blank, right),
            (left, blank),
        )
        for z, halves in enumerate(rows):
            for s in range(2):
                band_ref[e, z * C : (z + 1) * C, s * 2 * C : (s + 1) * 2 * C] = halves[s]


def options(at):
    return [(at + 1, 0)] + ([(5, 1)] if at == 0 else []) + ([(0, -1)] if at == 3 else [])


def offset_of(dx, dy, dz):
    return (dx + 1) * 9 + (dy + 1) * 3 + dz + 1


def stack_lanes(value, lanes):
    return jnp.concatenate([value[:, p * lanes : (p + 1) * lanes] for p in range(value.shape[1] // lanes)], axis=0)


def stack_parities(value):
    stacked = []
    for v in range(8):
        cx, cy, cz = (v // 4, v // 2 % 2, v % 2)
        lanes = []
        for parity in range(4):
            at = ((2 * cx + parity // 2) * 4 + 2 * cy + parity % 2) * RUN + cz * 2 * C
            lanes.append(value[:, at : at + 2 * C])
        stacked.append(jnp.concatenate(lanes, axis=1))
    return jnp.concatenate(stacked, axis=0)


def stack_runs(ref):
    return jnp.concatenate([ref[:, p * RUN : (p + 1) * RUN] for p in range(16)], axis=0)


def split_two(value):
    head = value.astype(BF)
    return head, (value - head.astype(F32)).astype(BF)


def table_grad_body(
    cot_ref, weight_ref, near_ref, lists_ref, parity_ref,
    ext_ref, low_ref, high_ref, turned_ref, mains_ref, ends_ref, again_ref, band_ref, pad_ref,
):
    again_ref[...] = lists_ref[...]
    again_ref[5:6] = parity_ref[...]
    bricks = cot_ref.shape[0]
    face = low_ref.shape[0]
    start = ext_ref.shape[0]
    rows = start + 2 * face
    build_bands(weight_ref, band_ref)
    cot = stack_runs(cot_ref)
    turned_ref[...] = cot.T
    pad_ref[...] = jnp.zeros(pad_ref.shape, F32)
    for e in range(9):
        ex, ey = (e // 3, e % 3)
        part = dot_nt(cot, band_ref[e]).reshape(4, 4, bricks, WIDE)
        pad_ref[ex : ex + 4, ey : ey + 4] += part
    near = [near_ref[o] for o in range(27)]

    def chooser(which):
        index = jnp.concatenate([near[o] for o in which], axis=1)
        return ones_where(iota((rows, index.shape[1]), 0) == index)

    lower_half = iota((rows, 2 * C), 1) < C
    cache = {}
    for x in range(4):
        for y in range(4):
            places = [(X, Y, dx, dy) for X, dx in options(x) for Y, dy in options(y)]
            key = tuple((dx, dy) for _, _, dx, dy in places)
            if key not in cache:
                moved = [d for d in key if d != (0, 0)]
                main = chooser([offset_of(*d, 0) for d in moved] * 2) if moved else None
                up = chooser([offset_of(*d, 1) for d in key] * 2)
                down = chooser([offset_of(*d, -1) for d in key] * 2)
                cache[key] = (main, jnp.concatenate([up, down], axis=0))
            main, ends = cache[key]
            own = pad_ref[x + 1, y + 1, :, :RUN]
            own = jnp.concatenate([own, jnp.zeros((rows - bricks, RUN), F32)], axis=0)
            if main is not None:
                parts = [split_two(pad_ref[X, Y, :, :RUN]) for X, Y, dx, dy in places if (dx, dy) != (0, 0)]
                value = jnp.concatenate([p[0] for p in parts] + [p[1] for p in parts], axis=0)
                own += dot(main, value)
            parts = [split_two(pad_ref[X, Y, :, RUN:]) for X, Y, _, _ in places]
            value = jnp.concatenate([p[0] for p in parts] + [p[1] for p in parts], axis=0)
            halo = dot(ends, value)
            first = own[:, : 2 * C] + jnp.where(lower_half, halo[:rows], 0.0)
            second = own[:, 2 * C :] + jnp.where(lower_half, 0.0, halo[rows:])
            total = jnp.concatenate([first, second], axis=1)
            at = (x * 4 + y) * RUN
            ext_ref[:, at : at + RUN] = total[:start]
            low_ref[:, at : at + RUN] = total[start : start + face].astype(BF)
            high_ref[:, at : at + RUN] = total[start + face :].astype(BF)
    make_choosers(near_ref, rows, mains_ref, ends_ref)


def make_choosers(near_ref, rows, mains_ref, ends_ref):
    bricks = mains_ref.shape[1]
    near = jnp.concatenate([near_ref[o] for o in range(27)] + [jnp.zeros((5, bricks), I32)], axis=0)
    near = near.astype(F32).T.astype(I32)
    place = iota((bricks, rows), 1)
    pair_place = iota((bricks, 2 * rows), 1)
    for d in range(9):
        down, straight, up = (near[:, 3 * d + z : 3 * d + z + 1] for z in range(3))
        mains_ref[d] = ones_where(place == straight)
        ends_ref[d] = ones_where(pair_place == jnp.where(pair_place < rows, up, down + rows))


def first_body(
    sends_hbm, items_hbm, sides_hbm, crosses_hbm, slots_hbm, out_ref, lists_ref,
    sends_ref, items_ref, sides_ref, crosses_ref, slots_ref, arrived,
):
    sources = (sends_hbm, items_hbm, sides_hbm, crosses_hbm, slots_hbm)
    places = (sends_ref, items_ref, sides_ref, crosses_ref, slots_ref)
    copies = [pltpu.make_async_copy(s, p, arrived.at[i]) for i, (s, p) in enumerate(zip(sources, places))]
    for copy in copies:
        copy.start()
    for copy in copies:
        copy.wait()
    face, bricks = (sides_ref.shape[1], slots_ref.shape[1])
    lists_ref[...] = jnp.zeros(lists_ref.shape, I32)
    lists_ref[0:2, :face] = sides_ref[...]
    lists_ref[2:4, :face] = crosses_ref[...]
    lists_ref[4:5, :bricks] = slots_ref[...]
    items_out(sends_ref, items_ref, out_ref)


def weight_grad_body(
    merged_ref, even_side_ref, odd_side_ref, even_cross_ref, odd_cross_ref, turned_ref, mains_ref, ends_ref, lists_ref,
    ext_ref, parents_ref, sums_ref, pad_ref, part_ref, to_even_ref, to_odd_ref, table_ref,
):
    bricks, width = merged_ref.shape
    face = even_side_ref.shape[0]
    rows = bricks + 4 * face
    high, low = from_pairs(lists_ref, GY, even_side_ref, odd_side_ref)
    above, below = from_pairs(lists_ref, GX, even_cross_ref, odd_cross_ref)
    table_ref[:bricks] = merged_ref[...]
    table_ref[bricks:] = stack_rows(low[:, :width], high[:, :width], below[:face], above[:face])
    total = add_rows(ext_ref[...], crosses_of(lists_ref, face), above[face:], below[face:])
    part_ref[...] = total[:bricks]
    to_even, to_odd = by_pair(lists_ref, GY, total[bricks + face :], total[bricks : bricks + face])
    to_even_ref[...] = to_even.astype(BF)
    to_odd_ref[...] = to_odd.astype(BF)
    side_parents = stack_lanes(stack_rows(low[:, width:], high[:, width:]), parents_ref.shape[1])
    grads = [stack_parities(total[:bricks].astype(BF)), stack_parities(total[bricks:].astype(BF))]
    up_sum = dot_tn(jnp.concatenate(grads, axis=0), jnp.concatenate([parents_ref[...], side_parents], axis=0))
    coarse = up_sum.shape[1]
    count = sums_ref.shape[0]
    parts = up_sum.shape[0] // count
    for q in range(parts):
        sums_ref[:, q * coarse : (q + 1) * coarse] = up_sum[q * count : (q + 1) * count].astype(BF)
    lower_half = iota((rows, 2 * C), 1) < C
    zero = jnp.zeros((rows, 2 * C), BF)
    for x in range(4):
        for y in range(4):
            places = [(X, Y, dx, dy) for X, dx in options(x) for Y, dy in options(y)]
            at = (x * 4 + y) * RUN
            columns = table_ref[:, at : at + RUN]
            first = jnp.where(lower_half, columns[:, : 2 * C], zero)
            second = jnp.where(lower_half, zero, columns[:, 2 * C :])
            ends = jnp.concatenate([ends_ref[3 * dx + dy + 4] for _, _, dx, dy in places], axis=0)
            halo = dot(ends, jnp.concatenate([first, second], axis=0)).astype(BF)
            for i, (X, Y, _, _) in enumerate(places):
                pad_ref[X, Y, :, RUN:] = halo[i * bricks : (i + 1) * bricks]
            pad_ref[x + 1, y + 1, :, :RUN] = columns[:bricks]
            moved = [p for p in places if p[2:] != (0, 0)]
            if moved:
                main = jnp.concatenate([mains_ref[3 * dx + dy + 4] for _, _, dx, dy in moved], axis=0)
                got = dot(main, columns).astype(BF)
                for i, (X, Y, _, _) in enumerate(moved):
                    pad_ref[X, Y, :, :RUN] = got[i * bricks : (i + 1) * bricks]

    turned = turned_ref[...]
    lanes_low = iota((C, 2 * C), 1) < C
    sums = []
    for e in range(9):
        wide = dot(turned, inputs_at(pad_ref, e))

        def block(z, s):
            return wide[z * C : (z + 1) * C, s * 2 * C : (s + 1) * 2 * C]

        low = jnp.where(lanes_low, block(1, 0) + block(3, 1), block(0, 2) + block(2, 0))
        mid = jnp.where(lanes_low, block(0, 0) + block(2, 1), block(1, 0) + block(3, 1))
        high = jnp.where(lanes_low, block(1, 1) + block(3, 2), block(0, 0) + block(2, 1))
        for value in (low, mid, high):
            sums.append(value + pltpu.roll(value, C, 1))
    sums.append(jnp.zeros((C, 2 * C), F32))
    for pair in range(7):
        both = [jnp.where(lanes_low, sums[14 * h + 2 * pair], sums[14 * h + 2 * pair + 1]) for h in range(2)]
        at = parts * coarse + pair * 2 * C
        sums_ref[:, at : at + 2 * C] = jnp.concatenate(both, axis=0).astype(BF)


def inputs_at(pad_ref, e):
    bricks = pad_ref.shape[2]
    ex, ey = (e // 3, e % 3)
    return pad_ref[ex : ex + 4, ey : ey + 4].reshape(16 * bricks, WIDE)


def conv_body(pad_ref, weight_ref, out_ref, band_ref):
    bricks = pad_ref.shape[2]
    build_bands(weight_ref, band_ref)
    total = None
    for e in range(9):
        part = dot(inputs_at(pad_ref, e), band_ref[e])
        total = part if total is None else total + part
    for p in range(16):
        out_ref[:, p * RUN : (p + 1) * RUN] = total[p * bricks : (p + 1) * bricks].astype(BF)


def add_rows(base, lists, first, second):
    count, face = (base.shape[0], lists.shape[1])
    index = jnp.concatenate([lists[0:1], lists[1:2]], axis=1)
    chosen = ones_where(iota((count, 2 * face), 0) == index)
    return base + dot(chosen, stack_rows(first, second))


def merge_body(received_ref, up_ref, fine_ref, lists_ref, merged_ref, parents_ref, a_ref, b_ref):
    bricks, width = fine_ref.shape
    face = a_ref.shape[0]
    parents = merge(received_ref, slots_of(lists_ref, bricks), up_ref, fine_ref, merged_ref, parents_ref)
    lists = sides_of(lists_ref, face)
    lists = by_pair(lists_ref, GY, lists[0:1], lists[1:2])
    for out_ref, rows, owners in zip((a_ref, b_ref), pick_rows(lists, merged_ref[...]), pick_rows(lists, parents)):
        out_ref[:, :width] = rows.astype(BF)
        out_ref[:, width:] = owners.astype(BF)


def fine_grad_body(part_ref, lists_ref, even_ref, odd_ref, up_ref, grad_ref, replies_ref):
    bricks = part_ref.shape[0]
    face = even_ref.shape[0]
    from_next, from_prev = from_pairs(lists_ref, GY, even_ref, odd_ref)
    total = add_rows(part_ref[...], sides_of(lists_ref, face), from_next, from_prev)
    grad_ref[...] = total.astype(BF)
    items = dot(stack_parities(grad_ref[...]), up_ref[...]).astype(BF)
    items = jnp.concatenate([items[v * bricks : (v + 1) * bricks] for v in range(8)], axis=1)
    half = items.shape[1] // 2
    count, item_lanes = replies_ref.shape
    slots = slots_of(lists_ref, bricks)
    for j in range(item_lanes // half):
        piece = iota((count, bricks), 0) * (item_lanes // half) + j
        named = piece // 2 == slots
        rows = dot(ones_where(named & (piece % 2 == 0)), items[:, :half])
        rows += dot(ones_where(named & (piece % 2 == 1)), items[:, half:])
        replies_ref[:, j * half : (j + 1) * half] = rows.astype(BF)


def share_body(sums_ref, lists_ref, out_ref, again_ref, devices):
    again_ref[...] = lists_ref[...]
    count = sums_ref.shape[0]
    share = count // devices
    same = iota((count, count), 0) % share == iota((count, count), 1) % share
    out_ref[...] = dot(ones_where(same), sums_ref[...]).astype(BF)


def coarse_grad_body(back_ref, sends_ref, out_ref):
    capacity, devices = sends_ref.shape
    count, item_width = out_ref.shape
    half = item_width // 2
    lanes = back_ref.shape[0]
    pieces = 2 * capacity * devices // lanes
    group = lanes // devices
    for h in range(2):
        total = None
        for j in range(pieces):
            index = send_index(sends_ref[...], group, pieces, j)
            place = iota((count, lanes), 1) % group * pieces + j
            chosen = (iota((count, lanes), 0) == index) & (place % 2 == h)
            part = dot(ones_where(chosen), back_ref[:, j * half : (j + 1) * half])
            total = part if total is None else total + part
        out_ref[:, h * half : (h + 1) * half] = total.astype(BF)


def last_body(back_ref, conv_ref, up_ref, scale):
    count = back_ref.shape[0]
    coarse = up_ref.shape[1]
    parts = up_ref.shape[0] // count
    at = 0
    for q in range(parts):
        up_ref[q * count : (q + 1) * count] = back_ref[:, at : at + coarse].astype(F32) * scale
        at += coarse
    for pair in range(7):
        turned = back_ref[:, at : at + 2 * C].astype(F32).T * scale
        at += 2 * C
        for h in range(2):
            for s in range(2):
                o = 14 * h + 2 * pair + s
                if o < 27:
                    conv_ref[o] = turned[s * C : (s + 1) * C, h * C : (h + 1) * C]


def swap_pairs(to_even, to_odd, axis):
    count = lax.axis_size(axis)

    def swap(value, first):
        lower = range(first, count - 1, 2)
        return lax.ppermute(value, axis, [(i, i + 1) for i in lower] + [(i + 1, i) for i in lower])

    from_odd = swap(to_odd, 1)
    return swap(to_even, 0), from_odd


def trade_rows(values, devices):
    rows, width = values.shape
    grid_view = values.reshape(devices, rows // devices, width)
    return lax.all_to_all(grid_view, ("gx", "gy"), split_axis=0, concat_axis=0, tiled=True).reshape(rows, width)


def on_device(
    fine_features, coarse_items, conv_weight, up_weight, neighbours,
    side_sends, cross_sends, parent_slots, coarse_sends, cotangent,
):
    fine = fine_features[0, 0]
    items = coarse_items[0, 0]
    cot = cotangent[0, 0]
    bricks, width = fine.shape
    face = side_sends.shape[-1]
    across_x, across_y = (lax.axis_size("gx"), lax.axis_size("gy"))
    devices = across_x * across_y
    capacity = coarse_sends.shape[-1]
    item_count, item_width = items.shape
    coarse = up_weight.shape[1]
    start = bricks + 2 * face
    sends = coarse_sends.transpose(0, 1, 3, 2)[0, 0]
    slots = parent_slots[0]
    sides = side_sends[0, 0]
    crosses = cross_sends[0, 0]
    near = neighbours.transpose(0, 3, 1, 2)[0]
    up_turned = up_weight.transpose(0, 2, 1).reshape(8 * C, coarse)
    half = item_width // 2
    count = 2 * C
    item_lanes = capacity * devices * item_width // count
    sums_width = 8 * C * coarse // count + 14 * C
    rows = shape((bricks, width))
    face_rows = shape((face, width))
    faces_and_parents = shape((face, width + item_width))
    two_faces = shape((2 * face, width))
    lists_shape = shape((8, 128), I32)
    band = pltpu.VMEM((9, WIDE, RUN), BF)
    conv_flops = 2 * 9 * 16 * bricks * WIDE * RUN

    listed = (sends, items, sides, crosses, slots)
    outgoing, lists = call(
        first_body, [shape((2 * capacity * devices, half)), lists_shape], *listed,
        scratch=[pltpu.VMEM(a.shape, a.dtype) for a in listed] + [pltpu.SemaphoreType.DMA((len(listed),))],
        in_hbm=True,
    )
    received = trade_rows(outgoing, devices)
    lane = jnp.arange(128, dtype=I32)[None]
    parity = jnp.where(lane == GX, lax.axis_index("gx") % 2, lax.axis_index("gy") % 2).astype(I32)
    table_rows = start + 2 * face
    ext_grad, low_cross, high_cross, turned, mains, ends, lists = call(
        table_grad_body,
        [
            shape((start, width), F32), face_rows, face_rows, shape((RUN, 16 * bricks)),
            shape((9, bricks, table_rows)), shape((9, bricks, 2 * table_rows)), lists_shape,
        ],
        cot, conv_weight, near, lists, parity,
        scratch=[band, pltpu.VMEM((6, 6, bricks, WIDE), F32)], flops=2 * conv_flops,
    )
    merged, parents, to_even, to_odd = call(
        merge_body, [rows, shape((8 * bricks, coarse)), faces_and_parents, faces_and_parents],
        received, up_turned, fine, lists,
    )
    sides = swap_pairs(to_even, to_odd, "gy")
    to_even, to_odd = call(cross_body, [two_faces, two_faces], merged, *sides, lists, low_cross, high_cross)
    crosses = swap_pairs(to_even, to_odd, "gx")
    sums, pad, fine_part, to_even, to_odd = call(
        weight_grad_body,
        [shape((count, sums_width)), shape((6, 6, bricks, WIDE)), shape((bricks, width), F32), face_rows, face_rows],
        merged, *sides, *crosses, turned, mains, ends, lists, ext_grad, parents,
        scratch=[pltpu.VMEM((table_rows, width), BF)], flops=conv_flops,
    )
    sums = trade_rows(sums, devices)
    side_grads = swap_pairs(to_even, to_odd, "gy")
    sums, lists = call(
        functools.partial(share_body, devices=devices), [shape((count, sums_width)), lists_shape], sums, lists
    )
    sums = trade_rows(sums, devices)
    grad_fine, replies = call(
        fine_grad_body, [rows, shape((count, item_lanes))], fine_part, lists, *side_grads, up_turned
    )
    replies = trade_rows(replies, devices)
    (output,) = call(conv_body, [rows], pad, conv_weight, scratch=[band], flops=conv_flops)
    scale = 1.0 / math.sqrt(64 * bricks * devices)
    grad_conv, grad_up = call(
        functools.partial(last_body, scale=scale), [shape((27, C, C), F32), shape((8 * C, coarse), F32)], sums
    )
    (coarse_grad,) = call(coarse_grad_body, [shape((item_count, item_width))], replies, sends)
    return (
        output.reshape(1, 1, bricks, width),
        grad_fine.reshape(1, 1, bricks, width),
        coarse_grad.reshape(1, 1, item_count, item_width),
        grad_conv,
        grad_up.reshape(8, C, coarse).transpose(0, 2, 1),
    )


def solution(mesh):
    split = P(("groups", "gx"), "gy", None, None)
    placed = (split, split, P(), P(), split, split, split, P(("groups", "gx"), "gy", None), split, split)
    return jax.shard_map(
        on_device,
        mesh=mesh,
        in_specs=placed,
        out_specs=(split, split, split, P("groups", None, None), P("groups", None, None)),
        check_vma=False,
    )
```

```python
import functools
import math

import jax
import jax.numpy as jnp
from jax import lax
from jax.experimental import pallas as pl
from jax.experimental.pallas import tpu as pltpu
from jax.sharding import PartitionSpec as P

BF = jnp.bfloat16
F32 = jnp.float32
I32 = jnp.int32

C = 64
RUN = 4 * C
WIDE = RUN + 2 * C


def iota(shape, axis):
    return lax.broadcasted_iota(I32, shape, axis)


def ones_where(mask):
    return jnp.where(mask, 1.0, 0.0).astype(BF)


def dot(a, b):
    return jnp.dot(a, b, preferred_element_type=F32)


def dot_tn(a, b):
    return lax.dot_general(a, b, (((0,), (0,)), ((), ())), preferred_element_type=F32)


def dot_nt(a, b):
    return lax.dot_general(a, b, (((1,), (1,)), ((), ())), preferred_element_type=F32)


def column_of(row):
    size = row.shape[1]
    diagonal = iota((size, size), 0) == iota((size, size), 1)
    spread = jnp.broadcast_to(row.astype(F32), (size, size))
    return jnp.sum(jnp.where(diagonal, spread, 0.0), axis=1, keepdims=True).astype(I32)


def call(body, outs, *args, scratch=(), flops=0, in_hbm=False):
    moved = sum(a.size * a.dtype.itemsize for a in list(args) + list(outs))
    return pl.pallas_call(
        body,
        out_shape=tuple(outs),
        in_specs=[pl.BlockSpec(memory_space=pltpu.HBM) if in_hbm else pl.BlockSpec() for _ in args],
        scratch_shapes=tuple(scratch),
        cost_estimate=pl.CostEstimate(flops=flops, bytes_accessed=moved, transcendentals=0),
        compiler_params=pltpu.CompilerParams(vmem_limit_bytes=None if in_hbm else 28 * 2**20),
    )(*args)


def shape(dims, dtype=BF):
    return jax.ShapeDtypeStruct(dims, dtype)


def send_index(sends, group, pieces=1, j=0):
    capacity, devices = sends.shape
    lanes = devices * group
    spread = ones_where(iota((devices, lanes), 1) // group == iota((devices, lanes), 0))
    rows = dot(sends.astype(F32).astype(BF), spread)
    slot = (iota((capacity, lanes), 1) % group * pieces + j) // 2
    picked = jnp.where(slot == iota((capacity, lanes), 0), rows, 0.0)
    return jnp.sum(picked, axis=0, keepdims=True).astype(I32)


def items_out(sends_ref, items_ref, out_ref):
    capacity, devices = sends_ref.shape
    count, width = items_ref.shape
    half = width // 2
    group = 2 * capacity
    lanes = devices * group
    spread = ones_where(iota((lanes, devices), 0) // group == iota((lanes, devices), 1))
    slot = iota((lanes, capacity), 0) % group // 2
    values = dot_nt(spread, sends_ref[...].astype(F32).astype(BF))
    item = jnp.sum(jnp.where(slot == iota((lanes, capacity), 1), values, 0.0), axis=1, keepdims=True).astype(I32)
    place = jnp.where(item < count, item + iota((lanes, 1), 0) % 2 * count, -1)
    chosen = ones_where(iota((lanes, 2 * count), 1) == place)
    out_ref[...] = dot(chosen, jnp.concatenate([items_ref[:, :half], items_ref[:, half:]], axis=0)).astype(BF)


def merge(received_ref, slots, up_ref, fine_ref, merged_ref, parents_ref):
    bricks = fine_ref.shape[0]
    lanes, half = received_ref.shape
    slot = column_of(slots)
    place = iota((bricks, lanes), 1)
    named = place // 2 == slot
    received = received_ref[...]
    parents = jnp.concatenate(
        [dot(ones_where(named & (place % 2 == h)), received) for h in (0, 1)], axis=1
    ).astype(BF)
    coarse = 2 * half // 8
    stacked = jnp.concatenate([parents[:, v * coarse : (v + 1) * coarse] for v in range(8)], axis=0)
    parents_ref[...] = stacked
    lifted = dot_nt(stacked, up_ref[...])
    for v in range(8):
        cx, cy, cz = (v // 4, v // 2 % 2, v % 2)
        for parity in range(4):
            vx, vy = (2 * cx + parity // 2, 2 * cy + parity % 2)
            at = (vx * 4 + vy) * RUN + cz * 2 * C
            add = lifted[v * bricks : (v + 1) * bricks, parity * 2 * C : (parity + 1) * 2 * C]
            merged_ref[:, at : at + 2 * C] = (fine_ref[:, at : at + 2 * C].astype(F32) + add).astype(BF)
    return parents


def pick_rows(lists, rows):
    return [dot_tn(ones_where(iota((rows.shape[0], one.shape[1]), 0) == one), rows) for one in lists]


GX, GY = (0, 1)


def by_pair(lists_ref, axis, of_next, of_prev):
    odd = jnp.broadcast_to(lists_ref[5:6, axis : axis + 1], of_next.shape) == 1
    return jnp.where(odd, of_prev, of_next), jnp.where(odd, of_next, of_prev)


def from_pairs(lists_ref, axis, even_ref, odd_ref):
    return by_pair(lists_ref, axis, even_ref[...].astype(F32), odd_ref[...].astype(F32))


def stack_rows(*parts):
    return jnp.concatenate([p.astype(F32) for p in parts], axis=0).astype(BF)


def sides_of(lists_ref, face):
    return lists_ref[0:2, :face]


def crosses_of(lists_ref, face):
    return lists_ref[2:4, :face]


def slots_of(lists_ref, bricks):
    return lists_ref[4:5, :bricks]


def cross_body(merged_ref, even_ref, odd_ref, lists_ref, low_grad_ref, high_grad_ref, a_ref, b_ref):
    face, width = low_grad_ref.shape
    high, low = from_pairs(lists_ref, GY, even_ref, odd_ref)
    rows = jnp.concatenate([merged_ref[...], stack_rows(low[:, :width], high[:, :width])], axis=0)
    lists = crosses_of(lists_ref, face)
    picked = pick_rows(by_pair(lists_ref, GX, lists[0:1], lists[1:2]), rows)
    grads = from_pairs(lists_ref, GX, high_grad_ref, low_grad_ref)
    a_ref[...] = stack_rows(picked[0], grads[0])
    b_ref[...] = stack_rows(picked[1], grads[1])


def build_bands(weight_ref, band_ref):
    zero = jnp.zeros((C, C), BF)
    blank = jnp.zeros((C, 2 * C), BF)

    def pair(a, b):
        return jnp.concatenate([a, b], axis=1)

    for e in range(9):
        low, mid, high = (weight_ref[3 * e + z] for z in range(3))
        first, second = (pair(mid, low), pair(high, mid))
        left, right = (pair(low, zero), pair(zero, high))
        rows = (
            (first, blank),
            (second, left),
            (right, first),
            (blank, second),
            (blank, right),
            (left, blank),
        )
        for z, halves in enumerate(rows):
            for s in range(2):
                band_ref[e, z * C : (z + 1) * C, s * 2 * C : (s + 1) * 2 * C] = halves[s]


def options(at):
    return [(at + 1, 0)] + ([(5, 1)] if at == 0 else []) + ([(0, -1)] if at == 3 else [])


def offset_of(dx, dy, dz):
    return (dx + 1) * 9 + (dy + 1) * 3 + dz + 1


def stack_lanes(value, lanes):
    return jnp.concatenate([value[:, p * lanes : (p + 1) * lanes] for p in range(value.shape[1] // lanes)], axis=0)


def stack_parities(value):
    stacked = []
    for v in range(8):
        cx, cy, cz = (v // 4, v // 2 % 2, v % 2)
        lanes = []
        for parity in range(4):
            at = ((2 * cx + parity // 2) * 4 + 2 * cy + parity % 2) * RUN + cz * 2 * C
            lanes.append(value[:, at : at + 2 * C])
        stacked.append(jnp.concatenate(lanes, axis=1))
    return jnp.concatenate(stacked, axis=0)


def stack_runs(ref):
    return jnp.concatenate([ref[:, p * RUN : (p + 1) * RUN] for p in range(16)], axis=0)


def split_two(value):
    head = value.astype(BF)
    return head, (value - head.astype(F32)).astype(BF)


def table_grad_body(
    cot_ref, weight_ref, near_ref, lists_ref, parity_ref,
    ext_ref, low_ref, high_ref, turned_ref, mains_ref, ends_ref, again_ref, band_ref, pad_ref,
):
    again_ref[...] = lists_ref[...]
    again_ref[5:6] = parity_ref[...]
    bricks = cot_ref.shape[0]
    face = low_ref.shape[0]
    start = ext_ref.shape[0]
    rows = start + 2 * face
    build_bands(weight_ref, band_ref)
    cot = stack_runs(cot_ref)
    turned_ref[...] = cot.T
    pad_ref[...] = jnp.zeros(pad_ref.shape, F32)
    for e in range(9):
        ex, ey = (e // 3, e % 3)
        part = dot_nt(cot, band_ref[e]).reshape(4, 4, bricks, WIDE)
        pad_ref[ex : ex + 4, ey : ey + 4] += part
    near = [near_ref[o] for o in range(27)]

    def chooser(which):
        index = jnp.concatenate([near[o] for o in which], axis=1)
        return ones_where(iota((rows, index.shape[1]), 0) == index)

    lower_half = iota((rows, 2 * C), 1) < C
    cache = {}
    for x in range(4):
        for y in range(4):
            places = [(X, Y, dx, dy) for X, dx in options(x) for Y, dy in options(y)]
            key = tuple((dx, dy) for _, _, dx, dy in places)
            if key not in cache:
                moved = [d for d in key if d != (0, 0)]
                main = chooser([offset_of(*d, 0) for d in moved] * 2) if moved else None
                up = chooser([offset_of(*d, 1) for d in key] * 2)
                down = chooser([offset_of(*d, -1) for d in key] * 2)
                cache[key] = (main, jnp.concatenate([up, down], axis=0))
            main, ends = cache[key]
            own = pad_ref[x + 1, y + 1, :, :RUN]
            own = jnp.concatenate([own, jnp.zeros((rows - bricks, RUN), F32)], axis=0)
            if main is not None:
                parts = [split_two(pad_ref[X, Y, :, :RUN]) for X, Y, dx, dy in places if (dx, dy) != (0, 0)]
                value = jnp.concatenate([p[0] for p in parts] + [p[1] for p in parts], axis=0)
                own += dot(main, value)
            parts = [split_two(pad_ref[X, Y, :, RUN:]) for X, Y, _, _ in places]
            value = jnp.concatenate([p[0] for p in parts] + [p[1] for p in parts], axis=0)
            halo = dot(ends, value)
            first = own[:, : 2 * C] + jnp.where(lower_half, halo[:rows], 0.0)
            second = own[:, 2 * C :] + jnp.where(lower_half, 0.0, halo[rows:])
            total = jnp.concatenate([first, second], axis=1)
            at = (x * 4 + y) * RUN
            ext_ref[:, at : at + RUN] = total[:start]
            low_ref[:, at : at + RUN] = total[start : start + face].astype(BF)
            high_ref[:, at : at + RUN] = total[start + face :].astype(BF)
    make_choosers(near_ref, rows, mains_ref, ends_ref)


def make_choosers(near_ref, rows, mains_ref, ends_ref):
    bricks = mains_ref.shape[1]
    near = jnp.concatenate([near_ref[o] for o in range(27)] + [jnp.zeros((5, bricks), I32)], axis=0)
    near = near.astype(F32).T.astype(I32)
    place = iota((bricks, rows), 1)
    pair_place = iota((bricks, 2 * rows), 1)
    for d in range(9):
        down, straight, up = (near[:, 3 * d + z : 3 * d + z + 1] for z in range(3))
        mains_ref[d] = ones_where(place == straight)
        ends_ref[d] = ones_where(pair_place == jnp.where(pair_place < rows, up, down + rows))


def first_body(
    sends_hbm, items_hbm, sides_hbm, crosses_hbm, slots_hbm, out_ref, lists_ref,
    sends_ref, items_ref, sides_ref, crosses_ref, slots_ref, arrived,
):
    sources = (sends_hbm, items_hbm, sides_hbm, crosses_hbm, slots_hbm)
    places = (sends_ref, items_ref, sides_ref, crosses_ref, slots_ref)
    copies = [pltpu.make_async_copy(s, p, arrived.at[i]) for i, (s, p) in enumerate(zip(sources, places))]
    for copy in copies:
        copy.start()
    for copy in copies:
        copy.wait()
    face, bricks = (sides_ref.shape[1], slots_ref.shape[1])
    lists_ref[...] = jnp.zeros(lists_ref.shape, I32)
    lists_ref[0:2, :face] = sides_ref[...]
    lists_ref[2:4, :face] = crosses_ref[...]
    lists_ref[4:5, :bricks] = slots_ref[...]
    items_out(sends_ref, items_ref, out_ref)


def weight_grad_body(
    merged_ref, even_side_ref, odd_side_ref, even_cross_ref, odd_cross_ref, turned_ref, mains_ref, ends_ref, lists_ref,
    ext_ref, parents_ref, sums_ref, pad_ref, part_ref, to_even_ref, to_odd_ref, table_ref,
):
    bricks, width = merged_ref.shape
    face = even_side_ref.shape[0]
    rows = bricks + 4 * face
    high, low = from_pairs(lists_ref, GY, even_side_ref, odd_side_ref)
    above, below = from_pairs(lists_ref, GX, even_cross_ref, odd_cross_ref)
    table_ref[:bricks] = merged_ref[...]
    table_ref[bricks:] = stack_rows(low[:, :width], high[:, :width], below[:face], above[:face])
    total = add_rows(ext_ref[...], crosses_of(lists_ref, face), above[face:], below[face:])
    part_ref[...] = total[:bricks]
    to_even, to_odd = by_pair(lists_ref, GY, total[bricks + face :], total[bricks : bricks + face])
    to_even_ref[...] = to_even.astype(BF)
    to_odd_ref[...] = to_odd.astype(BF)
    side_parents = stack_lanes(stack_rows(low[:, width:], high[:, width:]), parents_ref.shape[1])
    grads = [stack_parities(total[:bricks].astype(BF)), stack_parities(total[bricks:].astype(BF))]
    up_sum = dot_tn(jnp.concatenate(grads, axis=0), jnp.concatenate([parents_ref[...], side_parents], axis=0))
    coarse = up_sum.shape[1]
    count = sums_ref.shape[0]
    parts = up_sum.shape[0] // count
    for q in range(parts):
        sums_ref[:, q * coarse : (q + 1) * coarse] = up_sum[q * count : (q + 1) * count].astype(BF)
    lower_half = iota((rows, 2 * C), 1) < C
    zero = jnp.zeros((rows, 2 * C), BF)
    for x in range(4):
        for y in range(4):
            places = [(X, Y, dx, dy) for X, dx in options(x) for Y, dy in options(y)]
            at = (x * 4 + y) * RUN
            columns = table_ref[:, at : at + RUN]
            first = jnp.where(lower_half, columns[:, : 2 * C], zero)
            second = jnp.where(lower_half, zero, columns[:, 2 * C :])
            ends = jnp.concatenate([ends_ref[3 * dx + dy + 4] for _, _, dx, dy in places], axis=0)
            halo = dot(ends, jnp.concatenate([first, second], axis=0)).astype(BF)
            for i, (X, Y, _, _) in enumerate(places):
                pad_ref[X, Y, :, RUN:] = halo[i * bricks : (i + 1) * bricks]
            pad_ref[x + 1, y + 1, :, :RUN] = columns[:bricks]
            moved = [p for p in places if p[2:] != (0, 0)]
            if moved:
                main = jnp.concatenate([mains_ref[3 * dx + dy + 4] for _, _, dx, dy in moved], axis=0)
                got = dot(main, columns).astype(BF)
                for i, (X, Y, _, _) in enumerate(moved):
                    pad_ref[X, Y, :, :RUN] = got[i * bricks : (i + 1) * bricks]

    turned = turned_ref[...]
    lanes_low = iota((C, 2 * C), 1) < C
    sums = []
    for e in range(9):
        wide = dot(turned, inputs_at(pad_ref, e))

        def block(z, s):
            return wide[z * C : (z + 1) * C, s * 2 * C : (s + 1) * 2 * C]

        low = jnp.where(lanes_low, block(1, 0) + block(3, 1), block(0, 2) + block(2, 0))
        mid = jnp.where(lanes_low, block(0, 0) + block(2, 1), block(1, 0) + block(3, 1))
        high = jnp.where(lanes_low, block(1, 1) + block(3, 2), block(0, 0) + block(2, 1))
        for value in (low, mid, high):
            sums.append(value + pltpu.roll(value, C, 1))
    sums.append(jnp.zeros((C, 2 * C), F32))
    for pair in range(7):
        both = [jnp.where(lanes_low, sums[14 * h + 2 * pair], sums[14 * h + 2 * pair + 1]) for h in range(2)]
        at = parts * coarse + pair * 2 * C
        sums_ref[:, at : at + 2 * C] = jnp.concatenate(both, axis=0).astype(BF)


def inputs_at(pad_ref, e):
    bricks = pad_ref.shape[2]
    ex, ey = (e // 3, e % 3)
    return pad_ref[ex : ex + 4, ey : ey + 4].reshape(16 * bricks, WIDE)


def conv_body(pad_ref, weight_ref, out_ref, band_ref):
    bricks = pad_ref.shape[2]
    build_bands(weight_ref, band_ref)
    total = None
    for e in range(9):
        part = dot(inputs_at(pad_ref, e), band_ref[e])
        total = part if total is None else total + part
    for p in range(16):
        out_ref[:, p * RUN : (p + 1) * RUN] = total[p * bricks : (p + 1) * bricks].astype(BF)


def add_rows(base, lists, first, second):
    count, face = (base.shape[0], lists.shape[1])
    index = jnp.concatenate([lists[0:1], lists[1:2]], axis=1)
    chosen = ones_where(iota((count, 2 * face), 0) == index)
    return base + dot(chosen, stack_rows(first, second))


def merge_body(received_ref, up_ref, fine_ref, lists_ref, merged_ref, parents_ref, a_ref, b_ref):
    bricks, width = fine_ref.shape
    face = a_ref.shape[0]
    parents = merge(received_ref, slots_of(lists_ref, bricks), up_ref, fine_ref, merged_ref, parents_ref)
    lists = sides_of(lists_ref, face)
    lists = by_pair(lists_ref, GY, lists[0:1], lists[1:2])
    for out_ref, rows, owners in zip((a_ref, b_ref), pick_rows(lists, merged_ref[...]), pick_rows(lists, parents)):
        out_ref[:, :width] = rows.astype(BF)
        out_ref[:, width:] = owners.astype(BF)


def fine_grad_body(part_ref, lists_ref, even_ref, odd_ref, up_ref, grad_ref, replies_ref):
    bricks = part_ref.shape[0]
    face = even_ref.shape[0]
    from_next, from_prev = from_pairs(lists_ref, GY, even_ref, odd_ref)
    total = add_rows(part_ref[...], sides_of(lists_ref, face), from_next, from_prev)
    grad_ref[...] = total.astype(BF)
    items = dot(stack_parities(grad_ref[...]), up_ref[...]).astype(BF)
    items = jnp.concatenate([items[v * bricks : (v + 1) * bricks] for v in range(8)], axis=1)
    half = items.shape[1] // 2
    count, item_lanes = replies_ref.shape
    slots = slots_of(lists_ref, bricks)
    for j in range(item_lanes // half):
        piece = iota((count, bricks), 0) * (item_lanes // half) + j
        named = piece // 2 == slots
        rows = dot(ones_where(named & (piece % 2 == 0)), items[:, :half])
        rows += dot(ones_where(named & (piece % 2 == 1)), items[:, half:])
        replies_ref[:, j * half : (j + 1) * half] = rows.astype(BF)


def share_body(sums_ref, replies_ref, out_ref, devices):
    count, item_lanes = replies_ref.shape
    share = count // devices
    same = iota((count, count), 0) % share == iota((count, count), 1) % share
    out_ref[:, :item_lanes] = replies_ref[...]
    out_ref[:, item_lanes:] = dot(ones_where(same), sums_ref[...]).astype(BF)


def coarse_grad(back_ref, sends_ref, out_ref):
    capacity, devices = sends_ref.shape
    count, item_width = out_ref.shape
    half = item_width // 2
    lanes = back_ref.shape[0]
    pieces = 2 * capacity * devices // lanes
    group = lanes // devices
    for h in range(2):
        total = None
        for j in range(pieces):
            index = send_index(sends_ref[...], group, pieces, j)
            place = iota((count, lanes), 1) % group * pieces + j
            chosen = (iota((count, lanes), 0) == index) & (place % 2 == h)
            part = dot(ones_where(chosen), back_ref[:, j * half : (j + 1) * half])
            total = part if total is None else total + part
        out_ref[:, h * half : (h + 1) * half] = total.astype(BF)


def last_body(back_ref, sends_ref, conv_ref, up_ref, out_ref, scale):
    coarse_grad(back_ref, sends_ref, out_ref)
    count, width = back_ref.shape
    coarse = up_ref.shape[1]
    parts = up_ref.shape[0] // count
    at = width - 14 * C - parts * coarse
    for q in range(parts):
        up_ref[q * count : (q + 1) * count] = back_ref[:, at : at + coarse].astype(F32) * scale
        at += coarse
    for pair in range(7):
        turned = back_ref[:, at : at + 2 * C].astype(F32).T * scale
        at += 2 * C
        for h in range(2):
            for s in range(2):
                o = 14 * h + 2 * pair + s
                if o < 27:
                    conv_ref[o] = turned[s * C : (s + 1) * C, h * C : (h + 1) * C]


def swap_pairs(to_even, to_odd, axis):
    count = lax.axis_size(axis)

    def swap(value, first):
        lower = range(first, count - 1, 2)
        return lax.ppermute(value, axis, [(i, i + 1) for i in lower] + [(i + 1, i) for i in lower])

    from_odd = swap(to_odd, 1)
    return swap(to_even, 0), from_odd


def trade_rows(values, devices):
    rows, width = values.shape
    grid_view = values.reshape(devices, rows // devices, width)
    return lax.all_to_all(grid_view, ("gx", "gy"), split_axis=0, concat_axis=0, tiled=True).reshape(rows, width)


def on_device(
    fine_features, coarse_items, conv_weight, up_weight, neighbours,
    side_sends, cross_sends, parent_slots, coarse_sends, cotangent,
):
    fine = fine_features[0, 0]
    items = coarse_items[0, 0]
    cot = cotangent[0, 0]
    bricks, width = fine.shape
    face = side_sends.shape[-1]
    across_x, across_y = (lax.axis_size("gx"), lax.axis_size("gy"))
    devices = across_x * across_y
    capacity = coarse_sends.shape[-1]
    item_count, item_width = items.shape
    coarse = up_weight.shape[1]
    start = bricks + 2 * face
    sends = coarse_sends.transpose(0, 1, 3, 2)[0, 0]
    slots = parent_slots[0]
    sides = side_sends[0, 0]
    crosses = cross_sends[0, 0]
    near = neighbours.transpose(0, 3, 1, 2)[0]
    up_turned = up_weight.transpose(0, 2, 1).reshape(8 * C, coarse)
    half = item_width // 2
    count = 2 * C
    item_lanes = capacity * devices * item_width // count
    sums_width = 8 * C * coarse // count + 14 * C
    rows = shape((bricks, width))
    face_rows = shape((face, width))
    faces_and_parents = shape((face, width + item_width))
    two_faces = shape((2 * face, width))
    lists_shape = shape((8, 128), I32)
    band = pltpu.VMEM((9, WIDE, RUN), BF)
    conv_flops = 2 * 9 * 16 * bricks * WIDE * RUN

    listed = (sends, items, sides, crosses, slots)
    outgoing, lists = call(
        first_body, [shape((2 * capacity * devices, half)), lists_shape], *listed,
        scratch=[pltpu.VMEM(a.shape, a.dtype) for a in listed] + [pltpu.SemaphoreType.DMA((len(listed),))],
        in_hbm=True,
    )
    received = trade_rows(outgoing, devices)
    lane = jnp.arange(128, dtype=I32)[None]
    parity = jnp.where(lane == GX, lax.axis_index("gx") % 2, lax.axis_index("gy") % 2).astype(I32)
    table_rows = start + 2 * face
    ext_grad, low_cross, high_cross, turned, mains, ends, lists = call(
        table_grad_body,
        [
            shape((start, width), F32), face_rows, face_rows, shape((RUN, 16 * bricks)),
            shape((9, bricks, table_rows)), shape((9, bricks, 2 * table_rows)), lists_shape,
        ],
        cot, conv_weight, near, lists, parity,
        scratch=[band, pltpu.VMEM((6, 6, bricks, WIDE), F32)], flops=2 * conv_flops,
    )
    merged, parents, to_even, to_odd = call(
        merge_body, [rows, shape((8 * bricks, coarse)), faces_and_parents, faces_and_parents],
        received, up_turned, fine, lists,
    )
    sides = swap_pairs(to_even, to_odd, "gy")
    to_even, to_odd = call(cross_body, [two_faces, two_faces], merged, *sides, lists, low_cross, high_cross)
    crosses = swap_pairs(to_even, to_odd, "gx")
    sums, pad, fine_part, to_even, to_odd = call(
        weight_grad_body,
        [shape((count, sums_width)), shape((6, 6, bricks, WIDE)), shape((bricks, width), F32), face_rows, face_rows],
        merged, *sides, *crosses, turned, mains, ends, lists, ext_grad, parents,
        scratch=[pltpu.VMEM((table_rows, width), BF)], flops=conv_flops,
    )
    sums = trade_rows(sums, devices)
    side_grads = swap_pairs(to_even, to_odd, "gy")
    grad_fine, replies = call(
        fine_grad_body, [rows, shape((count, item_lanes))], fine_part, lists, *side_grads, up_turned
    )
    (output,) = call(conv_body, [rows], pad, conv_weight, scratch=[band], flops=conv_flops)
    (back,) = call(
        functools.partial(share_body, devices=devices), [shape((count, item_lanes + sums_width))], sums, replies
    )
    back = trade_rows(back, devices)
    scale = 1.0 / math.sqrt(64 * bricks * devices)
    grad_conv, grad_up, coarse_grad = call(
        functools.partial(last_body, scale=scale),
        [shape((27, C, C), F32), shape((8 * C, coarse), F32), shape((item_count, item_width))], back, sends,
    )
    return (
        output.reshape(1, 1, bricks, width),
        grad_fine.reshape(1, 1, bricks, width),
        coarse_grad.reshape(1, 1, item_count, item_width),
        grad_conv,
        grad_up.reshape(8, C, coarse).transpose(0, 2, 1),
    )


def solution(mesh):
    split = P(("groups", "gx"), "gy", None, None)
    placed = (split, split, P(), P(), split, split, split, P(("groups", "gx"), "gy", None), split, split)
    return jax.shard_map(
        on_device,
        mesh=mesh,
        in_specs=placed,
        out_specs=(split, split, split, P("groups", None, None), P("groups", None, None)),
        check_vma=False,
    )
```

```python
import functools
import math

import jax
import jax.numpy as jnp
from jax import lax
from jax.experimental import pallas as pl
from jax.experimental.pallas import tpu as pltpu
from jax.sharding import PartitionSpec as P

BF = jnp.bfloat16
F32 = jnp.float32
I32 = jnp.int32

C = 64
RUN = 4 * C
WIDE = RUN + 2 * C


def iota(shape, axis):
    return lax.broadcasted_iota(I32, shape, axis)


def ones_where(mask):
    return jnp.where(mask, 1.0, 0.0).astype(BF)


def dot(a, b):
    return jnp.dot(a, b, preferred_element_type=F32)


def dot_tn(a, b):
    return lax.dot_general(a, b, (((0,), (0,)), ((), ())), preferred_element_type=F32)


def dot_nt(a, b):
    return lax.dot_general(a, b, (((1,), (1,)), ((), ())), preferred_element_type=F32)


def column_of(row):
    size = row.shape[1]
    diagonal = iota((size, size), 0) == iota((size, size), 1)
    spread = jnp.broadcast_to(row.astype(F32), (size, size))
    return jnp.sum(jnp.where(diagonal, spread, 0.0), axis=1, keepdims=True).astype(I32)


def call(body, outs, *args, scratch=(), flops=0, in_hbm=False):
    moved = sum(a.size * a.dtype.itemsize for a in list(args) + list(outs))
    return pl.pallas_call(
        body,
        out_shape=tuple(outs),
        in_specs=[pl.BlockSpec(memory_space=pltpu.HBM) if in_hbm else pl.BlockSpec() for _ in args],
        scratch_shapes=tuple(scratch),
        cost_estimate=pl.CostEstimate(flops=flops, bytes_accessed=moved, transcendentals=0),
        compiler_params=pltpu.CompilerParams(vmem_limit_bytes=None if in_hbm else 28 * 2**20),
    )(*args)


def shape(dims, dtype=BF):
    return jax.ShapeDtypeStruct(dims, dtype)


def send_index(sends, group, pieces=1, j=0):
    capacity, devices = sends.shape
    lanes = devices * group
    spread = ones_where(iota((devices, lanes), 1) // group == iota((devices, lanes), 0))
    rows = dot(sends.astype(F32).astype(BF), spread)
    slot = (iota((capacity, lanes), 1) % group * pieces + j) // 2
    picked = jnp.where(slot == iota((capacity, lanes), 0), rows, 0.0)
    return jnp.sum(picked, axis=0, keepdims=True).astype(I32)


def items_out(sends_ref, items_ref, out_ref):
    capacity, devices = sends_ref.shape
    count, width = items_ref.shape
    half = width // 2
    group = 2 * capacity
    lanes = devices * group
    spread = ones_where(iota((lanes, devices), 0) // group == iota((lanes, devices), 1))
    slot = iota((lanes, capacity), 0) % group // 2
    values = dot_nt(spread, sends_ref[...].astype(F32).astype(BF))
    item = jnp.sum(jnp.where(slot == iota((lanes, capacity), 1), values, 0.0), axis=1, keepdims=True).astype(I32)
    place = jnp.where(item < count, item + iota((lanes, 1), 0) % 2 * count, -1)
    chosen = ones_where(iota((lanes, 2 * count), 1) == place)
    out_ref[...] = dot(chosen, jnp.concatenate([items_ref[:, :half], items_ref[:, half:]], axis=0)).astype(BF)


def merge(received_ref, slots, up_ref, fine_ref, merged_ref, parents_ref):
    bricks = fine_ref.shape[0]
    lanes, half = received_ref.shape
    slot = column_of(slots)
    place = iota((bricks, lanes), 1)
    named = place // 2 == slot
    received = received_ref[...]
    parents = jnp.concatenate(
        [dot(ones_where(named & (place % 2 == h)), received) for h in (0, 1)], axis=1
    ).astype(BF)
    coarse = 2 * half // 8
    stacked = jnp.concatenate([parents[:, v * coarse : (v + 1) * coarse] for v in range(8)], axis=0)
    parents_ref[...] = stacked
    lifted = dot_nt(stacked, up_ref[...])
    for v in range(8):
        cx, cy, cz = (v // 4, v // 2 % 2, v % 2)
        for parity in range(4):
            vx, vy = (2 * cx + parity // 2, 2 * cy + parity % 2)
            at = (vx * 4 + vy) * RUN + cz * 2 * C
            add = lifted[v * bricks : (v + 1) * bricks, parity * 2 * C : (parity + 1) * 2 * C]
            merged_ref[:, at : at + 2 * C] = (fine_ref[:, at : at + 2 * C].astype(F32) + add).astype(BF)
    return parents


def pick_rows(lists, rows):
    return [dot_tn(ones_where(iota((rows.shape[0], one.shape[1]), 0) == one), rows) for one in lists]


GX, GY = (0, 1)


def by_pair(lists_ref, axis, of_next, of_prev):
    odd = jnp.broadcast_to(lists_ref[5:6, axis : axis + 1], of_next.shape) == 1
    return jnp.where(odd, of_prev, of_next), jnp.where(odd, of_next, of_prev)


def from_pairs(lists_ref, axis, even_ref, odd_ref):
    return by_pair(lists_ref, axis, even_ref[...].astype(F32), odd_ref[...].astype(F32))


def stack_rows(*parts):
    return jnp.concatenate([p.astype(F32) for p in parts], axis=0).astype(BF)


def sides_of(lists_ref, face):
    return lists_ref[0:2, :face]


def crosses_of(lists_ref, face):
    return lists_ref[2:4, :face]


def slots_of(lists_ref, bricks):
    return lists_ref[4:5, :bricks]


def cross_body(merged_ref, even_ref, odd_ref, lists_ref, a_ref, b_ref):
    face, width = a_ref.shape
    high, low = from_pairs(lists_ref, GY, even_ref, odd_ref)
    rows = jnp.concatenate([merged_ref[...], stack_rows(low[:, :width], high[:, :width])], axis=0)
    lists = crosses_of(lists_ref, face)
    picked = pick_rows(by_pair(lists_ref, GX, lists[0:1], lists[1:2]), rows)
    a_ref[...] = picked[0].astype(BF)
    b_ref[...] = picked[1].astype(BF)


def build_bands(weight_ref, band_ref):
    zero = jnp.zeros((C, C), BF)
    blank = jnp.zeros((C, 2 * C), BF)

    def pair(a, b):
        return jnp.concatenate([a, b], axis=1)

    for e in range(9):
        low, mid, high = (weight_ref[3 * e + z] for z in range(3))
        first, second = (pair(mid, low), pair(high, mid))
        left, right = (pair(low, zero), pair(zero, high))
        rows = (
            (first, blank),
            (second, left),
            (right, first),
            (blank, second),
            (blank, right),
            (left, blank),
        )
        for z, halves in enumerate(rows):
            for s in range(2):
                band_ref[e, z * C : (z + 1) * C, s * 2 * C : (s + 1) * 2 * C] = halves[s]


def options(at):
    return [(at + 1, 0)] + ([(5, 1)] if at == 0 else []) + ([(0, -1)] if at == 3 else [])


def offset_of(dx, dy, dz):
    return (dx + 1) * 9 + (dy + 1) * 3 + dz + 1


def stack_lanes(value, lanes):
    return jnp.concatenate([value[:, p * lanes : (p + 1) * lanes] for p in range(value.shape[1] // lanes)], axis=0)


def stack_parities(value):
    stacked = []
    for v in range(8):
        cx, cy, cz = (v // 4, v // 2 % 2, v % 2)
        lanes = []
        for parity in range(4):
            at = ((2 * cx + parity // 2) * 4 + 2 * cy + parity % 2) * RUN + cz * 2 * C
            lanes.append(value[:, at : at + 2 * C])
        stacked.append(jnp.concatenate(lanes, axis=1))
    return jnp.concatenate(stacked, axis=0)


def stack_runs(ref):
    return jnp.concatenate([ref[:, p * RUN : (p + 1) * RUN] for p in range(16)], axis=0)


def split_two(value):
    head = value.astype(BF)
    return head, (value - head.astype(F32)).astype(BF)


def table_grad_body(
    cot_ref, weight_ref, near_ref, lists_ref, parity_ref,
    ext_ref, even_ref, odd_ref, turned_ref, mains_ref, ends_ref, again_ref, band_ref, pad_ref,
):
    again_ref[...] = lists_ref[...]
    again_ref[5:6] = parity_ref[...]
    bricks = cot_ref.shape[0]
    face = even_ref.shape[0]
    start = ext_ref.shape[0]
    rows = start + 2 * face
    build_bands(weight_ref, band_ref)
    cot = stack_runs(cot_ref)
    turned_ref[...] = cot.T
    pad_ref[...] = jnp.zeros(pad_ref.shape, F32)
    for e in range(9):
        ex, ey = (e // 3, e % 3)
        part = dot_nt(cot, band_ref[e]).reshape(4, 4, bricks, WIDE)
        pad_ref[ex : ex + 4, ey : ey + 4] += part
    near = [near_ref[o] for o in range(27)]

    def chooser(which):
        index = jnp.concatenate([near[o] for o in which], axis=1)
        return ones_where(iota((rows, index.shape[1]), 0) == index)

    lower_half = iota((rows, 2 * C), 1) < C
    cache = {}
    for x in range(4):
        for y in range(4):
            places = [(X, Y, dx, dy) for X, dx in options(x) for Y, dy in options(y)]
            key = tuple((dx, dy) for _, _, dx, dy in places)
            if key not in cache:
                moved = [d for d in key if d != (0, 0)]
                main = chooser([offset_of(*d, 0) for d in moved] * 2) if moved else None
                up = chooser([offset_of(*d, 1) for d in key] * 2)
                down = chooser([offset_of(*d, -1) for d in key] * 2)
                cache[key] = (main, jnp.concatenate([up, down], axis=0))
            main, ends = cache[key]
            own = pad_ref[x + 1, y + 1, :, :RUN]
            own = jnp.concatenate([own, jnp.zeros((rows - bricks, RUN), F32)], axis=0)
            if main is not None:
                parts = [split_two(pad_ref[X, Y, :, :RUN]) for X, Y, dx, dy in places if (dx, dy) != (0, 0)]
                value = jnp.concatenate([p[0] for p in parts] + [p[1] for p in parts], axis=0)
                own += dot(main, value)
            parts = [split_two(pad_ref[X, Y, :, RUN:]) for X, Y, _, _ in places]
            value = jnp.concatenate([p[0] for p in parts] + [p[1] for p in parts], axis=0)
            halo = dot(ends, value)
            first = own[:, : 2 * C] + jnp.where(lower_half, halo[:rows], 0.0)
            second = own[:, 2 * C :] + jnp.where(lower_half, 0.0, halo[rows:])
            total = jnp.concatenate([first, second], axis=1)
            at = (x * 4 + y) * RUN
            ext_ref[:, at : at + RUN] = total[:start]
            even, odd = by_pair(again_ref, GX, total[start + face :], total[start : start + face])
            even_ref[:, at : at + RUN] = even.astype(BF)
            odd_ref[:, at : at + RUN] = odd.astype(BF)
    make_choosers(near_ref, rows, mains_ref, ends_ref)


def make_choosers(near_ref, rows, mains_ref, ends_ref):
    bricks = mains_ref.shape[1]
    near = jnp.concatenate([near_ref[o] for o in range(27)] + [jnp.zeros((5, bricks), I32)], axis=0)
    near = near.astype(F32).T.astype(I32)
    place = iota((bricks, rows), 1)
    pair_place = iota((bricks, 2 * rows), 1)
    for d in range(9):
        down, straight, up = (near[:, 3 * d + z : 3 * d + z + 1] for z in range(3))
        mains_ref[d] = ones_where(place == straight)
        ends_ref[d] = ones_where(pair_place == jnp.where(pair_place < rows, up, down + rows))


def first_body(
    sends_hbm, items_hbm, sides_hbm, crosses_hbm, slots_hbm, out_ref, lists_ref,
    sends_ref, items_ref, sides_ref, crosses_ref, slots_ref, arrived,
):
    sources = (sends_hbm, items_hbm, sides_hbm, crosses_hbm, slots_hbm)
    places = (sends_ref, items_ref, sides_ref, crosses_ref, slots_ref)
    copies = [pltpu.make_async_copy(s, p, arrived.at[i]) for i, (s, p) in enumerate(zip(sources, places))]
    for copy in copies:
        copy.start()
    for copy in copies:
        copy.wait()
    face, bricks = (sides_ref.shape[1], slots_ref.shape[1])
    lists_ref[...] = jnp.zeros(lists_ref.shape, I32)
    lists_ref[0:2, :face] = sides_ref[...]
    lists_ref[2:4, :face] = crosses_ref[...]
    lists_ref[4:5, :bricks] = slots_ref[...]
    items_out(sends_ref, items_ref, out_ref)


def weight_grad_body(
    merged_ref, even_side_ref, odd_side_ref, even_cross_ref, odd_cross_ref, even_grad_ref, odd_grad_ref,
    turned_ref, mains_ref, ends_ref, lists_ref, ext_ref, parents_ref, sums_ref, pad_ref, part_ref, to_even_ref, to_odd_ref, table_ref,
):
    bricks, width = merged_ref.shape
    face = even_side_ref.shape[0]
    rows = bricks + 4 * face
    high, low = from_pairs(lists_ref, GY, even_side_ref, odd_side_ref)
    above, below = from_pairs(lists_ref, GX, even_cross_ref, odd_cross_ref)
    table_ref[:bricks] = merged_ref[...]
    table_ref[bricks:] = stack_rows(low[:, :width], high[:, :width], below, above)
    from_next, from_prev = from_pairs(lists_ref, GX, even_grad_ref, odd_grad_ref)
    total = add_rows(ext_ref[...], crosses_of(lists_ref, face), from_next, from_prev)
    part_ref[...] = total[:bricks]
    to_even, to_odd = by_pair(lists_ref, GY, total[bricks + face :], total[bricks : bricks + face])
    to_even_ref[...] = to_even.astype(BF)
    to_odd_ref[...] = to_odd.astype(BF)
    side_parents = stack_lanes(stack_rows(low[:, width:], high[:, width:]), parents_ref.shape[1])
    grads = [stack_parities(total[:bricks].astype(BF)), stack_parities(total[bricks:].astype(BF))]
    up_sum = dot_tn(jnp.concatenate(grads, axis=0), jnp.concatenate([parents_ref[...], side_parents], axis=0))
    coarse = up_sum.shape[1]
    count = sums_ref.shape[0]
    parts = up_sum.shape[0] // count
    for q in range(parts):
        sums_ref[:, q * coarse : (q + 1) * coarse] = up_sum[q * count : (q + 1) * count].astype(BF)
    lower_half = iota((rows, 2 * C), 1) < C
    zero = jnp.zeros((rows, 2 * C), BF)
    for x in range(4):
        for y in range(4):
            places = [(X, Y, dx, dy) for X, dx in options(x) for Y, dy in options(y)]
            at = (x * 4 + y) * RUN
            columns = table_ref[:, at : at + RUN]
            first = jnp.where(lower_half, columns[:, : 2 * C], zero)
            second = jnp.where(lower_half, zero, columns[:, 2 * C :])
            ends = jnp.concatenate([ends_ref[3 * dx + dy + 4] for _, _, dx, dy in places], axis=0)
            halo = dot(ends, jnp.concatenate([first, second], axis=0)).astype(BF)
            for i, (X, Y, _, _) in enumerate(places):
                pad_ref[X, Y, :, RUN:] = halo[i * bricks : (i + 1) * bricks]
            pad_ref[x + 1, y + 1, :, :RUN] = columns[:bricks]
            moved = [p for p in places if p[2:] != (0, 0)]
            if moved:
                main = jnp.concatenate([mains_ref[3 * dx + dy + 4] for _, _, dx, dy in moved], axis=0)
                got = dot(main, columns).astype(BF)
                for i, (X, Y, _, _) in enumerate(moved):
                    pad_ref[X, Y, :, :RUN] = got[i * bricks : (i + 1) * bricks]

    turned = turned_ref[...]
    lanes_low = iota((C, 2 * C), 1) < C
    sums = []
    for e in range(9):
        wide = dot(turned, inputs_at(pad_ref, e))

        def block(z, s):
            return wide[z * C : (z + 1) * C, s * 2 * C : (s + 1) * 2 * C]

        low = jnp.where(lanes_low, block(1, 0) + block(3, 1), block(0, 2) + block(2, 0))
        mid = jnp.where(lanes_low, block(0, 0) + block(2, 1), block(1, 0) + block(3, 1))
        high = jnp.where(lanes_low, block(1, 1) + block(3, 2), block(0, 0) + block(2, 1))
        for value in (low, mid, high):
            sums.append(value + pltpu.roll(value, C, 1))
    sums.append(jnp.zeros((C, 2 * C), F32))
    for pair in range(7):
        both = [jnp.where(lanes_low, sums[14 * h + 2 * pair], sums[14 * h + 2 * pair + 1]) for h in range(2)]
        at = parts * coarse + pair * 2 * C
        sums_ref[:, at : at + 2 * C] = jnp.concatenate(both, axis=0).astype(BF)


def inputs_at(pad_ref, e):
    bricks = pad_ref.shape[2]
    ex, ey = (e // 3, e % 3)
    return pad_ref[ex : ex + 4, ey : ey + 4].reshape(16 * bricks, WIDE)


def conv_body(pad_ref, weight_ref, out_ref, band_ref):
    bricks = pad_ref.shape[2]
    build_bands(weight_ref, band_ref)
    total = None
    for e in range(9):
        part = dot(inputs_at(pad_ref, e), band_ref[e])
        total = part if total is None else total + part
    for p in range(16):
        out_ref[:, p * RUN : (p + 1) * RUN] = total[p * bricks : (p + 1) * bricks].astype(BF)


def add_rows(base, lists, first, second):
    count, face = (base.shape[0], lists.shape[1])
    index = jnp.concatenate([lists[0:1], lists[1:2]], axis=1)
    chosen = ones_where(iota((count, 2 * face), 0) == index)
    return base + dot(chosen, stack_rows(first, second))


def merge_body(received_ref, up_ref, fine_ref, lists_ref, merged_ref, parents_ref, a_ref, b_ref):
    bricks, width = fine_ref.shape
    face = a_ref.shape[0]
    parents = merge(received_ref, slots_of(lists_ref, bricks), up_ref, fine_ref, merged_ref, parents_ref)
    lists = sides_of(lists_ref, face)
    lists = by_pair(lists_ref, GY, lists[0:1], lists[1:2])
    for out_ref, rows, owners in zip((a_ref, b_ref), pick_rows(lists, merged_ref[...]), pick_rows(lists, parents)):
        out_ref[:, :width] = rows.astype(BF)
        out_ref[:, width:] = owners.astype(BF)


def fine_grad_body(part_ref, lists_ref, even_ref, odd_ref, up_ref, grad_ref, replies_ref):
    bricks = part_ref.shape[0]
    face = even_ref.shape[0]
    from_next, from_prev = from_pairs(lists_ref, GY, even_ref, odd_ref)
    total = add_rows(part_ref[...], sides_of(lists_ref, face), from_next, from_prev)
    grad_ref[...] = total.astype(BF)
    items = dot(stack_parities(grad_ref[...]), up_ref[...]).astype(BF)
    items = jnp.concatenate([items[v * bricks : (v + 1) * bricks] for v in range(8)], axis=1)
    half = items.shape[1] // 2
    count, item_lanes = replies_ref.shape
    slots = slots_of(lists_ref, bricks)
    for j in range(item_lanes // half):
        piece = iota((count, bricks), 0) * (item_lanes // half) + j
        named = piece // 2 == slots
        rows = dot(ones_where(named & (piece % 2 == 0)), items[:, :half])
        rows += dot(ones_where(named & (piece % 2 == 1)), items[:, half:])
        replies_ref[:, j * half : (j + 1) * half] = rows.astype(BF)


def share_body(sums_ref, replies_ref, out_ref, devices):
    count, item_lanes = replies_ref.shape
    share = count // devices
    same = iota((count, count), 0) % share == iota((count, count), 1) % share
    out_ref[:, :item_lanes] = replies_ref[...]
    out_ref[:, item_lanes:] = dot(ones_where(same), sums_ref[...]).astype(BF)


def coarse_grad(back_ref, sends_ref, out_ref):
    capacity, devices = sends_ref.shape
    count, item_width = out_ref.shape
    half = item_width // 2
    lanes = back_ref.shape[0]
    pieces = 2 * capacity * devices // lanes
    group = lanes // devices
    for h in range(2):
        total = None
        for j in range(pieces):
            index = send_index(sends_ref[...], group, pieces, j)
            place = iota((count, lanes), 1) % group * pieces + j
            chosen = (iota((count, lanes), 0) == index) & (place % 2 == h)
            part = dot(ones_where(chosen), back_ref[:, j * half : (j + 1) * half])
            total = part if total is None else total + part
        out_ref[:, h * half : (h + 1) * half] = total.astype(BF)


def last_body(back_ref, sends_ref, conv_ref, up_ref, out_ref, scale):
    coarse_grad(back_ref, sends_ref, out_ref)
    count, width = back_ref.shape
    coarse = up_ref.shape[1]
    parts = up_ref.shape[0] // count
    at = width - 14 * C - parts * coarse
    for q in range(parts):
        up_ref[q * count : (q + 1) * count] = back_ref[:, at : at + coarse].astype(F32) * scale
        at += coarse
    for pair in range(7):
        turned = back_ref[:, at : at + 2 * C].astype(F32).T * scale
        at += 2 * C
        for h in range(2):
            for s in range(2):
                o = 14 * h + 2 * pair + s
                if o < 27:
                    conv_ref[o] = turned[s * C : (s + 1) * C, h * C : (h + 1) * C]


def swap_pairs(to_even, to_odd, axis):
    count = lax.axis_size(axis)

    def swap(value, first):
        lower = range(first, count - 1, 2)
        return lax.ppermute(value, axis, [(i, i + 1) for i in lower] + [(i + 1, i) for i in lower])

    from_odd = swap(to_odd, 1)
    return swap(to_even, 0), from_odd


def trade_rows(values, devices):
    rows, width = values.shape
    grid_view = values.reshape(devices, rows // devices, width)
    return lax.all_to_all(grid_view, ("gx", "gy"), split_axis=0, concat_axis=0, tiled=True).reshape(rows, width)


def on_device(
    fine_features, coarse_items, conv_weight, up_weight, neighbours,
    side_sends, cross_sends, parent_slots, coarse_sends, cotangent,
):
    fine = fine_features[0, 0]
    items = coarse_items[0, 0]
    cot = cotangent[0, 0]
    bricks, width = fine.shape
    face = side_sends.shape[-1]
    across_x, across_y = (lax.axis_size("gx"), lax.axis_size("gy"))
    devices = across_x * across_y
    capacity = coarse_sends.shape[-1]
    item_count, item_width = items.shape
    coarse = up_weight.shape[1]
    start = bricks + 2 * face
    sends = coarse_sends.transpose(0, 1, 3, 2)[0, 0]
    slots = parent_slots[0]
    sides = side_sends[0, 0]
    crosses = cross_sends[0, 0]
    near = neighbours.transpose(0, 3, 1, 2)[0]
    up_turned = up_weight.transpose(0, 2, 1).reshape(8 * C, coarse)
    half = item_width // 2
    count = 2 * C
    item_lanes = capacity * devices * item_width // count
    sums_width = 8 * C * coarse // count + 14 * C
    rows = shape((bricks, width))
    face_rows = shape((face, width))
    faces_and_parents = shape((face, width + item_width))
    lists_shape = shape((8, 128), I32)
    band = pltpu.VMEM((9, WIDE, RUN), BF)
    conv_flops = 2 * 9 * 16 * bricks * WIDE * RUN

    listed = (sends, items, sides, crosses, slots)
    outgoing, lists = call(
        first_body, [shape((2 * capacity * devices, half)), lists_shape], *listed,
        scratch=[pltpu.VMEM(a.shape, a.dtype) for a in listed] + [pltpu.SemaphoreType.DMA((len(listed),))],
        in_hbm=True,
    )
    received = trade_rows(outgoing, devices)
    lane = jnp.arange(128, dtype=I32)[None]
    parity = jnp.where(lane == GX, lax.axis_index("gx") % 2, lax.axis_index("gy") % 2).astype(I32)
    table_rows = start + 2 * face
    ext_grad, to_even, to_odd, turned, mains, ends, lists = call(
        table_grad_body,
        [
            shape((start, width), F32), face_rows, face_rows, shape((RUN, 16 * bricks)),
            shape((9, bricks, table_rows)), shape((9, bricks, 2 * table_rows)), lists_shape,
        ],
        cot, conv_weight, near, lists, parity,
        scratch=[band, pltpu.VMEM((6, 6, bricks, WIDE), F32)], flops=2 * conv_flops,
    )
    cross_grads = swap_pairs(to_even, to_odd, "gx")
    merged, parents, to_even, to_odd = call(
        merge_body, [rows, shape((8 * bricks, coarse)), faces_and_parents, faces_and_parents],
        received, up_turned, fine, lists,
    )
    sides = swap_pairs(to_even, to_odd, "gy")
    to_even, to_odd = call(cross_body, [face_rows, face_rows], merged, *sides, lists)
    crosses = swap_pairs(to_even, to_odd, "gx")
    sums, pad, fine_part, to_even, to_odd = call(
        weight_grad_body,
        [shape((count, sums_width)), shape((6, 6, bricks, WIDE)), shape((bricks, width), F32), face_rows, face_rows],
        merged, *sides, *crosses, *cross_grads, turned, mains, ends, lists, ext_grad, parents,
        scratch=[pltpu.VMEM((table_rows, width), BF)], flops=conv_flops,
    )
    sums = trade_rows(sums, devices)
    side_grads = swap_pairs(to_even, to_odd, "gy")
    grad_fine, replies = call(
        fine_grad_body, [rows, shape((count, item_lanes))], fine_part, lists, *side_grads, up_turned
    )
    (output,) = call(conv_body, [rows], pad, conv_weight, scratch=[band], flops=conv_flops)
    (back,) = call(
        functools.partial(share_body, devices=devices), [shape((count, item_lanes + sums_width))], sums, replies
    )
    back = trade_rows(back, devices)
    scale = 1.0 / math.sqrt(64 * bricks * devices)
    grad_conv, grad_up, coarse_grad = call(
        functools.partial(last_body, scale=scale),
        [shape((27, C, C), F32), shape((8 * C, coarse), F32), shape((item_count, item_width))], back, sends,
    )
    return (
        output.reshape(1, 1, bricks, width),
        grad_fine.reshape(1, 1, bricks, width),
        coarse_grad.reshape(1, 1, item_count, item_width),
        grad_conv,
        grad_up.reshape(8, C, coarse).transpose(0, 2, 1),
    )


def solution(mesh):
    split = P(("groups", "gx"), "gy", None, None)
    placed = (split, split, P(), P(), split, split, split, P(("groups", "gx"), "gy", None), split, split)
    return jax.shard_map(
        on_device,
        mesh=mesh,
        in_specs=placed,
        out_specs=(split, split, split, P("groups", None, None), P("groups", None, None)),
        check_vma=False,
    )
```

```python
import functools
import math

import jax
import jax.numpy as jnp
from jax import lax
from jax.experimental import pallas as pl
from jax.experimental.pallas import tpu as pltpu
from jax.sharding import Mesh
from jax.sharding import PartitionSpec as P

BF = jnp.bfloat16
F32 = jnp.float32
I32 = jnp.int32

C = 64
RUN = 4 * C
WIDE = RUN + 2 * C


def iota(shape, axis):
    return lax.broadcasted_iota(I32, shape, axis)


def ones_where(mask):
    return jnp.where(mask, 1.0, 0.0).astype(BF)


def dot(a, b):
    return jnp.dot(a, b, preferred_element_type=F32)


def dot_tn(a, b):
    return lax.dot_general(a, b, (((0,), (0,)), ((), ())), preferred_element_type=F32)


def dot_nt(a, b):
    return lax.dot_general(a, b, (((1,), (1,)), ((), ())), preferred_element_type=F32)


def column_of(row):
    size = row.shape[1]
    diagonal = iota((size, size), 0) == iota((size, size), 1)
    spread = jnp.broadcast_to(row.astype(F32), (size, size))
    return jnp.sum(jnp.where(diagonal, spread, 0.0), axis=1, keepdims=True).astype(I32)


def call(body, outs, *args, scratch=(), flops=0, in_hbm=False):
    moved = sum(a.size * a.dtype.itemsize for a in list(args) + list(outs))
    return pl.pallas_call(
        body,
        out_shape=tuple(outs),
        in_specs=[pl.BlockSpec(memory_space=pltpu.HBM) if in_hbm else pl.BlockSpec() for _ in args],
        scratch_shapes=tuple(scratch),
        cost_estimate=pl.CostEstimate(flops=flops, bytes_accessed=moved, transcendentals=0),
        compiler_params=pltpu.CompilerParams(vmem_limit_bytes=None if in_hbm else 28 * 2**20),
    )(*args)


def shape(dims, dtype=BF):
    return jax.ShapeDtypeStruct(dims, dtype)


def items_out(sends_ref, items_ref, out_ref):
    capacity, devices = sends_ref.shape
    count, width = items_ref.shape
    half = width // 2
    group = 2 * capacity
    lanes = devices * group
    spread = ones_where(iota((lanes, devices), 0) // group == iota((lanes, devices), 1))
    slot = iota((lanes, capacity), 0) % group // 2
    values = dot_nt(spread, sends_ref[...].astype(F32).astype(BF))
    item = jnp.sum(jnp.where(slot == iota((lanes, capacity), 1), values, 0.0), axis=1, keepdims=True).astype(I32)
    place = jnp.where(item < count, item + iota((lanes, 1), 0) % 2 * count, -1)
    chosen = ones_where(iota((lanes, 2 * count), 1) == place)
    out_ref[...] = dot(chosen, jnp.concatenate([items_ref[:, :half], items_ref[:, half:]], axis=0)).astype(BF)


def merge(received_ref, slots, up_ref, fine_ref, merged_ref, parents_ref):
    bricks = fine_ref.shape[0]
    lanes, half = received_ref.shape
    slot = column_of(slots)
    place = iota((bricks, lanes), 1)
    named = place // 2 == slot
    received = received_ref[...]
    parents = jnp.concatenate(
        [dot(ones_where(named & (place % 2 == h)), received) for h in (0, 1)], axis=1
    ).astype(BF)
    coarse = 2 * half // 8
    stacked = jnp.concatenate([parents[:, v * coarse : (v + 1) * coarse] for v in range(8)], axis=0)
    parents_ref[...] = stacked
    lifted = dot_nt(stacked, up_ref[...])
    for v in range(8):
        cx, cy, cz = (v // 4, v // 2 % 2, v % 2)
        for parity in range(4):
            vx, vy = (2 * cx + parity // 2, 2 * cy + parity % 2)
            at = (vx * 4 + vy) * RUN + cz * 2 * C
            add = lifted[v * bricks : (v + 1) * bricks, parity * 2 * C : (parity + 1) * 2 * C]
            merged_ref[:, at : at + 2 * C] = (fine_ref[:, at : at + 2 * C].astype(F32) + add).astype(BF)
    return parents


def pick_rows(lists, rows):
    return [dot_tn(ones_where(iota((rows.shape[0], one.shape[1]), 0) == one), rows) for one in lists]


GX, GY = (0, 1)
GX_AXES = ("x", "core")


def by_pair(lists_ref, axis, of_next, of_prev):
    odd = jnp.broadcast_to(lists_ref[5:6, axis : axis + 1], of_next.shape) == 1
    return jnp.where(odd, of_prev, of_next), jnp.where(odd, of_next, of_prev)


def from_pairs(lists_ref, axis, even_ref, odd_ref):
    return by_pair(lists_ref, axis, even_ref[...].astype(F32), odd_ref[...].astype(F32))


def stack_rows(*parts):
    return jnp.concatenate([p.astype(F32) for p in parts], axis=0).astype(BF)


def sides_of(lists_ref, face):
    return lists_ref[0:2, :face]


def crosses_of(lists_ref, face):
    return lists_ref[2:4, :face]


def slots_of(lists_ref, bricks):
    return lists_ref[4:5, :bricks]


def cross_body(merged_ref, even_ref, odd_ref, lists_ref, a_ref, b_ref):
    face, width = a_ref.shape
    high, low = from_pairs(lists_ref, GY, even_ref, odd_ref)
    rows = jnp.concatenate([merged_ref[...], stack_rows(low[:, :width], high[:, :width])], axis=0)
    lists = crosses_of(lists_ref, face)
    picked = pick_rows(by_pair(lists_ref, GX, lists[0:1], lists[1:2]), rows)
    a_ref[...] = picked[0].astype(BF)
    b_ref[...] = picked[1].astype(BF)


def build_bands(weight_ref, band_ref):
    zero = jnp.zeros((C, C), BF)
    blank = jnp.zeros((C, 2 * C), BF)

    def pair(a, b):
        return jnp.concatenate([a, b], axis=1)

    for e in range(9):
        low, mid, high = (weight_ref[3 * e + z] for z in range(3))
        first, second = (pair(mid, low), pair(high, mid))
        left, right = (pair(low, zero), pair(zero, high))
        rows = (
            (first, blank),
            (second, left),
            (right, first),
            (blank, second),
            (blank, right),
            (left, blank),
        )
        for z, halves in enumerate(rows):
            for s in range(2):
                band_ref[e, z * C : (z + 1) * C, s * 2 * C : (s + 1) * 2 * C] = halves[s]


def options(at):
    return [(at + 1, 0)] + ([(5, 1)] if at == 0 else []) + ([(0, -1)] if at == 3 else [])


def offset_of(dx, dy, dz):
    return (dx + 1) * 9 + (dy + 1) * 3 + dz + 1


def stack_lanes(value, lanes):
    return jnp.concatenate([value[:, p * lanes : (p + 1) * lanes] for p in range(value.shape[1] // lanes)], axis=0)


def stack_parities(value):
    stacked = []
    for v in range(8):
        cx, cy, cz = (v // 4, v // 2 % 2, v % 2)
        lanes = []
        for parity in range(4):
            at = ((2 * cx + parity // 2) * 4 + 2 * cy + parity % 2) * RUN + cz * 2 * C
            lanes.append(value[:, at : at + 2 * C])
        stacked.append(jnp.concatenate(lanes, axis=1))
    return jnp.concatenate(stacked, axis=0)


def stack_runs(ref):
    return jnp.concatenate([ref[:, p * RUN : (p + 1) * RUN] for p in range(16)], axis=0)


def split_two(value):
    head = value.astype(BF)
    return head, (value - head.astype(F32)).astype(BF)


def table_grad_body(
    cot_ref, weight_ref, near_ref, lists_ref, parity_ref,
    ext_ref, even_ref, odd_ref, turned_ref, mains_ref, ends_ref, again_ref, band_ref, pad_ref,
):
    again_ref[...] = lists_ref[...]
    again_ref[5:6] = parity_ref[...]
    bricks = cot_ref.shape[0]
    face = even_ref.shape[0]
    start = ext_ref.shape[0]
    rows = start + 2 * face
    build_bands(weight_ref, band_ref)
    cot = stack_runs(cot_ref)
    turned_ref[...] = cot.T
    pad_ref[...] = jnp.zeros(pad_ref.shape, F32)
    for e in range(9):
        ex, ey = (e // 3, e % 3)
        part = dot_nt(cot, band_ref[e]).reshape(4, 4, bricks, WIDE)
        pad_ref[ex : ex + 4, ey : ey + 4] += part
    near = [near_ref[o] for o in range(27)]

    def chooser(which):
        index = jnp.concatenate([near[o] for o in which], axis=1)
        return ones_where(iota((rows, index.shape[1]), 0) == index)

    lower_half = iota((rows, 2 * C), 1) < C
    cache = {}
    for x in range(4):
        for y in range(4):
            places = [(X, Y, dx, dy) for X, dx in options(x) for Y, dy in options(y)]
            key = tuple((dx, dy) for _, _, dx, dy in places)
            if key not in cache:
                moved = [d for d in key if d != (0, 0)]
                main = chooser([offset_of(*d, 0) for d in moved] * 2) if moved else None
                up = chooser([offset_of(*d, 1) for d in key] * 2)
                down = chooser([offset_of(*d, -1) for d in key] * 2)
                cache[key] = (main, jnp.concatenate([up, down], axis=0))
            main, ends = cache[key]
            own = pad_ref[x + 1, y + 1, :, :RUN]
            own = jnp.concatenate([own, jnp.zeros((rows - bricks, RUN), F32)], axis=0)
            if main is not None:
                parts = [split_two(pad_ref[X, Y, :, :RUN]) for X, Y, dx, dy in places if (dx, dy) != (0, 0)]
                value = jnp.concatenate([p[0] for p in parts] + [p[1] for p in parts], axis=0)
                own += dot(main, value)
            parts = [split_two(pad_ref[X, Y, :, RUN:]) for X, Y, _, _ in places]
            value = jnp.concatenate([p[0] for p in parts] + [p[1] for p in parts], axis=0)
            halo = dot(ends, value)
            first = own[:, : 2 * C] + jnp.where(lower_half, halo[:rows], 0.0)
            second = own[:, 2 * C :] + jnp.where(lower_half, 0.0, halo[rows:])
            total = jnp.concatenate([first, second], axis=1)
            at = (x * 4 + y) * RUN
            ext_ref[:, at : at + RUN] = total[:start]
            even, odd = by_pair(again_ref, GX, total[start + face :], total[start : start + face])
            even_ref[:, at : at + RUN] = even.astype(BF)
            odd_ref[:, at : at + RUN] = odd.astype(BF)
    make_choosers(near_ref, rows, mains_ref, ends_ref)


def make_choosers(near_ref, rows, mains_ref, ends_ref):
    bricks = mains_ref.shape[1]
    near = jnp.concatenate([near_ref[o] for o in range(27)] + [jnp.zeros((5, bricks), I32)], axis=0)
    near = near.astype(F32).T.astype(I32)
    place = iota((bricks, rows), 1)
    pair_place = iota((bricks, 2 * rows), 1)
    for d in range(9):
        down, straight, up = (near[:, 3 * d + z : 3 * d + z + 1] for z in range(3))
        mains_ref[d] = ones_where(place == straight)
        ends_ref[d] = ones_where(pair_place == jnp.where(pair_place < rows, up, down + rows))


def first_body(
    sends_hbm, items_hbm, sides_hbm, crosses_hbm, slots_hbm, out_ref, lists_ref,
    sends_ref, items_ref, sides_ref, crosses_ref, slots_ref, arrived,
):
    sources = (sends_hbm, items_hbm, sides_hbm, crosses_hbm, slots_hbm)
    places = (sends_ref, items_ref, sides_ref, crosses_ref, slots_ref)
    copies = [pltpu.make_async_copy(s, p, arrived.at[i]) for i, (s, p) in enumerate(zip(sources, places))]
    for copy in copies:
        copy.start()
    for copy in copies:
        copy.wait()
    face, bricks = (sides_ref.shape[1], slots_ref.shape[1])
    lists_ref[...] = jnp.zeros(lists_ref.shape, I32)
    lists_ref[0:2, :face] = sides_ref[...]
    lists_ref[2:4, :face] = crosses_ref[...]
    lists_ref[4:5, :bricks] = slots_ref[...]
    items_out(sends_ref, items_ref, out_ref)


def weight_grad_body(
    merged_ref, even_side_ref, odd_side_ref, even_cross_ref, odd_cross_ref, even_grad_ref, odd_grad_ref,
    turned_ref, mains_ref, ends_ref, lists_ref, ext_ref, parents_ref,
    kept_ref, given_ref, pad_ref, part_ref, to_even_ref, to_odd_ref, table_ref, sums_ref,
):
    bricks, width = merged_ref.shape
    face = even_side_ref.shape[0]
    rows = bricks + 4 * face
    high, low = from_pairs(lists_ref, GY, even_side_ref, odd_side_ref)
    above, below = from_pairs(lists_ref, GX, even_cross_ref, odd_cross_ref)
    table_ref[:bricks] = merged_ref[...]
    table_ref[bricks:] = stack_rows(low[:, :width], high[:, :width], below, above)
    from_next, from_prev = from_pairs(lists_ref, GX, even_grad_ref, odd_grad_ref)
    total = add_rows(ext_ref[...], crosses_of(lists_ref, face), from_next, from_prev)
    part_ref[...] = total[:bricks]
    to_even, to_odd = by_pair(lists_ref, GY, total[bricks + face :], total[bricks : bricks + face])
    to_even_ref[...] = to_even.astype(BF)
    to_odd_ref[...] = to_odd.astype(BF)
    side_parents = stack_lanes(stack_rows(low[:, width:], high[:, width:]), parents_ref.shape[1])
    grads = [stack_parities(total[:bricks].astype(BF)), stack_parities(total[bricks:].astype(BF))]
    up_sum = dot_tn(jnp.concatenate(grads, axis=0), jnp.concatenate([parents_ref[...], side_parents], axis=0))
    coarse = up_sum.shape[1]
    count = sums_ref.shape[0]
    parts = up_sum.shape[0] // count
    for q in range(parts):
        sums_ref[:, q * coarse : (q + 1) * coarse] = up_sum[q * count : (q + 1) * count]
    lower_half = iota((rows, 2 * C), 1) < C
    zero = jnp.zeros((rows, 2 * C), BF)
    for x in range(4):
        for y in range(4):
            places = [(X, Y, dx, dy) for X, dx in options(x) for Y, dy in options(y)]
            at = (x * 4 + y) * RUN
            columns = table_ref[:, at : at + RUN]
            first = jnp.where(lower_half, columns[:, : 2 * C], zero)
            second = jnp.where(lower_half, zero, columns[:, 2 * C :])
            ends = jnp.concatenate([ends_ref[3 * dx + dy + 4] for _, _, dx, dy in places], axis=0)
            halo = dot(ends, jnp.concatenate([first, second], axis=0)).astype(BF)
            for i, (X, Y, _, _) in enumerate(places):
                pad_ref[X, Y, :, RUN:] = halo[i * bricks : (i + 1) * bricks]
            pad_ref[x + 1, y + 1, :, :RUN] = columns[:bricks]
            moved = [p for p in places if p[2:] != (0, 0)]
            if moved:
                main = jnp.concatenate([mains_ref[3 * dx + dy + 4] for _, _, dx, dy in moved], axis=0)
                got = dot(main, columns).astype(BF)
                for i, (X, Y, _, _) in enumerate(moved):
                    pad_ref[X, Y, :, :RUN] = got[i * bricks : (i + 1) * bricks]

    turned = turned_ref[...]
    lanes_low = iota((C, 2 * C), 1) < C
    sums = []
    for e in range(9):
        wide = dot(turned, inputs_at(pad_ref, e))

        def block(z, s):
            return wide[z * C : (z + 1) * C, s * 2 * C : (s + 1) * 2 * C]

        low = jnp.where(lanes_low, block(1, 0) + block(3, 1), block(0, 2) + block(2, 0))
        mid = jnp.where(lanes_low, block(0, 0) + block(2, 1), block(1, 0) + block(3, 1))
        high = jnp.where(lanes_low, block(1, 1) + block(3, 2), block(0, 0) + block(2, 1))
        for value in (low, mid, high):
            sums.append(value + pltpu.roll(value, C, 1))
    sums.append(jnp.zeros((C, 2 * C), F32))
    for pair in range(7):
        both = [jnp.where(lanes_low, sums[14 * h + 2 * pair], sums[14 * h + 2 * pair + 1]) for h in range(2)]
        at = parts * coarse + pair * 2 * C
        sums_ref[:, at : at + 2 * C] = jnp.concatenate(both, axis=0)
    kept, given = by_pair(lists_ref, GX, sums_ref[: count // 2], sums_ref[count // 2 :])
    kept_ref[...] = kept
    given_ref[...] = given.astype(BF)


def pair_sum_body(kept_ref, given_ref, out_ref):
    out_ref[...] = (kept_ref[...] + given_ref[...].astype(F32)).astype(BF)


def inputs_at(pad_ref, e):
    bricks = pad_ref.shape[2]
    ex, ey = (e // 3, e % 3)
    return pad_ref[ex : ex + 4, ey : ey + 4].reshape(16 * bricks, WIDE)


def conv_body(pad_ref, weight_ref, out_ref, band_ref):
    bricks = pad_ref.shape[2]
    build_bands(weight_ref, band_ref)
    total = None
    for e in range(9):
        part = dot(inputs_at(pad_ref, e), band_ref[e])
        total = part if total is None else total + part
    for p in range(16):
        out_ref[:, p * RUN : (p + 1) * RUN] = total[p * bricks : (p + 1) * bricks].astype(BF)


def add_rows(base, lists, first, second):
    count, face = (base.shape[0], lists.shape[1])
    index = jnp.concatenate([lists[0:1], lists[1:2]], axis=1)
    chosen = ones_where(iota((count, 2 * face), 0) == index)
    return base + dot(chosen, stack_rows(first, second))


def merge_body(received_ref, up_ref, fine_ref, lists_ref, merged_ref, parents_ref, a_ref, b_ref):
    bricks, width = fine_ref.shape
    face = a_ref.shape[0]
    parents = merge(received_ref, slots_of(lists_ref, bricks), up_ref, fine_ref, merged_ref, parents_ref)
    lists = sides_of(lists_ref, face)
    lists = by_pair(lists_ref, GY, lists[0:1], lists[1:2])
    for out_ref, rows, owners in zip((a_ref, b_ref), pick_rows(lists, merged_ref[...]), pick_rows(lists, parents)):
        out_ref[:, :width] = rows.astype(BF)
        out_ref[:, width:] = owners.astype(BF)


def fine_grad_body(part_ref, lists_ref, even_ref, odd_ref, up_ref, grad_ref, replies_ref, across):
    bricks = part_ref.shape[0]
    face = even_ref.shape[0]
    from_next, from_prev = from_pairs(lists_ref, GY, even_ref, odd_ref)
    total = add_rows(part_ref[...], sides_of(lists_ref, face), from_next, from_prev)
    grad_ref[...] = total.astype(BF)
    items = dot(stack_parities(grad_ref[...]), up_ref[...]).astype(BF)
    items = jnp.concatenate([items[v * bricks : (v + 1) * bricks] for v in range(8)], axis=1)
    half = items.shape[1] // 2
    count, both_lanes = replies_ref.shape
    pieces = both_lanes // 2 // half
    capacity, group = chip_slots(count, pieces, across)
    slots = slots_of(lists_ref, bricks)
    row = iota((count, bricks), 0)
    for other in range(2):
        owner = device_of(row // group, lists_ref, other, across)
        for j in range(pieces):
            piece = row % group * pieces + j
            named = owner * capacity + piece // 2 == slots
            rows = dot(ones_where(named & (piece % 2 == 0)), items[:, :half])
            rows += dot(ones_where(named & (piece % 2 == 1)), items[:, half:])
            at = (other * pieces + j) * half
            replies_ref[:, at : at + half] = rows.astype(BF)


def chip_slots(count, pieces, across):
    group = count // (across[0] * across[1] // 2)
    return group * pieces // 2, group


def device_of(chip, lists_ref, other, across):
    core = jnp.broadcast_to(lists_ref[5:6, GX : GX + 1], chip.shape)
    core = 1 - core if other else core
    return (chip // across[1] * 2 + core) * across[1] + chip % across[1]


def share_body(sums_ref, replies_ref, out_ref, across):
    count, item_lanes = replies_ref.shape
    share = count // (across[0] * across[1] // 2)
    same = iota((count, count), 0) % share == iota((count, count), 1) % share
    out_ref[:, :item_lanes] = replies_ref[...]
    out_ref[:, item_lanes:] = dot(ones_where(same), sums_ref[...]).astype(BF)


def coarse_grad(arrivals, sends_ref, lists_ref, out_ref, across):
    capacity, devices = sends_ref.shape
    count, item_width = out_ref.shape
    half = item_width // 2
    lanes = arrivals[0].shape[0]
    pieces = arrivals[0].shape[1] // half
    _, group = chip_slots(lanes, pieces, across)
    sends = sends_ref[...].astype(F32).astype(BF)
    lane = iota((1, lanes), 1)
    totals = [None, None]
    for other in range(2):
        source = device_of(lane // group, lists_ref, other, across)
        rows = dot(sends, ones_where(source == iota((devices, lanes), 0)))
        for j in range(pieces):
            piece = lane % group * pieces + j
            picked = jnp.where(piece // 2 == iota((capacity, lanes), 0), rows, 0.0)
            index = jnp.sum(picked, axis=0, keepdims=True).astype(I32)
            named = iota((count, lanes), 0) == index
            for h in range(2):
                part = dot(ones_where(named & (piece % 2 == h)), arrivals[other][:, j * half : (j + 1) * half])
                totals[h] = part if totals[h] is None else totals[h] + part
    for h in range(2):
        out_ref[:, h * half : (h + 1) * half] = totals[h].astype(BF)


def last_body(back_ref, given_ref, sends_ref, lists_ref, conv_ref, up_ref, out_ref, item_lanes, across, scale):
    half_count = back_ref.shape[0]
    items = (back_ref[:, :item_lanes], given_ref[:, item_lanes : 2 * item_lanes])
    coarse_grad(items, sends_ref, lists_ref, out_ref, across)
    coarse = up_ref.shape[1]
    count = 2 * half_count
    parts = up_ref.shape[0] // count
    own = back_ref[:, 2 * item_lanes :].astype(F32) * scale
    others = given_ref[:, 2 * item_lanes :].astype(F32) * scale
    first, second = by_pair(lists_ref, GX, own, others)
    at = 0
    for q in range(parts):
        up_ref[q * count : q * count + half_count] = first[:, at : at + coarse]
        up_ref[q * count + half_count : (q + 1) * count] = second[:, at : at + coarse]
        at += coarse
    for pair in range(7):
        turned = jnp.concatenate([first[:, at : at + 2 * C], second[:, at : at + 2 * C]], axis=0).T
        at += 2 * C
        for h in range(2):
            for s in range(2):
                o = 14 * h + 2 * pair + s
                if o < 27:
                    conv_ref[o] = turned[s * C : (s + 1) * C, h * C : (h + 1) * C]


def swap(value, axis, first):
    count = lax.axis_size(axis)
    lower = range(first, count - 1, 2)
    return lax.ppermute(value, axis, [(i, i + 1) for i in lower] + [(i + 1, i) for i in lower])


def swap_pairs(to_even, to_odd, axis):
    return swap(to_even, axis, 0), swap(to_odd, axis, 1)


def trade_rows(values, axes):
    rows, width = values.shape
    devices = math.prod(lax.axis_size(axis) for axis in axes)
    grid_view = values.reshape(devices, rows // devices, width)
    return lax.all_to_all(grid_view, axes, split_axis=0, concat_axis=0, tiled=True).reshape(rows, width)


def on_device(
    fine_features, coarse_items, conv_weight, up_weight, neighbours,
    side_sends, cross_sends, parent_slots, coarse_sends, cotangent,
):
    fine = fine_features[0, 0]
    items = coarse_items[0, 0]
    cot = cotangent[0, 0]
    bricks, width = fine.shape
    face = side_sends.shape[-1]
    across = (lax.axis_size(GX_AXES), lax.axis_size("gy"))
    devices = across[0] * across[1]
    capacity = coarse_sends.shape[-1]
    item_count, item_width = items.shape
    coarse = up_weight.shape[1]
    start = bricks + 2 * face
    sends = coarse_sends.transpose(0, 1, 3, 2)[0, 0]
    slots = parent_slots[0]
    sides = side_sends[0, 0]
    crosses = cross_sends[0, 0]
    near = neighbours.transpose(0, 3, 1, 2)[0]
    up_turned = up_weight.transpose(0, 2, 1).reshape(8 * C, coarse)
    half = item_width // 2
    count = 2 * C
    item_lanes = capacity * devices // 2 * item_width // (count // 2)
    sums_width = 8 * C * coarse // count + 14 * C
    rows = shape((bricks, width))
    face_rows = shape((face, width))
    faces_and_parents = shape((face, width + item_width))
    lists_shape = shape((8, 128), I32)
    band = pltpu.VMEM((9, WIDE, RUN), BF)
    conv_flops = 2 * 9 * 16 * bricks * WIDE * RUN

    listed = (sends, items, sides, crosses, slots)
    outgoing, lists = call(
        first_body, [shape((2 * capacity * devices, half)), lists_shape], *listed,
        scratch=[pltpu.VMEM(a.shape, a.dtype) for a in listed] + [pltpu.SemaphoreType.DMA((len(listed),))],
        in_hbm=True,
    )
    received = trade_rows(outgoing, ("x", "core", "gy"))
    lane = jnp.arange(128, dtype=I32)[None]
    parity = jnp.where(lane == GX, lax.axis_index("core"), lax.axis_index("gy") % 2).astype(I32)
    table_rows = start + 2 * face
    ext_grad, to_even, to_odd, turned, mains, ends, lists = call(
        table_grad_body,
        [
            shape((start, width), F32), face_rows, face_rows, shape((RUN, 16 * bricks)),
            shape((9, bricks, table_rows)), shape((9, bricks, 2 * table_rows)), lists_shape,
        ],
        cot, conv_weight, near, lists, parity,
        scratch=[band, pltpu.VMEM((6, 6, bricks, WIDE), F32)], flops=2 * conv_flops,
    )
    cross_grads = swap_pairs(to_even, to_odd, GX_AXES)
    merged, parents, to_even, to_odd = call(
        merge_body, [rows, shape((8 * bricks, coarse)), faces_and_parents, faces_and_parents],
        received, up_turned, fine, lists,
    )
    sides = swap_pairs(to_even, to_odd, "gy")
    to_even, to_odd = call(cross_body, [face_rows, face_rows], merged, *sides, lists)
    crosses = swap_pairs(to_even, to_odd, GX_AXES)
    half_sums = (count // 2, sums_width)
    kept, given, pad, fine_part, to_even, to_odd = call(
        weight_grad_body,
        [
            shape(half_sums, F32), shape(half_sums), shape((6, 6, bricks, WIDE)), shape((bricks, width), F32),
            face_rows, face_rows,
        ],
        merged, *sides, *crosses, *cross_grads, turned, mains, ends, lists, ext_grad, parents,
        scratch=[pltpu.VMEM((table_rows, width), BF), pltpu.VMEM((count, sums_width), F32)], flops=conv_flops,
    )
    given = swap(given, "core", 0)
    (sums,) = call(pair_sum_body, [shape(half_sums)], kept, given)
    sums = trade_rows(sums, ("x", "gy"))
    side_grads = swap_pairs(to_even, to_odd, "gy")
    grad_fine, replies = call(
        functools.partial(fine_grad_body, across=across), [rows, shape((count // 2, 2 * item_lanes))],
        fine_part, lists, *side_grads, up_turned,
    )
    (output,) = call(conv_body, [rows], pad, conv_weight, scratch=[band], flops=conv_flops)
    (back,) = call(
        functools.partial(share_body, across=across), [shape((count // 2, 2 * item_lanes + sums_width))], sums, replies
    )
    back = trade_rows(back, ("x", "gy"))
    given = swap(back, "core", 0)
    scale = 1.0 / math.sqrt(64 * bricks * devices)
    grad_conv, grad_up, coarse_grad = call(
        functools.partial(last_body, item_lanes=item_lanes, across=across, scale=scale),
        [shape((27, C, C), F32), shape((8 * C, coarse), F32), shape((item_count, item_width))],
        back, given, sends, lists,
    )
    return (
        output.reshape(1, 1, bricks, width),
        grad_fine.reshape(1, 1, bricks, width),
        coarse_grad.reshape(1, 1, item_count, item_width),
        grad_conv,
        grad_up.reshape(8, C, coarse).transpose(0, 2, 1),
    )


def solution(mesh):
    groups, across_x, across_y = mesh.devices.shape
    split_mesh = Mesh(mesh.devices.reshape(groups, across_x // 2, 2, across_y), ("groups", "x", "core", "gy"))
    rows = ("groups", "x", "core")
    split = P(rows, "gy", None, None)
    placed = (split, split, P(), P(), split, split, split, P(rows, "gy", None), split, split)
    return jax.shard_map(
        on_device,
        mesh=split_mesh,
        in_specs=placed,
        out_specs=(split, split, split, P("groups", None, None), P("groups", None, None)),
        check_vma=False,
    )
```

```python
import functools
import math

import jax
import jax.numpy as jnp
from jax import lax
from jax.experimental import pallas as pl
from jax.experimental.pallas import tpu as pltpu
from jax.sharding import Mesh
from jax.sharding import PartitionSpec as P

BF = jnp.bfloat16
F32 = jnp.float32
I32 = jnp.int32

C = 64
RUN = 4 * C
WIDE = RUN + 2 * C


def iota(shape, axis):
    return lax.broadcasted_iota(I32, shape, axis)


def ones_where(mask):
    return jnp.where(mask, 1.0, 0.0).astype(BF)


def dot(a, b):
    return jnp.dot(a, b, preferred_element_type=F32)


def dot_tn(a, b):
    return lax.dot_general(a, b, (((0,), (0,)), ((), ())), preferred_element_type=F32)


def dot_nt(a, b):
    return lax.dot_general(a, b, (((1,), (1,)), ((), ())), preferred_element_type=F32)


def column_of(row):
    size = row.shape[1]
    diagonal = iota((size, size), 0) == iota((size, size), 1)
    spread = jnp.broadcast_to(row.astype(F32), (size, size))
    return jnp.sum(jnp.where(diagonal, spread, 0.0), axis=1, keepdims=True).astype(I32)


def call(body, outs, *args, scratch=(), flops=0, in_hbm=False):
    moved = sum(a.size * a.dtype.itemsize for a in list(args) + list(outs))
    return pl.pallas_call(
        body,
        out_shape=tuple(outs),
        in_specs=[pl.BlockSpec(memory_space=pltpu.HBM) if in_hbm else pl.BlockSpec() for _ in args],
        scratch_shapes=tuple(scratch),
        cost_estimate=pl.CostEstimate(flops=flops, bytes_accessed=moved, transcendentals=0),
        compiler_params=pltpu.CompilerParams(vmem_limit_bytes=None if in_hbm else 28 * 2**20),
    )(*args)


def shape(dims, dtype=BF):
    return jax.ShapeDtypeStruct(dims, dtype)


def items_out(sends_ref, items_ref, out_ref, across):
    capacity, devices = sends_ref.shape
    count, width = items_ref.shape
    half = width // 2
    group = 2 * capacity
    lanes = out_ref.shape[0]
    chip = iota((lanes, devices), 0) // group
    slot = iota((lanes, capacity), 0) % group // 2
    sends = sends_ref[...].astype(F32).astype(BF)
    items = jnp.concatenate([items_ref[:, :half], items_ref[:, half:]], axis=0)
    for core in range(2):
        device = (chip // across[1] * 2 + core) * across[1] + chip % across[1]
        values = dot_nt(ones_where(device == iota((lanes, devices), 1)), sends)
        item = jnp.sum(jnp.where(slot == iota((lanes, capacity), 1), values, 0.0), axis=1, keepdims=True).astype(I32)
        place = jnp.where(item < count, item + iota((lanes, 1), 0) % 2 * count, -1)
        chosen = ones_where(iota((lanes, 2 * count), 1) == place)
        out_ref[:, core * half : (core + 1) * half] = dot(chosen, items).astype(BF)


def merge(arrived_ref, given_ref, lists_ref, up_ref, fine_ref, merged_ref, parents_ref, across):
    bricks = fine_ref.shape[0]
    lanes = arrived_ref.shape[0]
    half = arrived_ref.shape[1] // 2
    own = [by_pair(lists_ref, GX, r[:, :half].astype(F32), r[:, half:].astype(F32))[0] for r in (arrived_ref, given_ref)]
    received = jnp.concatenate(own, axis=0).astype(BF)
    slot = column_of(slots_of(lists_ref, bricks))
    capacity, group = chip_slots(lanes, 1, across)
    row = iota((bricks, lanes), 1)
    sources = [device_of(row // group, lists_ref, other, across) for other in range(2)]
    named = slot == jnp.concatenate([source * capacity + row % group // 2 for source in sources], axis=1)
    odd = iota((bricks, 2 * lanes), 1) % 2
    parents = jnp.concatenate([dot(ones_where(named & (odd == h)), received) for h in (0, 1)], axis=1).astype(BF)
    coarse = 2 * half // 8
    stacked = jnp.concatenate([parents[:, v * coarse : (v + 1) * coarse] for v in range(8)], axis=0)
    parents_ref[...] = stacked
    lifted = dot_nt(stacked, up_ref[...])
    for v in range(8):
        cx, cy, cz = (v // 4, v // 2 % 2, v % 2)
        for parity in range(4):
            vx, vy = (2 * cx + parity // 2, 2 * cy + parity % 2)
            at = (vx * 4 + vy) * RUN + cz * 2 * C
            add = lifted[v * bricks : (v + 1) * bricks, parity * 2 * C : (parity + 1) * 2 * C]
            merged_ref[:, at : at + 2 * C] = (fine_ref[:, at : at + 2 * C].astype(F32) + add).astype(BF)
    return parents


def pick_rows(lists, rows):
    return [dot_tn(ones_where(iota((rows.shape[0], one.shape[1]), 0) == one), rows) for one in lists]


GX, GY = (0, 1)
GX_AXES = ("x", "core")


def by_pair(lists_ref, axis, of_next, of_prev):
    odd = jnp.broadcast_to(lists_ref[5:6, axis : axis + 1], of_next.shape) == 1
    return jnp.where(odd, of_prev, of_next), jnp.where(odd, of_next, of_prev)


def from_pairs(lists_ref, axis, even_ref, odd_ref):
    return by_pair(lists_ref, axis, even_ref[...].astype(F32), odd_ref[...].astype(F32))


def stack_rows(*parts):
    return jnp.concatenate([p.astype(F32) for p in parts], axis=0).astype(BF)


def sides_of(lists_ref, face):
    return lists_ref[0:2, :face]


def crosses_of(lists_ref, face):
    return lists_ref[2:4, :face]


def slots_of(lists_ref, bricks):
    return lists_ref[4:5, :bricks]


def cross_body(merged_ref, even_ref, odd_ref, lists_ref, a_ref, b_ref):
    face, width = a_ref.shape
    high, low = from_pairs(lists_ref, GY, even_ref, odd_ref)
    rows = jnp.concatenate([merged_ref[...], stack_rows(low[:, :width], high[:, :width])], axis=0)
    lists = crosses_of(lists_ref, face)
    picked = pick_rows(by_pair(lists_ref, GX, lists[0:1], lists[1:2]), rows)
    a_ref[...] = picked[0].astype(BF)
    b_ref[...] = picked[1].astype(BF)


def build_bands(weight_ref, band_ref):
    zero = jnp.zeros((C, C), BF)
    blank = jnp.zeros((C, 2 * C), BF)

    def pair(a, b):
        return jnp.concatenate([a, b], axis=1)

    for e in range(9):
        low, mid, high = (weight_ref[3 * e + z] for z in range(3))
        first, second = (pair(mid, low), pair(high, mid))
        left, right = (pair(low, zero), pair(zero, high))
        rows = (
            (first, blank),
            (second, left),
            (right, first),
            (blank, second),
            (blank, right),
            (left, blank),
        )
        for z, halves in enumerate(rows):
            for s in range(2):
                band_ref[e, z * C : (z + 1) * C, s * 2 * C : (s + 1) * 2 * C] = halves[s]


def options(at):
    return [(at + 1, 0)] + ([(5, 1)] if at == 0 else []) + ([(0, -1)] if at == 3 else [])


def offset_of(dx, dy, dz):
    return (dx + 1) * 9 + (dy + 1) * 3 + dz + 1


def stack_lanes(value, lanes):
    return jnp.concatenate([value[:, p * lanes : (p + 1) * lanes] for p in range(value.shape[1] // lanes)], axis=0)


def stack_parities(value):
    stacked = []
    for v in range(8):
        cx, cy, cz = (v // 4, v // 2 % 2, v % 2)
        lanes = []
        for parity in range(4):
            at = ((2 * cx + parity // 2) * 4 + 2 * cy + parity % 2) * RUN + cz * 2 * C
            lanes.append(value[:, at : at + 2 * C])
        stacked.append(jnp.concatenate(lanes, axis=1))
    return jnp.concatenate(stacked, axis=0)


def stack_runs(ref):
    return jnp.concatenate([ref[:, p * RUN : (p + 1) * RUN] for p in range(16)], axis=0)


def split_two(value):
    head = value.astype(BF)
    return head, (value - head.astype(F32)).astype(BF)


def table_grad_body(
    cot_ref, weight_ref, near_ref, lists_ref, parity_ref,
    ext_ref, even_ref, odd_ref, turned_ref, mains_ref, ends_ref, again_ref, band_ref, pad_ref,
):
    again_ref[...] = lists_ref[...]
    again_ref[5:6] = parity_ref[...]
    bricks = cot_ref.shape[0]
    face = even_ref.shape[0]
    start = ext_ref.shape[0]
    rows = start + 2 * face
    build_bands(weight_ref, band_ref)
    cot = stack_runs(cot_ref)
    turned_ref[...] = cot.T
    pad_ref[...] = jnp.zeros(pad_ref.shape, F32)
    for e in range(9):
        ex, ey = (e // 3, e % 3)
        part = dot_nt(cot, band_ref[e]).reshape(4, 4, bricks, WIDE)
        pad_ref[ex : ex + 4, ey : ey + 4] += part
    near = [near_ref[o] for o in range(27)]

    def chooser(which):
        index = jnp.concatenate([near[o] for o in which], axis=1)
        return ones_where(iota((rows, index.shape[1]), 0) == index)

    lower_half = iota((rows, 2 * C), 1) < C
    cache = {}
    for x in range(4):
        for y in range(4):
            places = [(X, Y, dx, dy) for X, dx in options(x) for Y, dy in options(y)]
            key = tuple((dx, dy) for _, _, dx, dy in places)
            if key not in cache:
                moved = [d for d in key if d != (0, 0)]
                main = chooser([offset_of(*d, 0) for d in moved] * 2) if moved else None
                up = chooser([offset_of(*d, 1) for d in key] * 2)
                down = chooser([offset_of(*d, -1) for d in key] * 2)
                cache[key] = (main, jnp.concatenate([up, down], axis=0))
            main, ends = cache[key]
            own = pad_ref[x + 1, y + 1, :, :RUN]
            own = jnp.concatenate([own, jnp.zeros((rows - bricks, RUN), F32)], axis=0)
            if main is not None:
                parts = [split_two(pad_ref[X, Y, :, :RUN]) for X, Y, dx, dy in places if (dx, dy) != (0, 0)]
                value = jnp.concatenate([p[0] for p in parts] + [p[1] for p in parts], axis=0)
                own += dot(main, value)
            parts = [split_two(pad_ref[X, Y, :, RUN:]) for X, Y, _, _ in places]
            value = jnp.concatenate([p[0] for p in parts] + [p[1] for p in parts], axis=0)
            halo = dot(ends, value)
            first = own[:, : 2 * C] + jnp.where(lower_half, halo[:rows], 0.0)
            second = own[:, 2 * C :] + jnp.where(lower_half, 0.0, halo[rows:])
            total = jnp.concatenate([first, second], axis=1)
            at = (x * 4 + y) * RUN
            ext_ref[:, at : at + RUN] = total[:start]
            even, odd = by_pair(again_ref, GX, total[start + face :], total[start : start + face])
            even_ref[:, at : at + RUN] = even.astype(BF)
            odd_ref[:, at : at + RUN] = odd.astype(BF)
    make_choosers(near_ref, rows, mains_ref, ends_ref)


def make_choosers(near_ref, rows, mains_ref, ends_ref):
    bricks = mains_ref.shape[1]
    near = jnp.concatenate([near_ref[o] for o in range(27)] + [jnp.zeros((5, bricks), I32)], axis=0)
    near = near.astype(F32).T.astype(I32)
    place = iota((bricks, rows), 1)
    pair_place = iota((bricks, 2 * rows), 1)
    for d in range(9):
        down, straight, up = (near[:, 3 * d + z : 3 * d + z + 1] for z in range(3))
        mains_ref[d] = ones_where(place == straight)
        ends_ref[d] = ones_where(pair_place == jnp.where(pair_place < rows, up, down + rows))


def first_body(
    sends_hbm, items_hbm, sides_hbm, crosses_hbm, slots_hbm, out_ref, lists_ref,
    sends_ref, items_ref, sides_ref, crosses_ref, slots_ref, arrived, across,
):
    sources = (sends_hbm, items_hbm, sides_hbm, crosses_hbm, slots_hbm)
    places = (sends_ref, items_ref, sides_ref, crosses_ref, slots_ref)
    copies = [pltpu.make_async_copy(s, p, arrived.at[i]) for i, (s, p) in enumerate(zip(sources, places))]
    for copy in copies:
        copy.start()
    for copy in copies:
        copy.wait()
    face, bricks = (sides_ref.shape[1], slots_ref.shape[1])
    lists_ref[...] = jnp.zeros(lists_ref.shape, I32)
    lists_ref[0:2, :face] = sides_ref[...]
    lists_ref[2:4, :face] = crosses_ref[...]
    lists_ref[4:5, :bricks] = slots_ref[...]
    items_out(sends_ref, items_ref, out_ref, across)


def side_grad_body(
    ext_ref, lists_ref, even_grad_ref, odd_grad_ref, even_side_ref, odd_side_ref, parents_ref,
    part_ref, to_even_ref, to_odd_ref, up_sums_ref,
):
    bricks, width = part_ref.shape
    face = to_even_ref.shape[0]
    from_next, from_prev = from_pairs(lists_ref, GX, even_grad_ref, odd_grad_ref)
    total = add_rows(ext_ref[...], crosses_of(lists_ref, face), from_next, from_prev)
    part_ref[...] = total[:bricks]
    to_even, to_odd = by_pair(lists_ref, GY, total[bricks + face :], total[bricks : bricks + face])
    to_even_ref[...] = to_even.astype(BF)
    to_odd_ref[...] = to_odd.astype(BF)
    high, low = by_pair(
        lists_ref, GY, even_side_ref[:, width:].astype(F32), odd_side_ref[:, width:].astype(F32)
    )
    side_parents = stack_lanes(stack_rows(low, high), parents_ref.shape[1])
    grads = [stack_parities(total[:bricks].astype(BF)), stack_parities(total[bricks:].astype(BF))]
    up_sum = dot_tn(jnp.concatenate(grads, axis=0), jnp.concatenate([parents_ref[...], side_parents], axis=0))
    coarse = up_sum.shape[1]
    count = up_sums_ref.shape[0]
    for q in range(up_sum.shape[0] // count):
        up_sums_ref[:, q * coarse : (q + 1) * coarse] = up_sum[q * count : (q + 1) * count]


def weight_grad_body(
    merged_ref, even_side_ref, odd_side_ref, even_cross_ref, odd_cross_ref, turned_ref, mains_ref, ends_ref, lists_ref,
    up_sums_ref, kept_ref, given_ref, pad_ref, table_ref, sums_ref,
):
    bricks, width = merged_ref.shape
    face = even_side_ref.shape[0]
    rows = bricks + 4 * face
    high, low = by_pair(lists_ref, GY, even_side_ref[:, :width].astype(F32), odd_side_ref[:, :width].astype(F32))
    above, below = from_pairs(lists_ref, GX, even_cross_ref, odd_cross_ref)
    table_ref[:bricks] = merged_ref[...]
    table_ref[bricks:] = stack_rows(low, high, below, above)
    count = sums_ref.shape[0]
    up_lanes = up_sums_ref.shape[1]
    sums_ref[:, :up_lanes] = up_sums_ref[...]
    lower_half = iota((rows, 2 * C), 1) < C
    zero = jnp.zeros((rows, 2 * C), BF)
    for x in range(4):
        for y in range(4):
            places = [(X, Y, dx, dy) for X, dx in options(x) for Y, dy in options(y)]
            at = (x * 4 + y) * RUN
            columns = table_ref[:, at : at + RUN]
            first = jnp.where(lower_half, columns[:, : 2 * C], zero)
            second = jnp.where(lower_half, zero, columns[:, 2 * C :])
            ends = jnp.concatenate([ends_ref[3 * dx + dy + 4] for _, _, dx, dy in places], axis=0)
            halo = dot(ends, jnp.concatenate([first, second], axis=0)).astype(BF)
            for i, (X, Y, _, _) in enumerate(places):
                pad_ref[X, Y, :, RUN:] = halo[i * bricks : (i + 1) * bricks]
            pad_ref[x + 1, y + 1, :, :RUN] = columns[:bricks]
            moved = [p for p in places if p[2:] != (0, 0)]
            if moved:
                main = jnp.concatenate([mains_ref[3 * dx + dy + 4] for _, _, dx, dy in moved], axis=0)
                got = dot(main, columns).astype(BF)
                for i, (X, Y, _, _) in enumerate(moved):
                    pad_ref[X, Y, :, :RUN] = got[i * bricks : (i + 1) * bricks]

    turned = turned_ref[...]
    lanes_low = iota((C, 2 * C), 1) < C
    sums = []
    for e in range(9):
        wide = dot(turned, inputs_at(pad_ref, e))

        def block(z, s):
            return wide[z * C : (z + 1) * C, s * 2 * C : (s + 1) * 2 * C]

        low = jnp.where(lanes_low, block(1, 0) + block(3, 1), block(0, 2) + block(2, 0))
        mid = jnp.where(lanes_low, block(0, 0) + block(2, 1), block(1, 0) + block(3, 1))
        high = jnp.where(lanes_low, block(1, 1) + block(3, 2), block(0, 0) + block(2, 1))
        for value in (low, mid, high):
            sums.append(value + pltpu.roll(value, C, 1))
    sums.append(jnp.zeros((C, 2 * C), F32))
    for pair in range(7):
        both = [jnp.where(lanes_low, sums[14 * h + 2 * pair], sums[14 * h + 2 * pair + 1]) for h in range(2)]
        at = up_lanes + pair * 2 * C
        sums_ref[:, at : at + 2 * C] = jnp.concatenate(both, axis=0)
    kept, given = by_pair(lists_ref, GX, sums_ref[: count // 2], sums_ref[count // 2 :])
    kept_ref[...] = kept
    given_ref[...] = given.astype(BF)


def pair_sum_body(kept_ref, given_ref, out_ref):
    out_ref[...] = (kept_ref[...] + given_ref[...].astype(F32)).astype(BF)


def inputs_at(pad_ref, e):
    bricks = pad_ref.shape[2]
    ex, ey = (e // 3, e % 3)
    return pad_ref[ex : ex + 4, ey : ey + 4].reshape(16 * bricks, WIDE)


def conv_body(pad_ref, weight_ref, lists_ref, out_ref, again_ref, band_ref):
    again_ref[...] = lists_ref[...]
    bricks = pad_ref.shape[2]
    build_bands(weight_ref, band_ref)
    total = None
    for e in range(9):
        part = dot(inputs_at(pad_ref, e), band_ref[e])
        total = part if total is None else total + part
    for p in range(16):
        out_ref[:, p * RUN : (p + 1) * RUN] = total[p * bricks : (p + 1) * bricks].astype(BF)


def add_rows(base, lists, first, second):
    count, face = (base.shape[0], lists.shape[1])
    index = jnp.concatenate([lists[0:1], lists[1:2]], axis=1)
    chosen = ones_where(iota((count, 2 * face), 0) == index)
    return base + dot(chosen, stack_rows(first, second))


def merge_body(
    arrived_ref, given_ref, up_ref, fine_ref, lists_ref, merged_ref, parents_ref, a_ref, b_ref, across
):
    bricks, width = fine_ref.shape
    face = a_ref.shape[0]
    parents = merge(arrived_ref, given_ref, lists_ref, up_ref, fine_ref, merged_ref, parents_ref, across)
    lists = sides_of(lists_ref, face)
    lists = by_pair(lists_ref, GY, lists[0:1], lists[1:2])
    for out_ref, rows, owners in zip((a_ref, b_ref), pick_rows(lists, merged_ref[...]), pick_rows(lists, parents)):
        out_ref[:, :width] = rows.astype(BF)
        out_ref[:, width:] = owners.astype(BF)


def fine_grad_body(part_ref, lists_ref, even_ref, odd_ref, up_ref, grad_ref, replies_ref, across):
    bricks = part_ref.shape[0]
    face = even_ref.shape[0]
    from_next, from_prev = from_pairs(lists_ref, GY, even_ref, odd_ref)
    total = add_rows(part_ref[...], sides_of(lists_ref, face), from_next, from_prev)
    grad_ref[...] = total.astype(BF)
    items = dot(stack_parities(grad_ref[...]), up_ref[...]).astype(BF)
    items = jnp.concatenate([items[v * bricks : (v + 1) * bricks] for v in range(8)], axis=1)
    half = items.shape[1] // 2
    count, both_lanes = replies_ref.shape
    pieces = both_lanes // 2 // half
    capacity, group = chip_slots(count, pieces, across)
    slots = slots_of(lists_ref, bricks)
    row = iota((count, bricks), 0)
    for other in range(2):
        owner = device_of(row // group, lists_ref, other, across)
        for j in range(pieces):
            piece = row % group * pieces + j
            named = owner * capacity + piece // 2 == slots
            rows = dot(ones_where(named & (piece % 2 == 0)), items[:, :half])
            rows += dot(ones_where(named & (piece % 2 == 1)), items[:, half:])
            at = (other * pieces + j) * half
            replies_ref[:, at : at + half] = rows.astype(BF)


def chip_slots(count, pieces, across):
    group = count // (across[0] * across[1] // 2)
    return group * pieces // 2, group


def device_of(chip, lists_ref, other, across):
    core = jnp.broadcast_to(lists_ref[5:6, GX : GX + 1], chip.shape)
    core = 1 - core if other else core
    return (chip // across[1] * 2 + core) * across[1] + chip % across[1]


def share_body(sums_ref, replies_ref, lists_ref, out_ref, again_ref, across):
    again_ref[...] = lists_ref[...]
    count, item_lanes = replies_ref.shape
    share = count // (across[0] * across[1] // 2)
    same = iota((count, count), 0) % share == iota((count, count), 1) % share
    out_ref[:, :item_lanes] = replies_ref[...]
    out_ref[:, item_lanes:] = dot(ones_where(same), sums_ref[...]).astype(BF)


def coarse_grad(arrivals, sends_ref, lists_ref, out_ref, across):
    capacity, devices = sends_ref.shape
    count, item_width = out_ref.shape
    half = item_width // 2
    lanes = arrivals[0].shape[0]
    pieces = arrivals[0].shape[1] // half
    _, group = chip_slots(lanes, pieces, across)
    sends = sends_ref[...].astype(F32).astype(BF)
    lane = iota((1, lanes), 1)
    totals = [None, None]
    for other in range(2):
        source = device_of(lane // group, lists_ref, other, across)
        rows = dot(sends, ones_where(source == iota((devices, lanes), 0)))
        for j in range(pieces):
            piece = lane % group * pieces + j
            picked = jnp.where(piece // 2 == iota((capacity, lanes), 0), rows, 0.0)
            index = jnp.sum(picked, axis=0, keepdims=True).astype(I32)
            named = iota((count, lanes), 0) == index
            for h in range(2):
                part = dot(ones_where(named & (piece % 2 == h)), arrivals[other][:, j * half : (j + 1) * half])
                totals[h] = part if totals[h] is None else totals[h] + part
    for h in range(2):
        out_ref[:, h * half : (h + 1) * half] = totals[h].astype(BF)


def last_body(back_ref, given_ref, sends_ref, lists_ref, conv_ref, up_ref, out_ref, item_lanes, across, scale):
    half_count = back_ref.shape[0]
    items = (back_ref[:, :item_lanes], given_ref[:, item_lanes : 2 * item_lanes])
    coarse_grad(items, sends_ref, lists_ref, out_ref, across)
    coarse = up_ref.shape[1]
    count = 2 * half_count
    parts = up_ref.shape[0] // count
    own = back_ref[:, 2 * item_lanes :].astype(F32) * scale
    others = given_ref[:, 2 * item_lanes :].astype(F32) * scale
    first, second = by_pair(lists_ref, GX, own, others)
    at = 0
    for q in range(parts):
        up_ref[q * count : q * count + half_count] = first[:, at : at + coarse]
        up_ref[q * count + half_count : (q + 1) * count] = second[:, at : at + coarse]
        at += coarse
    for pair in range(7):
        turned = jnp.concatenate([first[:, at : at + 2 * C], second[:, at : at + 2 * C]], axis=0).T
        at += 2 * C
        for h in range(2):
            for s in range(2):
                o = 14 * h + 2 * pair + s
                if o < 27:
                    conv_ref[o] = turned[s * C : (s + 1) * C, h * C : (h + 1) * C]


def swap(value, axis, first):
    count = lax.axis_size(axis)
    lower = range(first, count - 1, 2)
    return lax.ppermute(value, axis, [(i, i + 1) for i in lower] + [(i + 1, i) for i in lower])


def swap_pairs(to_even, to_odd, axis):
    return swap(to_even, axis, 0), swap(to_odd, axis, 1)


def trade_rows(values, axes):
    rows, width = values.shape
    devices = math.prod(lax.axis_size(axis) for axis in axes)
    grid_view = values.reshape(devices, rows // devices, width)
    return lax.all_to_all(grid_view, axes, split_axis=0, concat_axis=0, tiled=True).reshape(rows, width)


def on_device(
    fine_features, coarse_items, conv_weight, up_weight, neighbours,
    side_sends, cross_sends, parent_slots, coarse_sends, cotangent,
):
    fine = fine_features[0, 0]
    items = coarse_items[0, 0]
    cot = cotangent[0, 0]
    bricks, width = fine.shape
    face = side_sends.shape[-1]
    across = (lax.axis_size(GX_AXES), lax.axis_size("gy"))
    devices = across[0] * across[1]
    capacity = coarse_sends.shape[-1]
    item_count, item_width = items.shape
    coarse = up_weight.shape[1]
    start = bricks + 2 * face
    sends = coarse_sends.transpose(0, 1, 3, 2)[0, 0]
    slots = parent_slots[0]
    sides = side_sends[0, 0]
    crosses = cross_sends[0, 0]
    near = neighbours.transpose(0, 3, 1, 2)[0]
    up_turned = up_weight.transpose(0, 2, 1).reshape(8 * C, coarse)
    half = item_width // 2
    count = 2 * C
    item_lanes = capacity * devices // 2 * item_width // (count // 2)
    sums_width = 8 * C * coarse // count + 14 * C
    rows = shape((bricks, width))
    face_rows = shape((face, width))
    faces_and_parents = shape((face, width + item_width))
    lists_shape = shape((8, 128), I32)
    band = pltpu.VMEM((9, WIDE, RUN), BF)
    conv_flops = 2 * 9 * 16 * bricks * WIDE * RUN

    listed = (sends, items, sides, crosses, slots)
    outgoing, lists = call(
        functools.partial(first_body, across=across), [shape((capacity * devices, item_width)), lists_shape], *listed,
        scratch=[pltpu.VMEM(a.shape, a.dtype) for a in listed] + [pltpu.SemaphoreType.DMA((len(listed),))],
        in_hbm=True,
    )
    arrived = trade_rows(outgoing, ("x", "gy"))
    arrived = (arrived, swap(arrived, "core", 0))
    lane = jnp.arange(128, dtype=I32)[None]
    parity = jnp.where(lane == GX, lax.axis_index("core"), lax.axis_index("gy") % 2).astype(I32)
    table_rows = start + 2 * face
    ext_grad, to_even, to_odd, turned, mains, ends, lists = call(
        table_grad_body,
        [
            shape((start, width), F32), face_rows, face_rows, shape((RUN, 16 * bricks)),
            shape((9, bricks, table_rows)), shape((9, bricks, 2 * table_rows)), lists_shape,
        ],
        cot, conv_weight, near, lists, parity,
        scratch=[band, pltpu.VMEM((6, 6, bricks, WIDE), F32)], flops=2 * conv_flops,
    )
    cross_grads = swap_pairs(to_even, to_odd, GX_AXES)
    merged, parents, to_even, to_odd = call(
        functools.partial(merge_body, across=across), [rows, shape((8 * bricks, coarse)), faces_and_parents, faces_and_parents],
        *arrived, up_turned, fine, lists,
    )
    sides = swap_pairs(to_even, to_odd, "gy")
    to_even, to_odd = call(cross_body, [face_rows, face_rows], merged, *sides, lists)
    crosses = swap_pairs(to_even, to_odd, GX_AXES)
    half_sums = (count // 2, sums_width)
    fine_part, to_even, to_odd, up_sums = call(
        side_grad_body,
        [shape((bricks, width), F32), face_rows, face_rows, shape((count, sums_width - 14 * C), F32)],
        ext_grad, lists, *cross_grads, *sides, parents,
    )
    side_grads = swap_pairs(to_even, to_odd, "gy")
    kept, given, pad = call(
        weight_grad_body, [shape(half_sums, F32), shape(half_sums), shape((6, 6, bricks, WIDE))],
        merged, *sides, *crosses, turned, mains, ends, lists, up_sums,
        scratch=[pltpu.VMEM((table_rows, width), BF), pltpu.VMEM((count, sums_width), F32)], flops=conv_flops,
    )
    given = swap(given, "core", 0)
    (sums,) = call(pair_sum_body, [shape(half_sums)], kept, given)
    sums = trade_rows(sums, ("x", "gy"))
    grad_fine, replies = call(
        functools.partial(fine_grad_body, across=across), [rows, shape((count // 2, 2 * item_lanes))],
        fine_part, lists, *side_grads, up_turned,
    )
    output, lists = call(
        conv_body, [rows, lists_shape], pad, conv_weight, lists, scratch=[band], flops=conv_flops
    )
    back, lists = call(
        functools.partial(share_body, across=across),
        [shape((count // 2, 2 * item_lanes + sums_width)), lists_shape], sums, replies, lists,
    )
    back = trade_rows(back, ("x", "gy"))
    given = swap(back, "core", 0)
    scale = 1.0 / math.sqrt(64 * bricks * devices)
    grad_conv, grad_up, coarse_grad = call(
        functools.partial(last_body, item_lanes=item_lanes, across=across, scale=scale),
        [shape((27, C, C), F32), shape((8 * C, coarse), F32), shape((item_count, item_width))],
        back, given, sends, lists,
    )
    return (
        output.reshape(1, 1, bricks, width),
        grad_fine.reshape(1, 1, bricks, width),
        coarse_grad.reshape(1, 1, item_count, item_width),
        grad_conv,
        grad_up.reshape(8, C, coarse).transpose(0, 2, 1),
    )


def solution(mesh):
    groups, across_x, across_y = mesh.devices.shape
    split_mesh = Mesh(mesh.devices.reshape(groups, across_x // 2, 2, across_y), ("groups", "x", "core", "gy"))
    rows = ("groups", "x", "core")
    split = P(rows, "gy", None, None)
    placed = (split, split, P(), P(), split, split, split, P(rows, "gy", None), split, split)
    return jax.shard_map(
        on_device,
        mesh=split_mesh,
        in_specs=placed,
        out_specs=(split, split, split, P("groups", None, None), P("groups", None, None)),
        check_vma=False,
    )
```

```python
import functools
import math

import jax
import jax.numpy as jnp
from jax import lax
from jax.experimental import pallas as pl
from jax.experimental.pallas import tpu as pltpu
from jax.sharding import Mesh
from jax.sharding import PartitionSpec as P

BF = jnp.bfloat16
F32 = jnp.float32
I32 = jnp.int32

C = 64
RUN = 4 * C
WIDE = RUN + 2 * C


def iota(shape, axis):
    return lax.broadcasted_iota(I32, shape, axis)


def ones_where(mask):
    return jnp.where(mask, 1.0, 0.0).astype(BF)


def dot(a, b):
    return jnp.dot(a, b, preferred_element_type=F32)


def dot_tn(a, b):
    return lax.dot_general(a, b, (((0,), (0,)), ((), ())), preferred_element_type=F32)


def dot_nt(a, b):
    return lax.dot_general(a, b, (((1,), (1,)), ((), ())), preferred_element_type=F32)


def column_of(row):
    size = row.shape[1]
    diagonal = iota((size, size), 0) == iota((size, size), 1)
    spread = jnp.broadcast_to(row.astype(F32), (size, size))
    return jnp.sum(jnp.where(diagonal, spread, 0.0), axis=1, keepdims=True).astype(I32)


def call(body, outs, *args, scratch=(), flops=0, in_hbm=False):
    moved = sum(a.size * a.dtype.itemsize for a in list(args) + list(outs))
    return pl.pallas_call(
        body,
        out_shape=tuple(outs),
        in_specs=[pl.BlockSpec(memory_space=pltpu.HBM) if in_hbm else pl.BlockSpec() for _ in args],
        scratch_shapes=tuple(scratch),
        cost_estimate=pl.CostEstimate(flops=flops, bytes_accessed=moved, transcendentals=0),
        compiler_params=pltpu.CompilerParams(vmem_limit_bytes=None if in_hbm else 28 * 2**20),
    )(*args)


def shape(dims, dtype=BF):
    return jax.ShapeDtypeStruct(dims, dtype)


def items_out(sends_ref, items_ref, out_ref):
    capacity, devices = sends_ref.shape
    count, width = items_ref.shape
    half = width // 2
    group = 2 * capacity
    lanes = devices * group
    spread = ones_where(iota((lanes, devices), 0) // group == iota((lanes, devices), 1))
    slot = iota((lanes, capacity), 0) % group // 2
    values = dot_nt(spread, sends_ref[...].astype(F32).astype(BF))
    item = jnp.sum(jnp.where(slot == iota((lanes, capacity), 1), values, 0.0), axis=1, keepdims=True).astype(I32)
    place = jnp.where(item < count, item + iota((lanes, 1), 0) % 2 * count, -1)
    chosen = ones_where(iota((lanes, 2 * count), 1) == place)
    out_ref[...] = dot(chosen, jnp.concatenate([items_ref[:, :half], items_ref[:, half:]], axis=0)).astype(BF)


def merge(received_ref, slots, up_ref, fine_ref, merged_ref, parents_ref):
    bricks = fine_ref.shape[0]
    lanes, half = received_ref.shape
    slot = column_of(slots)
    place = iota((bricks, lanes), 1)
    named = place // 2 == slot
    received = received_ref[...]
    parents = jnp.concatenate(
        [dot(ones_where(named & (place % 2 == h)), received) for h in (0, 1)], axis=1
    ).astype(BF)
    coarse = 2 * half // 8
    stacked = jnp.concatenate([parents[:, v * coarse : (v + 1) * coarse] for v in range(8)], axis=0)
    parents_ref[...] = stacked
    lifted = dot_nt(stacked, up_ref[...])
    for v in range(8):
        cx, cy, cz = (v // 4, v // 2 % 2, v % 2)
        for parity in range(4):
            vx, vy = (2 * cx + parity // 2, 2 * cy + parity % 2)
            at = (vx * 4 + vy) * RUN + cz * 2 * C
            add = lifted[v * bricks : (v + 1) * bricks, parity * 2 * C : (parity + 1) * 2 * C]
            merged_ref[:, at : at + 2 * C] = (fine_ref[:, at : at + 2 * C].astype(F32) + add).astype(BF)
    return parents


def pick_rows(lists, rows):
    return [dot_tn(ones_where(iota((rows.shape[0], one.shape[1]), 0) == one), rows) for one in lists]


GX, GY = (0, 1)
GX_AXES = ("x", "core")


def by_pair(lists_ref, axis, of_next, of_prev):
    odd = jnp.broadcast_to(lists_ref[5:6, axis : axis + 1], of_next.shape) == 1
    return jnp.where(odd, of_prev, of_next), jnp.where(odd, of_next, of_prev)


def from_pairs(lists_ref, axis, even_ref, odd_ref):
    return by_pair(lists_ref, axis, even_ref[...].astype(F32), odd_ref[...].astype(F32))


def stack_rows(*parts):
    return jnp.concatenate([p.astype(F32) for p in parts], axis=0).astype(BF)


def sides_of(lists_ref, face):
    return lists_ref[0:2, :face]


def crosses_of(lists_ref, face):
    return lists_ref[2:4, :face]


def slots_of(lists_ref, bricks):
    return lists_ref[4:5, :bricks]


def cross_body(merged_ref, even_ref, odd_ref, lists_ref, a_ref, b_ref):
    face, width = a_ref.shape
    high, low = from_pairs(lists_ref, GY, even_ref, odd_ref)
    rows = jnp.concatenate([merged_ref[...], stack_rows(low[:, :width], high[:, :width])], axis=0)
    lists = crosses_of(lists_ref, face)
    picked = pick_rows(by_pair(lists_ref, GX, lists[0:1], lists[1:2]), rows)
    a_ref[...] = picked[0].astype(BF)
    b_ref[...] = picked[1].astype(BF)


def build_bands(weight_ref, band_ref):
    zero = jnp.zeros((C, C), BF)
    blank = jnp.zeros((C, 2 * C), BF)

    def pair(a, b):
        return jnp.concatenate([a, b], axis=1)

    for e in range(9):
        low, mid, high = (weight_ref[3 * e + z] for z in range(3))
        first, second = (pair(mid, low), pair(high, mid))
        left, right = (pair(low, zero), pair(zero, high))
        rows = (
            (first, blank),
            (second, left),
            (right, first),
            (blank, second),
            (blank, right),
            (left, blank),
        )
        for z, halves in enumerate(rows):
            for s in range(2):
                band_ref[e, z * C : (z + 1) * C, s * 2 * C : (s + 1) * 2 * C] = halves[s]


def options(at):
    return [(at + 1, 0)] + ([(5, 1)] if at == 0 else []) + ([(0, -1)] if at == 3 else [])


def offset_of(dx, dy, dz):
    return (dx + 1) * 9 + (dy + 1) * 3 + dz + 1


def stack_lanes(value, lanes):
    return jnp.concatenate([value[:, p * lanes : (p + 1) * lanes] for p in range(value.shape[1] // lanes)], axis=0)


def stack_parities(value):
    stacked = []
    for v in range(8):
        cx, cy, cz = (v // 4, v // 2 % 2, v % 2)
        lanes = []
        for parity in range(4):
            at = ((2 * cx + parity // 2) * 4 + 2 * cy + parity % 2) * RUN + cz * 2 * C
            lanes.append(value[:, at : at + 2 * C])
        stacked.append(jnp.concatenate(lanes, axis=1))
    return jnp.concatenate(stacked, axis=0)


def stack_runs(ref):
    return jnp.concatenate([ref[:, p * RUN : (p + 1) * RUN] for p in range(16)], axis=0)


def split_two(value):
    head = value.astype(BF)
    return head, (value - head.astype(F32)).astype(BF)


def table_grad_body(
    cot_ref, weight_ref, near_ref, lists_ref, parity_ref,
    ext_ref, even_ref, odd_ref, turned_ref, mains_ref, ends_ref, again_ref, band_ref, pad_ref,
):
    again_ref[...] = lists_ref[...]
    again_ref[5:6] = parity_ref[...]
    bricks = cot_ref.shape[0]
    face = even_ref.shape[0]
    start = ext_ref.shape[0]
    rows = start + 2 * face
    build_bands(weight_ref, band_ref)
    cot = stack_runs(cot_ref)
    turned_ref[...] = cot.T
    pad_ref[...] = jnp.zeros(pad_ref.shape, F32)
    for e in range(9):
        ex, ey = (e // 3, e % 3)
        part = dot_nt(cot, band_ref[e]).reshape(4, 4, bricks, WIDE)
        pad_ref[ex : ex + 4, ey : ey + 4] += part
    near = [near_ref[o] for o in range(27)]

    def chooser(which):
        index = jnp.concatenate([near[o] for o in which], axis=1)
        return ones_where(iota((rows, index.shape[1]), 0) == index)

    lower_half = iota((rows, 2 * C), 1) < C
    cache = {}
    for x in range(4):
        for y in range(4):
            places = [(X, Y, dx, dy) for X, dx in options(x) for Y, dy in options(y)]
            key = tuple((dx, dy) for _, _, dx, dy in places)
            if key not in cache:
                moved = [d for d in key if d != (0, 0)]
                main = chooser([offset_of(*d, 0) for d in moved] * 2) if moved else None
                up = chooser([offset_of(*d, 1) for d in key] * 2)
                down = chooser([offset_of(*d, -1) for d in key] * 2)
                cache[key] = (main, jnp.concatenate([up, down], axis=0))
            main, ends = cache[key]
            own = pad_ref[x + 1, y + 1, :, :RUN]
            own = jnp.concatenate([own, jnp.zeros((rows - bricks, RUN), F32)], axis=0)
            if main is not None:
                parts = [split_two(pad_ref[X, Y, :, :RUN]) for X, Y, dx, dy in places if (dx, dy) != (0, 0)]
                value = jnp.concatenate([p[0] for p in parts] + [p[1] for p in parts], axis=0)
                own += dot(main, value)
            parts = [split_two(pad_ref[X, Y, :, RUN:]) for X, Y, _, _ in places]
            value = jnp.concatenate([p[0] for p in parts] + [p[1] for p in parts], axis=0)
            halo = dot(ends, value)
            first = own[:, : 2 * C] + jnp.where(lower_half, halo[:rows], 0.0)
            second = own[:, 2 * C :] + jnp.where(lower_half, 0.0, halo[rows:])
            total = jnp.concatenate([first, second], axis=1)
            at = (x * 4 + y) * RUN
            ext_ref[:, at : at + RUN] = total[:start]
            even, odd = by_pair(again_ref, GX, total[start + face :], total[start : start + face])
            even_ref[:, at : at + RUN] = even.astype(BF)
            odd_ref[:, at : at + RUN] = odd.astype(BF)
    make_choosers(near_ref, rows, mains_ref, ends_ref)


def make_choosers(near_ref, rows, mains_ref, ends_ref):
    bricks = mains_ref.shape[1]
    near = jnp.concatenate([near_ref[o] for o in range(27)] + [jnp.zeros((5, bricks), I32)], axis=0)
    near = near.astype(F32).T.astype(I32)
    place = iota((bricks, rows), 1)
    pair_place = iota((bricks, 2 * rows), 1)
    for d in range(9):
        down, straight, up = (near[:, 3 * d + z : 3 * d + z + 1] for z in range(3))
        mains_ref[d] = ones_where(place == straight)
        ends_ref[d] = ones_where(pair_place == jnp.where(pair_place < rows, up, down + rows))


def first_body(
    sends_hbm, items_hbm, sides_hbm, crosses_hbm, slots_hbm, out_ref, lists_ref,
    sends_ref, items_ref, sides_ref, crosses_ref, slots_ref, arrived,
):
    sources = (sends_hbm, items_hbm, sides_hbm, crosses_hbm, slots_hbm)
    places = (sends_ref, items_ref, sides_ref, crosses_ref, slots_ref)
    copies = [pltpu.make_async_copy(s, p, arrived.at[i]) for i, (s, p) in enumerate(zip(sources, places))]
    for copy in copies:
        copy.start()
    for copy in copies:
        copy.wait()
    face, bricks = (sides_ref.shape[1], slots_ref.shape[1])
    lists_ref[...] = jnp.zeros(lists_ref.shape, I32)
    lists_ref[0:2, :face] = sides_ref[...]
    lists_ref[2:4, :face] = crosses_ref[...]
    lists_ref[4:5, :bricks] = slots_ref[...]
    items_out(sends_ref, items_ref, out_ref)


def side_grad_body(
    ext_ref, lists_ref, even_grad_ref, odd_grad_ref, even_side_ref, odd_side_ref, parents_ref,
    part_ref, to_even_ref, to_odd_ref, up_sums_ref,
):
    bricks, width = part_ref.shape
    face = to_even_ref.shape[0]
    from_next, from_prev = from_pairs(lists_ref, GX, even_grad_ref, odd_grad_ref)
    total = add_rows(ext_ref[...], crosses_of(lists_ref, face), from_next, from_prev)
    part_ref[...] = total[:bricks]
    to_even, to_odd = by_pair(lists_ref, GY, total[bricks + face :], total[bricks : bricks + face])
    to_even_ref[...] = to_even.astype(BF)
    to_odd_ref[...] = to_odd.astype(BF)
    high, low = by_pair(
        lists_ref, GY, even_side_ref[:, width:].astype(F32), odd_side_ref[:, width:].astype(F32)
    )
    side_parents = stack_lanes(stack_rows(low, high), parents_ref.shape[1])
    grads = [stack_parities(total[:bricks].astype(BF)), stack_parities(total[bricks:].astype(BF))]
    up_sum = dot_tn(jnp.concatenate(grads, axis=0), jnp.concatenate([parents_ref[...], side_parents], axis=0))
    coarse = up_sum.shape[1]
    count = up_sums_ref.shape[0]
    for q in range(up_sum.shape[0] // count):
        up_sums_ref[:, q * coarse : (q + 1) * coarse] = up_sum[q * count : (q + 1) * count]


def weight_grad_body(
    merged_ref, even_side_ref, odd_side_ref, even_cross_ref, odd_cross_ref, turned_ref, mains_ref, ends_ref, lists_ref,
    up_sums_ref, kept_ref, given_ref, pad_ref, table_ref, sums_ref,
):
    bricks, width = merged_ref.shape
    face = even_side_ref.shape[0]
    rows = bricks + 4 * face
    high, low = by_pair(lists_ref, GY, even_side_ref[:, :width].astype(F32), odd_side_ref[:, :width].astype(F32))
    above, below = from_pairs(lists_ref, GX, even_cross_ref, odd_cross_ref)
    table_ref[:bricks] = merged_ref[...]
    table_ref[bricks:] = stack_rows(low, high, below, above)
    count = sums_ref.shape[0]
    up_lanes = up_sums_ref.shape[1]
    sums_ref[:, :up_lanes] = up_sums_ref[...]
    lower_half = iota((rows, 2 * C), 1) < C
    zero = jnp.zeros((rows, 2 * C), BF)
    for x in range(4):
        for y in range(4):
            places = [(X, Y, dx, dy) for X, dx in options(x) for Y, dy in options(y)]
            at = (x * 4 + y) * RUN
            columns = table_ref[:, at : at + RUN]
            first = jnp.where(lower_half, columns[:, : 2 * C], zero)
            second = jnp.where(lower_half, zero, columns[:, 2 * C :])
            ends = jnp.concatenate([ends_ref[3 * dx + dy + 4] for _, _, dx, dy in places], axis=0)
            halo = dot(ends, jnp.concatenate([first, second], axis=0)).astype(BF)
            for i, (X, Y, _, _) in enumerate(places):
                pad_ref[X, Y, :, RUN:] = halo[i * bricks : (i + 1) * bricks]
            pad_ref[x + 1, y + 1, :, :RUN] = columns[:bricks]
            moved = [p for p in places if p[2:] != (0, 0)]
            if moved:
                main = jnp.concatenate([mains_ref[3 * dx + dy + 4] for _, _, dx, dy in moved], axis=0)
                got = dot(main, columns).astype(BF)
                for i, (X, Y, _, _) in enumerate(moved):
                    pad_ref[X, Y, :, :RUN] = got[i * bricks : (i + 1) * bricks]

    turned = turned_ref[...]
    lanes_low = iota((C, 2 * C), 1) < C
    sums = []
    for e in range(9):
        wide = dot(turned, inputs_at(pad_ref, e))

        def block(z, s):
            return wide[z * C : (z + 1) * C, s * 2 * C : (s + 1) * 2 * C]

        low = jnp.where(lanes_low, block(1, 0) + block(3, 1), block(0, 2) + block(2, 0))
        mid = jnp.where(lanes_low, block(0, 0) + block(2, 1), block(1, 0) + block(3, 1))
        high = jnp.where(lanes_low, block(1, 1) + block(3, 2), block(0, 0) + block(2, 1))
        for value in (low, mid, high):
            sums.append(value + pltpu.roll(value, C, 1))
    sums.append(jnp.zeros((C, 2 * C), F32))
    for pair in range(7):
        both = [jnp.where(lanes_low, sums[14 * h + 2 * pair], sums[14 * h + 2 * pair + 1]) for h in range(2)]
        at = up_lanes + pair * 2 * C
        sums_ref[:, at : at + 2 * C] = jnp.concatenate(both, axis=0)
    kept, given = by_pair(lists_ref, GX, sums_ref[: count // 2], sums_ref[count // 2 :])
    kept_ref[...] = kept
    given_ref[...] = given.astype(BF)


def pair_sum_body(kept_ref, given_ref, replies_ref, out_ref):
    at = replies_ref.shape[1]
    out_ref[:, :at] = replies_ref[...]
    out_ref[:, at:] = (kept_ref[...] + given_ref[...].astype(F32)).astype(BF)


def inputs_at(pad_ref, e):
    bricks = pad_ref.shape[2]
    ex, ey = (e // 3, e % 3)
    return pad_ref[ex : ex + 4, ey : ey + 4].reshape(16 * bricks, WIDE)


def conv_body(pad_ref, weight_ref, lists_ref, out_ref, again_ref, band_ref):
    again_ref[...] = lists_ref[...]
    bricks = pad_ref.shape[2]
    build_bands(weight_ref, band_ref)
    total = None
    for e in range(9):
        part = dot(inputs_at(pad_ref, e), band_ref[e])
        total = part if total is None else total + part
    for p in range(16):
        out_ref[:, p * RUN : (p + 1) * RUN] = total[p * bricks : (p + 1) * bricks].astype(BF)


def add_rows(base, lists, first, second):
    count, face = (base.shape[0], lists.shape[1])
    index = jnp.concatenate([lists[0:1], lists[1:2]], axis=1)
    chosen = ones_where(iota((count, 2 * face), 0) == index)
    return base + dot(chosen, stack_rows(first, second))


def merge_body(received_ref, up_ref, fine_ref, lists_ref, merged_ref, parents_ref, a_ref, b_ref):
    bricks, width = fine_ref.shape
    face = a_ref.shape[0]
    parents = merge(received_ref, slots_of(lists_ref, bricks), up_ref, fine_ref, merged_ref, parents_ref)
    lists = sides_of(lists_ref, face)
    lists = by_pair(lists_ref, GY, lists[0:1], lists[1:2])
    for out_ref, rows, owners in zip((a_ref, b_ref), pick_rows(lists, merged_ref[...]), pick_rows(lists, parents)):
        out_ref[:, :width] = rows.astype(BF)
        out_ref[:, width:] = owners.astype(BF)


def fine_grad_body(part_ref, lists_ref, even_ref, odd_ref, up_ref, grad_ref, replies_ref, across):
    bricks = part_ref.shape[0]
    face = even_ref.shape[0]
    from_next, from_prev = from_pairs(lists_ref, GY, even_ref, odd_ref)
    total = add_rows(part_ref[...], sides_of(lists_ref, face), from_next, from_prev)
    grad_ref[...] = total.astype(BF)
    items = dot(stack_parities(grad_ref[...]), up_ref[...]).astype(BF)
    items = jnp.concatenate([items[v * bricks : (v + 1) * bricks] for v in range(8)], axis=1)
    half = items.shape[1] // 2
    count, both_lanes = replies_ref.shape
    pieces = both_lanes // 2 // half
    capacity, group = chip_slots(count, pieces, across)
    slots = slots_of(lists_ref, bricks)
    row = iota((count, bricks), 0)
    for other in range(2):
        owner = device_of(row // group, lists_ref, other, across)
        for j in range(pieces):
            piece = row % group * pieces + j
            named = owner * capacity + piece // 2 == slots
            rows = dot(ones_where(named & (piece % 2 == 0)), items[:, :half])
            rows += dot(ones_where(named & (piece % 2 == 1)), items[:, half:])
            at = (other * pieces + j) * half
            replies_ref[:, at : at + half] = rows.astype(BF)


def chip_slots(count, pieces, across):
    group = count // (across[0] * across[1] // 2)
    return group * pieces // 2, group


def device_of(chip, lists_ref, other, across):
    core = jnp.broadcast_to(lists_ref[5:6, GX : GX + 1], chip.shape)
    core = 1 - core if other else core
    return (chip // across[1] * 2 + core) * across[1] + chip % across[1]


def share_body(back_ref, lists_ref, out_ref, given_ref, across):
    count, item_lanes = given_ref.shape
    given_ref[...] = back_ref[:, item_lanes : 2 * item_lanes]
    share = count // (across[0] * across[1] // 2)
    same = iota((count, count), 0) % share == iota((count, count), 1) % share
    out_ref[...] = dot(ones_where(same), back_ref[:, 2 * item_lanes :]).astype(BF)


def coarse_grad_body(back_ref, given_ref, sends_ref, lists_ref, out_ref, across):
    arrivals = (back_ref[:, : given_ref.shape[1]], given_ref[...])
    capacity, devices = sends_ref.shape
    count, item_width = out_ref.shape
    half = item_width // 2
    lanes = arrivals[0].shape[0]
    pieces = arrivals[0].shape[1] // half
    _, group = chip_slots(lanes, pieces, across)
    sends = sends_ref[...].astype(F32).astype(BF)
    lane = iota((1, lanes), 1)
    totals = [None, None]
    for other in range(2):
        source = device_of(lane // group, lists_ref, other, across)
        rows = dot(sends, ones_where(source == iota((devices, lanes), 0)))
        for j in range(pieces):
            piece = lane % group * pieces + j
            picked = jnp.where(piece // 2 == iota((capacity, lanes), 0), rows, 0.0)
            index = jnp.sum(picked, axis=0, keepdims=True).astype(I32)
            named = iota((count, lanes), 0) == index
            for h in range(2):
                part = dot(ones_where(named & (piece % 2 == h)), arrivals[other][:, j * half : (j + 1) * half])
                totals[h] = part if totals[h] is None else totals[h] + part
    for h in range(2):
        out_ref[:, h * half : (h + 1) * half] = totals[h].astype(BF)


def last_body(own_ref, other_ref, lists_ref, conv_ref, up_ref, scale):
    half_count = own_ref.shape[0]
    coarse = up_ref.shape[1]
    count = 2 * half_count
    parts = up_ref.shape[0] // count
    first, second = (half * scale for half in from_pairs(lists_ref, GX, own_ref, other_ref))
    at = 0
    for q in range(parts):
        up_ref[q * count : q * count + half_count] = first[:, at : at + coarse]
        up_ref[q * count + half_count : (q + 1) * count] = second[:, at : at + coarse]
        at += coarse
    for pair in range(7):
        turned = jnp.concatenate([first[:, at : at + 2 * C], second[:, at : at + 2 * C]], axis=0).T
        at += 2 * C
        for h in range(2):
            for s in range(2):
                o = 14 * h + 2 * pair + s
                if o < 27:
                    conv_ref[o] = turned[s * C : (s + 1) * C, h * C : (h + 1) * C]


def swap(value, axis, first):
    count = lax.axis_size(axis)
    lower = range(first, count - 1, 2)
    return lax.ppermute(value, axis, [(i, i + 1) for i in lower] + [(i + 1, i) for i in lower])


def swap_pairs(to_even, to_odd, axis):
    return swap(to_even, axis, 0), swap(to_odd, axis, 1)


def trade_rows(values, axes):
    rows, width = values.shape
    devices = math.prod(lax.axis_size(axis) for axis in axes)
    grid_view = values.reshape(devices, rows // devices, width)
    return lax.all_to_all(grid_view, axes, split_axis=0, concat_axis=0, tiled=True).reshape(rows, width)


def on_device(
    fine_features, coarse_items, conv_weight, up_weight, neighbours,
    side_sends, cross_sends, parent_slots, coarse_sends, cotangent,
):
    fine = fine_features[0, 0]
    items = coarse_items[0, 0]
    cot = cotangent[0, 0]
    bricks, width = fine.shape
    face = side_sends.shape[-1]
    across = (lax.axis_size(GX_AXES), lax.axis_size("gy"))
    devices = across[0] * across[1]
    capacity = coarse_sends.shape[-1]
    item_count, item_width = items.shape
    coarse = up_weight.shape[1]
    start = bricks + 2 * face
    sends = coarse_sends.transpose(0, 1, 3, 2)[0, 0]
    slots = parent_slots[0]
    sides = side_sends[0, 0]
    crosses = cross_sends[0, 0]
    near = neighbours.transpose(0, 3, 1, 2)[0]
    up_turned = up_weight.transpose(0, 2, 1).reshape(8 * C, coarse)
    half = item_width // 2
    count = 2 * C
    item_lanes = capacity * devices // 2 * item_width // (count // 2)
    sums_width = 8 * C * coarse // count + 14 * C
    rows = shape((bricks, width))
    face_rows = shape((face, width))
    faces_and_parents = shape((face, width + item_width))
    lists_shape = shape((8, 128), I32)
    band = pltpu.VMEM((9, WIDE, RUN), BF)
    conv_flops = 2 * 9 * 16 * bricks * WIDE * RUN

    listed = (sends, items, sides, crosses, slots)
    outgoing, lists = call(
        first_body, [shape((2 * capacity * devices, half)), lists_shape], *listed,
        scratch=[pltpu.VMEM(a.shape, a.dtype) for a in listed] + [pltpu.SemaphoreType.DMA((len(listed),))],
        in_hbm=True,
    )
    received = trade_rows(outgoing, ("x", "core", "gy"))
    lane = jnp.arange(128, dtype=I32)[None]
    parity = jnp.where(lane == GX, lax.axis_index("core"), lax.axis_index("gy") % 2).astype(I32)
    table_rows = start + 2 * face
    ext_grad, to_even, to_odd, turned, mains, ends, lists = call(
        table_grad_body,
        [
            shape((start, width), F32), face_rows, face_rows, shape((RUN, 16 * bricks)),
            shape((9, bricks, table_rows)), shape((9, bricks, 2 * table_rows)), lists_shape,
        ],
        cot, conv_weight, near, lists, parity,
        scratch=[band, pltpu.VMEM((6, 6, bricks, WIDE), F32)], flops=2 * conv_flops,
    )
    cross_grads = swap_pairs(to_even, to_odd, GX_AXES)
    merged, parents, to_even, to_odd = call(
        merge_body, [rows, shape((8 * bricks, coarse)), faces_and_parents, faces_and_parents],
        received, up_turned, fine, lists,
    )
    sides = swap_pairs(to_even, to_odd, "gy")
    to_even, to_odd = call(cross_body, [face_rows, face_rows], merged, *sides, lists)
    crosses = swap_pairs(to_even, to_odd, GX_AXES)
    half_sums = (count // 2, sums_width)
    fine_part, to_even, to_odd, up_sums = call(
        side_grad_body,
        [shape((bricks, width), F32), face_rows, face_rows, shape((count, sums_width - 14 * C), F32)],
        ext_grad, lists, *cross_grads, *sides, parents,
    )
    side_grads = swap_pairs(to_even, to_odd, "gy")
    kept, given, pad = call(
        weight_grad_body, [shape(half_sums, F32), shape(half_sums), shape((6, 6, bricks, WIDE))],
        merged, *sides, *crosses, turned, mains, ends, lists, up_sums,
        scratch=[pltpu.VMEM((table_rows, width), BF), pltpu.VMEM((count, sums_width), F32)], flops=conv_flops,
    )
    given = swap(given, "core", 0)
    grad_fine, replies = call(
        functools.partial(fine_grad_body, across=across), [rows, shape((count // 2, 2 * item_lanes))],
        fine_part, lists, *side_grads, up_turned,
    )
    (sums,) = call(pair_sum_body, [shape((count // 2, 2 * item_lanes + sums_width))], kept, given, replies)
    back = trade_rows(sums, ("x", "gy"))
    output, lists = call(
        conv_body, [rows, lists_shape], pad, conv_weight, lists, scratch=[band], flops=conv_flops
    )
    sums, given = call(
        functools.partial(share_body, across=across), [shape(half_sums), shape((count // 2, item_lanes))], back, lists
    )
    sums = trade_rows(sums, ("x", "gy"))
    other_sums = swap(sums, "core", 0)
    given = swap(given, "core", 0)
    (coarse_grad,) = call(
        functools.partial(coarse_grad_body, across=across), [shape((item_count, item_width))], back, given, sends, lists
    )
    scale = 1.0 / math.sqrt(64 * bricks * devices)
    grad_conv, grad_up = call(
        functools.partial(last_body, scale=scale),
        [shape((27, C, C), F32), shape((8 * C, coarse), F32)], sums, other_sums, lists,
    )
    return (
        output.reshape(1, 1, bricks, width),
        grad_fine.reshape(1, 1, bricks, width),
        coarse_grad.reshape(1, 1, item_count, item_width),
        grad_conv,
        grad_up.reshape(8, C, coarse).transpose(0, 2, 1),
    )


def solution(mesh):
    groups, across_x, across_y = mesh.devices.shape
    split_mesh = Mesh(mesh.devices.reshape(groups, across_x // 2, 2, across_y), ("groups", "x", "core", "gy"))
    rows = ("groups", "x", "core")
    split = P(rows, "gy", None, None)
    placed = (split, split, P(), P(), split, split, split, P(rows, "gy", None), split, split)
    return jax.shard_map(
        on_device,
        mesh=split_mesh,
        in_specs=placed,
        out_specs=(split, split, split, P("groups", None, None), P("groups", None, None)),
        check_vma=False,
    )
```

```python
import functools
import math

import jax
import jax.numpy as jnp
from jax import lax
from jax.experimental import pallas as pl
from jax.experimental.pallas import tpu as pltpu
from jax.sharding import Mesh
from jax.sharding import PartitionSpec as P

BF = jnp.bfloat16
F32 = jnp.float32
I32 = jnp.int32

C = 64
RUN = 4 * C
WIDE = RUN + 2 * C


def iota(shape, axis):
    return lax.broadcasted_iota(I32, shape, axis)


def ones_where(mask):
    return jnp.where(mask, 1.0, 0.0).astype(BF)


def dot(a, b):
    return jnp.dot(a, b, preferred_element_type=F32)


def dot_tn(a, b):
    return lax.dot_general(a, b, (((0,), (0,)), ((), ())), preferred_element_type=F32)


def dot_nt(a, b):
    return lax.dot_general(a, b, (((1,), (1,)), ((), ())), preferred_element_type=F32)


def column_of(row):
    size = row.shape[1]
    diagonal = iota((size, size), 0) == iota((size, size), 1)
    spread = jnp.broadcast_to(row.astype(F32), (size, size))
    return jnp.sum(jnp.where(diagonal, spread, 0.0), axis=1, keepdims=True).astype(I32)


def call(body, outs, *args, scratch=(), flops=0, in_hbm=False):
    moved = sum(a.size * a.dtype.itemsize for a in list(args) + list(outs))
    return pl.pallas_call(
        body,
        out_shape=tuple(outs),
        in_specs=[pl.BlockSpec(memory_space=pltpu.HBM) if in_hbm else pl.BlockSpec() for _ in args],
        scratch_shapes=tuple(scratch),
        cost_estimate=pl.CostEstimate(flops=flops, bytes_accessed=moved, transcendentals=0),
        compiler_params=pltpu.CompilerParams(vmem_limit_bytes=None if in_hbm else 28 * 2**20),
    )(*args)


def shape(dims, dtype=BF):
    return jax.ShapeDtypeStruct(dims, dtype)


def items_out(sends_ref, items_ref, out_ref):
    capacity, devices = sends_ref.shape
    count, width = items_ref.shape
    half = width // 2
    group = 2 * capacity
    lanes = devices * group
    spread = ones_where(iota((lanes, devices), 0) // group == iota((lanes, devices), 1))
    slot = iota((lanes, capacity), 0) % group // 2
    values = dot_nt(spread, sends_ref[...].astype(F32).astype(BF))
    item = jnp.sum(jnp.where(slot == iota((lanes, capacity), 1), values, 0.0), axis=1, keepdims=True).astype(I32)
    place = jnp.where(item < count, item + iota((lanes, 1), 0) % 2 * count, -1)
    chosen = ones_where(iota((lanes, 2 * count), 1) == place)
    out_ref[...] = dot(chosen, jnp.concatenate([items_ref[:, :half], items_ref[:, half:]], axis=0)).astype(BF)


def merge(received_ref, slots, up_ref, fine_ref, merged_ref, parents_ref):
    bricks = fine_ref.shape[0]
    lanes, half = received_ref.shape
    slot = column_of(slots)
    place = iota((bricks, lanes), 1)
    named = place // 2 == slot
    received = received_ref[...]
    parents = jnp.concatenate(
        [dot(ones_where(named & (place % 2 == h)), received) for h in (0, 1)], axis=1
    ).astype(BF)
    coarse = 2 * half // 8
    stacked = jnp.concatenate([parents[:, v * coarse : (v + 1) * coarse] for v in range(8)], axis=0)
    parents_ref[...] = stacked
    lifted = dot_nt(stacked, up_ref[...])
    for v in range(8):
        cx, cy, cz = (v // 4, v // 2 % 2, v % 2)
        for parity in range(4):
            vx, vy = (2 * cx + parity // 2, 2 * cy + parity % 2)
            at = (vx * 4 + vy) * RUN + cz * 2 * C
            add = lifted[v * bricks : (v + 1) * bricks, parity * 2 * C : (parity + 1) * 2 * C]
            merged_ref[:, at : at + 2 * C] = (fine_ref[:, at : at + 2 * C].astype(F32) + add).astype(BF)
    return parents


def pick_rows(lists, rows):
    return [dot_tn(ones_where(iota((rows.shape[0], one.shape[1]), 0) == one), rows) for one in lists]


GX, GY = (0, 1)
GX_AXES = ("x", "core")


def by_pair(lists_ref, axis, of_next, of_prev):
    odd = jnp.broadcast_to(lists_ref[5:6, axis : axis + 1], of_next.shape) == 1
    return jnp.where(odd, of_prev, of_next), jnp.where(odd, of_next, of_prev)


def from_pairs(lists_ref, axis, even_ref, odd_ref):
    return by_pair(lists_ref, axis, even_ref[...].astype(F32), odd_ref[...].astype(F32))


def stack_rows(*parts):
    return jnp.concatenate([p.astype(F32) for p in parts], axis=0).astype(BF)


def sides_of(lists_ref, face):
    return lists_ref[0:2, :face]


def crosses_of(lists_ref, face):
    return lists_ref[2:4, :face]


def slots_of(lists_ref, bricks):
    return lists_ref[4:5, :bricks]


def cross_body(merged_ref, even_ref, odd_ref, lists_ref, a_ref, b_ref):
    face, width = a_ref.shape
    high, low = from_pairs(lists_ref, GY, even_ref, odd_ref)
    rows = jnp.concatenate([merged_ref[...], stack_rows(low[:, :width], high[:, :width])], axis=0)
    lists = crosses_of(lists_ref, face)
    picked = pick_rows(by_pair(lists_ref, GX, lists[0:1], lists[1:2]), rows)
    a_ref[...] = picked[0].astype(BF)
    b_ref[...] = picked[1].astype(BF)


def build_bands(weight_ref, band_ref):
    zero = jnp.zeros((C, C), BF)
    blank = jnp.zeros((C, 2 * C), BF)

    def pair(a, b):
        return jnp.concatenate([a, b], axis=1)

    for e in range(9):
        low, mid, high = (weight_ref[3 * e + z] for z in range(3))
        first, second = (pair(mid, low), pair(high, mid))
        left, right = (pair(low, zero), pair(zero, high))
        rows = (
            (first, blank),
            (second, left),
            (right, first),
            (blank, second),
            (blank, right),
            (left, blank),
        )
        for z, halves in enumerate(rows):
            for s in range(2):
                band_ref[e, z * C : (z + 1) * C, s * 2 * C : (s + 1) * 2 * C] = halves[s]


def options(at):
    return [(at + 1, 0)] + ([(5, 1)] if at == 0 else []) + ([(0, -1)] if at == 3 else [])


def offset_of(dx, dy, dz):
    return (dx + 1) * 9 + (dy + 1) * 3 + dz + 1


def stack_lanes(value, lanes):
    return jnp.concatenate([value[:, p * lanes : (p + 1) * lanes] for p in range(value.shape[1] // lanes)], axis=0)


def stack_parities(value):
    stacked = []
    for v in range(8):
        cx, cy, cz = (v // 4, v // 2 % 2, v % 2)
        lanes = []
        for parity in range(4):
            at = ((2 * cx + parity // 2) * 4 + 2 * cy + parity % 2) * RUN + cz * 2 * C
            lanes.append(value[:, at : at + 2 * C])
        stacked.append(jnp.concatenate(lanes, axis=1))
    return jnp.concatenate(stacked, axis=0)


def stack_runs(ref):
    return jnp.concatenate([ref[:, p * RUN : (p + 1) * RUN] for p in range(16)], axis=0)


def split_two(value):
    head = value.astype(BF)
    return head, (value - head.astype(F32)).astype(BF)


def table_grad_body(
    cot_ref, weight_ref, near_ref, lists_ref, parity_ref,
    ext_ref, even_ref, odd_ref, turned_ref, mains_ref, ends_ref, again_ref, band_ref, pad_ref,
):
    again_ref[...] = lists_ref[...]
    again_ref[5:6] = parity_ref[...]
    bricks = cot_ref.shape[0]
    face = even_ref.shape[0]
    start = ext_ref.shape[0]
    rows = start + 2 * face
    build_bands(weight_ref, band_ref)
    cot = stack_runs(cot_ref)
    turned_ref[...] = cot.T
    pad_ref[...] = jnp.zeros(pad_ref.shape, F32)
    for e in range(9):
        ex, ey = (e // 3, e % 3)
        part = dot_nt(cot, band_ref[e]).reshape(4, 4, bricks, WIDE)
        pad_ref[ex : ex + 4, ey : ey + 4] += part
    near = [near_ref[o] for o in range(27)]

    def chooser(which):
        index = jnp.concatenate([near[o] for o in which], axis=1)
        return ones_where(iota((rows, index.shape[1]), 0) == index)

    lower_half = iota((rows, 2 * C), 1) < C
    cache = {}
    for x in range(4):
        for y in range(4):
            places = [(X, Y, dx, dy) for X, dx in options(x) for Y, dy in options(y)]
            key = tuple((dx, dy) for _, _, dx, dy in places)
            if key not in cache:
                moved = [d for d in key if d != (0, 0)]
                main = chooser([offset_of(*d, 0) for d in moved] * 2) if moved else None
                up = chooser([offset_of(*d, 1) for d in key] * 2)
                down = chooser([offset_of(*d, -1) for d in key] * 2)
                cache[key] = (main, jnp.concatenate([up, down], axis=0))
            main, ends = cache[key]
            own = pad_ref[x + 1, y + 1, :, :RUN]
            own = jnp.concatenate([own, jnp.zeros((rows - bricks, RUN), F32)], axis=0)
            if main is not None:
                parts = [split_two(pad_ref[X, Y, :, :RUN]) for X, Y, dx, dy in places if (dx, dy) != (0, 0)]
                value = jnp.concatenate([p[0] for p in parts] + [p[1] for p in parts], axis=0)
                own += dot(main, value)
            parts = [split_two(pad_ref[X, Y, :, RUN:]) for X, Y, _, _ in places]
            value = jnp.concatenate([p[0] for p in parts] + [p[1] for p in parts], axis=0)
            halo = dot(ends, value)
            first = own[:, : 2 * C] + jnp.where(lower_half, halo[:rows], 0.0)
            second = own[:, 2 * C :] + jnp.where(lower_half, 0.0, halo[rows:])
            total = jnp.concatenate([first, second], axis=1)
            at = (x * 4 + y) * RUN
            ext_ref[:, at : at + RUN] = total[:start]
            even, odd = by_pair(again_ref, GX, total[start + face :], total[start : start + face])
            even_ref[:, at : at + RUN] = even.astype(BF)
            odd_ref[:, at : at + RUN] = odd.astype(BF)
    make_choosers(near_ref, rows, mains_ref, ends_ref)


def make_choosers(near_ref, rows, mains_ref, ends_ref):
    bricks = mains_ref.shape[1]
    near = jnp.concatenate([near_ref[o] for o in range(27)] + [jnp.zeros((5, bricks), I32)], axis=0)
    near = near.astype(F32).T.astype(I32)
    place = iota((bricks, rows), 1)
    pair_place = iota((bricks, 2 * rows), 1)
    for d in range(9):
        down, straight, up = (near[:, 3 * d + z : 3 * d + z + 1] for z in range(3))
        mains_ref[d] = ones_where(place == straight)
        ends_ref[d] = ones_where(pair_place == jnp.where(pair_place < rows, up, down + rows))


def first_body(
    sends_hbm, items_hbm, sides_hbm, crosses_hbm, slots_hbm, out_ref, lists_ref,
    sends_ref, items_ref, sides_ref, crosses_ref, slots_ref, arrived,
):
    sources = (sends_hbm, items_hbm, sides_hbm, crosses_hbm, slots_hbm)
    places = (sends_ref, items_ref, sides_ref, crosses_ref, slots_ref)
    copies = [pltpu.make_async_copy(s, p, arrived.at[i]) for i, (s, p) in enumerate(zip(sources, places))]
    for copy in copies:
        copy.start()
    for copy in copies:
        copy.wait()
    face, bricks = (sides_ref.shape[1], slots_ref.shape[1])
    lists_ref[...] = jnp.zeros(lists_ref.shape, I32)
    lists_ref[0:2, :face] = sides_ref[...]
    lists_ref[2:4, :face] = crosses_ref[...]
    lists_ref[4:5, :bricks] = slots_ref[...]
    items_out(sends_ref, items_ref, out_ref)


def side_grad_body(
    ext_ref, lists_ref, even_grad_ref, odd_grad_ref, even_side_ref, odd_side_ref, parents_ref,
    part_ref, to_even_ref, to_odd_ref, up_sums_ref,
):
    bricks, width = part_ref.shape
    face = to_even_ref.shape[0]
    from_next, from_prev = from_pairs(lists_ref, GX, even_grad_ref, odd_grad_ref)
    total = add_rows(ext_ref[...], crosses_of(lists_ref, face), from_next, from_prev)
    part_ref[...] = total[:bricks]
    to_even, to_odd = by_pair(lists_ref, GY, total[bricks + face :], total[bricks : bricks + face])
    to_even_ref[...] = to_even.astype(BF)
    to_odd_ref[...] = to_odd.astype(BF)
    high, low = by_pair(
        lists_ref, GY, even_side_ref[:, width:].astype(F32), odd_side_ref[:, width:].astype(F32)
    )
    side_parents = stack_lanes(stack_rows(low, high), parents_ref.shape[1])
    grads = [stack_parities(total[:bricks].astype(BF)), stack_parities(total[bricks:].astype(BF))]
    up_sum = dot_tn(jnp.concatenate(grads, axis=0), jnp.concatenate([parents_ref[...], side_parents], axis=0))
    coarse = up_sum.shape[1]
    count = up_sums_ref.shape[0]
    for q in range(up_sum.shape[0] // count):
        up_sums_ref[:, q * coarse : (q + 1) * coarse] = up_sum[q * count : (q + 1) * count]


def weight_grad_body(
    merged_ref, even_side_ref, odd_side_ref, even_cross_ref, odd_cross_ref, turned_ref, mains_ref, ends_ref, lists_ref,
    up_sums_ref, kept_ref, given_ref, pad_ref, table_ref, sums_ref,
):
    bricks, width = merged_ref.shape
    face = even_side_ref.shape[0]
    rows = bricks + 4 * face
    high, low = by_pair(lists_ref, GY, even_side_ref[:, :width].astype(F32), odd_side_ref[:, :width].astype(F32))
    above, below = from_pairs(lists_ref, GX, even_cross_ref, odd_cross_ref)
    table_ref[:bricks] = merged_ref[...]
    table_ref[bricks:] = stack_rows(low, high, below, above)
    count = sums_ref.shape[0]
    up_lanes = up_sums_ref.shape[1]
    sums_ref[:, :up_lanes] = up_sums_ref[...]
    lower_half = iota((rows, 2 * C), 1) < C
    zero = jnp.zeros((rows, 2 * C), BF)
    for x in range(4):
        for y in range(4):
            places = [(X, Y, dx, dy) for X, dx in options(x) for Y, dy in options(y)]
            at = (x * 4 + y) * RUN
            columns = table_ref[:, at : at + RUN]
            first = jnp.where(lower_half, columns[:, : 2 * C], zero)
            second = jnp.where(lower_half, zero, columns[:, 2 * C :])
            ends = jnp.concatenate([ends_ref[3 * dx + dy + 4] for _, _, dx, dy in places], axis=0)
            halo = dot(ends, jnp.concatenate([first, second], axis=0)).astype(BF)
            for i, (X, Y, _, _) in enumerate(places):
                pad_ref[X, Y, :, RUN:] = halo[i * bricks : (i + 1) * bricks]
            pad_ref[x + 1, y + 1, :, :RUN] = columns[:bricks]
            moved = [p for p in places if p[2:] != (0, 0)]
            if moved:
                main = jnp.concatenate([mains_ref[3 * dx + dy + 4] for _, _, dx, dy in moved], axis=0)
                got = dot(main, columns).astype(BF)
                for i, (X, Y, _, _) in enumerate(moved):
                    pad_ref[X, Y, :, :RUN] = got[i * bricks : (i + 1) * bricks]

    turned = turned_ref[...]
    lanes_low = iota((C, 2 * C), 1) < C
    sums = []
    for e in range(9):
        wide = dot(turned, inputs_at(pad_ref, e))

        def block(z, s):
            return wide[z * C : (z + 1) * C, s * 2 * C : (s + 1) * 2 * C]

        low = jnp.where(lanes_low, block(1, 0) + block(3, 1), block(0, 2) + block(2, 0))
        mid = jnp.where(lanes_low, block(0, 0) + block(2, 1), block(1, 0) + block(3, 1))
        high = jnp.where(lanes_low, block(1, 1) + block(3, 2), block(0, 0) + block(2, 1))
        for value in (low, mid, high):
            sums.append(value + pltpu.roll(value, C, 1))
    sums.append(jnp.zeros((C, 2 * C), F32))
    for pair in range(7):
        both = [jnp.where(lanes_low, sums[14 * h + 2 * pair], sums[14 * h + 2 * pair + 1]) for h in range(2)]
        at = up_lanes + pair * 2 * C
        sums_ref[:, at : at + 2 * C] = jnp.concatenate(both, axis=0)
    kept, given = by_pair(lists_ref, GX, sums_ref[: count // 2], sums_ref[count // 2 :])
    kept_ref[...] = kept
    given_ref[...] = given.astype(BF)


def pair_sum_body(kept_ref, given_ref, out_ref):
    out_ref[...] = (kept_ref[...] + given_ref[...].astype(F32)).astype(BF)


def inputs_at(pad_ref, e):
    bricks = pad_ref.shape[2]
    ex, ey = (e // 3, e % 3)
    return pad_ref[ex : ex + 4, ey : ey + 4].reshape(16 * bricks, WIDE)


def conv_body(pad_ref, weight_ref, lists_ref, out_ref, again_ref, band_ref):
    again_ref[...] = lists_ref[...]
    bricks = pad_ref.shape[2]
    build_bands(weight_ref, band_ref)
    total = None
    for e in range(9):
        part = dot(inputs_at(pad_ref, e), band_ref[e])
        total = part if total is None else total + part
    for p in range(16):
        out_ref[:, p * RUN : (p + 1) * RUN] = total[p * bricks : (p + 1) * bricks].astype(BF)


def add_rows(base, lists, first, second):
    count, face = (base.shape[0], lists.shape[1])
    index = jnp.concatenate([lists[0:1], lists[1:2]], axis=1)
    chosen = ones_where(iota((count, 2 * face), 0) == index)
    return base + dot(chosen, stack_rows(first, second))


def merge_body(received_ref, up_ref, fine_ref, lists_ref, merged_ref, parents_ref, a_ref, b_ref):
    bricks, width = fine_ref.shape
    face = a_ref.shape[0]
    parents = merge(received_ref, slots_of(lists_ref, bricks), up_ref, fine_ref, merged_ref, parents_ref)
    lists = sides_of(lists_ref, face)
    lists = by_pair(lists_ref, GY, lists[0:1], lists[1:2])
    for out_ref, rows, owners in zip((a_ref, b_ref), pick_rows(lists, merged_ref[...]), pick_rows(lists, parents)):
        out_ref[:, :width] = rows.astype(BF)
        out_ref[:, width:] = owners.astype(BF)


def fine_grad_body(part_ref, lists_ref, even_ref, odd_ref, up_ref, grad_ref, replies_ref, across):
    bricks = part_ref.shape[0]
    face = even_ref.shape[0]
    from_next, from_prev = from_pairs(lists_ref, GY, even_ref, odd_ref)
    total = add_rows(part_ref[...], sides_of(lists_ref, face), from_next, from_prev)
    grad_ref[...] = total.astype(BF)
    items = dot(stack_parities(grad_ref[...]), up_ref[...]).astype(BF)
    items = jnp.concatenate([items[v * bricks : (v + 1) * bricks] for v in range(8)], axis=1)
    half = items.shape[1] // 2
    count, both_lanes = replies_ref.shape
    pieces = both_lanes // 2 // half
    capacity, group = chip_slots(count, pieces, across)
    slots = slots_of(lists_ref, bricks)
    row = iota((count, bricks), 0)
    for other in range(2):
        owner = device_of(row // group, lists_ref, other, across)
        for j in range(pieces):
            piece = row % group * pieces + j
            named = owner * capacity + piece // 2 == slots
            rows = dot(ones_where(named & (piece % 2 == 0)), items[:, :half])
            rows += dot(ones_where(named & (piece % 2 == 1)), items[:, half:])
            at = (other * pieces + j) * half
            replies_ref[:, at : at + half] = rows.astype(BF)


def chip_slots(count, pieces, across):
    group = count // (across[0] * across[1] // 2)
    return group * pieces // 2, group


def device_of(chip, lists_ref, other, across):
    core = jnp.broadcast_to(lists_ref[5:6, GX : GX + 1], chip.shape)
    core = 1 - core if other else core
    return (chip // across[1] * 2 + core) * across[1] + chip % across[1]


def share_body(sums_ref, replies_ref, out_ref, across):
    count, item_lanes = replies_ref.shape
    share = count // (across[0] * across[1] // 2)
    same = iota((count, count), 0) % share == iota((count, count), 1) % share
    out_ref[:, :item_lanes] = replies_ref[...]
    out_ref[:, item_lanes:] = dot(ones_where(same), sums_ref[...]).astype(BF)


def coarse_grad(arrivals, sends_ref, lists_ref, out_ref, across):
    capacity, devices = sends_ref.shape
    count, item_width = out_ref.shape
    half = item_width // 2
    lanes = arrivals[0].shape[0]
    pieces = arrivals[0].shape[1] // half
    _, group = chip_slots(lanes, pieces, across)
    sends = sends_ref[...].astype(F32).astype(BF)
    lane = iota((1, lanes), 1)
    totals = [None, None]
    for other in range(2):
        source = device_of(lane // group, lists_ref, other, across)
        rows = dot(sends, ones_where(source == iota((devices, lanes), 0)))
        for j in range(pieces):
            piece = lane % group * pieces + j
            picked = jnp.where(piece // 2 == iota((capacity, lanes), 0), rows, 0.0)
            index = jnp.sum(picked, axis=0, keepdims=True).astype(I32)
            named = iota((count, lanes), 0) == index
            for h in range(2):
                part = dot(ones_where(named & (piece % 2 == h)), arrivals[other][:, j * half : (j + 1) * half])
                totals[h] = part if totals[h] is None else totals[h] + part
    for h in range(2):
        out_ref[:, h * half : (h + 1) * half] = totals[h].astype(BF)


def last_body(back_ref, given_ref, sends_ref, lists_ref, conv_ref, up_ref, out_ref, item_lanes, across, scale):
    half_count = back_ref.shape[0]
    items = (back_ref[:, :item_lanes], given_ref[:, item_lanes : 2 * item_lanes])
    coarse_grad(items, sends_ref, lists_ref, out_ref, across)
    coarse = up_ref.shape[1]
    count = 2 * half_count
    parts = up_ref.shape[0] // count
    own = back_ref[:, 2 * item_lanes :].astype(F32) * scale
    others = given_ref[:, 2 * item_lanes :].astype(F32) * scale
    first, second = by_pair(lists_ref, GX, own, others)
    at = 0
    for q in range(parts):
        up_ref[q * count : q * count + half_count] = first[:, at : at + coarse]
        up_ref[q * count + half_count : (q + 1) * count] = second[:, at : at + coarse]
        at += coarse
    for pair in range(7):
        turned = jnp.concatenate([first[:, at : at + 2 * C], second[:, at : at + 2 * C]], axis=0).T
        at += 2 * C
        for h in range(2):
            for s in range(2):
                o = 14 * h + 2 * pair + s
                if o < 27:
                    conv_ref[o] = turned[s * C : (s + 1) * C, h * C : (h + 1) * C]


def swap(value, axis, first):
    count = lax.axis_size(axis)
    lower = range(first, count - 1, 2)
    return lax.ppermute(value, axis, [(i, i + 1) for i in lower] + [(i + 1, i) for i in lower])


def swap_pairs(to_even, to_odd, axis):
    return swap(to_even, axis, 0), swap(to_odd, axis, 1)


def trade_rows(values, axes):
    rows, width = values.shape
    devices = math.prod(lax.axis_size(axis) for axis in axes)
    grid_view = values.reshape(devices, rows // devices, width)
    return lax.all_to_all(grid_view, axes, split_axis=0, concat_axis=0, tiled=True).reshape(rows, width)


def on_device(
    fine_features, coarse_items, conv_weight, up_weight, neighbours,
    side_sends, cross_sends, parent_slots, coarse_sends, cotangent,
):
    fine = fine_features[0, 0]
    items = coarse_items[0, 0]
    cot = cotangent[0, 0]
    bricks, width = fine.shape
    face = side_sends.shape[-1]
    across = (lax.axis_size(GX_AXES), lax.axis_size("gy"))
    devices = across[0] * across[1]
    capacity = coarse_sends.shape[-1]
    item_count, item_width = items.shape
    coarse = up_weight.shape[1]
    start = bricks + 2 * face
    sends = coarse_sends.transpose(0, 1, 3, 2)[0, 0]
    slots = parent_slots[0]
    sides = side_sends[0, 0]
    crosses = cross_sends[0, 0]
    near = neighbours.transpose(0, 3, 1, 2)[0]
    up_turned = up_weight.transpose(0, 2, 1).reshape(8 * C, coarse)
    half = item_width // 2
    count = 2 * C
    item_lanes = capacity * devices // 2 * item_width // (count // 2)
    sums_width = 8 * C * coarse // count + 14 * C
    rows = shape((bricks, width))
    face_rows = shape((face, width))
    faces_and_parents = shape((face, width + item_width))
    lists_shape = shape((8, 128), I32)
    band = pltpu.VMEM((9, WIDE, RUN), BF)
    conv_flops = 2 * 9 * 16 * bricks * WIDE * RUN

    listed = (sends, items, sides, crosses, slots)
    outgoing, lists = call(
        first_body, [shape((2 * capacity * devices, half)), lists_shape], *listed,
        scratch=[pltpu.VMEM(a.shape, a.dtype) for a in listed] + [pltpu.SemaphoreType.DMA((len(listed),))],
        in_hbm=True,
    )
    received = trade_rows(outgoing, ("x", "core", "gy"))
    lane = jnp.arange(128, dtype=I32)[None]
    parity = jnp.where(lane == GX, lax.axis_index("core"), lax.axis_index("gy") % 2).astype(I32)
    table_rows = start + 2 * face
    ext_grad, to_even, to_odd, turned, mains, ends, lists = call(
        table_grad_body,
        [
            shape((start, width), F32), face_rows, face_rows, shape((RUN, 16 * bricks)),
            shape((9, bricks, table_rows)), shape((9, bricks, 2 * table_rows)), lists_shape,
        ],
        cot, conv_weight, near, lists, parity,
        scratch=[band, pltpu.VMEM((6, 6, bricks, WIDE), F32)], flops=2 * conv_flops,
    )
    cross_grads = swap_pairs(to_even, to_odd, GX_AXES)
    merged, parents, to_even, to_odd = call(
        merge_body, [rows, shape((8 * bricks, coarse)), faces_and_parents, faces_and_parents],
        received, up_turned, fine, lists,
    )
    sides = swap_pairs(to_even, to_odd, "gy")
    to_even, to_odd = call(cross_body, [face_rows, face_rows], merged, *sides, lists)
    crosses = swap_pairs(to_even, to_odd, GX_AXES)
    half_sums = (count // 2, sums_width)
    fine_part, to_even, to_odd, up_sums = call(
        side_grad_body,
        [shape((bricks, width), F32), face_rows, face_rows, shape((count, sums_width - 14 * C), F32)],
        ext_grad, lists, *cross_grads, *sides, parents,
    )
    side_grads = swap_pairs(to_even, to_odd, "gy")
    kept, given, pad = call(
        weight_grad_body, [shape(half_sums, F32), shape(half_sums), shape((6, 6, bricks, WIDE))],
        merged, *sides, *crosses, turned, mains, ends, lists, up_sums,
        scratch=[pltpu.VMEM((table_rows, width), BF), pltpu.VMEM((count, sums_width), F32)], flops=conv_flops,
    )
    given = swap(given, "core", 0)
    (sums,) = call(pair_sum_body, [shape(half_sums)], kept, given)
    sums = trade_rows(sums, ("x", "gy"))
    output, lists = call(
        conv_body, [rows, lists_shape], pad, conv_weight, lists, scratch=[band], flops=conv_flops
    )
    grad_fine, replies = call(
        functools.partial(fine_grad_body, across=across), [rows, shape((count // 2, 2 * item_lanes))],
        fine_part, lists, *side_grads, up_turned,
    )
    (back,) = call(
        functools.partial(share_body, across=across), [shape((count // 2, 2 * item_lanes + sums_width))], sums, replies
    )
    back = trade_rows(back, ("x", "gy"))
    given = swap(back, "core", 0)
    scale = 1.0 / math.sqrt(64 * bricks * devices)
    grad_conv, grad_up, coarse_grad = call(
        functools.partial(last_body, item_lanes=item_lanes, across=across, scale=scale),
        [shape((27, C, C), F32), shape((8 * C, coarse), F32), shape((item_count, item_width))],
        back, given, sends, lists,
    )
    return (
        output.reshape(1, 1, bricks, width),
        grad_fine.reshape(1, 1, bricks, width),
        coarse_grad.reshape(1, 1, item_count, item_width),
        grad_conv,
        grad_up.reshape(8, C, coarse).transpose(0, 2, 1),
    )


def solution(mesh):
    groups, across_x, across_y = mesh.devices.shape
    split_mesh = Mesh(mesh.devices.reshape(groups, across_x // 2, 2, across_y), ("groups", "x", "core", "gy"))
    rows = ("groups", "x", "core")
    split = P(rows, "gy", None, None)
    placed = (split, split, P(), P(), split, split, split, P(rows, "gy", None), split, split)
    return jax.shard_map(
        on_device,
        mesh=split_mesh,
        in_specs=placed,
        out_specs=(split, split, split, P("groups", None, None), P("groups", None, None)),
        check_vma=False,
    )
```

```python
import functools
import math

import jax
import jax.numpy as jnp
from jax import lax
from jax.experimental import pallas as pl
from jax.experimental.pallas import tpu as pltpu
from jax.sharding import Mesh
from jax.sharding import PartitionSpec as P

BF = jnp.bfloat16
F32 = jnp.float32
I32 = jnp.int32

C = 64
RUN = 4 * C
WIDE = RUN + 2 * C


def iota(shape, axis):
    return lax.broadcasted_iota(I32, shape, axis)


def ones_where(mask):
    return jnp.where(mask, 1.0, 0.0).astype(BF)


def dot(a, b):
    return jnp.dot(a, b, preferred_element_type=F32)


def dot_tn(a, b):
    return lax.dot_general(a, b, (((0,), (0,)), ((), ())), preferred_element_type=F32)


def dot_nt(a, b):
    return lax.dot_general(a, b, (((1,), (1,)), ((), ())), preferred_element_type=F32)


def column_of(row):
    size = row.shape[1]
    diagonal = iota((size, size), 0) == iota((size, size), 1)
    spread = jnp.broadcast_to(row.astype(F32), (size, size))
    return jnp.sum(jnp.where(diagonal, spread, 0.0), axis=1, keepdims=True).astype(I32)


def call(body, outs, *args, scratch=(), flops=0, in_hbm=False):
    moved = sum(a.size * a.dtype.itemsize for a in list(args) + list(outs))
    return pl.pallas_call(
        body,
        out_shape=tuple(outs),
        in_specs=[pl.BlockSpec(memory_space=pltpu.HBM) if in_hbm else pl.BlockSpec() for _ in args],
        scratch_shapes=tuple(scratch),
        cost_estimate=pl.CostEstimate(flops=flops, bytes_accessed=moved, transcendentals=0),
        compiler_params=pltpu.CompilerParams(vmem_limit_bytes=None if in_hbm else 28 * 2**20),
    )(*args)


def shape(dims, dtype=BF):
    return jax.ShapeDtypeStruct(dims, dtype)


def items_out(sends_ref, items_ref, out_ref):
    capacity, devices = sends_ref.shape
    count, width = items_ref.shape
    half = width // 2
    group = 2 * capacity
    lanes = devices * group
    spread = ones_where(iota((lanes, devices), 0) // group == iota((lanes, devices), 1))
    slot = iota((lanes, capacity), 0) % group // 2
    values = dot_nt(spread, sends_ref[...].astype(F32).astype(BF))
    item = jnp.sum(jnp.where(slot == iota((lanes, capacity), 1), values, 0.0), axis=1, keepdims=True).astype(I32)
    place = jnp.where(item < count, item + iota((lanes, 1), 0) % 2 * count, -1)
    chosen = ones_where(iota((lanes, 2 * count), 1) == place)
    out_ref[...] = dot(chosen, jnp.concatenate([items_ref[:, :half], items_ref[:, half:]], axis=0)).astype(BF)


def merge(received_ref, slots, up_ref, fine_ref, merged_ref, parents_ref):
    bricks = fine_ref.shape[0]
    lanes, half = received_ref.shape
    slot = column_of(slots)
    place = iota((bricks, lanes), 1)
    named = place // 2 == slot
    received = received_ref[...]
    parents = jnp.concatenate(
        [dot(ones_where(named & (place % 2 == h)), received) for h in (0, 1)], axis=1
    ).astype(BF)
    coarse = 2 * half // 8
    stacked = jnp.concatenate([parents[:, v * coarse : (v + 1) * coarse] for v in range(8)], axis=0)
    parents_ref[...] = stacked
    lifted = dot_nt(stacked, up_ref[...])
    for v in range(8):
        cx, cy, cz = (v // 4, v // 2 % 2, v % 2)
        for parity in range(4):
            vx, vy = (2 * cx + parity // 2, 2 * cy + parity % 2)
            at = (vx * 4 + vy) * RUN + cz * 2 * C
            add = lifted[v * bricks : (v + 1) * bricks, parity * 2 * C : (parity + 1) * 2 * C]
            merged_ref[:, at : at + 2 * C] = (fine_ref[:, at : at + 2 * C].astype(F32) + add).astype(BF)
    return parents


def pick_rows(lists, rows):
    return [dot_tn(ones_where(iota((rows.shape[0], one.shape[1]), 0) == one), rows) for one in lists]


GX, GY = (0, 1)
GX_AXES = ("x", "core")


def by_pair(lists_ref, axis, of_next, of_prev):
    odd = jnp.broadcast_to(lists_ref[5:6, axis : axis + 1], of_next.shape) == 1
    return jnp.where(odd, of_prev, of_next), jnp.where(odd, of_next, of_prev)


def from_pairs(lists_ref, axis, even_ref, odd_ref):
    return by_pair(lists_ref, axis, even_ref[...].astype(F32), odd_ref[...].astype(F32))


def stack_rows(*parts):
    return jnp.concatenate([p.astype(F32) for p in parts], axis=0).astype(BF)


def sides_of(lists_ref, face):
    return lists_ref[0:2, :face]


def crosses_of(lists_ref, face):
    return lists_ref[2:4, :face]


def slots_of(lists_ref, bricks):
    return lists_ref[4:5, :bricks]


def cross_body(merged_ref, even_ref, odd_ref, lists_ref, a_ref, b_ref):
    face, width = a_ref.shape
    high, low = from_pairs(lists_ref, GY, even_ref, odd_ref)
    rows = jnp.concatenate([merged_ref[...], stack_rows(low[:, :width], high[:, :width])], axis=0)
    lists = crosses_of(lists_ref, face)
    picked = pick_rows(by_pair(lists_ref, GX, lists[0:1], lists[1:2]), rows)
    a_ref[...] = picked[0].astype(BF)
    b_ref[...] = picked[1].astype(BF)


def build_bands(weight_ref, band_ref):
    zero = jnp.zeros((C, C), BF)
    blank = jnp.zeros((C, 2 * C), BF)

    def pair(a, b):
        return jnp.concatenate([a, b], axis=1)

    for e in range(9):
        low, mid, high = (weight_ref[3 * e + z] for z in range(3))
        first, second = (pair(mid, low), pair(high, mid))
        left, right = (pair(low, zero), pair(zero, high))
        rows = (
            (first, blank),
            (second, left),
            (right, first),
            (blank, second),
            (blank, right),
            (left, blank),
        )
        for z, halves in enumerate(rows):
            for s in range(2):
                band_ref[e, z * C : (z + 1) * C, s * 2 * C : (s + 1) * 2 * C] = halves[s]


def options(at):
    return [(at + 1, 0)] + ([(5, 1)] if at == 0 else []) + ([(0, -1)] if at == 3 else [])


def offset_of(dx, dy, dz):
    return (dx + 1) * 9 + (dy + 1) * 3 + dz + 1


def stack_lanes(value, lanes):
    return jnp.concatenate([value[:, p * lanes : (p + 1) * lanes] for p in range(value.shape[1] // lanes)], axis=0)


def stack_parities(value):
    stacked = []
    for v in range(8):
        cx, cy, cz = (v // 4, v // 2 % 2, v % 2)
        lanes = []
        for parity in range(4):
            at = ((2 * cx + parity // 2) * 4 + 2 * cy + parity % 2) * RUN + cz * 2 * C
            lanes.append(value[:, at : at + 2 * C])
        stacked.append(jnp.concatenate(lanes, axis=1))
    return jnp.concatenate(stacked, axis=0)


def stack_runs(ref):
    return jnp.concatenate([ref[:, p * RUN : (p + 1) * RUN] for p in range(16)], axis=0)


def split_two(value):
    head = value.astype(BF)
    return head, (value - head.astype(F32)).astype(BF)


def table_grad_body(
    cot_ref, weight_ref, near_ref, lists_ref, parity_ref,
    ext_ref, even_ref, odd_ref, turned_ref, mains_ref, ends_ref, again_ref, band_ref, pad_ref,
):
    again_ref[...] = lists_ref[...]
    again_ref[5:6] = parity_ref[...]
    bricks = cot_ref.shape[0]
    face = even_ref.shape[0]
    start = ext_ref.shape[0]
    rows = start + 2 * face
    build_bands(weight_ref, band_ref)
    cot = stack_runs(cot_ref)
    turned_ref[...] = cot.T
    pad_ref[...] = jnp.zeros(pad_ref.shape, F32)
    for e in range(9):
        ex, ey = (e // 3, e % 3)
        part = dot_nt(cot, band_ref[e]).reshape(4, 4, bricks, WIDE)
        pad_ref[ex : ex + 4, ey : ey + 4] += part
    near = [near_ref[o] for o in range(27)]

    def chooser(which):
        index = jnp.concatenate([near[o] for o in which], axis=1)
        return ones_where(iota((rows, index.shape[1]), 0) == index)

    lower_half = iota((rows, 2 * C), 1) < C
    cache = {}
    for x in range(4):
        for y in range(4):
            places = [(X, Y, dx, dy) for X, dx in options(x) for Y, dy in options(y)]
            key = tuple((dx, dy) for _, _, dx, dy in places)
            if key not in cache:
                moved = [d for d in key if d != (0, 0)]
                main = chooser([offset_of(*d, 0) for d in moved] * 2) if moved else None
                up = chooser([offset_of(*d, 1) for d in key] * 2)
                down = chooser([offset_of(*d, -1) for d in key] * 2)
                cache[key] = (main, jnp.concatenate([up, down], axis=0))
            main, ends = cache[key]
            own = pad_ref[x + 1, y + 1, :, :RUN]
            own = jnp.concatenate([own, jnp.zeros((rows - bricks, RUN), F32)], axis=0)
            if main is not None:
                parts = [split_two(pad_ref[X, Y, :, :RUN]) for X, Y, dx, dy in places if (dx, dy) != (0, 0)]
                value = jnp.concatenate([p[0] for p in parts] + [p[1] for p in parts], axis=0)
                own += dot(main, value)
            parts = [split_two(pad_ref[X, Y, :, RUN:]) for X, Y, _, _ in places]
            value = jnp.concatenate([p[0] for p in parts] + [p[1] for p in parts], axis=0)
            halo = dot(ends, value)
            first = own[:, : 2 * C] + jnp.where(lower_half, halo[:rows], 0.0)
            second = own[:, 2 * C :] + jnp.where(lower_half, 0.0, halo[rows:])
            total = jnp.concatenate([first, second], axis=1)
            at = (x * 4 + y) * RUN
            ext_ref[:, at : at + RUN] = total[:start]
            even, odd = by_pair(again_ref, GX, total[start + face :], total[start : start + face])
            even_ref[:, at : at + RUN] = even.astype(BF)
            odd_ref[:, at : at + RUN] = odd.astype(BF)
    make_choosers(near_ref, rows, mains_ref, ends_ref)


def make_choosers(near_ref, rows, mains_ref, ends_ref):
    bricks = mains_ref.shape[1]
    near = jnp.concatenate([near_ref[o] for o in range(27)] + [jnp.zeros((5, bricks), I32)], axis=0)
    near = near.astype(F32).T.astype(I32)
    place = iota((bricks, rows), 1)
    pair_place = iota((bricks, 2 * rows), 1)
    for d in range(9):
        down, straight, up = (near[:, 3 * d + z : 3 * d + z + 1] for z in range(3))
        mains_ref[d] = ones_where(place == straight)
        ends_ref[d] = ones_where(pair_place == jnp.where(pair_place < rows, up, down + rows))


def first_body(
    sends_hbm, items_hbm, sides_hbm, crosses_hbm, slots_hbm, out_ref, lists_ref,
    sends_ref, items_ref, sides_ref, crosses_ref, slots_ref, arrived,
):
    sources = (sends_hbm, items_hbm, sides_hbm, crosses_hbm, slots_hbm)
    places = (sends_ref, items_ref, sides_ref, crosses_ref, slots_ref)
    copies = [pltpu.make_async_copy(s, p, arrived.at[i]) for i, (s, p) in enumerate(zip(sources, places))]
    for copy in copies:
        copy.start()
    for copy in copies:
        copy.wait()
    face, bricks = (sides_ref.shape[1], slots_ref.shape[1])
    lists_ref[...] = jnp.zeros(lists_ref.shape, I32)
    lists_ref[0:2, :face] = sides_ref[...]
    lists_ref[2:4, :face] = crosses_ref[...]
    lists_ref[4:5, :bricks] = slots_ref[...]
    items_out(sends_ref, items_ref, out_ref)


def side_grad_body(
    ext_ref, lists_ref, even_grad_ref, odd_grad_ref, even_side_ref, odd_side_ref, parents_ref,
    part_ref, to_even_ref, to_odd_ref, up_sums_ref,
):
    bricks, width = part_ref.shape
    face = to_even_ref.shape[0]
    from_next, from_prev = from_pairs(lists_ref, GX, even_grad_ref, odd_grad_ref)
    total = add_rows(ext_ref[...], crosses_of(lists_ref, face), from_next, from_prev)
    part_ref[...] = total[:bricks]
    to_even, to_odd = by_pair(lists_ref, GY, total[bricks + face :], total[bricks : bricks + face])
    to_even_ref[...] = to_even.astype(BF)
    to_odd_ref[...] = to_odd.astype(BF)
    high, low = by_pair(
        lists_ref, GY, even_side_ref[:, width:].astype(F32), odd_side_ref[:, width:].astype(F32)
    )
    side_parents = stack_lanes(stack_rows(low, high), parents_ref.shape[1])
    grads = [stack_parities(total[:bricks].astype(BF)), stack_parities(total[bricks:].astype(BF))]
    up_sum = dot_tn(jnp.concatenate(grads, axis=0), jnp.concatenate([parents_ref[...], side_parents], axis=0))
    coarse = up_sum.shape[1]
    count = up_sums_ref.shape[0]
    for q in range(up_sum.shape[0] // count):
        up_sums_ref[:, q * coarse : (q + 1) * coarse] = up_sum[q * count : (q + 1) * count]


def weight_grad_body(
    merged_ref, even_side_ref, odd_side_ref, even_cross_ref, odd_cross_ref, turned_ref, mains_ref, ends_ref, lists_ref,
    up_sums_ref, sums_ref, pad_ref, table_ref,
):
    bricks, width = merged_ref.shape
    face = even_side_ref.shape[0]
    rows = bricks + 4 * face
    high, low = by_pair(lists_ref, GY, even_side_ref[:, :width].astype(F32), odd_side_ref[:, :width].astype(F32))
    above, below = from_pairs(lists_ref, GX, even_cross_ref, odd_cross_ref)
    table_ref[:bricks] = merged_ref[...]
    table_ref[bricks:] = stack_rows(low, high, below, above)
    count = sums_ref.shape[0]
    up_lanes = up_sums_ref.shape[1]
    sums_ref[:, :up_lanes] = up_sums_ref[...]
    lower_half = iota((rows, 2 * C), 1) < C
    zero = jnp.zeros((rows, 2 * C), BF)
    for x in range(4):
        for y in range(4):
            places = [(X, Y, dx, dy) for X, dx in options(x) for Y, dy in options(y)]
            at = (x * 4 + y) * RUN
            columns = table_ref[:, at : at + RUN]
            first = jnp.where(lower_half, columns[:, : 2 * C], zero)
            second = jnp.where(lower_half, zero, columns[:, 2 * C :])
            ends = jnp.concatenate([ends_ref[3 * dx + dy + 4] for _, _, dx, dy in places], axis=0)
            halo = dot(ends, jnp.concatenate([first, second], axis=0)).astype(BF)
            for i, (X, Y, _, _) in enumerate(places):
                pad_ref[X, Y, :, RUN:] = halo[i * bricks : (i + 1) * bricks]
            pad_ref[x + 1, y + 1, :, :RUN] = columns[:bricks]
            moved = [p for p in places if p[2:] != (0, 0)]
            if moved:
                main = jnp.concatenate([mains_ref[3 * dx + dy + 4] for _, _, dx, dy in moved], axis=0)
                got = dot(main, columns).astype(BF)
                for i, (X, Y, _, _) in enumerate(moved):
                    pad_ref[X, Y, :, :RUN] = got[i * bricks : (i + 1) * bricks]

    turned = turned_ref[...]
    lanes_low = iota((C, 2 * C), 1) < C
    sums = []
    for e in range(9):
        wide = dot(turned, inputs_at(pad_ref, e))

        def block(z, s):
            return wide[z * C : (z + 1) * C, s * 2 * C : (s + 1) * 2 * C]

        low = jnp.where(lanes_low, block(1, 0) + block(3, 1), block(0, 2) + block(2, 0))
        mid = jnp.where(lanes_low, block(0, 0) + block(2, 1), block(1, 0) + block(3, 1))
        high = jnp.where(lanes_low, block(1, 1) + block(3, 2), block(0, 0) + block(2, 1))
        for value in (low, mid, high):
            sums.append(value + pltpu.roll(value, C, 1))
    sums.append(jnp.zeros((C, 2 * C), F32))
    for pair in range(7):
        both = [jnp.where(lanes_low, sums[14 * h + 2 * pair], sums[14 * h + 2 * pair + 1]) for h in range(2)]
        at = up_lanes + pair * 2 * C
        sums_ref[:, at : at + 2 * C] = jnp.concatenate(both, axis=0)


def pair_sum_body(kept_ref, given_ref, replies_ref, out_ref):
    at = replies_ref.shape[1]
    out_ref[:, :at] = replies_ref[...]
    out_ref[:, at:] = (kept_ref[...] + given_ref[...].astype(F32)).astype(BF)


def inputs_at(pad_ref, e):
    bricks = pad_ref.shape[2]
    ex, ey = (e // 3, e % 3)
    return pad_ref[ex : ex + 4, ey : ey + 4].reshape(16 * bricks, WIDE)


def conv_body(pad_ref, weight_ref, lists_ref, out_ref, again_ref, band_ref):
    again_ref[...] = lists_ref[...]
    bricks = pad_ref.shape[2]
    build_bands(weight_ref, band_ref)
    total = None
    for e in range(9):
        part = dot(inputs_at(pad_ref, e), band_ref[e])
        total = part if total is None else total + part
    for p in range(16):
        out_ref[:, p * RUN : (p + 1) * RUN] = total[p * bricks : (p + 1) * bricks].astype(BF)


def add_rows(base, lists, first, second):
    count, face = (base.shape[0], lists.shape[1])
    index = jnp.concatenate([lists[0:1], lists[1:2]], axis=1)
    chosen = ones_where(iota((count, 2 * face), 0) == index)
    return base + dot(chosen, stack_rows(first, second))


def merge_body(received_ref, up_ref, fine_ref, lists_ref, merged_ref, parents_ref, a_ref, b_ref):
    bricks, width = fine_ref.shape
    face = a_ref.shape[0]
    parents = merge(received_ref, slots_of(lists_ref, bricks), up_ref, fine_ref, merged_ref, parents_ref)
    lists = sides_of(lists_ref, face)
    lists = by_pair(lists_ref, GY, lists[0:1], lists[1:2])
    for out_ref, rows, owners in zip((a_ref, b_ref), pick_rows(lists, merged_ref[...]), pick_rows(lists, parents)):
        out_ref[:, :width] = rows.astype(BF)
        out_ref[:, width:] = owners.astype(BF)


def fine_grad_body(
    part_ref, lists_ref, even_ref, odd_ref, up_ref, sums_ref, grad_ref, replies_ref, kept_ref, given_ref, across
):
    half_count = kept_ref.shape[0]
    kept, given = by_pair(lists_ref, GX, sums_ref[:half_count], sums_ref[half_count:])
    kept_ref[...] = kept
    given_ref[...] = given.astype(BF)
    bricks = part_ref.shape[0]
    face = even_ref.shape[0]
    from_next, from_prev = from_pairs(lists_ref, GY, even_ref, odd_ref)
    total = add_rows(part_ref[...], sides_of(lists_ref, face), from_next, from_prev)
    grad_ref[...] = total.astype(BF)
    items = dot(stack_parities(grad_ref[...]), up_ref[...]).astype(BF)
    items = jnp.concatenate([items[v * bricks : (v + 1) * bricks] for v in range(8)], axis=1)
    half = items.shape[1] // 2
    count, both_lanes = replies_ref.shape
    pieces = both_lanes // 2 // half
    capacity, group = chip_slots(count, pieces, across)
    slots = slots_of(lists_ref, bricks)
    row = iota((count, bricks), 0)
    for other in range(2):
        owner = device_of(row // group, lists_ref, other, across)
        for j in range(pieces):
            piece = row % group * pieces + j
            named = owner * capacity + piece // 2 == slots
            rows = dot(ones_where(named & (piece % 2 == 0)), items[:, :half])
            rows += dot(ones_where(named & (piece % 2 == 1)), items[:, half:])
            at = (other * pieces + j) * half
            replies_ref[:, at : at + half] = rows.astype(BF)


def chip_slots(count, pieces, across):
    group = count // (across[0] * across[1] // 2)
    return group * pieces // 2, group


def device_of(chip, lists_ref, other, across):
    core = jnp.broadcast_to(lists_ref[5:6, GX : GX + 1], chip.shape)
    core = 1 - core if other else core
    return (chip // across[1] * 2 + core) * across[1] + chip % across[1]


def share_body(back_ref, lists_ref, out_ref, given_ref, across):
    count, item_lanes = given_ref.shape
    given_ref[...] = back_ref[:, item_lanes : 2 * item_lanes]
    share = count // (across[0] * across[1] // 2)
    same = iota((count, count), 0) % share == iota((count, count), 1) % share
    out_ref[...] = dot(ones_where(same), back_ref[:, 2 * item_lanes :]).astype(BF)


def coarse_grad(back_ref, given_ref, sends_ref, lists_ref, out_ref, across):
    arrivals = (back_ref[:, : given_ref.shape[1]], given_ref[...])
    capacity, devices = sends_ref.shape
    count, item_width = out_ref.shape
    half = item_width // 2
    lanes = arrivals[0].shape[0]
    pieces = arrivals[0].shape[1] // half
    _, group = chip_slots(lanes, pieces, across)
    sends = sends_ref[...].astype(F32).astype(BF)
    lane = iota((1, lanes), 1)
    totals = [None, None]
    for other in range(2):
        source = device_of(lane // group, lists_ref, other, across)
        rows = dot(sends, ones_where(source == iota((devices, lanes), 0)))
        for j in range(pieces):
            piece = lane % group * pieces + j
            picked = jnp.where(piece // 2 == iota((capacity, lanes), 0), rows, 0.0)
            index = jnp.sum(picked, axis=0, keepdims=True).astype(I32)
            named = iota((count, lanes), 0) == index
            for h in range(2):
                part = dot(ones_where(named & (piece % 2 == h)), arrivals[other][:, j * half : (j + 1) * half])
                totals[h] = part if totals[h] is None else totals[h] + part
    for h in range(2):
        out_ref[:, h * half : (h + 1) * half] = totals[h].astype(BF)


def last_body(
    own_ref, other_ref, back_ref, given_ref, sends_ref, lists_ref, conv_ref, up_ref, out_ref, across, scale
):
    coarse_grad(back_ref, given_ref, sends_ref, lists_ref, out_ref, across)
    half_count = own_ref.shape[0]
    coarse = up_ref.shape[1]
    count = 2 * half_count
    parts = up_ref.shape[0] // count
    first, second = (half * scale for half in from_pairs(lists_ref, GX, own_ref, other_ref))
    at = 0
    for q in range(parts):
        up_ref[q * count : q * count + half_count] = first[:, at : at + coarse]
        up_ref[q * count + half_count : (q + 1) * count] = second[:, at : at + coarse]
        at += coarse
    for pair in range(7):
        turned = jnp.concatenate([first[:, at : at + 2 * C], second[:, at : at + 2 * C]], axis=0).T
        at += 2 * C
        for h in range(2):
            for s in range(2):
                o = 14 * h + 2 * pair + s
                if o < 27:
                    conv_ref[o] = turned[s * C : (s + 1) * C, h * C : (h + 1) * C]


def swap(value, axis, first):
    count = lax.axis_size(axis)
    lower = range(first, count - 1, 2)
    return lax.ppermute(value, axis, [(i, i + 1) for i in lower] + [(i + 1, i) for i in lower])


def swap_pairs(to_even, to_odd, axis):
    return swap(to_even, axis, 0), swap(to_odd, axis, 1)


def trade_rows(values, axes):
    rows, width = values.shape
    devices = math.prod(lax.axis_size(axis) for axis in axes)
    grid_view = values.reshape(devices, rows // devices, width)
    return lax.all_to_all(grid_view, axes, split_axis=0, concat_axis=0, tiled=True).reshape(rows, width)


def on_device(
    fine_features, coarse_items, conv_weight, up_weight, neighbours,
    side_sends, cross_sends, parent_slots, coarse_sends, cotangent,
):
    fine = fine_features[0, 0]
    items = coarse_items[0, 0]
    cot = cotangent[0, 0]
    bricks, width = fine.shape
    face = side_sends.shape[-1]
    across = (lax.axis_size(GX_AXES), lax.axis_size("gy"))
    devices = across[0] * across[1]
    capacity = coarse_sends.shape[-1]
    item_count, item_width = items.shape
    coarse = up_weight.shape[1]
    start = bricks + 2 * face
    sends = coarse_sends.transpose(0, 1, 3, 2)[0, 0]
    slots = parent_slots[0]
    sides = side_sends[0, 0]
    crosses = cross_sends[0, 0]
    near = neighbours.transpose(0, 3, 1, 2)[0]
    up_turned = up_weight.transpose(0, 2, 1).reshape(8 * C, coarse)
    half = item_width // 2
    count = 2 * C
    item_lanes = capacity * devices // 2 * item_width // (count // 2)
    sums_width = 8 * C * coarse // count + 14 * C
    rows = shape((bricks, width))
    face_rows = shape((face, width))
    faces_and_parents = shape((face, width + item_width))
    lists_shape = shape((8, 128), I32)
    band = pltpu.VMEM((9, WIDE, RUN), BF)
    conv_flops = 2 * 9 * 16 * bricks * WIDE * RUN

    listed = (sends, items, sides, crosses, slots)
    outgoing, lists = call(
        first_body, [shape((2 * capacity * devices, half)), lists_shape], *listed,
        scratch=[pltpu.VMEM(a.shape, a.dtype) for a in listed] + [pltpu.SemaphoreType.DMA((len(listed),))],
        in_hbm=True,
    )
    received = trade_rows(outgoing, ("x", "core", "gy"))
    lane = jnp.arange(128, dtype=I32)[None]
    parity = jnp.where(lane == GX, lax.axis_index("core"), lax.axis_index("gy") % 2).astype(I32)
    table_rows = start + 2 * face
    ext_grad, to_even, to_odd, turned, mains, ends, lists = call(
        table_grad_body,
        [
            shape((start, width), F32), face_rows, face_rows, shape((RUN, 16 * bricks)),
            shape((9, bricks, table_rows)), shape((9, bricks, 2 * table_rows)), lists_shape,
        ],
        cot, conv_weight, near, lists, parity,
        scratch=[band, pltpu.VMEM((6, 6, bricks, WIDE), F32)], flops=2 * conv_flops,
    )
    cross_grads = swap_pairs(to_even, to_odd, GX_AXES)
    merged, parents, to_even, to_odd = call(
        merge_body, [rows, shape((8 * bricks, coarse)), faces_and_parents, faces_and_parents],
        received, up_turned, fine, lists,
    )
    sides = swap_pairs(to_even, to_odd, "gy")
    to_even, to_odd = call(cross_body, [face_rows, face_rows], merged, *sides, lists)
    crosses = swap_pairs(to_even, to_odd, GX_AXES)
    half_sums = (count // 2, sums_width)
    fine_part, to_even, to_odd, up_sums = call(
        side_grad_body,
        [shape((bricks, width), F32), face_rows, face_rows, shape((count, sums_width - 14 * C), F32)],
        ext_grad, lists, *cross_grads, *sides, parents,
    )
    side_grads = swap_pairs(to_even, to_odd, "gy")
    sums, pad = call(
        weight_grad_body, [shape((count, sums_width), F32), shape((6, 6, bricks, WIDE))],
        merged, *sides, *crosses, turned, mains, ends, lists, up_sums,
        scratch=[pltpu.VMEM((table_rows, width), BF)], flops=conv_flops,
    )
    grad_fine, replies, kept, given = call(
        functools.partial(fine_grad_body, across=across),
        [rows, shape((count // 2, 2 * item_lanes)), shape(half_sums, F32), shape(half_sums)],
        fine_part, lists, *side_grads, up_turned, sums,
    )
    given = swap(given, "core", 0)
    (sums,) = call(pair_sum_body, [shape((count // 2, 2 * item_lanes + sums_width))], kept, given, replies)
    back = trade_rows(sums, ("x", "gy"))
    output, lists = call(
        conv_body, [rows, lists_shape], pad, conv_weight, lists, scratch=[band], flops=conv_flops
    )
    sums, given = call(
        functools.partial(share_body, across=across), [shape(half_sums), shape((count // 2, item_lanes))], back, lists
    )
    sums = trade_rows(sums, ("x", "gy"))
    other_sums = swap(sums, "core", 0)
    given = swap(given, "core", 0)
    scale = 1.0 / math.sqrt(64 * bricks * devices)
    grad_conv, grad_up, coarse_grad = call(
        functools.partial(last_body, across=across, scale=scale),
        [shape((27, C, C), F32), shape((8 * C, coarse), F32), shape((item_count, item_width))],
        sums, other_sums, back, given, sends, lists,
    )
    return (
        output.reshape(1, 1, bricks, width),
        grad_fine.reshape(1, 1, bricks, width),
        coarse_grad.reshape(1, 1, item_count, item_width),
        grad_conv,
        grad_up.reshape(8, C, coarse).transpose(0, 2, 1),
    )


def solution(mesh):
    groups, across_x, across_y = mesh.devices.shape
    split_mesh = Mesh(mesh.devices.reshape(groups, across_x // 2, 2, across_y), ("groups", "x", "core", "gy"))
    rows = ("groups", "x", "core")
    split = P(rows, "gy", None, None)
    placed = (split, split, P(), P(), split, split, split, P(rows, "gy", None), split, split)
    return jax.shard_map(
        on_device,
        mesh=split_mesh,
        in_specs=placed,
        out_specs=(split, split, split, P("groups", None, None), P("groups", None, None)),
        check_vma=False,
    )
```

```python
import functools
import math

import jax
import jax.numpy as jnp
from jax import lax
from jax.experimental import pallas as pl
from jax.experimental.pallas import tpu as pltpu
from jax.sharding import Mesh
from jax.sharding import PartitionSpec as P

BF = jnp.bfloat16
F32 = jnp.float32
I32 = jnp.int32

C = 64
RUN = 4 * C
WIDE = RUN + 2 * C


def iota(shape, axis):
    return lax.broadcasted_iota(I32, shape, axis)


def ones_where(mask):
    return jnp.where(mask, 1.0, 0.0).astype(BF)


def dot(a, b):
    return jnp.dot(a, b, preferred_element_type=F32)


def dot_tn(a, b):
    return lax.dot_general(a, b, (((0,), (0,)), ((), ())), preferred_element_type=F32)


def dot_nt(a, b):
    return lax.dot_general(a, b, (((1,), (1,)), ((), ())), preferred_element_type=F32)


def column_of(row):
    size = row.shape[1]
    diagonal = iota((size, size), 0) == iota((size, size), 1)
    spread = jnp.broadcast_to(row.astype(F32), (size, size))
    return jnp.sum(jnp.where(diagonal, spread, 0.0), axis=1, keepdims=True).astype(I32)


def call(body, outs, *args, scratch=(), flops=0, in_hbm=False):
    moved = sum(a.size * a.dtype.itemsize for a in list(args) + list(outs))
    return pl.pallas_call(
        body,
        out_shape=tuple(outs),
        in_specs=[pl.BlockSpec(memory_space=pltpu.HBM) if in_hbm else pl.BlockSpec() for _ in args],
        scratch_shapes=tuple(scratch),
        cost_estimate=pl.CostEstimate(flops=flops, bytes_accessed=moved, transcendentals=0),
        compiler_params=pltpu.CompilerParams(vmem_limit_bytes=None if in_hbm else 28 * 2**20),
    )(*args)


def shape(dims, dtype=BF):
    return jax.ShapeDtypeStruct(dims, dtype)


def items_named(sends_ref, count):
    capacity, devices = sends_ref.shape
    group = 2 * capacity
    lanes = devices * group
    spread = ones_where(iota((lanes, devices), 0) // group == iota((lanes, devices), 1))
    slot = iota((lanes, capacity), 0) % group // 2
    values = dot_nt(spread, sends_ref[...].astype(F32).astype(BF))
    item = jnp.sum(jnp.where(slot == iota((lanes, capacity), 1), values, 0.0), axis=1, keepdims=True).astype(I32)
    place = jnp.where(item < count, item + iota((lanes, 1), 0) % 2 * count, -1)
    return ones_where(iota((lanes, 2 * count), 1) == place)


def merge(received_ref, slots, up_ref, fine_ref, merged_ref, parents_ref):
    bricks = fine_ref.shape[0]
    lanes, half = received_ref.shape
    slot = column_of(slots)
    place = iota((bricks, lanes), 1)
    named = place // 2 == slot
    received = received_ref[...]
    parents = jnp.concatenate(
        [dot(ones_where(named & (place % 2 == h)), received) for h in (0, 1)], axis=1
    ).astype(BF)
    coarse = 2 * half // 8
    stacked = jnp.concatenate([parents[:, v * coarse : (v + 1) * coarse] for v in range(8)], axis=0)
    parents_ref[...] = stacked
    lifted = dot_nt(stacked, up_ref[...])
    for v in range(8):
        cx, cy, cz = (v // 4, v // 2 % 2, v % 2)
        for parity in range(4):
            vx, vy = (2 * cx + parity // 2, 2 * cy + parity % 2)
            at = (vx * 4 + vy) * RUN + cz * 2 * C
            add = lifted[v * bricks : (v + 1) * bricks, parity * 2 * C : (parity + 1) * 2 * C]
            merged_ref[:, at : at + 2 * C] = (fine_ref[:, at : at + 2 * C].astype(F32) + add).astype(BF)
    return parents


def pick_rows(lists, rows):
    return [dot_tn(ones_where(iota((rows.shape[0], one.shape[1]), 0) == one), rows) for one in lists]


GX, GY = (0, 1)
GX_AXES = ("x", "core")


def by_pair(lists_ref, axis, of_next, of_prev):
    odd = jnp.broadcast_to(lists_ref[5:6, axis : axis + 1], of_next.shape) == 1
    return jnp.where(odd, of_prev, of_next), jnp.where(odd, of_next, of_prev)


def from_pairs(lists_ref, axis, even_ref, odd_ref):
    return by_pair(lists_ref, axis, even_ref[...].astype(F32), odd_ref[...].astype(F32))


def stack_rows(*parts):
    return jnp.concatenate([p.astype(F32) for p in parts], axis=0).astype(BF)


def sides_of(lists_ref, face):
    return lists_ref[0:2, :face]


def crosses_of(lists_ref, face):
    return lists_ref[2:4, :face]


def slots_of(lists_ref, bricks):
    return lists_ref[4:5, :bricks]


def cross_body(merged_ref, even_ref, odd_ref, lists_ref, a_ref, b_ref):
    face, width = a_ref.shape
    high, low = from_pairs(lists_ref, GY, even_ref, odd_ref)
    rows = jnp.concatenate([merged_ref[...], stack_rows(low[:, :width], high[:, :width])], axis=0)
    lists = crosses_of(lists_ref, face)
    picked = pick_rows(by_pair(lists_ref, GX, lists[0:1], lists[1:2]), rows)
    a_ref[...] = picked[0].astype(BF)
    b_ref[...] = picked[1].astype(BF)


def build_bands(weight_ref, band_ref):
    zero = jnp.zeros((C, C), BF)
    blank = jnp.zeros((C, 2 * C), BF)

    def pair(a, b):
        return jnp.concatenate([a, b], axis=1)

    for e in range(9):
        low, mid, high = (weight_ref[3 * e + z] for z in range(3))
        first, second = (pair(mid, low), pair(high, mid))
        left, right = (pair(low, zero), pair(zero, high))
        rows = (
            (first, blank),
            (second, left),
            (right, first),
            (blank, second),
            (blank, right),
            (left, blank),
        )
        for z, halves in enumerate(rows):
            for s in range(2):
                band_ref[e, z * C : (z + 1) * C, s * 2 * C : (s + 1) * 2 * C] = halves[s]


def options(at):
    return [(at + 1, 0)] + ([(5, 1)] if at == 0 else []) + ([(0, -1)] if at == 3 else [])


def offset_of(dx, dy, dz):
    return (dx + 1) * 9 + (dy + 1) * 3 + dz + 1


def stack_lanes(value, lanes):
    return jnp.concatenate([value[:, p * lanes : (p + 1) * lanes] for p in range(value.shape[1] // lanes)], axis=0)


def stack_parities(value):
    stacked = []
    for v in range(8):
        cx, cy, cz = (v // 4, v // 2 % 2, v % 2)
        lanes = []
        for parity in range(4):
            at = ((2 * cx + parity // 2) * 4 + 2 * cy + parity % 2) * RUN + cz * 2 * C
            lanes.append(value[:, at : at + 2 * C])
        stacked.append(jnp.concatenate(lanes, axis=1))
    return jnp.concatenate(stacked, axis=0)


def stack_runs(ref):
    return jnp.concatenate([ref[:, p * RUN : (p + 1) * RUN] for p in range(16)], axis=0)


def split_two(value):
    head = value.astype(BF)
    return head, (value - head.astype(F32)).astype(BF)


def table_grad_body(
    cot_ref, weight_ref, near_ref, lists_ref, parity_ref,
    ext_ref, even_ref, odd_ref, turned_ref, mains_ref, ends_ref, again_ref, band_ref, pad_ref,
):
    again_ref[...] = lists_ref[...]
    again_ref[5:6] = parity_ref[...]
    bricks = cot_ref.shape[0]
    face = even_ref.shape[0]
    start = ext_ref.shape[0]
    rows = start + 2 * face
    build_bands(weight_ref, band_ref)
    cot = stack_runs(cot_ref)
    turned_ref[...] = cot.T
    pad_ref[...] = jnp.zeros(pad_ref.shape, F32)
    for e in range(9):
        ex, ey = (e // 3, e % 3)
        part = dot_nt(cot, band_ref[e]).reshape(4, 4, bricks, WIDE)
        pad_ref[ex : ex + 4, ey : ey + 4] += part
    near = [near_ref[o] for o in range(27)]

    def chooser(which):
        index = jnp.concatenate([near[o] for o in which], axis=1)
        return ones_where(iota((rows, index.shape[1]), 0) == index)

    lower_half = iota((rows, 2 * C), 1) < C
    cache = {}
    for x in range(4):
        for y in range(4):
            places = [(X, Y, dx, dy) for X, dx in options(x) for Y, dy in options(y)]
            key = tuple((dx, dy) for _, _, dx, dy in places)
            if key not in cache:
                moved = [d for d in key if d != (0, 0)]
                main = chooser([offset_of(*d, 0) for d in moved] * 2) if moved else None
                up = chooser([offset_of(*d, 1) for d in key] * 2)
                down = chooser([offset_of(*d, -1) for d in key] * 2)
                cache[key] = (main, jnp.concatenate([up, down], axis=0))
            main, ends = cache[key]
            own = pad_ref[x + 1, y + 1, :, :RUN]
            own = jnp.concatenate([own, jnp.zeros((rows - bricks, RUN), F32)], axis=0)
            if main is not None:
                parts = [split_two(pad_ref[X, Y, :, :RUN]) for X, Y, dx, dy in places if (dx, dy) != (0, 0)]
                value = jnp.concatenate([p[0] for p in parts] + [p[1] for p in parts], axis=0)
                own += dot(main, value)
            parts = [split_two(pad_ref[X, Y, :, RUN:]) for X, Y, _, _ in places]
            value = jnp.concatenate([p[0] for p in parts] + [p[1] for p in parts], axis=0)
            halo = dot(ends, value)
            first = own[:, : 2 * C] + jnp.where(lower_half, halo[:rows], 0.0)
            second = own[:, 2 * C :] + jnp.where(lower_half, 0.0, halo[rows:])
            total = jnp.concatenate([first, second], axis=1)
            at = (x * 4 + y) * RUN
            ext_ref[:, at : at + RUN] = total[:start]
            even, odd = by_pair(again_ref, GX, total[start + face :], total[start : start + face])
            even_ref[:, at : at + RUN] = even.astype(BF)
            odd_ref[:, at : at + RUN] = odd.astype(BF)
    make_choosers(near_ref, rows, mains_ref, ends_ref)


def make_choosers(near_ref, rows, mains_ref, ends_ref):
    bricks = mains_ref.shape[1]
    near = jnp.concatenate([near_ref[o] for o in range(27)] + [jnp.zeros((5, bricks), I32)], axis=0)
    near = near.astype(F32).T.astype(I32)
    place = iota((bricks, rows), 1)
    pair_place = iota((bricks, 2 * rows), 1)
    for d in range(9):
        down, straight, up = (near[:, 3 * d + z : 3 * d + z + 1] for z in range(3))
        mains_ref[d] = ones_where(place == straight)
        ends_ref[d] = ones_where(pair_place == jnp.where(pair_place < rows, up, down + rows))


def first_body(
    sends_hbm, items_hbm, sides_hbm, crosses_hbm, slots_hbm, out_ref, lists_ref,
    sends_ref, items_ref, sides_ref, crosses_ref, slots_ref, arrived,
):
    sources = (sends_hbm, items_hbm, sides_hbm, crosses_hbm, slots_hbm)
    places = (sends_ref, items_ref, sides_ref, crosses_ref, slots_ref)
    copies = [pltpu.make_async_copy(s, p, arrived.at[i]) for i, (s, p) in enumerate(zip(sources, places))]
    for copy in copies:
        copy.start()
    copies[0].wait()
    chosen = items_named(sends_ref, items_ref.shape[0])
    copies[1].wait()
    half = out_ref.shape[1]
    items = jnp.concatenate([items_ref[:, :half], items_ref[:, half:]], axis=0)
    out_ref[...] = dot(chosen, items).astype(BF)
    for copy in copies[2:]:
        copy.wait()
    face, bricks = (sides_ref.shape[1], slots_ref.shape[1])
    lists_ref[...] = jnp.zeros(lists_ref.shape, I32)
    lists_ref[0:2, :face] = sides_ref[...]
    lists_ref[2:4, :face] = crosses_ref[...]
    lists_ref[4:5, :bricks] = slots_ref[...]


def side_grad_body(
    ext_ref, lists_ref, even_grad_ref, odd_grad_ref, even_side_ref, odd_side_ref, parents_ref,
    part_ref, to_even_ref, to_odd_ref, up_sums_ref,
):
    bricks, width = part_ref.shape
    face = to_even_ref.shape[0]
    from_next, from_prev = from_pairs(lists_ref, GX, even_grad_ref, odd_grad_ref)
    total = add_rows(ext_ref[...], crosses_of(lists_ref, face), from_next, from_prev)
    part_ref[...] = total[:bricks]
    to_even, to_odd = by_pair(lists_ref, GY, total[bricks + face :], total[bricks : bricks + face])
    to_even_ref[...] = to_even.astype(BF)
    to_odd_ref[...] = to_odd.astype(BF)
    high, low = by_pair(
        lists_ref, GY, even_side_ref[:, width:].astype(F32), odd_side_ref[:, width:].astype(F32)
    )
    side_parents = stack_lanes(stack_rows(low, high), parents_ref.shape[1])
    grads = [stack_parities(total[:bricks].astype(BF)), stack_parities(total[bricks:].astype(BF))]
    up_sum = dot_tn(jnp.concatenate(grads, axis=0), jnp.concatenate([parents_ref[...], side_parents], axis=0))
    coarse = up_sum.shape[1]
    count = up_sums_ref.shape[0]
    for q in range(up_sum.shape[0] // count):
        up_sums_ref[:, q * coarse : (q + 1) * coarse] = up_sum[q * count : (q + 1) * count]


def weight_grad_body(
    odd_cross_ref, even_cross_ref, merged_ref, even_side_ref, odd_side_ref, turned_ref, mains_ref, ends_ref, lists_ref,
    up_sums_ref, kept_ref, given_ref, pad_ref, table_ref, sums_ref,
):
    bricks, width = merged_ref.shape
    face = even_side_ref.shape[0]
    rows = bricks + 4 * face
    high, low = by_pair(lists_ref, GY, even_side_ref[:, :width].astype(F32), odd_side_ref[:, :width].astype(F32))
    above, below = from_pairs(lists_ref, GX, even_cross_ref, odd_cross_ref)
    table_ref[:bricks] = merged_ref[...]
    table_ref[bricks:] = stack_rows(low, high, below, above)
    count = sums_ref.shape[0]
    up_lanes = up_sums_ref.shape[1]
    sums_ref[:, :up_lanes] = up_sums_ref[...]
    lower_half = iota((rows, 2 * C), 1) < C
    zero = jnp.zeros((rows, 2 * C), BF)
    for x in range(4):
        for y in range(4):
            places = [(X, Y, dx, dy) for X, dx in options(x) for Y, dy in options(y)]
            at = (x * 4 + y) * RUN
            columns = table_ref[:, at : at + RUN]
            first = jnp.where(lower_half, columns[:, : 2 * C], zero)
            second = jnp.where(lower_half, zero, columns[:, 2 * C :])
            ends = jnp.concatenate([ends_ref[3 * dx + dy + 4] for _, _, dx, dy in places], axis=0)
            halo = dot(ends, jnp.concatenate([first, second], axis=0)).astype(BF)
            for i, (X, Y, _, _) in enumerate(places):
                pad_ref[X, Y, :, RUN:] = halo[i * bricks : (i + 1) * bricks]
            pad_ref[x + 1, y + 1, :, :RUN] = columns[:bricks]
            moved = [p for p in places if p[2:] != (0, 0)]
            if moved:
                main = jnp.concatenate([mains_ref[3 * dx + dy + 4] for _, _, dx, dy in moved], axis=0)
                got = dot(main, columns).astype(BF)
                for i, (X, Y, _, _) in enumerate(moved):
                    pad_ref[X, Y, :, :RUN] = got[i * bricks : (i + 1) * bricks]

    turned = turned_ref[...]
    lanes_low = iota((C, 2 * C), 1) < C
    sums = []
    for e in range(9):
        wide = dot(turned, inputs_at(pad_ref, e))

        def block(z, s):
            return wide[z * C : (z + 1) * C, s * 2 * C : (s + 1) * 2 * C]

        low = jnp.where(lanes_low, block(1, 0) + block(3, 1), block(0, 2) + block(2, 0))
        mid = jnp.where(lanes_low, block(0, 0) + block(2, 1), block(1, 0) + block(3, 1))
        high = jnp.where(lanes_low, block(1, 1) + block(3, 2), block(0, 0) + block(2, 1))
        for value in (low, mid, high):
            sums.append(value + pltpu.roll(value, C, 1))
    sums.append(jnp.zeros((C, 2 * C), F32))
    for pair in range(7):
        both = [jnp.where(lanes_low, sums[14 * h + 2 * pair], sums[14 * h + 2 * pair + 1]) for h in range(2)]
        at = up_lanes + pair * 2 * C
        sums_ref[:, at : at + 2 * C] = jnp.concatenate(both, axis=0)
    kept, given = by_pair(lists_ref, GX, sums_ref[: count // 2], sums_ref[count // 2 :])
    kept_ref[...] = kept
    given_ref[...] = given.astype(BF)


def pair_sum_body(kept_ref, given_ref, out_ref):
    out_ref[...] = (kept_ref[...] + given_ref[...].astype(F32)).astype(BF)


def inputs_at(pad_ref, e):
    bricks = pad_ref.shape[2]
    ex, ey = (e // 3, e % 3)
    return pad_ref[ex : ex + 4, ey : ey + 4].reshape(16 * bricks, WIDE)


def conv_body(pad_ref, weight_ref, lists_ref, out_ref, again_ref, band_ref):
    again_ref[...] = lists_ref[...]
    bricks = pad_ref.shape[2]
    build_bands(weight_ref, band_ref)
    total = None
    for e in range(9):
        part = dot(inputs_at(pad_ref, e), band_ref[e])
        total = part if total is None else total + part
    for p in range(16):
        out_ref[:, p * RUN : (p + 1) * RUN] = total[p * bricks : (p + 1) * bricks].astype(BF)


def add_rows(base, lists, first, second):
    count, face = (base.shape[0], lists.shape[1])
    index = jnp.concatenate([lists[0:1], lists[1:2]], axis=1)
    chosen = ones_where(iota((count, 2 * face), 0) == index)
    return base + dot(chosen, stack_rows(first, second))


def merge_body(received_ref, up_ref, fine_ref, lists_ref, merged_ref, parents_ref, a_ref, b_ref):
    bricks, width = fine_ref.shape
    face = a_ref.shape[0]
    parents = merge(received_ref, slots_of(lists_ref, bricks), up_ref, fine_ref, merged_ref, parents_ref)
    lists = sides_of(lists_ref, face)
    lists = by_pair(lists_ref, GY, lists[0:1], lists[1:2])
    for out_ref, rows, owners in zip((a_ref, b_ref), pick_rows(lists, merged_ref[...]), pick_rows(lists, parents)):
        out_ref[:, :width] = rows.astype(BF)
        out_ref[:, width:] = owners.astype(BF)


def fine_grad_body(part_ref, lists_ref, even_ref, odd_ref, up_ref, grad_ref, replies_ref, across):
    bricks = part_ref.shape[0]
    face = even_ref.shape[0]
    from_next, from_prev = from_pairs(lists_ref, GY, even_ref, odd_ref)
    total = add_rows(part_ref[...], sides_of(lists_ref, face), from_next, from_prev)
    grad_ref[...] = total.astype(BF)
    items = dot(stack_parities(grad_ref[...]), up_ref[...]).astype(BF)
    items = jnp.concatenate([items[v * bricks : (v + 1) * bricks] for v in range(8)], axis=1)
    half = items.shape[1] // 2
    count, both_lanes = replies_ref.shape
    pieces = both_lanes // 2 // half
    capacity, group = chip_slots(count, pieces, across)
    slots = slots_of(lists_ref, bricks)
    row = iota((count, bricks), 0)
    for other in range(2):
        owner = device_of(row // group, lists_ref, other, across)
        for j in range(pieces):
            piece = row % group * pieces + j
            named = owner * capacity + piece // 2 == slots
            rows = dot(ones_where(named & (piece % 2 == 0)), items[:, :half])
            rows += dot(ones_where(named & (piece % 2 == 1)), items[:, half:])
            at = (other * pieces + j) * half
            replies_ref[:, at : at + half] = rows.astype(BF)


def chip_slots(count, pieces, across):
    group = count // (across[0] * across[1] // 2)
    return group * pieces // 2, group


def device_of(chip, lists_ref, other, across):
    core = jnp.broadcast_to(lists_ref[5:6, GX : GX + 1], chip.shape)
    core = 1 - core if other else core
    return (chip // across[1] * 2 + core) * across[1] + chip % across[1]


def share_body(sums_ref, replies_ref, out_ref, across):
    count, item_lanes = replies_ref.shape
    share = count // (across[0] * across[1] // 2)
    same = iota((count, count), 0) % share == iota((count, count), 1) % share
    out_ref[:, :item_lanes] = replies_ref[...]
    out_ref[:, item_lanes:] = dot(ones_where(same), sums_ref[...]).astype(BF)


def coarse_grad(arrivals, sends_ref, lists_ref, out_ref, across):
    capacity, devices = sends_ref.shape
    count, item_width = out_ref.shape
    half = item_width // 2
    lanes = arrivals[0].shape[0]
    pieces = arrivals[0].shape[1] // half
    _, group = chip_slots(lanes, pieces, across)
    sends = sends_ref[...].astype(F32).astype(BF)
    lane = iota((1, lanes), 1)
    totals = [None, None]
    for other in range(2):
        source = device_of(lane // group, lists_ref, other, across)
        rows = dot(sends, ones_where(source == iota((devices, lanes), 0)))
        for j in range(pieces):
            piece = lane % group * pieces + j
            picked = jnp.where(piece // 2 == iota((capacity, lanes), 0), rows, 0.0)
            index = jnp.sum(picked, axis=0, keepdims=True).astype(I32)
            named = iota((count, lanes), 0) == index
            for h in range(2):
                part = dot(ones_where(named & (piece % 2 == h)), arrivals[other][:, j * half : (j + 1) * half])
                totals[h] = part if totals[h] is None else totals[h] + part
    for h in range(2):
        out_ref[:, h * half : (h + 1) * half] = totals[h].astype(BF)


def last_body(back_ref, given_ref, sends_ref, lists_ref, conv_ref, up_ref, out_ref, item_lanes, across, scale):
    half_count = back_ref.shape[0]
    items = (back_ref[:, :item_lanes], given_ref[:, item_lanes : 2 * item_lanes])
    coarse_grad(items, sends_ref, lists_ref, out_ref, across)
    coarse = up_ref.shape[1]
    count = 2 * half_count
    parts = up_ref.shape[0] // count
    own = back_ref[:, 2 * item_lanes :].astype(F32) * scale
    others = given_ref[:, 2 * item_lanes :].astype(F32) * scale
    first, second = by_pair(lists_ref, GX, own, others)
    at = 0
    for q in range(parts):
        up_ref[q * count : q * count + half_count] = first[:, at : at + coarse]
        up_ref[q * count + half_count : (q + 1) * count] = second[:, at : at + coarse]
        at += coarse
    for pair in range(7):
        turned = jnp.concatenate([first[:, at : at + 2 * C], second[:, at : at + 2 * C]], axis=0).T
        at += 2 * C
        for h in range(2):
            for s in range(2):
                o = 14 * h + 2 * pair + s
                if o < 27:
                    conv_ref[o] = turned[s * C : (s + 1) * C, h * C : (h + 1) * C]


def swap(value, axis, first):
    count = lax.axis_size(axis)
    lower = range(first, count - 1, 2)
    return lax.ppermute(value, axis, [(i, i + 1) for i in lower] + [(i + 1, i) for i in lower])


def swap_pairs(to_even, to_odd, axis):
    return swap(to_even, axis, 0), swap(to_odd, axis, 1)


def trade_rows(values, axes):
    rows, width = values.shape
    devices = math.prod(lax.axis_size(axis) for axis in axes)
    grid_view = values.reshape(devices, rows // devices, width)
    return lax.all_to_all(grid_view, axes, split_axis=0, concat_axis=0, tiled=True).reshape(rows, width)


def on_device(
    fine_features, coarse_items, conv_weight, up_weight, neighbours,
    side_sends, cross_sends, parent_slots, coarse_sends, cotangent,
):
    fine = fine_features[0, 0]
    items = coarse_items[0, 0]
    cot = cotangent[0, 0]
    bricks, width = fine.shape
    face = side_sends.shape[-1]
    across = (lax.axis_size(GX_AXES), lax.axis_size("gy"))
    devices = across[0] * across[1]
    capacity = coarse_sends.shape[-1]
    item_count, item_width = items.shape
    coarse = up_weight.shape[1]
    start = bricks + 2 * face
    sends = coarse_sends.transpose(0, 1, 3, 2)[0, 0]
    slots = parent_slots[0]
    sides = side_sends[0, 0]
    crosses = cross_sends[0, 0]
    near = neighbours.transpose(0, 3, 1, 2)[0]
    up_turned = up_weight.transpose(0, 2, 1).reshape(8 * C, coarse)
    half = item_width // 2
    count = 2 * C
    item_lanes = capacity * devices // 2 * item_width // (count // 2)
    sums_width = 8 * C * coarse // count + 14 * C
    rows = shape((bricks, width))
    face_rows = shape((face, width))
    faces_and_parents = shape((face, width + item_width))
    lists_shape = shape((8, 128), I32)
    band = pltpu.VMEM((9, WIDE, RUN), BF)
    conv_flops = 2 * 9 * 16 * bricks * WIDE * RUN

    listed = (sends, items, sides, crosses, slots)
    outgoing, lists = call(
        first_body, [shape((2 * capacity * devices, half)), lists_shape], *listed,
        scratch=[pltpu.VMEM(a.shape, a.dtype) for a in listed] + [pltpu.SemaphoreType.DMA((len(listed),))],
        in_hbm=True,
    )
    received = trade_rows(outgoing, ("x", "core", "gy"))
    lane = jnp.arange(128, dtype=I32)[None]
    parity = jnp.where(lane == GX, lax.axis_index("core"), lax.axis_index("gy") % 2).astype(I32)
    table_rows = start + 2 * face
    ext_grad, to_even, to_odd, turned, mains, ends, lists = call(
        table_grad_body,
        [
            shape((start, width), F32), face_rows, face_rows, shape((RUN, 16 * bricks)),
            shape((9, bricks, table_rows)), shape((9, bricks, 2 * table_rows)), lists_shape,
        ],
        cot, conv_weight, near, lists, parity,
        scratch=[band, pltpu.VMEM((6, 6, bricks, WIDE), F32)], flops=2 * conv_flops,
    )
    cross_grads = swap_pairs(to_even, to_odd, GX_AXES)
    merged, parents, to_even, to_odd = call(
        merge_body, [rows, shape((8 * bricks, coarse)), faces_and_parents, faces_and_parents],
        received, up_turned, fine, lists,
    )
    sides = swap_pairs(to_even, to_odd, "gy")
    to_even, to_odd = call(cross_body, [face_rows, face_rows], merged, *sides, lists)
    crosses = swap_pairs(to_even, to_odd, GX_AXES)
    half_sums = (count // 2, sums_width)
    fine_part, to_even, to_odd, up_sums = call(
        side_grad_body,
        [shape((bricks, width), F32), face_rows, face_rows, shape((count, sums_width - 14 * C), F32)],
        ext_grad, lists, *cross_grads, *sides, parents,
    )
    side_grads = swap_pairs(to_even, to_odd, "gy")
    kept, given, pad = call(
        weight_grad_body, [shape(half_sums, F32), shape(half_sums), shape((6, 6, bricks, WIDE))],
        *crosses[::-1], merged, *sides, turned, mains, ends, lists, up_sums,
        scratch=[pltpu.VMEM((table_rows, width), BF), pltpu.VMEM((count, sums_width), F32)], flops=conv_flops,
    )
    given = swap(given, "core", 0)
    (sums,) = call(pair_sum_body, [shape(half_sums)], kept, given)
    sums = trade_rows(sums, ("x", "gy"))
    output, lists = call(
        conv_body, [rows, lists_shape], pad, conv_weight, lists, scratch=[band], flops=conv_flops
    )
    grad_fine, replies = call(
        functools.partial(fine_grad_body, across=across), [rows, shape((count // 2, 2 * item_lanes))],
        fine_part, lists, *side_grads, up_turned,
    )
    (back,) = call(
        functools.partial(share_body, across=across), [shape((count // 2, 2 * item_lanes + sums_width))], sums, replies
    )
    back = trade_rows(back, ("x", "gy"))
    given = swap(back, "core", 0)
    scale = 1.0 / math.sqrt(64 * bricks * devices)
    grad_conv, grad_up, coarse_grad = call(
        functools.partial(last_body, item_lanes=item_lanes, across=across, scale=scale),
        [shape((27, C, C), F32), shape((8 * C, coarse), F32), shape((item_count, item_width))],
        back, given, sends, lists,
    )
    return (
        output.reshape(1, 1, bricks, width),
        grad_fine.reshape(1, 1, bricks, width),
        coarse_grad.reshape(1, 1, item_count, item_width),
        grad_conv,
        grad_up.reshape(8, C, coarse).transpose(0, 2, 1),
    )


def solution(mesh):
    groups, across_x, across_y = mesh.devices.shape
    split_mesh = Mesh(mesh.devices.reshape(groups, across_x // 2, 2, across_y), ("groups", "x", "core", "gy"))
    rows = ("groups", "x", "core")
    split = P(rows, "gy", None, None)
    placed = (split, split, P(), P(), split, split, split, P(rows, "gy", None), split, split)
    return jax.shard_map(
        on_device,
        mesh=split_mesh,
        in_specs=placed,
        out_specs=(split, split, split, P("groups", None, None), P("groups", None, None)),
        check_vma=False,
    )
```

```python
import functools
import math

import jax
import jax.numpy as jnp
from jax import lax
from jax.experimental import pallas as pl
from jax.experimental.pallas import tpu as pltpu
from jax.sharding import Mesh
from jax.sharding import PartitionSpec as P

BF = jnp.bfloat16
F32 = jnp.float32
I32 = jnp.int32

C = 64
RUN = 4 * C
WIDE = RUN + 2 * C


def iota(shape, axis):
    return lax.broadcasted_iota(I32, shape, axis)


def ones_where(mask):
    return jnp.where(mask, 1.0, 0.0).astype(BF)


def dot(a, b):
    return jnp.dot(a, b, preferred_element_type=F32)


def dot_tn(a, b):
    return lax.dot_general(a, b, (((0,), (0,)), ((), ())), preferred_element_type=F32)


def dot_nt(a, b):
    return lax.dot_general(a, b, (((1,), (1,)), ((), ())), preferred_element_type=F32)


def column_of(row):
    size = row.shape[1]
    diagonal = iota((size, size), 0) == iota((size, size), 1)
    spread = jnp.broadcast_to(row.astype(F32), (size, size))
    return jnp.sum(jnp.where(diagonal, spread, 0.0), axis=1, keepdims=True).astype(I32)


def call(body, outs, *args, scratch=(), flops=0, in_hbm=False):
    moved = sum(a.size * a.dtype.itemsize for a in list(args) + list(outs))
    return pl.pallas_call(
        body,
        out_shape=tuple(outs),
        in_specs=[pl.BlockSpec(memory_space=pltpu.HBM) if in_hbm else pl.BlockSpec() for _ in args],
        scratch_shapes=tuple(scratch),
        cost_estimate=pl.CostEstimate(flops=flops, bytes_accessed=moved, transcendentals=0),
        compiler_params=pltpu.CompilerParams(vmem_limit_bytes=None if in_hbm else 28 * 2**20),
    )(*args)


def shape(dims, dtype=BF):
    return jax.ShapeDtypeStruct(dims, dtype)


def items_named(sends_ref, count):
    capacity, devices = sends_ref.shape
    group = 2 * capacity
    lanes = devices * group
    spread = ones_where(iota((lanes, devices), 0) // group == iota((lanes, devices), 1))
    slot = iota((lanes, capacity), 0) % group // 2
    values = dot_nt(spread, sends_ref[...].astype(F32).astype(BF))
    item = jnp.sum(jnp.where(slot == iota((lanes, capacity), 1), values, 0.0), axis=1, keepdims=True).astype(I32)
    place = jnp.where(item < count, item + iota((lanes, 1), 0) % 2 * count, -1)
    return ones_where(iota((lanes, 2 * count), 1) == place)


def merge(received_ref, slots, up_ref, fine_ref, merged_ref, parents_ref):
    bricks = fine_ref.shape[0]
    lanes, half = received_ref.shape
    slot = column_of(slots)
    place = iota((bricks, lanes), 1)
    named = place // 2 == slot
    received = received_ref[...]
    parents = jnp.concatenate(
        [dot(ones_where(named & (place % 2 == h)), received) for h in (0, 1)], axis=1
    ).astype(BF)
    coarse = 2 * half // 8
    stacked = jnp.concatenate([parents[:, v * coarse : (v + 1) * coarse] for v in range(8)], axis=0)
    parents_ref[...] = stacked
    lifted = dot_nt(stacked, up_ref[...])
    for v in range(8):
        cx, cy, cz = (v // 4, v // 2 % 2, v % 2)
        for parity in range(4):
            vx, vy = (2 * cx + parity // 2, 2 * cy + parity % 2)
            at = (vx * 4 + vy) * RUN + cz * 2 * C
            add = lifted[v * bricks : (v + 1) * bricks, parity * 2 * C : (parity + 1) * 2 * C]
            merged_ref[:, at : at + 2 * C] = (fine_ref[:, at : at + 2 * C].astype(F32) + add).astype(BF)
    return parents


def pick_rows(lists, rows):
    return [dot_tn(ones_where(iota((rows.shape[0], one.shape[1]), 0) == one), rows) for one in lists]


GX, GY = (0, 1)
GX_AXES = ("x", "core")


def by_pair(lists_ref, axis, of_next, of_prev):
    odd = jnp.broadcast_to(lists_ref[5:6, axis : axis + 1], of_next.shape) == 1
    return jnp.where(odd, of_prev, of_next), jnp.where(odd, of_next, of_prev)


def from_pairs(lists_ref, axis, even_ref, odd_ref):
    return by_pair(lists_ref, axis, even_ref[...].astype(F32), odd_ref[...].astype(F32))


def stack_rows(*parts):
    return jnp.concatenate([p.astype(F32) for p in parts], axis=0).astype(BF)


def sides_of(lists_ref, face):
    return lists_ref[0:2, :face]


def crosses_of(lists_ref, face):
    return lists_ref[2:4, :face]


def slots_of(lists_ref, bricks):
    return lists_ref[4:5, :bricks]


def cross_body(odd_ref, even_ref, merged_ref, lists_ref, a_ref, b_ref):
    face, width = a_ref.shape
    high, low = from_pairs(lists_ref, GY, even_ref, odd_ref)
    rows = jnp.concatenate([merged_ref[...], stack_rows(low[:, :width], high[:, :width])], axis=0)
    lists = crosses_of(lists_ref, face)
    picked = pick_rows(by_pair(lists_ref, GX, lists[0:1], lists[1:2]), rows)
    a_ref[...] = picked[0].astype(BF)
    b_ref[...] = picked[1].astype(BF)


def build_bands(weight_ref, band_ref):
    zero = jnp.zeros((C, C), BF)
    blank = jnp.zeros((C, 2 * C), BF)

    def pair(a, b):
        return jnp.concatenate([a, b], axis=1)

    for e in range(9):
        low, mid, high = (weight_ref[3 * e + z] for z in range(3))
        first, second = (pair(mid, low), pair(high, mid))
        left, right = (pair(low, zero), pair(zero, high))
        rows = (
            (first, blank),
            (second, left),
            (right, first),
            (blank, second),
            (blank, right),
            (left, blank),
        )
        for z, halves in enumerate(rows):
            for s in range(2):
                band_ref[e, z * C : (z + 1) * C, s * 2 * C : (s + 1) * 2 * C] = halves[s]


def options(at):
    return [(at + 1, 0)] + ([(5, 1)] if at == 0 else []) + ([(0, -1)] if at == 3 else [])


def offset_of(dx, dy, dz):
    return (dx + 1) * 9 + (dy + 1) * 3 + dz + 1


def stack_lanes(value, lanes):
    return jnp.concatenate([value[:, p * lanes : (p + 1) * lanes] for p in range(value.shape[1] // lanes)], axis=0)


def stack_parities(value):
    stacked = []
    for v in range(8):
        cx, cy, cz = (v // 4, v // 2 % 2, v % 2)
        lanes = []
        for parity in range(4):
            at = ((2 * cx + parity // 2) * 4 + 2 * cy + parity % 2) * RUN + cz * 2 * C
            lanes.append(value[:, at : at + 2 * C])
        stacked.append(jnp.concatenate(lanes, axis=1))
    return jnp.concatenate(stacked, axis=0)


def stack_runs(ref):
    return jnp.concatenate([ref[:, p * RUN : (p + 1) * RUN] for p in range(16)], axis=0)


def split_two(value):
    head = value.astype(BF)
    return head, (value - head.astype(F32)).astype(BF)


def table_grad_body(
    cot_ref, weight_ref, near_ref, lists_ref, parity_ref,
    ext_ref, even_ref, odd_ref, turned_ref, mains_ref, ends_ref, again_ref, band_ref, pad_ref,
):
    again_ref[...] = lists_ref[...]
    again_ref[5:6] = parity_ref[...]
    bricks = cot_ref.shape[0]
    face = even_ref.shape[0]
    start = ext_ref.shape[0]
    rows = start + 2 * face
    build_bands(weight_ref, band_ref)
    cot = stack_runs(cot_ref)
    turned_ref[...] = cot.T
    pad_ref[...] = jnp.zeros(pad_ref.shape, F32)
    for e in range(9):
        ex, ey = (e // 3, e % 3)
        part = dot_nt(cot, band_ref[e]).reshape(4, 4, bricks, WIDE)
        pad_ref[ex : ex + 4, ey : ey + 4] += part
    near = [near_ref[o] for o in range(27)]

    def chooser(which):
        index = jnp.concatenate([near[o] for o in which], axis=1)
        return ones_where(iota((rows, index.shape[1]), 0) == index)

    lower_half = iota((rows, 2 * C), 1) < C
    cache = {}
    for x in range(4):
        for y in range(4):
            places = [(X, Y, dx, dy) for X, dx in options(x) for Y, dy in options(y)]
            key = tuple((dx, dy) for _, _, dx, dy in places)
            if key not in cache:
                moved = [d for d in key if d != (0, 0)]
                main = chooser([offset_of(*d, 0) for d in moved] * 2) if moved else None
                up = chooser([offset_of(*d, 1) for d in key] * 2)
                down = chooser([offset_of(*d, -1) for d in key] * 2)
                cache[key] = (main, jnp.concatenate([up, down], axis=0))
            main, ends = cache[key]
            own = pad_ref[x + 1, y + 1, :, :RUN]
            own = jnp.concatenate([own, jnp.zeros((rows - bricks, RUN), F32)], axis=0)
            if main is not None:
                parts = [split_two(pad_ref[X, Y, :, :RUN]) for X, Y, dx, dy in places if (dx, dy) != (0, 0)]
                value = jnp.concatenate([p[0] for p in parts] + [p[1] for p in parts], axis=0)
                own += dot(main, value)
            parts = [split_two(pad_ref[X, Y, :, RUN:]) for X, Y, _, _ in places]
            value = jnp.concatenate([p[0] for p in parts] + [p[1] for p in parts], axis=0)
            halo = dot(ends, value)
            first = own[:, : 2 * C] + jnp.where(lower_half, halo[:rows], 0.0)
            second = own[:, 2 * C :] + jnp.where(lower_half, 0.0, halo[rows:])
            total = jnp.concatenate([first, second], axis=1)
            at = (x * 4 + y) * RUN
            ext_ref[:, at : at + RUN] = total[:start]
            even, odd = by_pair(again_ref, GX, total[start + face :], total[start : start + face])
            even_ref[:, at : at + RUN] = even.astype(BF)
            odd_ref[:, at : at + RUN] = odd.astype(BF)
    make_choosers(near_ref, rows, mains_ref, ends_ref)


def make_choosers(near_ref, rows, mains_ref, ends_ref):
    bricks = mains_ref.shape[1]
    near = jnp.concatenate([near_ref[o] for o in range(27)] + [jnp.zeros((5, bricks), I32)], axis=0)
    near = near.astype(F32).T.astype(I32)
    place = iota((bricks, rows), 1)
    pair_place = iota((bricks, 2 * rows), 1)
    for d in range(9):
        down, straight, up = (near[:, 3 * d + z : 3 * d + z + 1] for z in range(3))
        mains_ref[d] = ones_where(place == straight)
        ends_ref[d] = ones_where(pair_place == jnp.where(pair_place < rows, up, down + rows))


def first_body(
    sends_hbm, items_hbm, sides_hbm, crosses_hbm, slots_hbm, out_ref, lists_ref,
    sends_ref, items_ref, sides_ref, crosses_ref, slots_ref, arrived,
):
    sources = (sends_hbm, items_hbm, sides_hbm, crosses_hbm, slots_hbm)
    places = (sends_ref, items_ref, sides_ref, crosses_ref, slots_ref)
    copies = [pltpu.make_async_copy(s, p, arrived.at[i]) for i, (s, p) in enumerate(zip(sources, places))]
    for copy in copies:
        copy.start()
    copies[0].wait()
    chosen = items_named(sends_ref, items_ref.shape[0])
    copies[1].wait()
    half = out_ref.shape[1]
    items = jnp.concatenate([items_ref[:, :half], items_ref[:, half:]], axis=0)
    out_ref[...] = dot(chosen, items).astype(BF)
    for copy in copies[2:]:
        copy.wait()
    face, bricks = (sides_ref.shape[1], slots_ref.shape[1])
    lists_ref[...] = jnp.zeros(lists_ref.shape, I32)
    lists_ref[0:2, :face] = sides_ref[...]
    lists_ref[2:4, :face] = crosses_ref[...]
    lists_ref[4:5, :bricks] = slots_ref[...]


def side_grad_body(
    ext_ref, lists_ref, even_grad_ref, odd_grad_ref, even_side_ref, odd_side_ref, parents_ref,
    part_ref, to_even_ref, to_odd_ref, up_sums_ref,
):
    bricks, width = part_ref.shape
    face = to_even_ref.shape[0]
    from_next, from_prev = from_pairs(lists_ref, GX, even_grad_ref, odd_grad_ref)
    total = add_rows(ext_ref[...], crosses_of(lists_ref, face), from_next, from_prev)
    part_ref[...] = total[:bricks]
    to_even, to_odd = by_pair(lists_ref, GY, total[bricks + face :], total[bricks : bricks + face])
    to_even_ref[...] = to_even.astype(BF)
    to_odd_ref[...] = to_odd.astype(BF)
    high, low = by_pair(
        lists_ref, GY, even_side_ref[:, width:].astype(F32), odd_side_ref[:, width:].astype(F32)
    )
    side_parents = stack_lanes(stack_rows(low, high), parents_ref.shape[1])
    grads = [stack_parities(total[:bricks].astype(BF)), stack_parities(total[bricks:].astype(BF))]
    up_sum = dot_tn(jnp.concatenate(grads, axis=0), jnp.concatenate([parents_ref[...], side_parents], axis=0))
    coarse = up_sum.shape[1]
    count = up_sums_ref.shape[0]
    for q in range(up_sum.shape[0] // count):
        up_sums_ref[:, q * coarse : (q + 1) * coarse] = up_sum[q * count : (q + 1) * count]


def weight_grad_body(
    odd_cross_ref, even_cross_ref, merged_ref, even_side_ref, odd_side_ref, turned_ref, mains_ref, ends_ref, lists_ref,
    up_sums_ref, kept_ref, given_ref, pad_ref, table_ref, sums_ref,
):
    bricks, width = merged_ref.shape
    face = even_side_ref.shape[0]
    rows = bricks + 4 * face
    high, low = by_pair(lists_ref, GY, even_side_ref[:, :width].astype(F32), odd_side_ref[:, :width].astype(F32))
    above, below = from_pairs(lists_ref, GX, even_cross_ref, odd_cross_ref)
    table_ref[:bricks] = merged_ref[...]
    table_ref[bricks:] = stack_rows(low, high, below, above)
    count = sums_ref.shape[0]
    up_lanes = up_sums_ref.shape[1]
    sums_ref[:, :up_lanes] = up_sums_ref[...]
    lower_half = iota((rows, 2 * C), 1) < C
    zero = jnp.zeros((rows, 2 * C), BF)
    for x in range(4):
        for y in range(4):
            places = [(X, Y, dx, dy) for X, dx in options(x) for Y, dy in options(y)]
            at = (x * 4 + y) * RUN
            columns = table_ref[:, at : at + RUN]
            first = jnp.where(lower_half, columns[:, : 2 * C], zero)
            second = jnp.where(lower_half, zero, columns[:, 2 * C :])
            ends = jnp.concatenate([ends_ref[3 * dx + dy + 4] for _, _, dx, dy in places], axis=0)
            halo = dot(ends, jnp.concatenate([first, second], axis=0)).astype(BF)
            for i, (X, Y, _, _) in enumerate(places):
                pad_ref[X, Y, :, RUN:] = halo[i * bricks : (i + 1) * bricks]
            pad_ref[x + 1, y + 1, :, :RUN] = columns[:bricks]
            moved = [p for p in places if p[2:] != (0, 0)]
            if moved:
                main = jnp.concatenate([mains_ref[3 * dx + dy + 4] for _, _, dx, dy in moved], axis=0)
                got = dot(main, columns).astype(BF)
                for i, (X, Y, _, _) in enumerate(moved):
                    pad_ref[X, Y, :, :RUN] = got[i * bricks : (i + 1) * bricks]

    turned = turned_ref[...]
    lanes_low = iota((C, 2 * C), 1) < C
    sums = []
    for e in range(9):
        wide = dot(turned, inputs_at(pad_ref, e))

        def block(z, s):
            return wide[z * C : (z + 1) * C, s * 2 * C : (s + 1) * 2 * C]

        low = jnp.where(lanes_low, block(1, 0) + block(3, 1), block(0, 2) + block(2, 0))
        mid = jnp.where(lanes_low, block(0, 0) + block(2, 1), block(1, 0) + block(3, 1))
        high = jnp.where(lanes_low, block(1, 1) + block(3, 2), block(0, 0) + block(2, 1))
        for value in (low, mid, high):
            sums.append(value + pltpu.roll(value, C, 1))
    sums.append(jnp.zeros((C, 2 * C), F32))
    for pair in range(7):
        both = [jnp.where(lanes_low, sums[14 * h + 2 * pair], sums[14 * h + 2 * pair + 1]) for h in range(2)]
        at = up_lanes + pair * 2 * C
        sums_ref[:, at : at + 2 * C] = jnp.concatenate(both, axis=0)
    kept, given = by_pair(lists_ref, GX, sums_ref[: count // 2], sums_ref[count // 2 :])
    kept_ref[...] = kept
    given_ref[...] = given.astype(BF)


def pair_sum_body(kept_ref, given_ref, out_ref):
    out_ref[...] = (kept_ref[...] + given_ref[...].astype(F32)).astype(BF)


def inputs_at(pad_ref, e):
    bricks = pad_ref.shape[2]
    ex, ey = (e // 3, e % 3)
    return pad_ref[ex : ex + 4, ey : ey + 4].reshape(16 * bricks, WIDE)


def conv_body(pad_ref, weight_ref, lists_ref, out_ref, again_ref, band_ref):
    again_ref[...] = lists_ref[...]
    bricks = pad_ref.shape[2]
    build_bands(weight_ref, band_ref)
    total = None
    for e in range(9):
        part = dot(inputs_at(pad_ref, e), band_ref[e])
        total = part if total is None else total + part
    for p in range(16):
        out_ref[:, p * RUN : (p + 1) * RUN] = total[p * bricks : (p + 1) * bricks].astype(BF)


def add_rows(base, lists, first, second):
    count, face = (base.shape[0], lists.shape[1])
    index = jnp.concatenate([lists[0:1], lists[1:2]], axis=1)
    chosen = ones_where(iota((count, 2 * face), 0) == index)
    return base + dot(chosen, stack_rows(first, second))


def merge_body(received_ref, up_ref, fine_ref, lists_ref, merged_ref, parents_ref, a_ref, b_ref):
    bricks, width = fine_ref.shape
    face = a_ref.shape[0]
    parents = merge(received_ref, slots_of(lists_ref, bricks), up_ref, fine_ref, merged_ref, parents_ref)
    lists = sides_of(lists_ref, face)
    lists = by_pair(lists_ref, GY, lists[0:1], lists[1:2])
    for out_ref, rows, owners in zip((a_ref, b_ref), pick_rows(lists, merged_ref[...]), pick_rows(lists, parents)):
        out_ref[:, :width] = rows.astype(BF)
        out_ref[:, width:] = owners.astype(BF)


def fine_grad_body(odd_ref, even_ref, part_ref, lists_ref, up_ref, grad_ref, replies_ref, across):
    bricks = part_ref.shape[0]
    face = even_ref.shape[0]
    from_next, from_prev = from_pairs(lists_ref, GY, even_ref, odd_ref)
    total = add_rows(part_ref[...], sides_of(lists_ref, face), from_next, from_prev)
    grad_ref[...] = total.astype(BF)
    items = dot(stack_parities(grad_ref[...]), up_ref[...]).astype(BF)
    items = jnp.concatenate([items[v * bricks : (v + 1) * bricks] for v in range(8)], axis=1)
    half = items.shape[1] // 2
    count, both_lanes = replies_ref.shape
    pieces = both_lanes // 2 // half
    capacity, group = chip_slots(count, pieces, across)
    slots = slots_of(lists_ref, bricks)
    row = iota((count, bricks), 0)
    for other in range(2):
        owner = device_of(row // group, lists_ref, other, across)
        for j in range(pieces):
            piece = row % group * pieces + j
            named = owner * capacity + piece // 2 == slots
            rows = dot(ones_where(named & (piece % 2 == 0)), items[:, :half])
            rows += dot(ones_where(named & (piece % 2 == 1)), items[:, half:])
            at = (other * pieces + j) * half
            replies_ref[:, at : at + half] = rows.astype(BF)


def chip_slots(count, pieces, across):
    group = count // (across[0] * across[1] // 2)
    return group * pieces // 2, group


def device_of(chip, lists_ref, other, across):
    core = jnp.broadcast_to(lists_ref[5:6, GX : GX + 1], chip.shape)
    core = 1 - core if other else core
    return (chip // across[1] * 2 + core) * across[1] + chip % across[1]


def share_body(sums_ref, replies_ref, out_ref, across):
    count, item_lanes = replies_ref.shape
    share = count // (across[0] * across[1] // 2)
    same = iota((count, count), 0) % share == iota((count, count), 1) % share
    out_ref[:, :item_lanes] = replies_ref[...]
    out_ref[:, item_lanes:] = dot(ones_where(same), sums_ref[...]).astype(BF)


def coarse_grad(arrivals, sends_ref, lists_ref, out_ref, across):
    capacity, devices = sends_ref.shape
    count, item_width = out_ref.shape
    half = item_width // 2
    lanes = arrivals[0].shape[0]
    pieces = arrivals[0].shape[1] // half
    _, group = chip_slots(lanes, pieces, across)
    sends = sends_ref[...].astype(F32).astype(BF)
    lane = iota((1, lanes), 1)
    totals = [None, None]
    for other in range(2):
        source = device_of(lane // group, lists_ref, other, across)
        rows = dot(sends, ones_where(source == iota((devices, lanes), 0)))
        for j in range(pieces):
            piece = lane % group * pieces + j
            picked = jnp.where(piece // 2 == iota((capacity, lanes), 0), rows, 0.0)
            index = jnp.sum(picked, axis=0, keepdims=True).astype(I32)
            named = iota((count, lanes), 0) == index
            for h in range(2):
                part = dot(ones_where(named & (piece % 2 == h)), arrivals[other][:, j * half : (j + 1) * half])
                totals[h] = part if totals[h] is None else totals[h] + part
    for h in range(2):
        out_ref[:, h * half : (h + 1) * half] = totals[h].astype(BF)


def last_body(back_ref, given_ref, sends_ref, lists_ref, conv_ref, up_ref, out_ref, item_lanes, across, scale):
    half_count = back_ref.shape[0]
    items = (back_ref[:, :item_lanes], given_ref[:, item_lanes : 2 * item_lanes])
    coarse_grad(items, sends_ref, lists_ref, out_ref, across)
    coarse = up_ref.shape[1]
    count = 2 * half_count
    parts = up_ref.shape[0] // count
    own = back_ref[:, 2 * item_lanes :].astype(F32) * scale
    others = given_ref[:, 2 * item_lanes :].astype(F32) * scale
    first, second = by_pair(lists_ref, GX, own, others)
    at = 0
    for q in range(parts):
        up_ref[q * count : q * count + half_count] = first[:, at : at + coarse]
        up_ref[q * count + half_count : (q + 1) * count] = second[:, at : at + coarse]
        at += coarse
    for pair in range(7):
        turned = jnp.concatenate([first[:, at : at + 2 * C], second[:, at : at + 2 * C]], axis=0).T
        at += 2 * C
        for h in range(2):
            for s in range(2):
                o = 14 * h + 2 * pair + s
                if o < 27:
                    conv_ref[o] = turned[s * C : (s + 1) * C, h * C : (h + 1) * C]


def swap(value, axis, first):
    count = lax.axis_size(axis)
    lower = range(first, count - 1, 2)
    return lax.ppermute(value, axis, [(i, i + 1) for i in lower] + [(i + 1, i) for i in lower])


def swap_pairs(to_even, to_odd, axis):
    return swap(to_even, axis, 0), swap(to_odd, axis, 1)


def trade_rows(values, axes):
    rows, width = values.shape
    devices = math.prod(lax.axis_size(axis) for axis in axes)
    grid_view = values.reshape(devices, rows // devices, width)
    return lax.all_to_all(grid_view, axes, split_axis=0, concat_axis=0, tiled=True).reshape(rows, width)


def on_device(
    fine_features, coarse_items, conv_weight, up_weight, neighbours,
    side_sends, cross_sends, parent_slots, coarse_sends, cotangent,
):
    fine = fine_features[0, 0]
    items = coarse_items[0, 0]
    cot = cotangent[0, 0]
    bricks, width = fine.shape
    face = side_sends.shape[-1]
    across = (lax.axis_size(GX_AXES), lax.axis_size("gy"))
    devices = across[0] * across[1]
    capacity = coarse_sends.shape[-1]
    item_count, item_width = items.shape
    coarse = up_weight.shape[1]
    start = bricks + 2 * face
    sends = coarse_sends.transpose(0, 1, 3, 2)[0, 0]
    slots = parent_slots[0]
    sides = side_sends[0, 0]
    crosses = cross_sends[0, 0]
    near = neighbours.transpose(0, 3, 1, 2)[0]
    up_turned = up_weight.transpose(0, 2, 1).reshape(8 * C, coarse)
    half = item_width // 2
    count = 2 * C
    item_lanes = capacity * devices // 2 * item_width // (count // 2)
    sums_width = 8 * C * coarse // count + 14 * C
    rows = shape((bricks, width))
    face_rows = shape((face, width))
    faces_and_parents = shape((face, width + item_width))
    lists_shape = shape((8, 128), I32)
    band = pltpu.VMEM((9, WIDE, RUN), BF)
    conv_flops = 2 * 9 * 16 * bricks * WIDE * RUN

    listed = (sends, items, sides, crosses, slots)
    outgoing, lists = call(
        first_body, [shape((2 * capacity * devices, half)), lists_shape], *listed,
        scratch=[pltpu.VMEM(a.shape, a.dtype) for a in listed] + [pltpu.SemaphoreType.DMA((len(listed),))],
        in_hbm=True,
    )
    received = trade_rows(outgoing, ("x", "core", "gy"))
    lane = jnp.arange(128, dtype=I32)[None]
    parity = jnp.where(lane == GX, lax.axis_index("core"), lax.axis_index("gy") % 2).astype(I32)
    table_rows = start + 2 * face
    ext_grad, to_even, to_odd, turned, mains, ends, lists = call(
        table_grad_body,
        [
            shape((start, width), F32), face_rows, face_rows, shape((RUN, 16 * bricks)),
            shape((9, bricks, table_rows)), shape((9, bricks, 2 * table_rows)), lists_shape,
        ],
        cot, conv_weight, near, lists, parity,
        scratch=[band, pltpu.VMEM((6, 6, bricks, WIDE), F32)], flops=2 * conv_flops,
    )
    cross_grads = swap_pairs(to_even, to_odd, GX_AXES)
    merged, parents, to_even, to_odd = call(
        merge_body, [rows, shape((8 * bricks, coarse)), faces_and_parents, faces_and_parents],
        received, up_turned, fine, lists,
    )
    sides = swap_pairs(to_even, to_odd, "gy")
    to_even, to_odd = call(cross_body, [face_rows, face_rows], *sides[::-1], merged, lists)
    crosses = swap_pairs(to_even, to_odd, GX_AXES)
    half_sums = (count // 2, sums_width)
    fine_part, to_even, to_odd, up_sums = call(
        side_grad_body,
        [shape((bricks, width), F32), face_rows, face_rows, shape((count, sums_width - 14 * C), F32)],
        ext_grad, lists, *cross_grads, *sides, parents,
    )
    side_grads = swap_pairs(to_even, to_odd, "gy")
    kept, given, pad = call(
        weight_grad_body, [shape(half_sums, F32), shape(half_sums), shape((6, 6, bricks, WIDE))],
        *crosses[::-1], merged, *sides, turned, mains, ends, lists, up_sums,
        scratch=[pltpu.VMEM((table_rows, width), BF), pltpu.VMEM((count, sums_width), F32)], flops=conv_flops,
    )
    given = swap(given, "core", 0)
    (sums,) = call(pair_sum_body, [shape(half_sums)], kept, given)
    sums = trade_rows(sums, ("x", "gy"))
    output, lists = call(
        conv_body, [rows, lists_shape], pad, conv_weight, lists, scratch=[band], flops=conv_flops
    )
    grad_fine, replies = call(
        functools.partial(fine_grad_body, across=across), [rows, shape((count // 2, 2 * item_lanes))],
        *side_grads[::-1], fine_part, lists, up_turned,
    )
    (back,) = call(
        functools.partial(share_body, across=across), [shape((count // 2, 2 * item_lanes + sums_width))], sums, replies
    )
    back = trade_rows(back, ("x", "gy"))
    given = swap(back, "core", 0)
    scale = 1.0 / math.sqrt(64 * bricks * devices)
    grad_conv, grad_up, coarse_grad = call(
        functools.partial(last_body, item_lanes=item_lanes, across=across, scale=scale),
        [shape((27, C, C), F32), shape((8 * C, coarse), F32), shape((item_count, item_width))],
        back, given, sends, lists,
    )
    return (
        output.reshape(1, 1, bricks, width),
        grad_fine.reshape(1, 1, bricks, width),
        coarse_grad.reshape(1, 1, item_count, item_width),
        grad_conv,
        grad_up.reshape(8, C, coarse).transpose(0, 2, 1),
    )


def solution(mesh):
    groups, across_x, across_y = mesh.devices.shape
    split_mesh = Mesh(mesh.devices.reshape(groups, across_x // 2, 2, across_y), ("groups", "x", "core", "gy"))
    rows = ("groups", "x", "core")
    split = P(rows, "gy", None, None)
    placed = (split, split, P(), P(), split, split, split, P(rows, "gy", None), split, split)
    return jax.shard_map(
        on_device,
        mesh=split_mesh,
        in_specs=placed,
        out_specs=(split, split, split, P("groups", None, None), P("groups", None, None)),
        check_vma=False,
    )
```

```python
import functools
import math

import jax
import jax.numpy as jnp
from jax import lax
from jax.experimental import pallas as pl
from jax.experimental.pallas import tpu as pltpu
from jax.sharding import Mesh
from jax.sharding import PartitionSpec as P

BF = jnp.bfloat16
F32 = jnp.float32
I32 = jnp.int32

C = 64
RUN = 4 * C
WIDE = RUN + 2 * C


def iota(shape, axis):
    return lax.broadcasted_iota(I32, shape, axis)


def ones_where(mask):
    return jnp.where(mask, 1.0, 0.0).astype(BF)


def dot(a, b):
    return jnp.dot(a, b, preferred_element_type=F32)


def dot_tn(a, b):
    return lax.dot_general(a, b, (((0,), (0,)), ((), ())), preferred_element_type=F32)


def dot_nt(a, b):
    return lax.dot_general(a, b, (((1,), (1,)), ((), ())), preferred_element_type=F32)


def column_of(row):
    size = row.shape[1]
    diagonal = iota((size, size), 0) == iota((size, size), 1)
    spread = jnp.broadcast_to(row.astype(F32), (size, size))
    return jnp.sum(jnp.where(diagonal, spread, 0.0), axis=1, keepdims=True).astype(I32)


def call(body, outs, *args, scratch=(), flops=0, in_hbm=False, results_in_hbm=0, aliases={}):
    moved = sum(a.size * a.dtype.itemsize for a in list(args) + list(outs))
    in_place = [pltpu.HBM if in_hbm else pl.ANY if i in aliases else None for i in range(len(args))]
    out_place = [pl.ANY if i < results_in_hbm else None for i in range(len(outs))]
    return pl.pallas_call(
        body,
        out_shape=tuple(outs),
        in_specs=[pl.BlockSpec(memory_space=place) for place in in_place],
        out_specs=tuple(pl.BlockSpec(memory_space=place) for place in out_place),
        scratch_shapes=tuple(scratch),
        input_output_aliases=aliases,
        cost_estimate=pl.CostEstimate(flops=flops, bytes_accessed=moved, transcendentals=0),
        compiler_params=pltpu.CompilerParams(vmem_limit_bytes=None if in_hbm else 28 * 2**20),
    )(*args)


def shape(dims, dtype=BF):
    return jax.ShapeDtypeStruct(dims, dtype)


def items_named(sends_ref, count):
    capacity, devices = sends_ref.shape
    group = 2 * capacity
    lanes = devices * group
    spread = ones_where(iota((lanes, devices), 0) // group == iota((lanes, devices), 1))
    slot = iota((lanes, capacity), 0) % group // 2
    values = dot_nt(spread, sends_ref[...].astype(F32).astype(BF))
    item = jnp.sum(jnp.where(slot == iota((lanes, capacity), 1), values, 0.0), axis=1, keepdims=True).astype(I32)
    place = jnp.where(item < count, item + iota((lanes, 1), 0) % 2 * count, -1)
    return ones_where(iota((lanes, 2 * count), 1) == place)


def merge(received_ref, slots, up_ref, fine_ref, merged_ref, parents_ref):
    bricks = fine_ref.shape[0]
    lanes, half = received_ref.shape
    slot = column_of(slots)
    place = iota((bricks, lanes), 1)
    named = place // 2 == slot
    received = received_ref[...]
    parents = jnp.concatenate(
        [dot(ones_where(named & (place % 2 == h)), received) for h in (0, 1)], axis=1
    ).astype(BF)
    coarse = 2 * half // 8
    stacked = jnp.concatenate([parents[:, v * coarse : (v + 1) * coarse] for v in range(8)], axis=0)
    parents_ref[...] = stacked
    lifted = dot_nt(stacked, up_ref[...])
    for v in range(8):
        cx, cy, cz = (v // 4, v // 2 % 2, v % 2)
        for parity in range(4):
            vx, vy = (2 * cx + parity // 2, 2 * cy + parity % 2)
            at = (vx * 4 + vy) * RUN + cz * 2 * C
            add = lifted[v * bricks : (v + 1) * bricks, parity * 2 * C : (parity + 1) * 2 * C]
            merged_ref[:, at : at + 2 * C] = (fine_ref[:, at : at + 2 * C].astype(F32) + add).astype(BF)
    return parents


def pick_rows(lists, rows):
    return [dot_tn(ones_where(iota((rows.shape[0], one.shape[1]), 0) == one), rows) for one in lists]


GX, GY = (0, 1)
GX_AXES = ("x", "core")


def by_pair(lists_ref, axis, of_next, of_prev):
    odd = jnp.broadcast_to(lists_ref[5:6, axis : axis + 1], of_next.shape) == 1
    return jnp.where(odd, of_prev, of_next), jnp.where(odd, of_next, of_prev)


def from_pairs(lists_ref, axis, even_ref, odd_ref):
    return by_pair(lists_ref, axis, even_ref[...].astype(F32), odd_ref[...].astype(F32))


def stack_rows(*parts):
    return jnp.concatenate([p.astype(F32) for p in parts], axis=0).astype(BF)


def sides_of(lists_ref, face):
    return lists_ref[0:2, :face]


def crosses_of(lists_ref, face):
    return lists_ref[2:4, :face]


def slots_of(lists_ref, bricks):
    return lists_ref[4:5, :bricks]


def cross_body(merged_ref, even_ref, odd_ref, lists_ref, a_ref, b_ref):
    face, width = a_ref.shape
    high, low = from_pairs(lists_ref, GY, even_ref, odd_ref)
    rows = jnp.concatenate([merged_ref[...], stack_rows(low[:, :width], high[:, :width])], axis=0)
    lists = crosses_of(lists_ref, face)
    picked = pick_rows(by_pair(lists_ref, GX, lists[0:1], lists[1:2]), rows)
    a_ref[...] = picked[0].astype(BF)
    b_ref[...] = picked[1].astype(BF)


def build_bands(weight_ref, band_ref):
    zero = jnp.zeros((C, C), BF)
    blank = jnp.zeros((C, 2 * C), BF)

    def pair(a, b):
        return jnp.concatenate([a, b], axis=1)

    for e in range(9):
        low, mid, high = (weight_ref[3 * e + z] for z in range(3))
        first, second = (pair(mid, low), pair(high, mid))
        left, right = (pair(low, zero), pair(zero, high))
        rows = (
            (first, blank),
            (second, left),
            (right, first),
            (blank, second),
            (blank, right),
            (left, blank),
        )
        for z, halves in enumerate(rows):
            for s in range(2):
                band_ref[e, z * C : (z + 1) * C, s * 2 * C : (s + 1) * 2 * C] = halves[s]


def options(at):
    return [(at + 1, 0)] + ([(5, 1)] if at == 0 else []) + ([(0, -1)] if at == 3 else [])


def offset_of(dx, dy, dz):
    return (dx + 1) * 9 + (dy + 1) * 3 + dz + 1


def stack_lanes(value, lanes):
    return jnp.concatenate([value[:, p * lanes : (p + 1) * lanes] for p in range(value.shape[1] // lanes)], axis=0)


def stack_parities(value):
    stacked = []
    for v in range(8):
        cx, cy, cz = (v // 4, v // 2 % 2, v % 2)
        lanes = []
        for parity in range(4):
            at = ((2 * cx + parity // 2) * 4 + 2 * cy + parity % 2) * RUN + cz * 2 * C
            lanes.append(value[:, at : at + 2 * C])
        stacked.append(jnp.concatenate(lanes, axis=1))
    return jnp.concatenate(stacked, axis=0)


def stack_runs(ref):
    return jnp.concatenate([ref[:, p * RUN : (p + 1) * RUN] for p in range(16)], axis=0)


def split_two(value):
    head = value.astype(BF)
    return head, (value - head.astype(F32)).astype(BF)


def table_grad_body(
    cot_ref, weight_ref, near_ref, lists_ref, parity_ref,
    ext_ref, even_ref, odd_ref, turned_ref, mains_ref, ends_ref, again_ref, band_ref, pad_ref,
):
    again_ref[...] = lists_ref[...]
    again_ref[5:6] = parity_ref[...]
    bricks = cot_ref.shape[0]
    face = even_ref.shape[0]
    start = ext_ref.shape[0]
    rows = start + 2 * face
    build_bands(weight_ref, band_ref)
    cot = stack_runs(cot_ref)
    turned_ref[...] = cot.T
    pad_ref[...] = jnp.zeros(pad_ref.shape, F32)
    for e in range(9):
        ex, ey = (e // 3, e % 3)
        part = dot_nt(cot, band_ref[e]).reshape(4, 4, bricks, WIDE)
        pad_ref[ex : ex + 4, ey : ey + 4] += part
    near = [near_ref[o] for o in range(27)]

    def chooser(which):
        index = jnp.concatenate([near[o] for o in which], axis=1)
        return ones_where(iota((rows, index.shape[1]), 0) == index)

    lower_half = iota((rows, 2 * C), 1) < C
    cache = {}
    for x in range(4):
        for y in range(4):
            places = [(X, Y, dx, dy) for X, dx in options(x) for Y, dy in options(y)]
            key = tuple((dx, dy) for _, _, dx, dy in places)
            if key not in cache:
                moved = [d for d in key if d != (0, 0)]
                main = chooser([offset_of(*d, 0) for d in moved] * 2) if moved else None
                up = chooser([offset_of(*d, 1) for d in key] * 2)
                down = chooser([offset_of(*d, -1) for d in key] * 2)
                cache[key] = (main, jnp.concatenate([up, down], axis=0))
            main, ends = cache[key]
            own = pad_ref[x + 1, y + 1, :, :RUN]
            own = jnp.concatenate([own, jnp.zeros((rows - bricks, RUN), F32)], axis=0)
            if main is not None:
                parts = [split_two(pad_ref[X, Y, :, :RUN]) for X, Y, dx, dy in places if (dx, dy) != (0, 0)]
                value = jnp.concatenate([p[0] for p in parts] + [p[1] for p in parts], axis=0)
                own += dot(main, value)
            parts = [split_two(pad_ref[X, Y, :, RUN:]) for X, Y, _, _ in places]
            value = jnp.concatenate([p[0] for p in parts] + [p[1] for p in parts], axis=0)
            halo = dot(ends, value)
            first = own[:, : 2 * C] + jnp.where(lower_half, halo[:rows], 0.0)
            second = own[:, 2 * C :] + jnp.where(lower_half, 0.0, halo[rows:])
            total = jnp.concatenate([first, second], axis=1)
            at = (x * 4 + y) * RUN
            ext_ref[:, at : at + RUN] = total[:start]
            even, odd = by_pair(again_ref, GX, total[start + face :], total[start : start + face])
            even_ref[:, at : at + RUN] = even.astype(BF)
            odd_ref[:, at : at + RUN] = odd.astype(BF)
    make_choosers(near_ref, rows, mains_ref, ends_ref)


def make_choosers(near_ref, rows, mains_ref, ends_ref):
    bricks = mains_ref.shape[1]
    near = jnp.concatenate([near_ref[o] for o in range(27)] + [jnp.zeros((5, bricks), I32)], axis=0)
    near = near.astype(F32).T.astype(I32)
    place = iota((bricks, rows), 1)
    pair_place = iota((bricks, 2 * rows), 1)
    for d in range(9):
        down, straight, up = (near[:, 3 * d + z : 3 * d + z + 1] for z in range(3))
        mains_ref[d] = ones_where(place == straight)
        ends_ref[d] = ones_where(pair_place == jnp.where(pair_place < rows, up, down + rows))


def first_body(
    sends_hbm, items_hbm, sides_hbm, crosses_hbm, slots_hbm, out_ref, lists_ref,
    sends_ref, items_ref, sides_ref, crosses_ref, slots_ref, arrived,
):
    sources = (sends_hbm, items_hbm, sides_hbm, crosses_hbm, slots_hbm)
    places = (sends_ref, items_ref, sides_ref, crosses_ref, slots_ref)
    copies = [pltpu.make_async_copy(s, p, arrived.at[i]) for i, (s, p) in enumerate(zip(sources, places))]
    for copy in copies:
        copy.start()
    copies[0].wait()
    chosen = items_named(sends_ref, items_ref.shape[0])
    copies[1].wait()
    half = out_ref.shape[1]
    items = jnp.concatenate([items_ref[:, :half], items_ref[:, half:]], axis=0)
    out_ref[...] = dot(chosen, items).astype(BF)
    for copy in copies[2:]:
        copy.wait()
    face, bricks = (sides_ref.shape[1], slots_ref.shape[1])
    lists_ref[...] = jnp.zeros(lists_ref.shape, I32)
    lists_ref[0:2, :face] = sides_ref[...]
    lists_ref[2:4, :face] = crosses_ref[...]
    lists_ref[4:5, :bricks] = slots_ref[...]


def side_grad_body(
    ext_ref, lists_ref, even_grad_ref, odd_grad_ref, even_side_ref, odd_side_ref, parents_ref,
    part_ref, to_even_ref, to_odd_ref, up_sums_ref,
):
    bricks, width = part_ref.shape
    face = to_even_ref.shape[0]
    from_next, from_prev = from_pairs(lists_ref, GX, even_grad_ref, odd_grad_ref)
    total = add_rows(ext_ref[...], crosses_of(lists_ref, face), from_next, from_prev)
    part_ref[...] = total[:bricks]
    to_even, to_odd = by_pair(lists_ref, GY, total[bricks + face :], total[bricks : bricks + face])
    to_even_ref[...] = to_even.astype(BF)
    to_odd_ref[...] = to_odd.astype(BF)
    high, low = by_pair(
        lists_ref, GY, even_side_ref[:, width:].astype(F32), odd_side_ref[:, width:].astype(F32)
    )
    side_parents = stack_lanes(stack_rows(low, high), parents_ref.shape[1])
    grads = [stack_parities(total[:bricks].astype(BF)), stack_parities(total[bricks:].astype(BF))]
    up_sum = dot_tn(jnp.concatenate(grads, axis=0), jnp.concatenate([parents_ref[...], side_parents], axis=0))
    coarse = up_sum.shape[1]
    count = up_sums_ref.shape[0]
    for q in range(up_sum.shape[0] // count):
        up_sums_ref[:, q * coarse : (q + 1) * coarse] = up_sum[q * count : (q + 1) * count]


def given_sums_body(
    odd_cross_ref, even_cross_ref, merged_ref, even_side_ref, odd_side_ref, turned_ref, mains_ref, ends_ref, lists_ref,
    up_sums_ref, given_ref, pad_ref, table_ref,
):
    bricks, width = merged_ref.shape
    face = even_side_ref.shape[0]
    rows = bricks + 4 * face
    high, low = by_pair(lists_ref, GY, even_side_ref[:, :width].astype(F32), odd_side_ref[:, :width].astype(F32))
    above, below = from_pairs(lists_ref, GX, even_cross_ref, odd_cross_ref)
    table_ref[:bricks] = merged_ref[...]
    table_ref[bricks:] = stack_rows(low, high, below, above)
    lower_half = iota((rows, 2 * C), 1) < C
    zero = jnp.zeros((rows, 2 * C), BF)
    for x in range(4):
        for y in range(4):
            places = [(X, Y, dx, dy) for X, dx in options(x) for Y, dy in options(y)]
            at = (x * 4 + y) * RUN
            columns = table_ref[:, at : at + RUN]
            first = jnp.where(lower_half, columns[:, : 2 * C], zero)
            second = jnp.where(lower_half, zero, columns[:, 2 * C :])
            ends = jnp.concatenate([ends_ref[3 * dx + dy + 4] for _, _, dx, dy in places], axis=0)
            halo = dot(ends, jnp.concatenate([first, second], axis=0)).astype(BF)
            for i, (X, Y, _, _) in enumerate(places):
                pad_ref[X, Y, :, RUN:] = halo[i * bricks : (i + 1) * bricks]
            pad_ref[x + 1, y + 1, :, :RUN] = columns[:bricks]
            moved = [p for p in places if p[2:] != (0, 0)]
            if moved:
                main = jnp.concatenate([mains_ref[3 * dx + dy + 4] for _, _, dx, dy in moved], axis=0)
                got = dot(main, columns).astype(BF)
                for i, (X, Y, _, _) in enumerate(moved):
                    pad_ref[X, Y, :, :RUN] = got[i * bricks : (i + 1) * bricks]

    half_sums(1 - lists_ref[5, GX], pad_ref, turned_ref, up_sums_ref, given_ref)


def half_sums(group, pad_ref, turned_ref, up_sums_ref, out_ref):
    turned = turned_ref[...]
    half_count = out_ref.shape[0]
    up_lanes = up_sums_ref.shape[1]
    up_half = jnp.where(group == 0, up_sums_ref[:half_count], up_sums_ref[half_count:])
    out_ref[:, :up_lanes] = up_half.astype(out_ref.dtype)
    bricks = pad_ref.shape[2]
    lanes_low = iota((C, 2 * C), 1) < C
    sums = []
    for i in range(5):
        ex, ey = (jnp.where(group == 0, i // 3, (i + 4) // 3), jnp.where(group == 0, i % 3, (i + 4) % 3))
        wide = dot(turned, pad_ref[pl.ds(ex, 4), pl.ds(ey, 4)].reshape(16 * bricks, WIDE))

        def block(z, s):
            return wide[z * C : (z + 1) * C, s * 2 * C : (s + 1) * 2 * C]

        low = jnp.where(lanes_low, block(1, 0) + block(3, 1), block(0, 2) + block(2, 0))
        mid = jnp.where(lanes_low, block(0, 0) + block(2, 1), block(1, 0) + block(3, 1))
        high = jnp.where(lanes_low, block(1, 1) + block(3, 2), block(0, 0) + block(2, 1))
        for value in (low, mid, high):
            sums.append(value + pltpu.roll(value, C, 1))
    sums.append(jnp.zeros((C, 2 * C), F32))
    pairs = [jnp.where(lanes_low, sums[2 * k], sums[2 * k + 1]) for k in range(8)]
    for p in range(7):
        at = up_lanes + p * 2 * C
        out_ref[:, at : at + 2 * C] = jnp.where(group == 0, pairs[p], pairs[p + 1]).astype(out_ref.dtype)


def kept_sums_body(pad_ref, turned_ref, up_sums_ref, lists_ref, kept_ref):
    half_sums(lists_ref[5, GX], pad_ref, turned_ref, up_sums_ref, kept_ref)


def pair_sum_body(kept_ref, given_ref, out_ref):
    out_ref[...] = (kept_ref[...] + given_ref[...].astype(F32)).astype(BF)


def inputs_at(pad_ref, e):
    bricks = pad_ref.shape[2]
    ex, ey = (e // 3, e % 3)
    return pad_ref[ex : ex + 4, ey : ey + 4].reshape(16 * bricks, WIDE)


def conv_body(pad_ref, weight_ref, lists_ref, out_ref, again_ref, band_ref):
    again_ref[...] = lists_ref[...]
    bricks = pad_ref.shape[2]
    build_bands(weight_ref, band_ref)
    total = None
    for e in range(9):
        part = dot(inputs_at(pad_ref, e), band_ref[e])
        total = part if total is None else total + part
    for p in range(16):
        out_ref[:, p * RUN : (p + 1) * RUN] = total[p * bricks : (p + 1) * bricks].astype(BF)


def add_rows(base, lists, first, second):
    count, face = (base.shape[0], lists.shape[1])
    index = jnp.concatenate([lists[0:1], lists[1:2]], axis=1)
    chosen = ones_where(iota((count, 2 * face), 0) == index)
    return base + dot(chosen, stack_rows(first, second))


def merge_body(received_ref, up_ref, fine_ref, lists_ref, merged_ref, parents_ref, a_ref, b_ref):
    bricks, width = fine_ref.shape
    face = a_ref.shape[0]
    parents = merge(received_ref, slots_of(lists_ref, bricks), up_ref, fine_ref, merged_ref, parents_ref)
    lists = sides_of(lists_ref, face)
    lists = by_pair(lists_ref, GY, lists[0:1], lists[1:2])
    for out_ref, rows, owners in zip((a_ref, b_ref), pick_rows(lists, merged_ref[...]), pick_rows(lists, parents)):
        out_ref[:, :width] = rows.astype(BF)
        out_ref[:, width:] = owners.astype(BF)


def fine_grad_body(part_ref, lists_ref, even_ref, odd_ref, up_ref, grad_ref, replies_ref, across):
    bricks = part_ref.shape[0]
    face = even_ref.shape[0]
    from_next, from_prev = from_pairs(lists_ref, GY, even_ref, odd_ref)
    total = add_rows(part_ref[...], sides_of(lists_ref, face), from_next, from_prev)
    grad_ref[...] = total.astype(BF)
    items = dot(stack_parities(grad_ref[...]), up_ref[...]).astype(BF)
    items = jnp.concatenate([items[v * bricks : (v + 1) * bricks] for v in range(8)], axis=1)
    half = items.shape[1] // 2
    count, both_lanes = replies_ref.shape
    pieces = both_lanes // 2 // half
    capacity, group = chip_slots(count, pieces, across)
    slots = slots_of(lists_ref, bricks)
    row = iota((count, bricks), 0)
    for other in range(2):
        owner = device_of(row // group, lists_ref, other, across)
        for j in range(pieces):
            piece = row % group * pieces + j
            named = owner * capacity + piece // 2 == slots
            rows = dot(ones_where(named & (piece % 2 == 0)), items[:, :half])
            rows += dot(ones_where(named & (piece % 2 == 1)), items[:, half:])
            at = (other * pieces + j) * half
            replies_ref[:, at : at + half] = rows.astype(BF)


def chip_slots(count, pieces, across):
    group = count // (across[0] * across[1] // 2)
    return group * pieces // 2, group


def device_of(chip, lists_ref, other, across):
    core = jnp.broadcast_to(lists_ref[5:6, GX : GX + 1], chip.shape)
    core = 1 - core if other else core
    return (chip // across[1] * 2 + core) * across[1] + chip % across[1]


def share_body(sums_ref, replies_ref, out_ref, across):
    count, item_lanes = replies_ref.shape
    share = count // (across[0] * across[1] // 2)
    same = iota((count, count), 0) % share == iota((count, count), 1) % share
    out_ref[:, :item_lanes] = replies_ref[...]
    out_ref[:, item_lanes:] = dot(ones_where(same), sums_ref[...]).astype(BF)


def coarse_part(arrived, sends_ref, lists_ref, other, out_dims, across):
    capacity, devices = sends_ref.shape
    count, item_width = out_dims
    half = item_width // 2
    lanes = arrived.shape[0]
    pieces = arrived.shape[1] // half
    _, group = chip_slots(lanes, pieces, across)
    sends = sends_ref[...].astype(F32).astype(BF)
    lane = iota((1, lanes), 1)
    source = device_of(lane // group, lists_ref, other, across)
    rows = dot(sends, ones_where(source == iota((devices, lanes), 0)))
    totals = [None, None]
    for j in range(pieces):
        piece = lane % group * pieces + j
        picked = jnp.where(piece // 2 == iota((capacity, lanes), 0), rows, 0.0)
        index = jnp.sum(picked, axis=0, keepdims=True).astype(I32)
        named = iota((count, lanes), 0) == index
        for h in range(2):
            part = dot(ones_where(named & (piece % 2 == h)), arrived[:, j * half : (j + 1) * half])
            totals[h] = part if totals[h] is None else totals[h] + part
    return jnp.concatenate(totals, axis=1)


def write_half(group, half, conv_hbm, up_hbm, conv_ref, up_ref, done, scale):
    half_count, coarse = up_ref.shape[1:]
    parts = up_ref.shape[0]
    at = 0
    copies = []
    for q in range(parts):
        up_ref[q] = half[:, at : at + coarse].astype(F32) * scale
        at += coarse
        place = pl.ds(pl.multiple_of((2 * q + group) * half_count, half_count), half_count)
        copies.append(pltpu.make_async_copy(up_ref.at[q], up_hbm.at[place], done.at[q]))
        copies[-1].start()
    for pair in range(7):
        turned = half[:, at : at + 2 * C].astype(F32).T * scale
        at += 2 * C
        for s in range(2):
            conv_ref[2 * pair + s] = turned[s * C : (s + 1) * C]
    copies.append(pltpu.make_async_copy(conv_ref.at[pl.ds(0, 13)], conv_hbm.at[pl.ds(14 * group, 13)], done.at[parts]))
    copies[-1].start()
    last = pltpu.make_async_copy(conv_ref.at[13], conv_hbm.at[13], done.at[parts + 1])

    @pl.when(group == 0)
    def _():
        last.start()

    return copies, last


def end_half(group, copies, last):
    for copy in copies:
        copy.wait()

    @pl.when(group == 0)
    def _():
        last.wait()


def own_half_body(
    back_ref, sends_ref, lists_ref, conv_hbm, up_hbm, part_ref, conv_ref, up_ref, done, item_lanes, across, scale
):
    group = lists_ref[5, GX]
    started = write_half(group, back_ref[:, 2 * item_lanes :], conv_hbm, up_hbm, conv_ref, up_ref, done, scale)
    part_ref[...] = coarse_part(back_ref[:, :item_lanes], sends_ref, lists_ref, 0, part_ref.shape, across)
    end_half(group, *started)


def other_half_body(
    given_ref, part_ref, sends_ref, lists_ref, conv_in, up_in,
    conv_hbm, up_hbm, out_ref, conv_ref, up_ref, done, item_lanes, across, scale,
):
    group = 1 - lists_ref[5, GX]
    started = write_half(group, given_ref[:, 2 * item_lanes :], conv_hbm, up_hbm, conv_ref, up_ref, done, scale)
    came = given_ref[:, item_lanes : 2 * item_lanes]
    other = coarse_part(came, sends_ref, lists_ref, 1, out_ref.shape, across)
    out_ref[...] = (part_ref[...] + other).astype(BF)
    end_half(group, *started)


def swap(value, axis, first):
    count = lax.axis_size(axis)
    lower = range(first, count - 1, 2)
    return lax.ppermute(value, axis, [(i, i + 1) for i in lower] + [(i + 1, i) for i in lower])


def swap_pairs(to_even, to_odd, axis):
    return swap(to_even, axis, 0), swap(to_odd, axis, 1)


def trade_rows(values, axes):
    rows, width = values.shape
    devices = math.prod(lax.axis_size(axis) for axis in axes)
    grid_view = values.reshape(devices, rows // devices, width)
    return lax.all_to_all(grid_view, axes, split_axis=0, concat_axis=0, tiled=True).reshape(rows, width)


def on_device(
    fine_features, coarse_items, conv_weight, up_weight, neighbours,
    side_sends, cross_sends, parent_slots, coarse_sends, cotangent,
):
    fine = fine_features[0, 0]
    items = coarse_items[0, 0]
    cot = cotangent[0, 0]
    bricks, width = fine.shape
    face = side_sends.shape[-1]
    across = (lax.axis_size(GX_AXES), lax.axis_size("gy"))
    devices = across[0] * across[1]
    capacity = coarse_sends.shape[-1]
    item_count, item_width = items.shape
    coarse = up_weight.shape[1]
    start = bricks + 2 * face
    sends = coarse_sends.transpose(0, 1, 3, 2)[0, 0]
    slots = parent_slots[0]
    sides = side_sends[0, 0]
    crosses = cross_sends[0, 0]
    near = neighbours.transpose(0, 3, 1, 2)[0]
    up_turned = up_weight.transpose(0, 2, 1).reshape(8 * C, coarse)
    half = item_width // 2
    count = 2 * C
    item_lanes = capacity * devices // 2 * item_width // (count // 2)
    sums_width = 8 * C * coarse // count + 14 * C
    rows = shape((bricks, width))
    face_rows = shape((face, width))
    faces_and_parents = shape((face, width + item_width))
    lists_shape = shape((8, 128), I32)
    band = pltpu.VMEM((9, WIDE, RUN), BF)
    conv_flops = 2 * 9 * 16 * bricks * WIDE * RUN

    listed = (sends, items, sides, crosses, slots)
    outgoing, lists = call(
        first_body, [shape((2 * capacity * devices, half)), lists_shape], *listed,
        scratch=[pltpu.VMEM(a.shape, a.dtype) for a in listed] + [pltpu.SemaphoreType.DMA((len(listed),))],
        in_hbm=True,
    )
    received = trade_rows(outgoing, ("x", "core", "gy"))
    lane = jnp.arange(128, dtype=I32)[None]
    parity = jnp.where(lane == GX, lax.axis_index("core"), lax.axis_index("gy") % 2).astype(I32)
    table_rows = start + 2 * face
    ext_grad, to_even, to_odd, turned, mains, ends, lists = call(
        table_grad_body,
        [
            shape((start, width), F32), face_rows, face_rows, shape((RUN, 16 * bricks)),
            shape((9, bricks, table_rows)), shape((9, bricks, 2 * table_rows)), lists_shape,
        ],
        cot, conv_weight, near, lists, parity,
        scratch=[band, pltpu.VMEM((6, 6, bricks, WIDE), F32)], flops=2 * conv_flops,
    )
    cross_grads = swap_pairs(to_even, to_odd, GX_AXES)
    merged, parents, to_even, to_odd = call(
        merge_body, [rows, shape((8 * bricks, coarse)), faces_and_parents, faces_and_parents],
        received, up_turned, fine, lists,
    )
    sides = swap_pairs(to_even, to_odd, "gy")
    to_even, to_odd = call(cross_body, [face_rows, face_rows], merged, *sides, lists)
    crosses = swap_pairs(to_even, to_odd, GX_AXES)
    half_sums_dims = (count // 2, sums_width)
    fine_part, to_even, to_odd, up_sums = call(
        side_grad_body,
        [shape((bricks, width), F32), face_rows, face_rows, shape((count, sums_width - 14 * C), F32)],
        ext_grad, lists, *cross_grads, *sides, parents,
    )
    side_grads = swap_pairs(to_even, to_odd, "gy")
    given, pad = call(
        given_sums_body, [shape(half_sums_dims), shape((6, 6, bricks, WIDE))],
        *crosses[::-1], merged, *sides, turned, mains, ends, lists, up_sums,
        scratch=[pltpu.VMEM((table_rows, width), BF)], flops=conv_flops,
    )
    (kept,) = call(kept_sums_body, [shape(half_sums_dims, F32)], pad, turned, up_sums, lists, flops=conv_flops)
    given = swap(given, "core", 0)
    (sums,) = call(pair_sum_body, [shape(half_sums_dims)], kept, given)
    sums = trade_rows(sums, ("x", "gy"))
    output, lists = call(
        conv_body, [rows, lists_shape], pad, conv_weight, lists, scratch=[band], flops=conv_flops
    )
    grad_fine, replies = call(
        functools.partial(fine_grad_body, across=across), [rows, shape((count // 2, 2 * item_lanes))],
        fine_part, lists, *side_grads, up_turned,
    )
    (back,) = call(
        functools.partial(share_body, across=across), [shape((count // 2, 2 * item_lanes + sums_width))], sums, replies
    )
    back = trade_rows(back, ("x", "gy"))
    given = swap(back, "core", 0)
    scale = 1.0 / math.sqrt(64 * bricks * devices)
    results = [shape((27, C, C), F32), shape((8 * C, coarse), F32)]
    halves = dict(
        scratch=[
            pltpu.VMEM((14, C, C), F32), pltpu.VMEM((8 * C // count, count // 2, coarse), F32),
            pltpu.SemaphoreType.DMA((8 * C // count + 2,)),
        ],
        results_in_hbm=2,
    )
    sizes = dict(item_lanes=item_lanes, across=across, scale=scale)
    grad_conv, grad_up, part = call(
        functools.partial(own_half_body, **sizes), results + [shape((item_count, item_width), F32)],
        back, sends, lists, **halves,
    )
    grad_conv, grad_up, coarse_grad = call(
        functools.partial(other_half_body, **sizes), results + [shape((item_count, item_width))],
        given, part, sends, lists, grad_conv, grad_up, aliases={4: 0, 5: 1}, **halves,
    )
    return (
        output.reshape(1, 1, bricks, width),
        grad_fine.reshape(1, 1, bricks, width),
        coarse_grad.reshape(1, 1, item_count, item_width),
        grad_conv,
        grad_up.reshape(8, C, coarse).transpose(0, 2, 1),
    )


def solution(mesh):
    groups, across_x, across_y = mesh.devices.shape
    split_mesh = Mesh(mesh.devices.reshape(groups, across_x // 2, 2, across_y), ("groups", "x", "core", "gy"))
    rows = ("groups", "x", "core")
    split = P(rows, "gy", None, None)
    placed = (split, split, P(), P(), split, split, split, P(rows, "gy", None), split, split)
    return jax.shard_map(
        on_device,
        mesh=split_mesh,
        in_specs=placed,
        out_specs=(split, split, split, P("groups", None, None), P("groups", None, None)),
        check_vma=False,
    )
```

```python
import functools
import math

import jax
import jax.numpy as jnp
from jax import lax
from jax.experimental import pallas as pl
from jax.experimental.pallas import tpu as pltpu
from jax.sharding import Mesh
from jax.sharding import PartitionSpec as P

BF = jnp.bfloat16
F32 = jnp.float32
I32 = jnp.int32

C = 64
RUN = 4 * C
WIDE = RUN + 2 * C


def iota(shape, axis):
    return lax.broadcasted_iota(I32, shape, axis)


def ones_where(mask):
    return jnp.where(mask, 1.0, 0.0).astype(BF)


def dot(a, b):
    return jnp.dot(a, b, preferred_element_type=F32)


def dot_tn(a, b):
    return lax.dot_general(a, b, (((0,), (0,)), ((), ())), preferred_element_type=F32)


def dot_nt(a, b):
    return lax.dot_general(a, b, (((1,), (1,)), ((), ())), preferred_element_type=F32)


def column_of(row):
    size = row.shape[1]
    diagonal = iota((size, size), 0) == iota((size, size), 1)
    spread = jnp.broadcast_to(row.astype(F32), (size, size))
    return jnp.sum(jnp.where(diagonal, spread, 0.0), axis=1, keepdims=True).astype(I32)


def call(body, outs, *args, scratch=(), flops=0, in_hbm=False):
    moved = sum(a.size * a.dtype.itemsize for a in list(args) + list(outs))
    return pl.pallas_call(
        body,
        out_shape=tuple(outs),
        in_specs=[pl.BlockSpec(memory_space=pltpu.HBM) if in_hbm else pl.BlockSpec() for _ in args],
        scratch_shapes=tuple(scratch),
        cost_estimate=pl.CostEstimate(flops=flops, bytes_accessed=moved, transcendentals=0),
        compiler_params=pltpu.CompilerParams(vmem_limit_bytes=None if in_hbm else 28 * 2**20),
    )(*args)


def shape(dims, dtype=BF):
    return jax.ShapeDtypeStruct(dims, dtype)


def items_named(sends_ref, count):
    capacity, devices = sends_ref.shape
    group = 2 * capacity
    lanes = devices * group
    spread = ones_where(iota((lanes, devices), 0) // group == iota((lanes, devices), 1))
    slot = iota((lanes, capacity), 0) % group // 2
    values = dot_nt(spread, sends_ref[...].astype(F32).astype(BF))
    item = jnp.sum(jnp.where(slot == iota((lanes, capacity), 1), values, 0.0), axis=1, keepdims=True).astype(I32)
    place = jnp.where(item < count, item + iota((lanes, 1), 0) % 2 * count, -1)
    return ones_where(iota((lanes, 2 * count), 1) == place)


def merge(received_ref, slots, up_ref, fine_ref, merged_ref, parents_ref):
    bricks = fine_ref.shape[0]
    lanes, half = received_ref.shape
    slot = column_of(slots)
    place = iota((bricks, lanes), 1)
    named = place // 2 == slot
    received = received_ref[...]
    parents = jnp.concatenate(
        [dot(ones_where(named & (place % 2 == h)), received) for h in (0, 1)], axis=1
    ).astype(BF)
    coarse = 2 * half // 8
    stacked = jnp.concatenate([parents[:, v * coarse : (v + 1) * coarse] for v in range(8)], axis=0)
    parents_ref[...] = stacked
    lifted = dot_nt(stacked, up_ref[...])
    for v in range(8):
        cx, cy, cz = (v // 4, v // 2 % 2, v % 2)
        for parity in range(4):
            vx, vy = (2 * cx + parity // 2, 2 * cy + parity % 2)
            at = (vx * 4 + vy) * RUN + cz * 2 * C
            add = lifted[v * bricks : (v + 1) * bricks, parity * 2 * C : (parity + 1) * 2 * C]
            merged_ref[:, at : at + 2 * C] = (fine_ref[:, at : at + 2 * C].astype(F32) + add).astype(BF)
    return parents


def pick_rows(lists, rows):
    return [dot_tn(ones_where(iota((rows.shape[0], one.shape[1]), 0) == one), rows) for one in lists]


GX, GY = (0, 1)
GX_AXES = ("x", "core")


def by_pair(lists_ref, axis, of_next, of_prev):
    odd = jnp.broadcast_to(lists_ref[5:6, axis : axis + 1], of_next.shape) == 1
    return jnp.where(odd, of_prev, of_next), jnp.where(odd, of_next, of_prev)


def from_pairs(lists_ref, axis, even_ref, odd_ref):
    return by_pair(lists_ref, axis, even_ref[...].astype(F32), odd_ref[...].astype(F32))


def stack_rows(*parts):
    return jnp.concatenate([p.astype(F32) for p in parts], axis=0).astype(BF)


def sides_of(lists_ref, face):
    return lists_ref[0:2, :face]


def crosses_of(lists_ref, face):
    return lists_ref[2:4, :face]


def slots_of(lists_ref, bricks):
    return lists_ref[4:5, :bricks]


def cross_body(merged_ref, even_ref, odd_ref, lists_ref, a_ref, b_ref):
    face, width = a_ref.shape
    high, low = from_pairs(lists_ref, GY, even_ref, odd_ref)
    rows = jnp.concatenate([merged_ref[...], stack_rows(low[:, :width], high[:, :width])], axis=0)
    lists = crosses_of(lists_ref, face)
    picked = pick_rows(by_pair(lists_ref, GX, lists[0:1], lists[1:2]), rows)
    a_ref[...] = picked[0].astype(BF)
    b_ref[...] = picked[1].astype(BF)


def build_bands(weight_ref, band_ref):
    zero = jnp.zeros((C, C), BF)
    blank = jnp.zeros((C, 2 * C), BF)

    def pair(a, b):
        return jnp.concatenate([a, b], axis=1)

    for e in range(9):
        low, mid, high = (weight_ref[3 * e + z] for z in range(3))
        first, second = (pair(mid, low), pair(high, mid))
        left, right = (pair(low, zero), pair(zero, high))
        rows = (
            (first, blank),
            (second, left),
            (right, first),
            (blank, second),
            (blank, right),
            (left, blank),
        )
        for z, halves in enumerate(rows):
            for s in range(2):
                band_ref[e, z * C : (z + 1) * C, s * 2 * C : (s + 1) * 2 * C] = halves[s]


def options(at):
    return [(at + 1, 0)] + ([(5, 1)] if at == 0 else []) + ([(0, -1)] if at == 3 else [])


def offset_of(dx, dy, dz):
    return (dx + 1) * 9 + (dy + 1) * 3 + dz + 1


def stack_lanes(value, lanes):
    return jnp.concatenate([value[:, p * lanes : (p + 1) * lanes] for p in range(value.shape[1] // lanes)], axis=0)


def stack_parities(value):
    stacked = []
    for v in range(8):
        cx, cy, cz = (v // 4, v // 2 % 2, v % 2)
        lanes = []
        for parity in range(4):
            at = ((2 * cx + parity // 2) * 4 + 2 * cy + parity % 2) * RUN + cz * 2 * C
            lanes.append(value[:, at : at + 2 * C])
        stacked.append(jnp.concatenate(lanes, axis=1))
    return jnp.concatenate(stacked, axis=0)


def stack_runs(ref):
    return jnp.concatenate([ref[:, p * RUN : (p + 1) * RUN] for p in range(16)], axis=0)


def split_two(value):
    head = value.astype(BF)
    return head, (value - head.astype(F32)).astype(BF)


def table_grad_body(
    cot_ref, weight_ref, near_ref, lists_ref, parity_ref,
    ext_ref, even_ref, odd_ref, turned_ref, mains_ref, ends_ref, again_ref, band_ref, pad_ref,
):
    again_ref[...] = lists_ref[...]
    again_ref[5:6] = parity_ref[...]
    bricks = cot_ref.shape[0]
    face = even_ref.shape[0]
    start = ext_ref.shape[0]
    rows = start + 2 * face
    build_bands(weight_ref, band_ref)
    cot = stack_runs(cot_ref)
    turned_ref[...] = cot.T
    pad_ref[...] = jnp.zeros(pad_ref.shape, F32)
    for e in range(9):
        ex, ey = (e // 3, e % 3)
        part = dot_nt(cot, band_ref[e]).reshape(4, 4, bricks, WIDE)
        pad_ref[ex : ex + 4, ey : ey + 4] += part
    near = [near_ref[o] for o in range(27)]

    def chooser(which):
        index = jnp.concatenate([near[o] for o in which], axis=1)
        return ones_where(iota((rows, index.shape[1]), 0) == index)

    lower_half = iota((rows, 2 * C), 1) < C
    cache = {}
    for x in range(4):
        for y in range(4):
            places = [(X, Y, dx, dy) for X, dx in options(x) for Y, dy in options(y)]
            key = tuple((dx, dy) for _, _, dx, dy in places)
            if key not in cache:
                moved = [d for d in key if d != (0, 0)]
                main = chooser([offset_of(*d, 0) for d in moved] * 2) if moved else None
                up = chooser([offset_of(*d, 1) for d in key] * 2)
                down = chooser([offset_of(*d, -1) for d in key] * 2)
                cache[key] = (main, jnp.concatenate([up, down], axis=0))
            main, ends = cache[key]
            own = pad_ref[x + 1, y + 1, :, :RUN]
            own = jnp.concatenate([own, jnp.zeros((rows - bricks, RUN), F32)], axis=0)
            if main is not None:
                parts = [split_two(pad_ref[X, Y, :, :RUN]) for X, Y, dx, dy in places if (dx, dy) != (0, 0)]
                value = jnp.concatenate([p[0] for p in parts] + [p[1] for p in parts], axis=0)
                own += dot(main, value)
            parts = [split_two(pad_ref[X, Y, :, RUN:]) for X, Y, _, _ in places]
            value = jnp.concatenate([p[0] for p in parts] + [p[1] for p in parts], axis=0)
            halo = dot(ends, value)
            first = own[:, : 2 * C] + jnp.where(lower_half, halo[:rows], 0.0)
            second = own[:, 2 * C :] + jnp.where(lower_half, 0.0, halo[rows:])
            total = jnp.concatenate([first, second], axis=1)
            at = (x * 4 + y) * RUN
            ext_ref[:, at : at + RUN] = total[:start]
            even, odd = by_pair(again_ref, GX, total[start + face :], total[start : start + face])
            even_ref[:, at : at + RUN] = even.astype(BF)
            odd_ref[:, at : at + RUN] = odd.astype(BF)
    make_choosers(near_ref, rows, mains_ref, ends_ref)


def make_choosers(near_ref, rows, mains_ref, ends_ref):
    bricks = mains_ref.shape[1]
    near = jnp.concatenate([near_ref[o] for o in range(27)] + [jnp.zeros((5, bricks), I32)], axis=0)
    near = near.astype(F32).T.astype(I32)
    place = iota((bricks, rows), 1)
    pair_place = iota((bricks, 2 * rows), 1)
    for d in range(9):
        down, straight, up = (near[:, 3 * d + z : 3 * d + z + 1] for z in range(3))
        mains_ref[d] = ones_where(place == straight)
        ends_ref[d] = ones_where(pair_place == jnp.where(pair_place < rows, up, down + rows))


def first_body(
    sends_hbm, items_hbm, sides_hbm, crosses_hbm, slots_hbm, out_ref, lists_ref,
    sends_ref, items_ref, sides_ref, crosses_ref, slots_ref, arrived,
):
    sources = (sends_hbm, items_hbm, sides_hbm, crosses_hbm, slots_hbm)
    places = (sends_ref, items_ref, sides_ref, crosses_ref, slots_ref)
    copies = [pltpu.make_async_copy(s, p, arrived.at[i]) for i, (s, p) in enumerate(zip(sources, places))]
    for copy in copies:
        copy.start()
    copies[0].wait()
    chosen = items_named(sends_ref, items_ref.shape[0])
    copies[1].wait()
    half = out_ref.shape[1]
    items = jnp.concatenate([items_ref[:, :half], items_ref[:, half:]], axis=0)
    out_ref[...] = dot(chosen, items).astype(BF)
    for copy in copies[2:]:
        copy.wait()
    face, bricks = (sides_ref.shape[1], slots_ref.shape[1])
    lists_ref[...] = jnp.zeros(lists_ref.shape, I32)
    lists_ref[0:2, :face] = sides_ref[...]
    lists_ref[2:4, :face] = crosses_ref[...]
    lists_ref[4:5, :bricks] = slots_ref[...]


def side_grad_body(
    ext_ref, lists_ref, even_grad_ref, odd_grad_ref, even_side_ref, odd_side_ref, parents_ref,
    part_ref, to_even_ref, to_odd_ref, up_sums_ref,
):
    bricks, width = part_ref.shape
    face = to_even_ref.shape[0]
    from_next, from_prev = from_pairs(lists_ref, GX, even_grad_ref, odd_grad_ref)
    total = add_rows(ext_ref[...], crosses_of(lists_ref, face), from_next, from_prev)
    part_ref[...] = total[:bricks]
    to_even, to_odd = by_pair(lists_ref, GY, total[bricks + face :], total[bricks : bricks + face])
    to_even_ref[...] = to_even.astype(BF)
    to_odd_ref[...] = to_odd.astype(BF)
    high, low = by_pair(
        lists_ref, GY, even_side_ref[:, width:].astype(F32), odd_side_ref[:, width:].astype(F32)
    )
    side_parents = stack_lanes(stack_rows(low, high), parents_ref.shape[1])
    grads = [stack_parities(total[:bricks].astype(BF)), stack_parities(total[bricks:].astype(BF))]
    up_sum = dot_tn(jnp.concatenate(grads, axis=0), jnp.concatenate([parents_ref[...], side_parents], axis=0))
    coarse = up_sum.shape[1]
    count = up_sums_ref.shape[0]
    for q in range(up_sum.shape[0] // count):
        up_sums_ref[:, q * coarse : (q + 1) * coarse] = up_sum[q * count : (q + 1) * count]


def given_sums_body(
    odd_cross_ref, even_cross_ref, merged_ref, even_side_ref, odd_side_ref, turned_ref, mains_ref, ends_ref, lists_ref,
    up_sums_ref, given_ref, pad_ref, table_ref,
):
    bricks, width = merged_ref.shape
    face = even_side_ref.shape[0]
    rows = bricks + 4 * face
    high, low = by_pair(lists_ref, GY, even_side_ref[:, :width].astype(F32), odd_side_ref[:, :width].astype(F32))
    above, below = from_pairs(lists_ref, GX, even_cross_ref, odd_cross_ref)
    table_ref[:bricks] = merged_ref[...]
    table_ref[bricks:] = stack_rows(low, high, below, above)
    lower_half = iota((rows, 2 * C), 1) < C
    zero = jnp.zeros((rows, 2 * C), BF)
    for x in range(4):
        for y in range(4):
            places = [(X, Y, dx, dy) for X, dx in options(x) for Y, dy in options(y)]
            at = (x * 4 + y) * RUN
            columns = table_ref[:, at : at + RUN]
            first = jnp.where(lower_half, columns[:, : 2 * C], zero)
            second = jnp.where(lower_half, zero, columns[:, 2 * C :])
            ends = jnp.concatenate([ends_ref[3 * dx + dy + 4] for _, _, dx, dy in places], axis=0)
            halo = dot(ends, jnp.concatenate([first, second], axis=0)).astype(BF)
            for i, (X, Y, _, _) in enumerate(places):
                pad_ref[X, Y, :, RUN:] = halo[i * bricks : (i + 1) * bricks]
            pad_ref[x + 1, y + 1, :, :RUN] = columns[:bricks]
            moved = [p for p in places if p[2:] != (0, 0)]
            if moved:
                main = jnp.concatenate([mains_ref[3 * dx + dy + 4] for _, _, dx, dy in moved], axis=0)
                got = dot(main, columns).astype(BF)
                for i, (X, Y, _, _) in enumerate(moved):
                    pad_ref[X, Y, :, :RUN] = got[i * bricks : (i + 1) * bricks]

    half_sums(1 - lists_ref[5, GX], pad_ref, turned_ref, up_sums_ref, given_ref)


def half_sums(group, pad_ref, turned_ref, up_sums_ref, out_ref):
    turned = turned_ref[...]
    half_count = out_ref.shape[0]
    up_lanes = up_sums_ref.shape[1]
    up_half = jnp.where(group == 0, up_sums_ref[:half_count], up_sums_ref[half_count:])
    out_ref[:, :up_lanes] = up_half.astype(out_ref.dtype)
    bricks = pad_ref.shape[2]
    lanes_low = iota((C, 2 * C), 1) < C
    sums = []
    for i in range(5):
        ex, ey = (jnp.where(group == 0, i // 3, (i + 4) // 3), jnp.where(group == 0, i % 3, (i + 4) % 3))
        wide = dot(turned, pad_ref[pl.ds(ex, 4), pl.ds(ey, 4)].reshape(16 * bricks, WIDE))

        def block(z, s):
            return wide[z * C : (z + 1) * C, s * 2 * C : (s + 1) * 2 * C]

        low = jnp.where(lanes_low, block(1, 0) + block(3, 1), block(0, 2) + block(2, 0))
        mid = jnp.where(lanes_low, block(0, 0) + block(2, 1), block(1, 0) + block(3, 1))
        high = jnp.where(lanes_low, block(1, 1) + block(3, 2), block(0, 0) + block(2, 1))
        for value in (low, mid, high):
            sums.append(value + pltpu.roll(value, C, 1))
    sums.append(jnp.zeros((C, 2 * C), F32))
    pairs = [jnp.where(lanes_low, sums[2 * k], sums[2 * k + 1]) for k in range(8)]
    for p in range(7):
        at = up_lanes + p * 2 * C
        out_ref[:, at : at + 2 * C] = jnp.where(group == 0, pairs[p], pairs[p + 1]).astype(out_ref.dtype)


def kept_sums_body(pad_ref, turned_ref, up_sums_ref, lists_ref, kept_ref):
    half_sums(lists_ref[5, GX], pad_ref, turned_ref, up_sums_ref, kept_ref)


def pair_sum_body(kept_ref, given_ref, out_ref):
    out_ref[...] = (kept_ref[...] + given_ref[...].astype(F32)).astype(BF)


def inputs_at(pad_ref, e):
    bricks = pad_ref.shape[2]
    ex, ey = (e // 3, e % 3)
    return pad_ref[ex : ex + 4, ey : ey + 4].reshape(16 * bricks, WIDE)


def conv_body(pad_ref, weight_ref, lists_ref, out_ref, again_ref, band_ref):
    again_ref[...] = lists_ref[...]
    bricks = pad_ref.shape[2]
    build_bands(weight_ref, band_ref)
    total = None
    for e in range(9):
        part = dot(inputs_at(pad_ref, e), band_ref[e])
        total = part if total is None else total + part
    for p in range(16):
        out_ref[:, p * RUN : (p + 1) * RUN] = total[p * bricks : (p + 1) * bricks].astype(BF)


def add_rows(base, lists, first, second):
    count, face = (base.shape[0], lists.shape[1])
    index = jnp.concatenate([lists[0:1], lists[1:2]], axis=1)
    chosen = ones_where(iota((count, 2 * face), 0) == index)
    return base + dot(chosen, stack_rows(first, second))


def merge_body(received_ref, up_ref, fine_ref, lists_ref, merged_ref, parents_ref, a_ref, b_ref):
    bricks, width = fine_ref.shape
    face = a_ref.shape[0]
    parents = merge(received_ref, slots_of(lists_ref, bricks), up_ref, fine_ref, merged_ref, parents_ref)
    lists = sides_of(lists_ref, face)
    lists = by_pair(lists_ref, GY, lists[0:1], lists[1:2])
    for out_ref, rows, owners in zip((a_ref, b_ref), pick_rows(lists, merged_ref[...]), pick_rows(lists, parents)):
        out_ref[:, :width] = rows.astype(BF)
        out_ref[:, width:] = owners.astype(BF)


def fine_grad_body(part_ref, lists_ref, even_ref, odd_ref, up_ref, grad_ref, replies_ref, across):
    bricks = part_ref.shape[0]
    face = even_ref.shape[0]
    from_next, from_prev = from_pairs(lists_ref, GY, even_ref, odd_ref)
    total = add_rows(part_ref[...], sides_of(lists_ref, face), from_next, from_prev)
    grad_ref[...] = total.astype(BF)
    items = dot(stack_parities(grad_ref[...]), up_ref[...]).astype(BF)
    items = jnp.concatenate([items[v * bricks : (v + 1) * bricks] for v in range(8)], axis=1)
    half = items.shape[1] // 2
    count, both_lanes = replies_ref.shape
    pieces = both_lanes // 2 // half
    capacity, group = chip_slots(count, pieces, across)
    slots = slots_of(lists_ref, bricks)
    row = iota((count, bricks), 0)
    for other in range(2):
        owner = device_of(row // group, lists_ref, other, across)
        for j in range(pieces):
            piece = row % group * pieces + j
            named = owner * capacity + piece // 2 == slots
            rows = dot(ones_where(named & (piece % 2 == 0)), items[:, :half])
            rows += dot(ones_where(named & (piece % 2 == 1)), items[:, half:])
            at = (other * pieces + j) * half
            replies_ref[:, at : at + half] = rows.astype(BF)


def chip_slots(count, pieces, across):
    group = count // (across[0] * across[1] // 2)
    return group * pieces // 2, group


def device_of(chip, lists_ref, other, across):
    core = jnp.broadcast_to(lists_ref[5:6, GX : GX + 1], chip.shape)
    core = 1 - core if other else core
    return (chip // across[1] * 2 + core) * across[1] + chip % across[1]


def share_body(sums_ref, replies_ref, out_ref, across):
    count, item_lanes = replies_ref.shape
    share = count // (across[0] * across[1] // 2)
    same = iota((count, count), 0) % share == iota((count, count), 1) % share
    out_ref[:, :item_lanes] = replies_ref[...]
    out_ref[:, item_lanes:] = dot(ones_where(same), sums_ref[...]).astype(BF)


def coarse_grad(arrivals, sends_ref, lists_ref, out_ref, across):
    capacity, devices = sends_ref.shape
    count, item_width = out_ref.shape
    half = item_width // 2
    lanes = arrivals[0].shape[0]
    pieces = arrivals[0].shape[1] // half
    _, group = chip_slots(lanes, pieces, across)
    sends = sends_ref[...].astype(F32).astype(BF)
    lane = iota((1, lanes), 1)
    totals = [None, None]
    for other in range(2):
        source = device_of(lane // group, lists_ref, other, across)
        rows = dot(sends, ones_where(source == iota((devices, lanes), 0)))
        for j in range(pieces):
            piece = lane % group * pieces + j
            picked = jnp.where(piece // 2 == iota((capacity, lanes), 0), rows, 0.0)
            index = jnp.sum(picked, axis=0, keepdims=True).astype(I32)
            named = iota((count, lanes), 0) == index
            for h in range(2):
                part = dot(ones_where(named & (piece % 2 == h)), arrivals[other][:, j * half : (j + 1) * half])
                totals[h] = part if totals[h] is None else totals[h] + part
    for h in range(2):
        out_ref[:, h * half : (h + 1) * half] = totals[h].astype(BF)


def last_body(back_ref, given_ref, sends_ref, lists_ref, conv_ref, up_ref, out_ref, item_lanes, across, scale):
    half_count = back_ref.shape[0]
    items = (back_ref[:, :item_lanes], given_ref[:, item_lanes : 2 * item_lanes])
    coarse_grad(items, sends_ref, lists_ref, out_ref, across)
    coarse = up_ref.shape[1]
    count = 2 * half_count
    parts = up_ref.shape[0] // count
    own = back_ref[:, 2 * item_lanes :].astype(F32) * scale
    others = given_ref[:, 2 * item_lanes :].astype(F32) * scale
    first, second = by_pair(lists_ref, GX, own, others)
    at = 0
    for q in range(parts):
        up_ref[q * count : q * count + half_count] = first[:, at : at + coarse]
        up_ref[q * count + half_count : (q + 1) * count] = second[:, at : at + coarse]
        at += coarse
    for pair in range(7):
        turned = jnp.concatenate([first[:, at : at + 2 * C], second[:, at : at + 2 * C]], axis=0).T
        at += 2 * C
        for h in range(2):
            for s in range(2):
                o = 14 * h + 2 * pair + s
                if o < 27:
                    conv_ref[o] = turned[s * C : (s + 1) * C, h * C : (h + 1) * C]


def swap(value, axis, first):
    count = lax.axis_size(axis)
    lower = range(first, count - 1, 2)
    return lax.ppermute(value, axis, [(i, i + 1) for i in lower] + [(i + 1, i) for i in lower])


def swap_pairs(to_even, to_odd, axis):
    return swap(to_even, axis, 0), swap(to_odd, axis, 1)


def trade_rows(values, axes):
    rows, width = values.shape
    devices = math.prod(lax.axis_size(axis) for axis in axes)
    grid_view = values.reshape(devices, rows // devices, width)
    return lax.all_to_all(grid_view, axes, split_axis=0, concat_axis=0, tiled=True).reshape(rows, width)


def on_device(
    fine_features, coarse_items, conv_weight, up_weight, neighbours,
    side_sends, cross_sends, parent_slots, coarse_sends, cotangent,
):
    fine = fine_features[0, 0]
    items = coarse_items[0, 0]
    cot = cotangent[0, 0]
    bricks, width = fine.shape
    face = side_sends.shape[-1]
    across = (lax.axis_size(GX_AXES), lax.axis_size("gy"))
    devices = across[0] * across[1]
    capacity = coarse_sends.shape[-1]
    item_count, item_width = items.shape
    coarse = up_weight.shape[1]
    start = bricks + 2 * face
    sends = coarse_sends.transpose(0, 1, 3, 2)[0, 0]
    slots = parent_slots[0]
    sides = side_sends[0, 0]
    crosses = cross_sends[0, 0]
    near = neighbours.transpose(0, 3, 1, 2)[0]
    up_turned = up_weight.transpose(0, 2, 1).reshape(8 * C, coarse)
    half = item_width // 2
    count = 2 * C
    item_lanes = capacity * devices // 2 * item_width // (count // 2)
    sums_width = 8 * C * coarse // count + 14 * C
    rows = shape((bricks, width))
    face_rows = shape((face, width))
    faces_and_parents = shape((face, width + item_width))
    lists_shape = shape((8, 128), I32)
    band = pltpu.VMEM((9, WIDE, RUN), BF)
    conv_flops = 2 * 9 * 16 * bricks * WIDE * RUN

    listed = (sends, items, sides, crosses, slots)
    outgoing, lists = call(
        first_body, [shape((2 * capacity * devices, half)), lists_shape], *listed,
        scratch=[pltpu.VMEM(a.shape, a.dtype) for a in listed] + [pltpu.SemaphoreType.DMA((len(listed),))],
        in_hbm=True,
    )
    received = trade_rows(outgoing, ("x", "core", "gy"))
    lane = jnp.arange(128, dtype=I32)[None]
    parity = jnp.where(lane == GX, lax.axis_index("core"), lax.axis_index("gy") % 2).astype(I32)
    table_rows = start + 2 * face
    ext_grad, to_even, to_odd, turned, mains, ends, lists = call(
        table_grad_body,
        [
            shape((start, width), F32), face_rows, face_rows, shape((RUN, 16 * bricks)),
            shape((9, bricks, table_rows)), shape((9, bricks, 2 * table_rows)), lists_shape,
        ],
        cot, conv_weight, near, lists, parity,
        scratch=[band, pltpu.VMEM((6, 6, bricks, WIDE), F32)], flops=2 * conv_flops,
    )
    cross_grads = swap_pairs(to_even, to_odd, GX_AXES)
    merged, parents, to_even, to_odd = call(
        merge_body, [rows, shape((8 * bricks, coarse)), faces_and_parents, faces_and_parents],
        received, up_turned, fine, lists,
    )
    sides = swap_pairs(to_even, to_odd, "gy")
    to_even, to_odd = call(cross_body, [face_rows, face_rows], merged, *sides, lists)
    crosses = swap_pairs(to_even, to_odd, GX_AXES)
    half_sums_dims = (count // 2, sums_width)
    fine_part, to_even, to_odd, up_sums = call(
        side_grad_body,
        [shape((bricks, width), F32), face_rows, face_rows, shape((count, sums_width - 14 * C), F32)],
        ext_grad, lists, *cross_grads, *sides, parents,
    )
    side_grads = swap_pairs(to_even, to_odd, "gy")
    given, pad = call(
        given_sums_body, [shape(half_sums_dims), shape((6, 6, bricks, WIDE))],
        *crosses[::-1], merged, *sides, turned, mains, ends, lists, up_sums,
        scratch=[pltpu.VMEM((table_rows, width), BF)], flops=conv_flops,
    )
    (kept,) = call(kept_sums_body, [shape(half_sums_dims, F32)], pad, turned, up_sums, lists, flops=conv_flops)
    given = swap(given, "core", 0)
    (sums,) = call(pair_sum_body, [shape(half_sums_dims)], kept, given)
    sums = trade_rows(sums, ("x", "gy"))
    output, lists = call(
        conv_body, [rows, lists_shape], pad, conv_weight, lists, scratch=[band], flops=conv_flops
    )
    grad_fine, replies = call(
        functools.partial(fine_grad_body, across=across), [rows, shape((count // 2, 2 * item_lanes))],
        fine_part, lists, *side_grads, up_turned,
    )
    (back,) = call(
        functools.partial(share_body, across=across), [shape((count // 2, 2 * item_lanes + sums_width))], sums, replies
    )
    back = trade_rows(back, ("x", "gy"))
    given = swap(back, "core", 0)
    scale = 1.0 / math.sqrt(64 * bricks * devices)
    grad_conv, grad_up, coarse_grad = call(
        functools.partial(last_body, item_lanes=item_lanes, across=across, scale=scale),
        [shape((27, C, C), F32), shape((8 * C, coarse), F32), shape((item_count, item_width))],
        back, given, sends, lists,
    )
    return (
        output.reshape(1, 1, bricks, width),
        grad_fine.reshape(1, 1, bricks, width),
        coarse_grad.reshape(1, 1, item_count, item_width),
        grad_conv,
        grad_up.reshape(8, C, coarse).transpose(0, 2, 1),
    )


def solution(mesh):
    groups, across_x, across_y = mesh.devices.shape
    split_mesh = Mesh(mesh.devices.reshape(groups, across_x // 2, 2, across_y), ("groups", "x", "core", "gy"))
    rows = ("groups", "x", "core")
    split = P(rows, "gy", None, None)
    placed = (split, split, P(), P(), split, split, split, P(rows, "gy", None), split, split)
    return jax.shard_map(
        on_device,
        mesh=split_mesh,
        in_specs=placed,
        out_specs=(split, split, split, P("groups", None, None), P("groups", None, None)),
        check_vma=False,
    )
```

```python
import functools
import math

import jax
import jax.numpy as jnp
from jax import lax
from jax.experimental import pallas as pl
from jax.experimental.pallas import tpu as pltpu
from jax.sharding import Mesh
from jax.sharding import PartitionSpec as P

BF = jnp.bfloat16
F32 = jnp.float32
I32 = jnp.int32

C = 64
RUN = 4 * C
WIDE = RUN + 2 * C


def iota(shape, axis):
    return lax.broadcasted_iota(I32, shape, axis)


def ones_where(mask):
    return jnp.where(mask, 1.0, 0.0).astype(BF)


def dot(a, b):
    return jnp.dot(a, b, preferred_element_type=F32)


def dot_tn(a, b):
    return lax.dot_general(a, b, (((0,), (0,)), ((), ())), preferred_element_type=F32)


def dot_nt(a, b):
    return lax.dot_general(a, b, (((1,), (1,)), ((), ())), preferred_element_type=F32)


def column_of(row):
    size = row.shape[1]
    diagonal = iota((size, size), 0) == iota((size, size), 1)
    spread = jnp.broadcast_to(row.astype(F32), (size, size))
    return jnp.sum(jnp.where(diagonal, spread, 0.0), axis=1, keepdims=True).astype(I32)


def call(body, outs, *args, scratch=(), flops=0, in_hbm=False):
    moved = sum(a.size * a.dtype.itemsize for a in list(args) + list(outs))
    return pl.pallas_call(
        body,
        out_shape=tuple(outs),
        in_specs=[pl.BlockSpec(memory_space=pltpu.HBM) if in_hbm else pl.BlockSpec() for _ in args],
        scratch_shapes=tuple(scratch),
        cost_estimate=pl.CostEstimate(flops=flops, bytes_accessed=moved, transcendentals=0),
        compiler_params=pltpu.CompilerParams(vmem_limit_bytes=None if in_hbm else 28 * 2**20),
    )(*args)


def shape(dims, dtype=BF):
    return jax.ShapeDtypeStruct(dims, dtype)


def items_named(sends_ref, count):
    capacity, devices = sends_ref.shape
    group = 2 * capacity
    lanes = devices * group
    spread = ones_where(iota((lanes, devices), 0) // group == iota((lanes, devices), 1))
    slot = iota((lanes, capacity), 0) % group // 2
    values = dot_nt(spread, sends_ref[...].astype(F32).astype(BF))
    item = jnp.sum(jnp.where(slot == iota((lanes, capacity), 1), values, 0.0), axis=1, keepdims=True).astype(I32)
    place = jnp.where(item < count, item + iota((lanes, 1), 0) % 2 * count, -1)
    return ones_where(iota((lanes, 2 * count), 1) == place)


def merge(received_ref, slots, up_ref, fine_ref, merged_ref, parents_ref):
    bricks = fine_ref.shape[0]
    lanes, half = received_ref.shape
    slot = column_of(slots)
    place = iota((bricks, lanes), 1)
    named = place // 2 == slot
    received = received_ref[...]
    parents = jnp.concatenate(
        [dot(ones_where(named & (place % 2 == h)), received) for h in (0, 1)], axis=1
    ).astype(BF)
    coarse = 2 * half // 8
    stacked = jnp.concatenate([parents[:, v * coarse : (v + 1) * coarse] for v in range(8)], axis=0)
    parents_ref[...] = stacked
    lifted = dot_nt(stacked, up_ref[...])
    for v in range(8):
        cx, cy, cz = (v // 4, v // 2 % 2, v % 2)
        for parity in range(4):
            vx, vy = (2 * cx + parity // 2, 2 * cy + parity % 2)
            at = (vx * 4 + vy) * RUN + cz * 2 * C
            add = lifted[v * bricks : (v + 1) * bricks, parity * 2 * C : (parity + 1) * 2 * C]
            merged_ref[:, at : at + 2 * C] = (fine_ref[:, at : at + 2 * C].astype(F32) + add).astype(BF)
    return parents


def pick_rows(lists, rows):
    return [dot_tn(ones_where(iota((rows.shape[0], one.shape[1]), 0) == one), rows) for one in lists]


GX, GY = (0, 1)
GX_AXES = ("x", "core")


def by_pair(lists_ref, axis, of_next, of_prev):
    odd = jnp.broadcast_to(lists_ref[5:6, axis : axis + 1], of_next.shape) == 1
    return jnp.where(odd, of_prev, of_next), jnp.where(odd, of_next, of_prev)


def from_pairs(lists_ref, axis, even_ref, odd_ref):
    return by_pair(lists_ref, axis, even_ref[...].astype(F32), odd_ref[...].astype(F32))


def stack_rows(*parts):
    return jnp.concatenate([p.astype(F32) for p in parts], axis=0).astype(BF)


def sides_of(lists_ref, face):
    return lists_ref[0:2, :face]


def crosses_of(lists_ref, face):
    return lists_ref[2:4, :face]


def slots_of(lists_ref, bricks):
    return lists_ref[4:5, :bricks]


def cross_body(merged_ref, even_ref, odd_ref, lists_ref, a_ref, b_ref):
    face, width = a_ref.shape
    high, low = from_pairs(lists_ref, GY, even_ref, odd_ref)
    rows = jnp.concatenate([merged_ref[...], stack_rows(low[:, :width], high[:, :width])], axis=0)
    lists = crosses_of(lists_ref, face)
    picked = pick_rows(by_pair(lists_ref, GX, lists[0:1], lists[1:2]), rows)
    a_ref[...] = picked[0].astype(BF)
    b_ref[...] = picked[1].astype(BF)


def build_bands(weight_ref, band_ref):
    zero = jnp.zeros((C, C), BF)
    blank = jnp.zeros((C, 2 * C), BF)

    def pair(a, b):
        return jnp.concatenate([a, b], axis=1)

    for e in range(9):
        low, mid, high = (weight_ref[3 * e + z] for z in range(3))
        first, second = (pair(mid, low), pair(high, mid))
        left, right = (pair(low, zero), pair(zero, high))
        rows = (
            (first, blank),
            (second, left),
            (right, first),
            (blank, second),
            (blank, right),
            (left, blank),
        )
        for z, halves in enumerate(rows):
            for s in range(2):
                band_ref[e, z * C : (z + 1) * C, s * 2 * C : (s + 1) * 2 * C] = halves[s]


def options(at):
    return [(at + 1, 0)] + ([(5, 1)] if at == 0 else []) + ([(0, -1)] if at == 3 else [])


def offset_of(dx, dy, dz):
    return (dx + 1) * 9 + (dy + 1) * 3 + dz + 1


def stack_lanes(value, lanes):
    return jnp.concatenate([value[:, p * lanes : (p + 1) * lanes] for p in range(value.shape[1] // lanes)], axis=0)


def stack_parities(value):
    stacked = []
    for v in range(8):
        cx, cy, cz = (v // 4, v // 2 % 2, v % 2)
        lanes = []
        for parity in range(4):
            at = ((2 * cx + parity // 2) * 4 + 2 * cy + parity % 2) * RUN + cz * 2 * C
            lanes.append(value[:, at : at + 2 * C])
        stacked.append(jnp.concatenate(lanes, axis=1))
    return jnp.concatenate(stacked, axis=0)


def stack_runs(ref):
    return jnp.concatenate([ref[:, p * RUN : (p + 1) * RUN] for p in range(16)], axis=0)


def split_two(value):
    head = value.astype(BF)
    return head, (value - head.astype(F32)).astype(BF)


def table_grad_body(
    cot_ref, weight_ref, near_ref, lists_ref, parity_ref,
    ext_ref, even_ref, odd_ref, turned_ref, mains_ref, ends_ref, again_ref, band_ref, pad_ref,
):
    again_ref[...] = lists_ref[...]
    again_ref[5:6] = parity_ref[...]
    bricks = cot_ref.shape[0]
    face = even_ref.shape[0]
    start = ext_ref.shape[0]
    rows = start + 2 * face
    build_bands(weight_ref, band_ref)
    cot = stack_runs(cot_ref)
    turned_ref[...] = cot.T
    pad_ref[...] = jnp.zeros(pad_ref.shape, F32)
    for e in range(9):
        ex, ey = (e // 3, e % 3)
        part = dot_nt(cot, band_ref[e]).reshape(4, 4, bricks, WIDE)
        pad_ref[ex : ex + 4, ey : ey + 4] += part
    near = [near_ref[o] for o in range(27)]

    def chooser(which):
        index = jnp.concatenate([near[o] for o in which], axis=1)
        return ones_where(iota((rows, index.shape[1]), 0) == index)

    lower_half = iota((rows, 2 * C), 1) < C
    cache = {}
    for x in range(4):
        for y in range(4):
            places = [(X, Y, dx, dy) for X, dx in options(x) for Y, dy in options(y)]
            key = tuple((dx, dy) for _, _, dx, dy in places)
            if key not in cache:
                moved = [d for d in key if d != (0, 0)]
                main = chooser([offset_of(*d, 0) for d in moved] * 2) if moved else None
                up = chooser([offset_of(*d, 1) for d in key] * 2)
                down = chooser([offset_of(*d, -1) for d in key] * 2)
                cache[key] = (main, jnp.concatenate([up, down], axis=0))
            main, ends = cache[key]
            own = pad_ref[x + 1, y + 1, :, :RUN]
            own = jnp.concatenate([own, jnp.zeros((rows - bricks, RUN), F32)], axis=0)
            if main is not None:
                parts = [split_two(pad_ref[X, Y, :, :RUN]) for X, Y, dx, dy in places if (dx, dy) != (0, 0)]
                value = jnp.concatenate([p[0] for p in parts] + [p[1] for p in parts], axis=0)
                own += dot(main, value)
            parts = [split_two(pad_ref[X, Y, :, RUN:]) for X, Y, _, _ in places]
            value = jnp.concatenate([p[0] for p in parts] + [p[1] for p in parts], axis=0)
            halo = dot(ends, value)
            first = own[:, : 2 * C] + jnp.where(lower_half, halo[:rows], 0.0)
            second = own[:, 2 * C :] + jnp.where(lower_half, 0.0, halo[rows:])
            total = jnp.concatenate([first, second], axis=1)
            at = (x * 4 + y) * RUN
            ext_ref[:, at : at + RUN] = total[:start]
            even, odd = by_pair(again_ref, GX, total[start + face :], total[start : start + face])
            even_ref[:, at : at + RUN] = even.astype(BF)
            odd_ref[:, at : at + RUN] = odd.astype(BF)
    make_choosers(near_ref, rows, mains_ref, ends_ref)


def make_choosers(near_ref, rows, mains_ref, ends_ref):
    bricks = mains_ref.shape[1]
    near = jnp.concatenate([near_ref[o] for o in range(27)] + [jnp.zeros((5, bricks), I32)], axis=0)
    near = near.astype(F32).T.astype(I32)
    place = iota((bricks, rows), 1)
    pair_place = iota((bricks, 2 * rows), 1)
    for d in range(9):
        down, straight, up = (near[:, 3 * d + z : 3 * d + z + 1] for z in range(3))
        mains_ref[d] = ones_where(place == straight)
        ends_ref[d] = ones_where(pair_place == jnp.where(pair_place < rows, up, down + rows))


def first_body(
    sends_hbm, items_hbm, sides_hbm, crosses_hbm, slots_hbm, out_ref, lists_ref,
    sends_ref, items_ref, sides_ref, crosses_ref, slots_ref, arrived,
):
    sources = (sends_hbm, items_hbm, sides_hbm, crosses_hbm, slots_hbm)
    places = (sends_ref, items_ref, sides_ref, crosses_ref, slots_ref)
    copies = [pltpu.make_async_copy(s, p, arrived.at[i]) for i, (s, p) in enumerate(zip(sources, places))]
    for copy in copies:
        copy.start()
    copies[0].wait()
    chosen = items_named(sends_ref, items_ref.shape[0])
    copies[1].wait()
    half = out_ref.shape[1]
    items = jnp.concatenate([items_ref[:, :half], items_ref[:, half:]], axis=0)
    out_ref[...] = dot(chosen, items).astype(BF)
    for copy in copies[2:]:
        copy.wait()
    face, bricks = (sides_ref.shape[1], slots_ref.shape[1])
    lists_ref[...] = jnp.zeros(lists_ref.shape, I32)
    lists_ref[0:2, :face] = sides_ref[...]
    lists_ref[2:4, :face] = crosses_ref[...]
    lists_ref[4:5, :bricks] = slots_ref[...]


def side_grad_body(
    odd_grad_ref, even_grad_ref, ext_ref, lists_ref, even_side_ref, odd_side_ref, parents_ref,
    part_ref, to_even_ref, to_odd_ref, up_sums_ref,
):
    bricks, width = part_ref.shape
    face = to_even_ref.shape[0]
    from_next, from_prev = from_pairs(lists_ref, GX, even_grad_ref, odd_grad_ref)
    total = add_rows(ext_ref[...], crosses_of(lists_ref, face), from_next, from_prev)
    part_ref[...] = total[:bricks]
    to_even, to_odd = by_pair(lists_ref, GY, total[bricks + face :], total[bricks : bricks + face])
    to_even_ref[...] = to_even.astype(BF)
    to_odd_ref[...] = to_odd.astype(BF)
    high, low = by_pair(
        lists_ref, GY, even_side_ref[:, width:].astype(F32), odd_side_ref[:, width:].astype(F32)
    )
    side_parents = stack_lanes(stack_rows(low, high), parents_ref.shape[1])
    grads = [stack_parities(total[:bricks].astype(BF)), stack_parities(total[bricks:].astype(BF))]
    up_sum = dot_tn(jnp.concatenate(grads, axis=0), jnp.concatenate([parents_ref[...], side_parents], axis=0))
    coarse = up_sum.shape[1]
    count = up_sums_ref.shape[0]
    for q in range(up_sum.shape[0] // count):
        up_sums_ref[:, q * coarse : (q + 1) * coarse] = up_sum[q * count : (q + 1) * count]


def given_sums_body(
    odd_cross_ref, even_cross_ref, merged_ref, even_side_ref, odd_side_ref, turned_ref, mains_ref, ends_ref, lists_ref,
    up_sums_ref, given_ref, pad_ref, table_ref,
):
    bricks, width = merged_ref.shape
    face = even_side_ref.shape[0]
    rows = bricks + 4 * face
    high, low = by_pair(lists_ref, GY, even_side_ref[:, :width].astype(F32), odd_side_ref[:, :width].astype(F32))
    above, below = from_pairs(lists_ref, GX, even_cross_ref, odd_cross_ref)
    table_ref[:bricks] = merged_ref[...]
    table_ref[bricks:] = stack_rows(low, high, below, above)
    lower_half = iota((rows, 2 * C), 1) < C
    zero = jnp.zeros((rows, 2 * C), BF)
    for x in range(4):
        for y in range(4):
            places = [(X, Y, dx, dy) for X, dx in options(x) for Y, dy in options(y)]
            at = (x * 4 + y) * RUN
            columns = table_ref[:, at : at + RUN]
            first = jnp.where(lower_half, columns[:, : 2 * C], zero)
            second = jnp.where(lower_half, zero, columns[:, 2 * C :])
            ends = jnp.concatenate([ends_ref[3 * dx + dy + 4] for _, _, dx, dy in places], axis=0)
            halo = dot(ends, jnp.concatenate([first, second], axis=0)).astype(BF)
            for i, (X, Y, _, _) in enumerate(places):
                pad_ref[X, Y, :, RUN:] = halo[i * bricks : (i + 1) * bricks]
            pad_ref[x + 1, y + 1, :, :RUN] = columns[:bricks]
            moved = [p for p in places if p[2:] != (0, 0)]
            if moved:
                main = jnp.concatenate([mains_ref[3 * dx + dy + 4] for _, _, dx, dy in moved], axis=0)
                got = dot(main, columns).astype(BF)
                for i, (X, Y, _, _) in enumerate(moved):
                    pad_ref[X, Y, :, :RUN] = got[i * bricks : (i + 1) * bricks]

    half_sums(1 - lists_ref[5, GX], pad_ref, turned_ref, up_sums_ref, given_ref)


def half_sums(group, pad_ref, turned_ref, up_sums_ref, out_ref):
    turned = turned_ref[...]
    half_count = out_ref.shape[0]
    up_lanes = up_sums_ref.shape[1]
    up_half = jnp.where(group == 0, up_sums_ref[:half_count], up_sums_ref[half_count:])
    out_ref[:, :up_lanes] = up_half.astype(out_ref.dtype)
    bricks = pad_ref.shape[2]
    lanes_low = iota((C, 2 * C), 1) < C
    sums = []
    for i in range(5):
        ex, ey = (jnp.where(group == 0, i // 3, (i + 4) // 3), jnp.where(group == 0, i % 3, (i + 4) % 3))
        wide = dot(turned, pad_ref[pl.ds(ex, 4), pl.ds(ey, 4)].reshape(16 * bricks, WIDE))

        def block(z, s):
            return wide[z * C : (z + 1) * C, s * 2 * C : (s + 1) * 2 * C]

        low = jnp.where(lanes_low, block(1, 0) + block(3, 1), block(0, 2) + block(2, 0))
        mid = jnp.where(lanes_low, block(0, 0) + block(2, 1), block(1, 0) + block(3, 1))
        high = jnp.where(lanes_low, block(1, 1) + block(3, 2), block(0, 0) + block(2, 1))
        for value in (low, mid, high):
            sums.append(value + pltpu.roll(value, C, 1))
    sums.append(jnp.zeros((C, 2 * C), F32))
    pairs = [jnp.where(lanes_low, sums[2 * k], sums[2 * k + 1]) for k in range(8)]
    for p in range(7):
        at = up_lanes + p * 2 * C
        out_ref[:, at : at + 2 * C] = jnp.where(group == 0, pairs[p], pairs[p + 1]).astype(out_ref.dtype)


def kept_sums_body(pad_ref, turned_ref, up_sums_ref, lists_ref, kept_ref):
    half_sums(lists_ref[5, GX], pad_ref, turned_ref, up_sums_ref, kept_ref)


def pair_sum_body(kept_ref, given_ref, out_ref):
    out_ref[...] = (kept_ref[...] + given_ref[...].astype(F32)).astype(BF)


def inputs_at(pad_ref, e):
    bricks = pad_ref.shape[2]
    ex, ey = (e // 3, e % 3)
    return pad_ref[ex : ex + 4, ey : ey + 4].reshape(16 * bricks, WIDE)


def conv_body(pad_ref, weight_ref, lists_ref, out_ref, again_ref, band_ref):
    again_ref[...] = lists_ref[...]
    bricks = pad_ref.shape[2]
    build_bands(weight_ref, band_ref)
    total = None
    for e in range(9):
        part = dot(inputs_at(pad_ref, e), band_ref[e])
        total = part if total is None else total + part
    for p in range(16):
        out_ref[:, p * RUN : (p + 1) * RUN] = total[p * bricks : (p + 1) * bricks].astype(BF)


def add_rows(base, lists, first, second):
    count, face = (base.shape[0], lists.shape[1])
    index = jnp.concatenate([lists[0:1], lists[1:2]], axis=1)
    chosen = ones_where(iota((count, 2 * face), 0) == index)
    return base + dot(chosen, stack_rows(first, second))


def merge_body(received_ref, up_ref, fine_ref, lists_ref, merged_ref, parents_ref, a_ref, b_ref):
    bricks, width = fine_ref.shape
    face = a_ref.shape[0]
    parents = merge(received_ref, slots_of(lists_ref, bricks), up_ref, fine_ref, merged_ref, parents_ref)
    lists = sides_of(lists_ref, face)
    lists = by_pair(lists_ref, GY, lists[0:1], lists[1:2])
    for out_ref, rows, owners in zip((a_ref, b_ref), pick_rows(lists, merged_ref[...]), pick_rows(lists, parents)):
        out_ref[:, :width] = rows.astype(BF)
        out_ref[:, width:] = owners.astype(BF)


def fine_grad_body(part_ref, lists_ref, even_ref, odd_ref, up_ref, grad_ref, replies_ref, across):
    bricks = part_ref.shape[0]
    face = even_ref.shape[0]
    from_next, from_prev = from_pairs(lists_ref, GY, even_ref, odd_ref)
    total = add_rows(part_ref[...], sides_of(lists_ref, face), from_next, from_prev)
    grad_ref[...] = total.astype(BF)
    items = dot(stack_parities(grad_ref[...]), up_ref[...]).astype(BF)
    items = jnp.concatenate([items[v * bricks : (v + 1) * bricks] for v in range(8)], axis=1)
    half = items.shape[1] // 2
    count, both_lanes = replies_ref.shape
    pieces = both_lanes // 2 // half
    capacity, group = chip_slots(count, pieces, across)
    slots = slots_of(lists_ref, bricks)
    row = iota((count, bricks), 0)
    for other in range(2):
        owner = device_of(row // group, lists_ref, other, across)
        for j in range(pieces):
            piece = row % group * pieces + j
            named = owner * capacity + piece // 2 == slots
            rows = dot(ones_where(named & (piece % 2 == 0)), items[:, :half])
            rows += dot(ones_where(named & (piece % 2 == 1)), items[:, half:])
            at = (other * pieces + j) * half
            replies_ref[:, at : at + half] = rows.astype(BF)


def chip_slots(count, pieces, across):
    group = count // (across[0] * across[1] // 2)
    return group * pieces // 2, group


def device_of(chip, lists_ref, other, across):
    core = jnp.broadcast_to(lists_ref[5:6, GX : GX + 1], chip.shape)
    core = 1 - core if other else core
    return (chip // across[1] * 2 + core) * across[1] + chip % across[1]


def share_body(sums_ref, replies_ref, out_ref, across):
    count, item_lanes = replies_ref.shape
    share = count // (across[0] * across[1] // 2)
    same = iota((count, count), 0) % share == iota((count, count), 1) % share
    out_ref[:, :item_lanes] = replies_ref[...]
    out_ref[:, item_lanes:] = dot(ones_where(same), sums_ref[...]).astype(BF)


def coarse_grad(arrivals, sends_ref, lists_ref, out_ref, across):
    capacity, devices = sends_ref.shape
    count, item_width = out_ref.shape
    half = item_width // 2
    lanes = arrivals[0].shape[0]
    pieces = arrivals[0].shape[1] // half
    _, group = chip_slots(lanes, pieces, across)
    sends = sends_ref[...].astype(F32).astype(BF)
    lane = iota((1, lanes), 1)
    totals = [None, None]
    for other in range(2):
        source = device_of(lane // group, lists_ref, other, across)
        rows = dot(sends, ones_where(source == iota((devices, lanes), 0)))
        for j in range(pieces):
            piece = lane % group * pieces + j
            picked = jnp.where(piece // 2 == iota((capacity, lanes), 0), rows, 0.0)
            index = jnp.sum(picked, axis=0, keepdims=True).astype(I32)
            named = iota((count, lanes), 0) == index
            for h in range(2):
                part = dot(ones_where(named & (piece % 2 == h)), arrivals[other][:, j * half : (j + 1) * half])
                totals[h] = part if totals[h] is None else totals[h] + part
    for h in range(2):
        out_ref[:, h * half : (h + 1) * half] = totals[h].astype(BF)


def last_body(back_ref, given_ref, sends_ref, lists_ref, conv_ref, up_ref, out_ref, item_lanes, across, scale):
    half_count = back_ref.shape[0]
    items = (back_ref[:, :item_lanes], given_ref[:, item_lanes : 2 * item_lanes])
    coarse_grad(items, sends_ref, lists_ref, out_ref, across)
    coarse = up_ref.shape[1]
    count = 2 * half_count
    parts = up_ref.shape[0] // count
    own = back_ref[:, 2 * item_lanes :].astype(F32) * scale
    others = given_ref[:, 2 * item_lanes :].astype(F32) * scale
    first, second = by_pair(lists_ref, GX, own, others)
    at = 0
    for q in range(parts):
        up_ref[q * count : q * count + half_count] = first[:, at : at + coarse]
        up_ref[q * count + half_count : (q + 1) * count] = second[:, at : at + coarse]
        at += coarse
    for pair in range(7):
        turned = jnp.concatenate([first[:, at : at + 2 * C], second[:, at : at + 2 * C]], axis=0).T
        at += 2 * C
        for h in range(2):
            for s in range(2):
                o = 14 * h + 2 * pair + s
                if o < 27:
                    conv_ref[o] = turned[s * C : (s + 1) * C, h * C : (h + 1) * C]


def swap(value, axis, first):
    count = lax.axis_size(axis)
    lower = range(first, count - 1, 2)
    return lax.ppermute(value, axis, [(i, i + 1) for i in lower] + [(i + 1, i) for i in lower])


def swap_pairs(to_even, to_odd, axis):
    return swap(to_even, axis, 0), swap(to_odd, axis, 1)


def trade_rows(values, axes):
    rows, width = values.shape
    devices = math.prod(lax.axis_size(axis) for axis in axes)
    grid_view = values.reshape(devices, rows // devices, width)
    return lax.all_to_all(grid_view, axes, split_axis=0, concat_axis=0, tiled=True).reshape(rows, width)


def on_device(
    fine_features, coarse_items, conv_weight, up_weight, neighbours,
    side_sends, cross_sends, parent_slots, coarse_sends, cotangent,
):
    fine = fine_features[0, 0]
    items = coarse_items[0, 0]
    cot = cotangent[0, 0]
    bricks, width = fine.shape
    face = side_sends.shape[-1]
    across = (lax.axis_size(GX_AXES), lax.axis_size("gy"))
    devices = across[0] * across[1]
    capacity = coarse_sends.shape[-1]
    item_count, item_width = items.shape
    coarse = up_weight.shape[1]
    start = bricks + 2 * face
    sends = coarse_sends.transpose(0, 1, 3, 2)[0, 0]
    slots = parent_slots[0]
    sides = side_sends[0, 0]
    crosses = cross_sends[0, 0]
    near = neighbours.transpose(0, 3, 1, 2)[0]
    up_turned = up_weight.transpose(0, 2, 1).reshape(8 * C, coarse)
    half = item_width // 2
    count = 2 * C
    item_lanes = capacity * devices // 2 * item_width // (count // 2)
    sums_width = 8 * C * coarse // count + 14 * C
    rows = shape((bricks, width))
    face_rows = shape((face, width))
    faces_and_parents = shape((face, width + item_width))
    lists_shape = shape((8, 128), I32)
    band = pltpu.VMEM((9, WIDE, RUN), BF)
    conv_flops = 2 * 9 * 16 * bricks * WIDE * RUN

    listed = (sends, items, sides, crosses, slots)
    outgoing, lists = call(
        first_body, [shape((2 * capacity * devices, half)), lists_shape], *listed,
        scratch=[pltpu.VMEM(a.shape, a.dtype) for a in listed] + [pltpu.SemaphoreType.DMA((len(listed),))],
        in_hbm=True,
    )
    received = trade_rows(outgoing, ("x", "core", "gy"))
    lane = jnp.arange(128, dtype=I32)[None]
    parity = jnp.where(lane == GX, lax.axis_index("core"), lax.axis_index("gy") % 2).astype(I32)
    table_rows = start + 2 * face
    ext_grad, to_even, to_odd, turned, mains, ends, lists = call(
        table_grad_body,
        [
            shape((start, width), F32), face_rows, face_rows, shape((RUN, 16 * bricks)),
            shape((9, bricks, table_rows)), shape((9, bricks, 2 * table_rows)), lists_shape,
        ],
        cot, conv_weight, near, lists, parity,
        scratch=[band, pltpu.VMEM((6, 6, bricks, WIDE), F32)], flops=2 * conv_flops,
    )
    cross_grads = swap_pairs(to_even, to_odd, GX_AXES)
    merged, parents, to_even, to_odd = call(
        merge_body, [rows, shape((8 * bricks, coarse)), faces_and_parents, faces_and_parents],
        received, up_turned, fine, lists,
    )
    sides = swap_pairs(to_even, to_odd, "gy")
    to_even, to_odd = call(cross_body, [face_rows, face_rows], merged, *sides, lists)
    crosses = swap_pairs(to_even, to_odd, GX_AXES)
    half_sums_dims = (count // 2, sums_width)
    fine_part, to_even, to_odd, up_sums = call(
        side_grad_body,
        [shape((bricks, width), F32), face_rows, face_rows, shape((count, sums_width - 14 * C), F32)],
        *cross_grads[::-1], ext_grad, lists, *sides, parents,
    )
    side_grads = swap_pairs(to_even, to_odd, "gy")
    given, pad = call(
        given_sums_body, [shape(half_sums_dims), shape((6, 6, bricks, WIDE))],
        *crosses[::-1], merged, *sides, turned, mains, ends, lists, up_sums,
        scratch=[pltpu.VMEM((table_rows, width), BF)], flops=conv_flops,
    )
    (kept,) = call(kept_sums_body, [shape(half_sums_dims, F32)], pad, turned, up_sums, lists, flops=conv_flops)
    given = swap(given, "core", 0)
    (sums,) = call(pair_sum_body, [shape(half_sums_dims)], kept, given)
    sums = trade_rows(sums, ("x", "gy"))
    output, lists = call(
        conv_body, [rows, lists_shape], pad, conv_weight, lists, scratch=[band], flops=20 * conv_flops
    )
    grad_fine, replies = call(
        functools.partial(fine_grad_body, across=across), [rows, shape((count // 2, 2 * item_lanes))],
        fine_part, lists, *side_grads, up_turned, flops=10 * conv_flops,
    )
    (back,) = call(
        functools.partial(share_body, across=across), [shape((count // 2, 2 * item_lanes + sums_width))], sums, replies
    )
    back = trade_rows(back, ("x", "gy"))
    given = swap(back, "core", 0)
    scale = 1.0 / math.sqrt(64 * bricks * devices)
    grad_conv, grad_up, coarse_grad = call(
        functools.partial(last_body, item_lanes=item_lanes, across=across, scale=scale),
        [shape((27, C, C), F32), shape((8 * C, coarse), F32), shape((item_count, item_width))],
        back, given, sends, lists,
    )
    return (
        output.reshape(1, 1, bricks, width),
        grad_fine.reshape(1, 1, bricks, width),
        coarse_grad.reshape(1, 1, item_count, item_width),
        grad_conv,
        grad_up.reshape(8, C, coarse).transpose(0, 2, 1),
    )


def solution(mesh):
    groups, across_x, across_y = mesh.devices.shape
    split_mesh = Mesh(mesh.devices.reshape(groups, across_x // 2, 2, across_y), ("groups", "x", "core", "gy"))
    rows = ("groups", "x", "core")
    split = P(rows, "gy", None, None)
    placed = (split, split, P(), P(), split, split, split, P(rows, "gy", None), split, split)
    return jax.shard_map(
        on_device,
        mesh=split_mesh,
        in_specs=placed,
        out_specs=(split, split, split, P("groups", None, None), P("groups", None, None)),
        check_vma=False,
    )
```

```python
import functools
import math

import jax
import jax.numpy as jnp
from jax import lax
from jax.experimental import pallas as pl
from jax.experimental.pallas import tpu as pltpu
from jax.sharding import Mesh
from jax.sharding import PartitionSpec as P

BF = jnp.bfloat16
F32 = jnp.float32
I32 = jnp.int32

C = 64
RUN = 4 * C
WIDE = RUN + 2 * C


def iota(shape, axis):
    return lax.broadcasted_iota(I32, shape, axis)


def ones_where(mask):
    return jnp.where(mask, 1.0, 0.0).astype(BF)


def dot(a, b):
    return jnp.dot(a, b, preferred_element_type=F32)


def dot_tn(a, b):
    return lax.dot_general(a, b, (((0,), (0,)), ((), ())), preferred_element_type=F32)


def dot_nt(a, b):
    return lax.dot_general(a, b, (((1,), (1,)), ((), ())), preferred_element_type=F32)


def column_of(row):
    size = row.shape[1]
    diagonal = iota((size, size), 0) == iota((size, size), 1)
    spread = jnp.broadcast_to(row.astype(F32), (size, size))
    return jnp.sum(jnp.where(diagonal, spread, 0.0), axis=1, keepdims=True).astype(I32)


def call(body, outs, *args, scratch=(), flops=0, in_hbm=False):
    moved = sum(a.size * a.dtype.itemsize for a in list(args) + list(outs))
    return pl.pallas_call(
        body,
        out_shape=tuple(outs),
        in_specs=[pl.BlockSpec(memory_space=pltpu.HBM) if in_hbm else pl.BlockSpec() for _ in args],
        scratch_shapes=tuple(scratch),
        cost_estimate=pl.CostEstimate(flops=flops, bytes_accessed=moved, transcendentals=0),
        compiler_params=pltpu.CompilerParams(vmem_limit_bytes=None if in_hbm else 28 * 2**20),
    )(*args)


def shape(dims, dtype=BF):
    return jax.ShapeDtypeStruct(dims, dtype)


def items_named(sends_ref, count):
    capacity, devices = sends_ref.shape
    group = 2 * capacity
    lanes = devices * group
    spread = ones_where(iota((lanes, devices), 0) // group == iota((lanes, devices), 1))
    slot = iota((lanes, capacity), 0) % group // 2
    values = dot_nt(spread, sends_ref[...].astype(F32).astype(BF))
    item = jnp.sum(jnp.where(slot == iota((lanes, capacity), 1), values, 0.0), axis=1, keepdims=True).astype(I32)
    place = jnp.where(item < count, item + iota((lanes, 1), 0) % 2 * count, -1)
    return ones_where(iota((lanes, 2 * count), 1) == place)


def merge(received_ref, slots, up_ref, fine_ref, merged_ref, parents_ref):
    bricks = fine_ref.shape[0]
    lanes, half = received_ref.shape
    slot = column_of(slots)
    place = iota((bricks, lanes), 1)
    named = place // 2 == slot
    received = received_ref[...]
    parents = jnp.concatenate(
        [dot(ones_where(named & (place % 2 == h)), received) for h in (0, 1)], axis=1
    ).astype(BF)
    coarse = 2 * half // 8
    stacked = jnp.concatenate([parents[:, v * coarse : (v + 1) * coarse] for v in range(8)], axis=0)
    parents_ref[...] = stacked
    lifted = dot_nt(stacked, up_ref[...])
    for v in range(8):
        cx, cy, cz = (v // 4, v // 2 % 2, v % 2)
        for parity in range(4):
            vx, vy = (2 * cx + parity // 2, 2 * cy + parity % 2)
            at = (vx * 4 + vy) * RUN + cz * 2 * C
            add = lifted[v * bricks : (v + 1) * bricks, parity * 2 * C : (parity + 1) * 2 * C]
            merged_ref[:, at : at + 2 * C] = (fine_ref[:, at : at + 2 * C].astype(F32) + add).astype(BF)
    return parents


def pick_rows(lists, rows):
    return [dot_tn(ones_where(iota((rows.shape[0], one.shape[1]), 0) == one), rows) for one in lists]


GX, GY = (0, 1)
GX_AXES = ("x", "core")


def by_pair(lists_ref, axis, of_next, of_prev):
    odd = jnp.broadcast_to(lists_ref[5:6, axis : axis + 1], of_next.shape) == 1
    return jnp.where(odd, of_prev, of_next), jnp.where(odd, of_next, of_prev)


def from_pairs(lists_ref, axis, even_ref, odd_ref):
    return by_pair(lists_ref, axis, even_ref[...].astype(F32), odd_ref[...].astype(F32))


def stack_rows(*parts):
    return jnp.concatenate([p.astype(F32) for p in parts], axis=0).astype(BF)


def sides_of(lists_ref, face):
    return lists_ref[0:2, :face]


def crosses_of(lists_ref, face):
    return lists_ref[2:4, :face]


def slots_of(lists_ref, bricks):
    return lists_ref[4:5, :bricks]


def cross_body(merged_ref, even_ref, odd_ref, lists_ref, a_ref, b_ref):
    face, width = a_ref.shape
    high, low = from_pairs(lists_ref, GY, even_ref, odd_ref)
    rows = jnp.concatenate([merged_ref[...], stack_rows(low[:, :width], high[:, :width])], axis=0)
    lists = crosses_of(lists_ref, face)
    picked = pick_rows(by_pair(lists_ref, GX, lists[0:1], lists[1:2]), rows)
    a_ref[...] = picked[0].astype(BF)
    b_ref[...] = picked[1].astype(BF)


def build_bands(weight_ref, band_ref):
    zero = jnp.zeros((C, C), BF)
    blank = jnp.zeros((C, 2 * C), BF)

    def pair(a, b):
        return jnp.concatenate([a, b], axis=1)

    for e in range(9):
        low, mid, high = (weight_ref[3 * e + z] for z in range(3))
        first, second = (pair(mid, low), pair(high, mid))
        left, right = (pair(low, zero), pair(zero, high))
        rows = (
            (first, blank),
            (second, left),
            (right, first),
            (blank, second),
            (blank, right),
            (left, blank),
        )
        for z, halves in enumerate(rows):
            for s in range(2):
                band_ref[e, z * C : (z + 1) * C, s * 2 * C : (s + 1) * 2 * C] = halves[s]


def options(at):
    return [(at + 1, 0)] + ([(5, 1)] if at == 0 else []) + ([(0, -1)] if at == 3 else [])


def offset_of(dx, dy, dz):
    return (dx + 1) * 9 + (dy + 1) * 3 + dz + 1


def stack_lanes(value, lanes):
    return jnp.concatenate([value[:, p * lanes : (p + 1) * lanes] for p in range(value.shape[1] // lanes)], axis=0)


def stack_parities(value):
    stacked = []
    for v in range(8):
        cx, cy, cz = (v // 4, v // 2 % 2, v % 2)
        lanes = []
        for parity in range(4):
            at = ((2 * cx + parity // 2) * 4 + 2 * cy + parity % 2) * RUN + cz * 2 * C
            lanes.append(value[:, at : at + 2 * C])
        stacked.append(jnp.concatenate(lanes, axis=1))
    return jnp.concatenate(stacked, axis=0)


def stack_runs(ref):
    return jnp.concatenate([ref[:, p * RUN : (p + 1) * RUN] for p in range(16)], axis=0)


def split_two(value):
    head = value.astype(BF)
    return head, (value - head.astype(F32)).astype(BF)


def table_grad_body(
    cot_ref, weight_ref, near_ref, lists_ref, parity_ref,
    ext_ref, even_ref, odd_ref, turned_ref, mains_ref, ends_ref, again_ref, band_ref, pad_ref,
):
    again_ref[...] = lists_ref[...]
    again_ref[5:6] = parity_ref[...]
    bricks = cot_ref.shape[0]
    face = even_ref.shape[0]
    start = ext_ref.shape[0]
    rows = start + 2 * face
    build_bands(weight_ref, band_ref)
    cot = stack_runs(cot_ref)
    turned_ref[...] = cot.T
    pad_ref[...] = jnp.zeros(pad_ref.shape, F32)
    for e in range(9):
        ex, ey = (e // 3, e % 3)
        part = dot_nt(cot, band_ref[e]).reshape(4, 4, bricks, WIDE)
        pad_ref[ex : ex + 4, ey : ey + 4] += part
    near = [near_ref[o] for o in range(27)]

    def chooser(which):
        index = jnp.concatenate([near[o] for o in which], axis=1)
        return ones_where(iota((rows, index.shape[1]), 0) == index)

    lower_half = iota((rows, 2 * C), 1) < C
    cache = {}
    for x in range(4):
        for y in range(4):
            places = [(X, Y, dx, dy) for X, dx in options(x) for Y, dy in options(y)]
            key = tuple((dx, dy) for _, _, dx, dy in places)
            if key not in cache:
                moved = [d for d in key if d != (0, 0)]
                main = chooser([offset_of(*d, 0) for d in moved] * 2) if moved else None
                up = chooser([offset_of(*d, 1) for d in key] * 2)
                down = chooser([offset_of(*d, -1) for d in key] * 2)
                cache[key] = (main, jnp.concatenate([up, down], axis=0))
            main, ends = cache[key]
            own = pad_ref[x + 1, y + 1, :, :RUN]
            own = jnp.concatenate([own, jnp.zeros((rows - bricks, RUN), F32)], axis=0)
            if main is not None:
                parts = [split_two(pad_ref[X, Y, :, :RUN]) for X, Y, dx, dy in places if (dx, dy) != (0, 0)]
                value = jnp.concatenate([p[0] for p in parts] + [p[1] for p in parts], axis=0)
                own += dot(main, value)
            parts = [split_two(pad_ref[X, Y, :, RUN:]) for X, Y, _, _ in places]
            value = jnp.concatenate([p[0] for p in parts] + [p[1] for p in parts], axis=0)
            halo = dot(ends, value)
            first = own[:, : 2 * C] + jnp.where(lower_half, halo[:rows], 0.0)
            second = own[:, 2 * C :] + jnp.where(lower_half, 0.0, halo[rows:])
            total = jnp.concatenate([first, second], axis=1)
            at = (x * 4 + y) * RUN
            ext_ref[:, at : at + RUN] = total[:start]
            even, odd = by_pair(again_ref, GX, total[start + face :], total[start : start + face])
            even_ref[:, at : at + RUN] = even.astype(BF)
            odd_ref[:, at : at + RUN] = odd.astype(BF)
    make_choosers(near_ref, rows, mains_ref, ends_ref)


def make_choosers(near_ref, rows, mains_ref, ends_ref):
    bricks = mains_ref.shape[1]
    near = jnp.concatenate([near_ref[o] for o in range(27)] + [jnp.zeros((5, bricks), I32)], axis=0)
    near = near.astype(F32).T.astype(I32)
    place = iota((bricks, rows), 1)
    pair_place = iota((bricks, 2 * rows), 1)
    for d in range(9):
        down, straight, up = (near[:, 3 * d + z : 3 * d + z + 1] for z in range(3))
        mains_ref[d] = ones_where(place == straight)
        ends_ref[d] = ones_where(pair_place == jnp.where(pair_place < rows, up, down + rows))


def first_body(
    sends_hbm, items_hbm, sides_hbm, crosses_hbm, slots_hbm, out_ref, lists_ref,
    sends_ref, items_ref, sides_ref, crosses_ref, slots_ref, arrived,
):
    sources = (sends_hbm, items_hbm, sides_hbm, crosses_hbm, slots_hbm)
    places = (sends_ref, items_ref, sides_ref, crosses_ref, slots_ref)
    copies = [pltpu.make_async_copy(s, p, arrived.at[i]) for i, (s, p) in enumerate(zip(sources, places))]
    for copy in copies:
        copy.start()
    copies[0].wait()
    chosen = items_named(sends_ref, items_ref.shape[0])
    copies[1].wait()
    half = out_ref.shape[1]
    items = jnp.concatenate([items_ref[:, :half], items_ref[:, half:]], axis=0)
    out_ref[...] = dot(chosen, items).astype(BF)
    for copy in copies[2:]:
        copy.wait()
    face, bricks = (sides_ref.shape[1], slots_ref.shape[1])
    lists_ref[...] = jnp.zeros(lists_ref.shape, I32)
    lists_ref[0:2, :face] = sides_ref[...]
    lists_ref[2:4, :face] = crosses_ref[...]
    lists_ref[4:5, :bricks] = slots_ref[...]


def side_grad_body(
    odd_grad_ref, even_grad_ref, ext_ref, lists_ref, even_side_ref, odd_side_ref, parents_ref,
    part_ref, to_even_ref, to_odd_ref, up_sums_ref,
):
    bricks, width = part_ref.shape
    face = to_even_ref.shape[0]
    from_next, from_prev = from_pairs(lists_ref, GX, even_grad_ref, odd_grad_ref)
    total = add_rows(ext_ref[...], crosses_of(lists_ref, face), from_next, from_prev)
    part_ref[...] = total[:bricks]
    to_even, to_odd = by_pair(lists_ref, GY, total[bricks + face :], total[bricks : bricks + face])
    to_even_ref[...] = to_even.astype(BF)
    to_odd_ref[...] = to_odd.astype(BF)
    high, low = by_pair(
        lists_ref, GY, even_side_ref[:, width:].astype(F32), odd_side_ref[:, width:].astype(F32)
    )
    side_parents = stack_lanes(stack_rows(low, high), parents_ref.shape[1])
    grads = [stack_parities(total[:bricks].astype(BF)), stack_parities(total[bricks:].astype(BF))]
    up_sum = dot_tn(jnp.concatenate(grads, axis=0), jnp.concatenate([parents_ref[...], side_parents], axis=0))
    coarse = up_sum.shape[1]
    count = up_sums_ref.shape[0]
    for q in range(up_sum.shape[0] // count):
        up_sums_ref[:, q * coarse : (q + 1) * coarse] = up_sum[q * count : (q + 1) * count]


def given_sums_body(
    odd_cross_ref, even_cross_ref, merged_ref, even_side_ref, odd_side_ref, turned_ref, mains_ref, ends_ref, lists_ref,
    up_sums_ref, given_ref, pad_ref, table_ref,
):
    bricks, width = merged_ref.shape
    face = even_side_ref.shape[0]
    rows = bricks + 4 * face
    high, low = by_pair(lists_ref, GY, even_side_ref[:, :width].astype(F32), odd_side_ref[:, :width].astype(F32))
    above, below = from_pairs(lists_ref, GX, even_cross_ref, odd_cross_ref)
    table_ref[:bricks] = merged_ref[...]
    table_ref[bricks:] = stack_rows(low, high, below, above)
    lower_half = iota((rows, 2 * C), 1) < C
    zero = jnp.zeros((rows, 2 * C), BF)
    for x in range(4):
        for y in range(4):
            places = [(X, Y, dx, dy) for X, dx in options(x) for Y, dy in options(y)]
            at = (x * 4 + y) * RUN
            columns = table_ref[:, at : at + RUN]
            first = jnp.where(lower_half, columns[:, : 2 * C], zero)
            second = jnp.where(lower_half, zero, columns[:, 2 * C :])
            ends = jnp.concatenate([ends_ref[3 * dx + dy + 4] for _, _, dx, dy in places], axis=0)
            halo = dot(ends, jnp.concatenate([first, second], axis=0)).astype(BF)
            for i, (X, Y, _, _) in enumerate(places):
                pad_ref[X, Y, :, RUN:] = halo[i * bricks : (i + 1) * bricks]
            pad_ref[x + 1, y + 1, :, :RUN] = columns[:bricks]
            moved = [p for p in places if p[2:] != (0, 0)]
            if moved:
                main = jnp.concatenate([mains_ref[3 * dx + dy + 4] for _, _, dx, dy in moved], axis=0)
                got = dot(main, columns).astype(BF)
                for i, (X, Y, _, _) in enumerate(moved):
                    pad_ref[X, Y, :, :RUN] = got[i * bricks : (i + 1) * bricks]

    half_sums(1 - lists_ref[5, GX], pad_ref, turned_ref, up_sums_ref, given_ref)


def half_sums(group, pad_ref, turned_ref, up_sums_ref, out_ref):
    turned = turned_ref[...]
    half_count = out_ref.shape[0]
    up_lanes = up_sums_ref.shape[1]
    up_half = jnp.where(group == 0, up_sums_ref[:half_count], up_sums_ref[half_count:])
    out_ref[:, :up_lanes] = up_half.astype(out_ref.dtype)
    bricks = pad_ref.shape[2]
    lanes_low = iota((C, 2 * C), 1) < C
    sums = []
    for i in range(5):
        ex, ey = (jnp.where(group == 0, i // 3, (i + 4) // 3), jnp.where(group == 0, i % 3, (i + 4) % 3))
        wide = dot(turned, pad_ref[pl.ds(ex, 4), pl.ds(ey, 4)].reshape(16 * bricks, WIDE))

        def block(z, s):
            return wide[z * C : (z + 1) * C, s * 2 * C : (s + 1) * 2 * C]

        low = jnp.where(lanes_low, block(1, 0) + block(3, 1), block(0, 2) + block(2, 0))
        mid = jnp.where(lanes_low, block(0, 0) + block(2, 1), block(1, 0) + block(3, 1))
        high = jnp.where(lanes_low, block(1, 1) + block(3, 2), block(0, 0) + block(2, 1))
        for value in (low, mid, high):
            sums.append(value + pltpu.roll(value, C, 1))
    sums.append(jnp.zeros((C, 2 * C), F32))
    pairs = [jnp.where(lanes_low, sums[2 * k], sums[2 * k + 1]) for k in range(8)]
    for p in range(7):
        at = up_lanes + p * 2 * C
        out_ref[:, at : at + 2 * C] = jnp.where(group == 0, pairs[p], pairs[p + 1]).astype(out_ref.dtype)


def kept_sums_body(pad_ref, turned_ref, up_sums_ref, lists_ref, kept_ref):
    half_sums(lists_ref[5, GX], pad_ref, turned_ref, up_sums_ref, kept_ref)


def pair_sum_body(kept_ref, given_ref, lists_ref, out_ref, again_ref):
    again_ref[...] = lists_ref[...]
    out_ref[...] = (kept_ref[...] + given_ref[...].astype(F32)).astype(BF)


def inputs_at(pad_ref, e):
    bricks = pad_ref.shape[2]
    ex, ey = (e // 3, e % 3)
    return pad_ref[ex : ex + 4, ey : ey + 4].reshape(16 * bricks, WIDE)


def conv_body(pad_ref, weight_ref, lists_ref, out_ref, again_ref, band_ref):
    again_ref[...] = lists_ref[...]
    bricks = pad_ref.shape[2]
    build_bands(weight_ref, band_ref)
    total = None
    for e in range(9):
        part = dot(inputs_at(pad_ref, e), band_ref[e])
        total = part if total is None else total + part
    for p in range(16):
        out_ref[:, p * RUN : (p + 1) * RUN] = total[p * bricks : (p + 1) * bricks].astype(BF)


def add_rows(base, lists, first, second):
    count, face = (base.shape[0], lists.shape[1])
    index = jnp.concatenate([lists[0:1], lists[1:2]], axis=1)
    chosen = ones_where(iota((count, 2 * face), 0) == index)
    return base + dot(chosen, stack_rows(first, second))


def merge_body(received_ref, up_ref, fine_ref, lists_ref, merged_ref, parents_ref, a_ref, b_ref):
    bricks, width = fine_ref.shape
    face = a_ref.shape[0]
    parents = merge(received_ref, slots_of(lists_ref, bricks), up_ref, fine_ref, merged_ref, parents_ref)
    lists = sides_of(lists_ref, face)
    lists = by_pair(lists_ref, GY, lists[0:1], lists[1:2])
    for out_ref, rows, owners in zip((a_ref, b_ref), pick_rows(lists, merged_ref[...]), pick_rows(lists, parents)):
        out_ref[:, :width] = rows.astype(BF)
        out_ref[:, width:] = owners.astype(BF)


def fine_grad_body(part_ref, lists_ref, even_ref, odd_ref, up_ref, grad_ref, replies_ref, across):
    bricks = part_ref.shape[0]
    face = even_ref.shape[0]
    from_next, from_prev = from_pairs(lists_ref, GY, even_ref, odd_ref)
    total = add_rows(part_ref[...], sides_of(lists_ref, face), from_next, from_prev)
    grad_ref[...] = total.astype(BF)
    items = dot(stack_parities(grad_ref[...]), up_ref[...]).astype(BF)
    items = jnp.concatenate([items[v * bricks : (v + 1) * bricks] for v in range(8)], axis=1)
    half = items.shape[1] // 2
    count, both_lanes = replies_ref.shape
    pieces = both_lanes // 2 // half
    capacity, group = chip_slots(count, pieces, across)
    slots = slots_of(lists_ref, bricks)
    row = iota((count, bricks), 0)
    for other in range(2):
        owner = device_of(row // group, lists_ref, other, across)
        for j in range(pieces):
            piece = row % group * pieces + j
            named = owner * capacity + piece // 2 == slots
            rows = dot(ones_where(named & (piece % 2 == 0)), items[:, :half])
            rows += dot(ones_where(named & (piece % 2 == 1)), items[:, half:])
            at = (other * pieces + j) * half
            replies_ref[:, at : at + half] = rows.astype(BF)


def chip_slots(count, pieces, across):
    group = count // (across[0] * across[1] // 2)
    return group * pieces // 2, group


def device_of(chip, lists_ref, other, across):
    core = jnp.broadcast_to(lists_ref[5:6, GX : GX + 1], chip.shape)
    core = 1 - core if other else core
    return (chip // across[1] * 2 + core) * across[1] + chip % across[1]


def share_body(sums_ref, replies_ref, lists_ref, out_ref, across):
    count, item_lanes = replies_ref.shape
    share = count // (across[0] * across[1] // 2)
    same = iota((count, count), 0) % share == iota((count, count), 1) % share
    out_ref[:, :item_lanes] = replies_ref[...]
    out_ref[:, item_lanes:] = dot(ones_where(same), sums_ref[...]).astype(BF)


def coarse_grad(arrivals, sends_ref, lists_ref, out_ref, across):
    capacity, devices = sends_ref.shape
    count, item_width = out_ref.shape
    half = item_width // 2
    lanes = arrivals[0].shape[0]
    pieces = arrivals[0].shape[1] // half
    _, group = chip_slots(lanes, pieces, across)
    sends = sends_ref[...].astype(F32).astype(BF)
    lane = iota((1, lanes), 1)
    totals = [None, None]
    for other in range(2):
        source = device_of(lane // group, lists_ref, other, across)
        rows = dot(sends, ones_where(source == iota((devices, lanes), 0)))
        for j in range(pieces):
            piece = lane % group * pieces + j
            picked = jnp.where(piece // 2 == iota((capacity, lanes), 0), rows, 0.0)
            index = jnp.sum(picked, axis=0, keepdims=True).astype(I32)
            named = iota((count, lanes), 0) == index
            for h in range(2):
                part = dot(ones_where(named & (piece % 2 == h)), arrivals[other][:, j * half : (j + 1) * half])
                totals[h] = part if totals[h] is None else totals[h] + part
    for h in range(2):
        out_ref[:, h * half : (h + 1) * half] = totals[h].astype(BF)


def last_body(back_ref, given_ref, sends_ref, lists_ref, conv_ref, up_ref, out_ref, item_lanes, across, scale):
    half_count = back_ref.shape[0]
    items = (back_ref[:, :item_lanes], given_ref[:, item_lanes : 2 * item_lanes])
    coarse_grad(items, sends_ref, lists_ref, out_ref, across)
    coarse = up_ref.shape[1]
    count = 2 * half_count
    parts = up_ref.shape[0] // count
    own = back_ref[:, 2 * item_lanes :].astype(F32) * scale
    others = given_ref[:, 2 * item_lanes :].astype(F32) * scale
    first, second = by_pair(lists_ref, GX, own, others)
    at = 0
    for q in range(parts):
        up_ref[q * count : q * count + half_count] = first[:, at : at + coarse]
        up_ref[q * count + half_count : (q + 1) * count] = second[:, at : at + coarse]
        at += coarse
    for pair in range(7):
        turned = jnp.concatenate([first[:, at : at + 2 * C], second[:, at : at + 2 * C]], axis=0).T
        at += 2 * C
        for h in range(2):
            for s in range(2):
                o = 14 * h + 2 * pair + s
                if o < 27:
                    conv_ref[o] = turned[s * C : (s + 1) * C, h * C : (h + 1) * C]


def swap(value, axis, first):
    count = lax.axis_size(axis)
    lower = range(first, count - 1, 2)
    return lax.ppermute(value, axis, [(i, i + 1) for i in lower] + [(i + 1, i) for i in lower])


def swap_pairs(to_even, to_odd, axis):
    return swap(to_even, axis, 0), swap(to_odd, axis, 1)


def trade_rows(values, axes):
    rows, width = values.shape
    devices = math.prod(lax.axis_size(axis) for axis in axes)
    grid_view = values.reshape(devices, rows // devices, width)
    return lax.all_to_all(grid_view, axes, split_axis=0, concat_axis=0, tiled=True).reshape(rows, width)


def on_device(
    fine_features, coarse_items, conv_weight, up_weight, neighbours,
    side_sends, cross_sends, parent_slots, coarse_sends, cotangent,
):
    fine = fine_features[0, 0]
    items = coarse_items[0, 0]
    cot = cotangent[0, 0]
    bricks, width = fine.shape
    face = side_sends.shape[-1]
    across = (lax.axis_size(GX_AXES), lax.axis_size("gy"))
    devices = across[0] * across[1]
    capacity = coarse_sends.shape[-1]
    item_count, item_width = items.shape
    coarse = up_weight.shape[1]
    start = bricks + 2 * face
    sends = coarse_sends.transpose(0, 1, 3, 2)[0, 0]
    slots = parent_slots[0]
    sides = side_sends[0, 0]
    crosses = cross_sends[0, 0]
    near = neighbours.transpose(0, 3, 1, 2)[0]
    up_turned = up_weight.transpose(0, 2, 1).reshape(8 * C, coarse)
    half = item_width // 2
    count = 2 * C
    item_lanes = capacity * devices // 2 * item_width // (count // 2)
    sums_width = 8 * C * coarse // count + 14 * C
    rows = shape((bricks, width))
    face_rows = shape((face, width))
    faces_and_parents = shape((face, width + item_width))
    lists_shape = shape((8, 128), I32)
    band = pltpu.VMEM((9, WIDE, RUN), BF)
    conv_flops = 2 * 9 * 16 * bricks * WIDE * RUN

    listed = (sends, items, sides, crosses, slots)
    outgoing, lists = call(
        first_body, [shape((2 * capacity * devices, half)), lists_shape], *listed,
        scratch=[pltpu.VMEM(a.shape, a.dtype) for a in listed] + [pltpu.SemaphoreType.DMA((len(listed),))],
        in_hbm=True,
    )
    received = trade_rows(outgoing, ("x", "core", "gy"))
    lane = jnp.arange(128, dtype=I32)[None]
    parity = jnp.where(lane == GX, lax.axis_index("core"), lax.axis_index("gy") % 2).astype(I32)
    table_rows = start + 2 * face
    ext_grad, to_even, to_odd, turned, mains, ends, lists = call(
        table_grad_body,
        [
            shape((start, width), F32), face_rows, face_rows, shape((RUN, 16 * bricks)),
            shape((9, bricks, table_rows)), shape((9, bricks, 2 * table_rows)), lists_shape,
        ],
        cot, conv_weight, near, lists, parity,
        scratch=[band, pltpu.VMEM((6, 6, bricks, WIDE), F32)], flops=2 * conv_flops,
    )
    cross_grads = swap_pairs(to_even, to_odd, GX_AXES)
    merged, parents, to_even, to_odd = call(
        merge_body, [rows, shape((8 * bricks, coarse)), faces_and_parents, faces_and_parents],
        received, up_turned, fine, lists,
    )
    sides = swap_pairs(to_even, to_odd, "gy")
    to_even, to_odd = call(cross_body, [face_rows, face_rows], merged, *sides, lists)
    crosses = swap_pairs(to_even, to_odd, GX_AXES)
    half_sums_dims = (count // 2, sums_width)
    fine_part, to_even, to_odd, up_sums = call(
        side_grad_body,
        [shape((bricks, width), F32), face_rows, face_rows, shape((count, sums_width - 14 * C), F32)],
        *cross_grads[::-1], ext_grad, lists, *sides, parents,
    )
    side_grads = swap_pairs(to_even, to_odd, "gy")
    given, pad = call(
        given_sums_body, [shape(half_sums_dims), shape((6, 6, bricks, WIDE))],
        *crosses[::-1], merged, *sides, turned, mains, ends, lists, up_sums,
        scratch=[pltpu.VMEM((table_rows, width), BF)], flops=conv_flops,
    )
    (kept,) = call(kept_sums_body, [shape(half_sums_dims, F32)], pad, turned, up_sums, lists, flops=conv_flops)
    given = swap(given, "core", 0)
    sums, after_sums = call(pair_sum_body, [shape(half_sums_dims), lists_shape], kept, given, lists)
    sums = trade_rows(sums, ("x", "gy"))
    output, after_conv = call(
        conv_body, [rows, lists_shape], pad, conv_weight, after_sums, scratch=[band], flops=conv_flops
    )
    grad_fine, replies = call(
        functools.partial(fine_grad_body, across=across), [rows, shape((count // 2, 2 * item_lanes))],
        fine_part, after_sums, *side_grads, up_turned, flops=10 * conv_flops,
    )
    (back,) = call(
        functools.partial(share_body, across=across), [shape((count // 2, 2 * item_lanes + sums_width))],
        sums, replies, after_conv,
    )
    back = trade_rows(back, ("x", "gy"))
    given = swap(back, "core", 0)
    scale = 1.0 / math.sqrt(64 * bricks * devices)
    grad_conv, grad_up, coarse_grad = call(
        functools.partial(last_body, item_lanes=item_lanes, across=across, scale=scale),
        [shape((27, C, C), F32), shape((8 * C, coarse), F32), shape((item_count, item_width))],
        back, given, sends, lists,
    )
    return (
        output.reshape(1, 1, bricks, width),
        grad_fine.reshape(1, 1, bricks, width),
        coarse_grad.reshape(1, 1, item_count, item_width),
        grad_conv,
        grad_up.reshape(8, C, coarse).transpose(0, 2, 1),
    )


def solution(mesh):
    groups, across_x, across_y = mesh.devices.shape
    split_mesh = Mesh(mesh.devices.reshape(groups, across_x // 2, 2, across_y), ("groups", "x", "core", "gy"))
    rows = ("groups", "x", "core")
    split = P(rows, "gy", None, None)
    placed = (split, split, P(), P(), split, split, split, P(rows, "gy", None), split, split)
    return jax.shard_map(
        on_device,
        mesh=split_mesh,
        in_specs=placed,
        out_specs=(split, split, split, P("groups", None, None), P("groups", None, None)),
        check_vma=False,
    )
```

```python
import functools
import math

import jax
import jax.numpy as jnp
from jax import lax
from jax.experimental import pallas as pl
from jax.experimental.pallas import tpu as pltpu
from jax.sharding import Mesh
from jax.sharding import PartitionSpec as P

BF = jnp.bfloat16
F32 = jnp.float32
I32 = jnp.int32

C = 64
RUN = 4 * C
WIDE = RUN + 2 * C


def iota(shape, axis):
    return lax.broadcasted_iota(I32, shape, axis)


def ones_where(mask):
    return jnp.where(mask, 1.0, 0.0).astype(BF)


def dot(a, b):
    return jnp.dot(a, b, preferred_element_type=F32)


def dot_tn(a, b):
    return lax.dot_general(a, b, (((0,), (0,)), ((), ())), preferred_element_type=F32)


def dot_nt(a, b):
    return lax.dot_general(a, b, (((1,), (1,)), ((), ())), preferred_element_type=F32)


def column_of(row):
    size = row.shape[1]
    diagonal = iota((size, size), 0) == iota((size, size), 1)
    spread = jnp.broadcast_to(row.astype(F32), (size, size))
    return jnp.sum(jnp.where(diagonal, spread, 0.0), axis=1, keepdims=True).astype(I32)


def call(body, outs, *args, scratch=(), flops=0, in_hbm=False):
    moved = sum(a.size * a.dtype.itemsize for a in list(args) + list(outs))
    return pl.pallas_call(
        body,
        out_shape=tuple(outs),
        in_specs=[pl.BlockSpec(memory_space=pltpu.HBM) if in_hbm else pl.BlockSpec() for _ in args],
        scratch_shapes=tuple(scratch),
        cost_estimate=pl.CostEstimate(flops=flops, bytes_accessed=moved, transcendentals=0),
        compiler_params=pltpu.CompilerParams(vmem_limit_bytes=None if in_hbm else 28 * 2**20),
    )(*args)


def shape(dims, dtype=BF):
    return jax.ShapeDtypeStruct(dims, dtype)


def items_named(sends_ref, count):
    capacity, devices = sends_ref.shape
    group = 2 * capacity
    lanes = devices * group
    spread = ones_where(iota((lanes, devices), 0) // group == iota((lanes, devices), 1))
    slot = iota((lanes, capacity), 0) % group // 2
    values = dot_nt(spread, sends_ref[...].astype(F32).astype(BF))
    item = jnp.sum(jnp.where(slot == iota((lanes, capacity), 1), values, 0.0), axis=1, keepdims=True).astype(I32)
    place = jnp.where(item < count, item + iota((lanes, 1), 0) % 2 * count, -1)
    return ones_where(iota((lanes, 2 * count), 1) == place)


def merge(received_ref, slots, up_ref, fine_ref, merged_ref, parents_ref):
    bricks = fine_ref.shape[0]
    lanes, half = received_ref.shape
    slot = column_of(slots)
    place = iota((bricks, lanes), 1)
    named = place // 2 == slot
    received = received_ref[...]
    parents = jnp.concatenate(
        [dot(ones_where(named & (place % 2 == h)), received) for h in (0, 1)], axis=1
    ).astype(BF)
    coarse = 2 * half // 8
    stacked = jnp.concatenate([parents[:, v * coarse : (v + 1) * coarse] for v in range(8)], axis=0)
    parents_ref[...] = stacked
    lifted = dot_nt(stacked, up_ref[...])
    for v in range(8):
        cx, cy, cz = (v // 4, v // 2 % 2, v % 2)
        for parity in range(4):
            vx, vy = (2 * cx + parity // 2, 2 * cy + parity % 2)
            at = (vx * 4 + vy) * RUN + cz * 2 * C
            add = lifted[v * bricks : (v + 1) * bricks, parity * 2 * C : (parity + 1) * 2 * C]
            merged_ref[:, at : at + 2 * C] = (fine_ref[:, at : at + 2 * C].astype(F32) + add).astype(BF)
    return parents


def pick_rows(lists, rows):
    return [dot_tn(ones_where(iota((rows.shape[0], one.shape[1]), 0) == one), rows) for one in lists]


GX, GY = (0, 1)
GX_AXES = ("x", "core")


def by_pair(lists_ref, axis, of_next, of_prev):
    odd = jnp.broadcast_to(lists_ref[5:6, axis : axis + 1], of_next.shape) == 1
    return jnp.where(odd, of_prev, of_next), jnp.where(odd, of_next, of_prev)


def from_pairs(lists_ref, axis, even_ref, odd_ref):
    return by_pair(lists_ref, axis, even_ref[...].astype(F32), odd_ref[...].astype(F32))


def stack_rows(*parts):
    return jnp.concatenate([p.astype(F32) for p in parts], axis=0).astype(BF)


def sides_of(lists_ref, face):
    return lists_ref[0:2, :face]


def crosses_of(lists_ref, face):
    return lists_ref[2:4, :face]


def slots_of(lists_ref, bricks):
    return lists_ref[4:5, :bricks]


def cross_body(merged_ref, even_ref, odd_ref, lists_ref, a_ref, b_ref):
    face, width = a_ref.shape
    high, low = from_pairs(lists_ref, GY, even_ref, odd_ref)
    rows = jnp.concatenate([merged_ref[...], stack_rows(low[:, :width], high[:, :width])], axis=0)
    lists = crosses_of(lists_ref, face)
    picked = pick_rows(by_pair(lists_ref, GX, lists[0:1], lists[1:2]), rows)
    a_ref[...] = picked[0].astype(BF)
    b_ref[...] = picked[1].astype(BF)


def build_bands(weight_ref, band_ref):
    zero = jnp.zeros((C, C), BF)
    blank = jnp.zeros((C, 2 * C), BF)

    def pair(a, b):
        return jnp.concatenate([a, b], axis=1)

    for e in range(9):
        low, mid, high = (weight_ref[3 * e + z] for z in range(3))
        first, second = (pair(mid, low), pair(high, mid))
        left, right = (pair(low, zero), pair(zero, high))
        rows = (
            (first, blank),
            (second, left),
            (right, first),
            (blank, second),
            (blank, right),
            (left, blank),
        )
        for z, halves in enumerate(rows):
            for s in range(2):
                band_ref[e, z * C : (z + 1) * C, s * 2 * C : (s + 1) * 2 * C] = halves[s]


def options(at):
    return [(at + 1, 0)] + ([(5, 1)] if at == 0 else []) + ([(0, -1)] if at == 3 else [])


def offset_of(dx, dy, dz):
    return (dx + 1) * 9 + (dy + 1) * 3 + dz + 1


def stack_lanes(value, lanes):
    return jnp.concatenate([value[:, p * lanes : (p + 1) * lanes] for p in range(value.shape[1] // lanes)], axis=0)


def stack_parities(value):
    stacked = []
    for v in range(8):
        cx, cy, cz = (v // 4, v // 2 % 2, v % 2)
        lanes = []
        for parity in range(4):
            at = ((2 * cx + parity // 2) * 4 + 2 * cy + parity % 2) * RUN + cz * 2 * C
            lanes.append(value[:, at : at + 2 * C])
        stacked.append(jnp.concatenate(lanes, axis=1))
    return jnp.concatenate(stacked, axis=0)


def stack_runs(ref):
    return jnp.concatenate([ref[:, p * RUN : (p + 1) * RUN] for p in range(16)], axis=0)


def split_two(value):
    head = value.astype(BF)
    return head, (value - head.astype(F32)).astype(BF)


def table_grad_body(
    cot_ref, weight_ref, near_ref, lists_ref, parity_ref,
    ext_ref, even_ref, odd_ref, turned_ref, mains_ref, ends_ref, again_ref, band_ref, pad_ref,
):
    again_ref[...] = lists_ref[...]
    again_ref[5:6] = parity_ref[...]
    bricks = cot_ref.shape[0]
    face = even_ref.shape[0]
    start = ext_ref.shape[0]
    rows = start + 2 * face
    build_bands(weight_ref, band_ref)
    cot = stack_runs(cot_ref)
    turned_ref[...] = cot.T
    pad_ref[...] = jnp.zeros(pad_ref.shape, F32)
    for e in range(9):
        ex, ey = (e // 3, e % 3)
        part = dot_nt(cot, band_ref[e]).reshape(4, 4, bricks, WIDE)
        pad_ref[ex : ex + 4, ey : ey + 4] += part
    near = [near_ref[o] for o in range(27)]

    def chooser(which):
        index = jnp.concatenate([near[o] for o in which], axis=1)
        return ones_where(iota((rows, index.shape[1]), 0) == index)

    lower_half = iota((rows, 2 * C), 1) < C
    cache = {}
    for x in range(4):
        for y in range(4):
            places = [(X, Y, dx, dy) for X, dx in options(x) for Y, dy in options(y)]
            key = tuple((dx, dy) for _, _, dx, dy in places)
            if key not in cache:
                moved = [d for d in key if d != (0, 0)]
                main = chooser([offset_of(*d, 0) for d in moved] * 2) if moved else None
                up = chooser([offset_of(*d, 1) for d in key] * 2)
                down = chooser([offset_of(*d, -1) for d in key] * 2)
                cache[key] = (main, jnp.concatenate([up, down], axis=0))
            main, ends = cache[key]
            own = pad_ref[x + 1, y + 1, :, :RUN]
            own = jnp.concatenate([own, jnp.zeros((rows - bricks, RUN), F32)], axis=0)
            if main is not None:
                parts = [split_two(pad_ref[X, Y, :, :RUN]) for X, Y, dx, dy in places if (dx, dy) != (0, 0)]
                value = jnp.concatenate([p[0] for p in parts] + [p[1] for p in parts], axis=0)
                own += dot(main, value)
            parts = [split_two(pad_ref[X, Y, :, RUN:]) for X, Y, _, _ in places]
            value = jnp.concatenate([p[0] for p in parts] + [p[1] for p in parts], axis=0)
            halo = dot(ends, value)
            first = own[:, : 2 * C] + jnp.where(lower_half, halo[:rows], 0.0)
            second = own[:, 2 * C :] + jnp.where(lower_half, 0.0, halo[rows:])
            total = jnp.concatenate([first, second], axis=1)
            at = (x * 4 + y) * RUN
            ext_ref[:, at : at + RUN] = total[:start]
            even, odd = by_pair(again_ref, GX, total[start + face :], total[start : start + face])
            even_ref[:, at : at + RUN] = even.astype(BF)
            odd_ref[:, at : at + RUN] = odd.astype(BF)
    make_choosers(near_ref, rows, mains_ref, ends_ref)


def make_choosers(near_ref, rows, mains_ref, ends_ref):
    bricks = mains_ref.shape[1]
    near = jnp.concatenate([near_ref[o] for o in range(27)] + [jnp.zeros((5, bricks), I32)], axis=0)
    near = near.astype(F32).T.astype(I32)
    place = iota((bricks, rows), 1)
    pair_place = iota((bricks, 2 * rows), 1)
    for d in range(9):
        down, straight, up = (near[:, 3 * d + z : 3 * d + z + 1] for z in range(3))
        mains_ref[d] = ones_where(place == straight)
        ends_ref[d] = ones_where(pair_place == jnp.where(pair_place < rows, up, down + rows))


def first_body(
    sends_hbm, items_hbm, sides_hbm, crosses_hbm, slots_hbm, out_ref, lists_ref,
    sends_ref, items_ref, sides_ref, crosses_ref, slots_ref, arrived,
):
    sources = (sends_hbm, items_hbm, sides_hbm, crosses_hbm, slots_hbm)
    places = (sends_ref, items_ref, sides_ref, crosses_ref, slots_ref)
    copies = [pltpu.make_async_copy(s, p, arrived.at[i]) for i, (s, p) in enumerate(zip(sources, places))]
    for copy in copies:
        copy.start()
    copies[0].wait()
    chosen = items_named(sends_ref, items_ref.shape[0])
    copies[1].wait()
    half = out_ref.shape[1]
    items = jnp.concatenate([items_ref[:, :half], items_ref[:, half:]], axis=0)
    out_ref[...] = dot(chosen, items).astype(BF)
    for copy in copies[2:]:
        copy.wait()
    face, bricks = (sides_ref.shape[1], slots_ref.shape[1])
    lists_ref[...] = jnp.zeros(lists_ref.shape, I32)
    lists_ref[0:2, :face] = sides_ref[...]
    lists_ref[2:4, :face] = crosses_ref[...]
    lists_ref[4:5, :bricks] = slots_ref[...]


def side_grad_body(
    ext_ref, lists_ref, even_grad_ref, odd_grad_ref, even_side_ref, odd_side_ref, parents_ref,
    part_ref, to_even_ref, to_odd_ref, up_sums_ref,
):
    bricks, width = part_ref.shape
    face = to_even_ref.shape[0]
    from_next, from_prev = from_pairs(lists_ref, GX, even_grad_ref, odd_grad_ref)
    total = add_rows(ext_ref[...], crosses_of(lists_ref, face), from_next, from_prev)
    part_ref[...] = total[:bricks]
    to_even, to_odd = by_pair(lists_ref, GY, total[bricks + face :], total[bricks : bricks + face])
    to_even_ref[...] = to_even.astype(BF)
    to_odd_ref[...] = to_odd.astype(BF)
    high, low = by_pair(
        lists_ref, GY, even_side_ref[:, width:].astype(F32), odd_side_ref[:, width:].astype(F32)
    )
    side_parents = stack_lanes(stack_rows(low, high), parents_ref.shape[1])
    grads = [stack_parities(total[:bricks].astype(BF)), stack_parities(total[bricks:].astype(BF))]
    up_sum = dot_tn(jnp.concatenate(grads, axis=0), jnp.concatenate([parents_ref[...], side_parents], axis=0))
    coarse = up_sum.shape[1]
    count = up_sums_ref.shape[0]
    for q in range(up_sum.shape[0] // count):
        up_sums_ref[:, q * coarse : (q + 1) * coarse] = up_sum[q * count : (q + 1) * count]


def given_sums_body(
    odd_cross_ref, even_cross_ref, merged_ref, even_side_ref, odd_side_ref, turned_ref, mains_ref, ends_ref, lists_ref,
    up_sums_ref, given_ref, pad_ref, table_ref,
):
    bricks, width = merged_ref.shape
    face = even_side_ref.shape[0]
    rows = bricks + 4 * face
    high, low = by_pair(lists_ref, GY, even_side_ref[:, :width].astype(F32), odd_side_ref[:, :width].astype(F32))
    above, below = from_pairs(lists_ref, GX, even_cross_ref, odd_cross_ref)
    table_ref[:bricks] = merged_ref[...]
    table_ref[bricks:] = stack_rows(low, high, below, above)
    lower_half = iota((rows, 2 * C), 1) < C
    zero = jnp.zeros((rows, 2 * C), BF)
    for x in range(4):
        for y in range(4):
            places = [(X, Y, dx, dy) for X, dx in options(x) for Y, dy in options(y)]
            at = (x * 4 + y) * RUN
            columns = table_ref[:, at : at + RUN]
            first = jnp.where(lower_half, columns[:, : 2 * C], zero)
            second = jnp.where(lower_half, zero, columns[:, 2 * C :])
            ends = jnp.concatenate([ends_ref[3 * dx + dy + 4] for _, _, dx, dy in places], axis=0)
            halo = dot(ends, jnp.concatenate([first, second], axis=0)).astype(BF)
            for i, (X, Y, _, _) in enumerate(places):
                pad_ref[X, Y, :, RUN:] = halo[i * bricks : (i + 1) * bricks]
            pad_ref[x + 1, y + 1, :, :RUN] = columns[:bricks]
            moved = [p for p in places if p[2:] != (0, 0)]
            if moved:
                main = jnp.concatenate([mains_ref[3 * dx + dy + 4] for _, _, dx, dy in moved], axis=0)
                got = dot(main, columns).astype(BF)
                for i, (X, Y, _, _) in enumerate(moved):
                    pad_ref[X, Y, :, :RUN] = got[i * bricks : (i + 1) * bricks]

    half_sums(1 - lists_ref[5, GX], pad_ref, turned_ref, up_sums_ref, given_ref)


def half_sums(group, pad_ref, turned_ref, up_sums_ref, out_ref):
    turned = turned_ref[...]
    half_count = out_ref.shape[0]
    up_lanes = up_sums_ref.shape[1]
    up_half = jnp.where(group == 0, up_sums_ref[:half_count], up_sums_ref[half_count:])
    out_ref[:, :up_lanes] = up_half.astype(out_ref.dtype)
    bricks = pad_ref.shape[2]
    lanes_low = iota((C, 2 * C), 1) < C
    sums = []
    for i in range(5):
        ex, ey = (jnp.where(group == 0, i // 3, (i + 4) // 3), jnp.where(group == 0, i % 3, (i + 4) % 3))
        wide = dot(turned, pad_ref[pl.ds(ex, 4), pl.ds(ey, 4)].reshape(16 * bricks, WIDE))

        def block(z, s):
            return wide[z * C : (z + 1) * C, s * 2 * C : (s + 1) * 2 * C]

        low = jnp.where(lanes_low, block(1, 0) + block(3, 1), block(0, 2) + block(2, 0))
        mid = jnp.where(lanes_low, block(0, 0) + block(2, 1), block(1, 0) + block(3, 1))
        high = jnp.where(lanes_low, block(1, 1) + block(3, 2), block(0, 0) + block(2, 1))
        for value in (low, mid, high):
            sums.append(value + pltpu.roll(value, C, 1))
    sums.append(jnp.zeros((C, 2 * C), F32))
    pairs = [jnp.where(lanes_low, sums[2 * k], sums[2 * k + 1]) for k in range(8)]
    for p in range(7):
        at = up_lanes + p * 2 * C
        out_ref[:, at : at + 2 * C] = jnp.where(group == 0, pairs[p], pairs[p + 1]).astype(out_ref.dtype)


def kept_sums_body(pad_ref, turned_ref, up_sums_ref, lists_ref, kept_ref):
    half_sums(lists_ref[5, GX], pad_ref, turned_ref, up_sums_ref, kept_ref)


def pair_sum_body(kept_ref, given_ref, out_ref):
    out_ref[...] = (kept_ref[...] + given_ref[...].astype(F32)).astype(BF)


def inputs_at(pad_ref, e):
    bricks = pad_ref.shape[2]
    ex, ey = (e // 3, e % 3)
    return pad_ref[ex : ex + 4, ey : ey + 4].reshape(16 * bricks, WIDE)


def conv_body(pad_ref, weight_ref, lists_ref, out_ref, again_ref, band_ref):
    again_ref[...] = lists_ref[...]
    bricks = pad_ref.shape[2]
    build_bands(weight_ref, band_ref)
    total = None
    for e in range(9):
        part = dot(inputs_at(pad_ref, e), band_ref[e])
        total = part if total is None else total + part
    for p in range(16):
        out_ref[:, p * RUN : (p + 1) * RUN] = total[p * bricks : (p + 1) * bricks].astype(BF)


def add_rows(base, lists, first, second):
    count, face = (base.shape[0], lists.shape[1])
    index = jnp.concatenate([lists[0:1], lists[1:2]], axis=1)
    chosen = ones_where(iota((count, 2 * face), 0) == index)
    return base + dot(chosen, stack_rows(first, second))


def merge_body(received_ref, up_ref, fine_ref, lists_ref, merged_ref, parents_ref, a_ref, b_ref):
    bricks, width = fine_ref.shape
    face = a_ref.shape[0]
    parents = merge(received_ref, slots_of(lists_ref, bricks), up_ref, fine_ref, merged_ref, parents_ref)
    lists = sides_of(lists_ref, face)
    lists = by_pair(lists_ref, GY, lists[0:1], lists[1:2])
    for out_ref, rows, owners in zip((a_ref, b_ref), pick_rows(lists, merged_ref[...]), pick_rows(lists, parents)):
        out_ref[:, :width] = rows.astype(BF)
        out_ref[:, width:] = owners.astype(BF)


def fine_grad_body(part_ref, lists_ref, even_ref, odd_ref, up_ref, grad_ref, replies_ref, across):
    bricks = part_ref.shape[0]
    face = even_ref.shape[0]
    from_next, from_prev = from_pairs(lists_ref, GY, even_ref, odd_ref)
    total = add_rows(part_ref[...], sides_of(lists_ref, face), from_next, from_prev)
    grad_ref[...] = total.astype(BF)
    items = dot(stack_parities(grad_ref[...]), up_ref[...]).astype(BF)
    items = jnp.concatenate([items[v * bricks : (v + 1) * bricks] for v in range(8)], axis=1)
    half = items.shape[1] // 2
    count, both_lanes = replies_ref.shape
    pieces = both_lanes // 2 // half
    capacity, group = chip_slots(count, pieces, across)
    slots = slots_of(lists_ref, bricks)
    row = iota((count, bricks), 0)
    for other in range(2):
        owner = device_of(row // group, lists_ref, other, across)
        for j in range(pieces):
            piece = row % group * pieces + j
            named = owner * capacity + piece // 2 == slots
            rows = dot(ones_where(named & (piece % 2 == 0)), items[:, :half])
            rows += dot(ones_where(named & (piece % 2 == 1)), items[:, half:])
            at = (other * pieces + j) * half
            replies_ref[:, at : at + half] = rows.astype(BF)


def chip_slots(count, pieces, across):
    group = count // (across[0] * across[1] // 2)
    return group * pieces // 2, group


def device_of(chip, lists_ref, other, across):
    core = jnp.broadcast_to(lists_ref[5:6, GX : GX + 1], chip.shape)
    core = 1 - core if other else core
    return (chip // across[1] * 2 + core) * across[1] + chip % across[1]


def share_body(sums_ref, replies_ref, out_ref, across):
    count, item_lanes = replies_ref.shape
    share = count // (across[0] * across[1] // 2)
    same = iota((count, count), 0) % share == iota((count, count), 1) % share
    out_ref[:, :item_lanes] = replies_ref[...]
    out_ref[:, item_lanes:] = dot(ones_where(same), sums_ref[...]).astype(BF)


def coarse_part(arrived, sends_ref, lists_ref, other, out_dims, across):
    capacity, devices = sends_ref.shape
    count, item_width = out_dims
    half = item_width // 2
    lanes = arrived.shape[0]
    pieces = arrived.shape[1] // half
    _, group = chip_slots(lanes, pieces, across)
    sends = sends_ref[...].astype(F32).astype(BF)
    lane = iota((1, lanes), 1)
    source = device_of(lane // group, lists_ref, other, across)
    rows = dot(sends, ones_where(source == iota((devices, lanes), 0)))
    totals = [None, None]
    for j in range(pieces):
        piece = lane % group * pieces + j
        picked = jnp.where(piece // 2 == iota((capacity, lanes), 0), rows, 0.0)
        index = jnp.sum(picked, axis=0, keepdims=True).astype(I32)
        named = iota((count, lanes), 0) == index
        for h in range(2):
            part = dot(ones_where(named & (piece % 2 == h)), arrived[:, j * half : (j + 1) * half])
            totals[h] = part if totals[h] is None else totals[h] + part
    return jnp.concatenate(totals, axis=1)


def finish_half(half, conv_ref, up_ref, scale):
    coarse = up_ref.shape[2]
    at = 0
    for q in range(up_ref.shape[0]):
        up_ref[q] = half[:, at : at + coarse].astype(F32) * scale
        at += coarse
    for pair in range(7):
        turned = half[:, at : at + 2 * C].astype(F32).T * scale
        at += 2 * C
        for s in range(2):
            conv_ref[2 * pair + s] = turned[s * C : (s + 1) * C]


def own_half_body(back_ref, sends_ref, lists_ref, conv_ref, up_ref, part_ref, item_lanes, across, scale):
    finish_half(back_ref[:, 2 * item_lanes :], conv_ref, up_ref, scale)
    part_ref[...] = coarse_part(back_ref[:, :item_lanes], sends_ref, lists_ref, 0, part_ref.shape, across)


def last_body(
    given_ref, own_conv_ref, own_up_ref, part_ref, sends_ref, lists_ref,
    conv_ref, up_ref, out_ref, other_conv_ref, other_up_ref, item_lanes, across, scale,
):
    finish_half(given_ref[:, 2 * item_lanes :], other_conv_ref, other_up_ref, scale)
    for o in range(14):
        first, second = by_pair(lists_ref, GX, own_conv_ref[o], other_conv_ref[o])
        conv_ref[o] = first
        if o < 13:
            conv_ref[14 + o] = second
    half_count = own_up_ref.shape[1]
    for q in range(own_up_ref.shape[0]):
        first, second = by_pair(lists_ref, GX, own_up_ref[q], other_up_ref[q])
        up_ref[2 * q * half_count : (2 * q + 1) * half_count] = first
        up_ref[(2 * q + 1) * half_count : (2 * q + 2) * half_count] = second
    came = given_ref[:, item_lanes : 2 * item_lanes]
    other = coarse_part(came, sends_ref, lists_ref, 1, out_ref.shape, across)
    out_ref[...] = (part_ref[...] + other).astype(BF)


def swap(value, axis, first):
    count = lax.axis_size(axis)
    lower = range(first, count - 1, 2)
    return lax.ppermute(value, axis, [(i, i + 1) for i in lower] + [(i + 1, i) for i in lower])


def swap_pairs(to_even, to_odd, axis):
    return swap(to_even, axis, 0), swap(to_odd, axis, 1)


def trade_rows(values, axes):
    rows, width = values.shape
    devices = math.prod(lax.axis_size(axis) for axis in axes)
    grid_view = values.reshape(devices, rows // devices, width)
    return lax.all_to_all(grid_view, axes, split_axis=0, concat_axis=0, tiled=True).reshape(rows, width)


def on_device(
    fine_features, coarse_items, conv_weight, up_weight, neighbours,
    side_sends, cross_sends, parent_slots, coarse_sends, cotangent,
):
    fine = fine_features[0, 0]
    items = coarse_items[0, 0]
    cot = cotangent[0, 0]
    bricks, width = fine.shape
    face = side_sends.shape[-1]
    across = (lax.axis_size(GX_AXES), lax.axis_size("gy"))
    devices = across[0] * across[1]
    capacity = coarse_sends.shape[-1]
    item_count, item_width = items.shape
    coarse = up_weight.shape[1]
    start = bricks + 2 * face
    sends = coarse_sends.transpose(0, 1, 3, 2)[0, 0]
    slots = parent_slots[0]
    sides = side_sends[0, 0]
    crosses = cross_sends[0, 0]
    near = neighbours.transpose(0, 3, 1, 2)[0]
    up_turned = up_weight.transpose(0, 2, 1).reshape(8 * C, coarse)
    half = item_width // 2
    count = 2 * C
    item_lanes = capacity * devices // 2 * item_width // (count // 2)
    sums_width = 8 * C * coarse // count + 14 * C
    rows = shape((bricks, width))
    face_rows = shape((face, width))
    faces_and_parents = shape((face, width + item_width))
    lists_shape = shape((8, 128), I32)
    band = pltpu.VMEM((9, WIDE, RUN), BF)
    conv_flops = 2 * 9 * 16 * bricks * WIDE * RUN

    listed = (sends, items, sides, crosses, slots)
    outgoing, lists = call(
        first_body, [shape((2 * capacity * devices, half)), lists_shape], *listed,
        scratch=[pltpu.VMEM(a.shape, a.dtype) for a in listed] + [pltpu.SemaphoreType.DMA((len(listed),))],
        in_hbm=True,
    )
    received = trade_rows(outgoing, ("x", "core", "gy"))
    lane = jnp.arange(128, dtype=I32)[None]
    parity = jnp.where(lane == GX, lax.axis_index("core"), lax.axis_index("gy") % 2).astype(I32)
    table_rows = start + 2 * face
    ext_grad, to_even, to_odd, turned, mains, ends, lists = call(
        table_grad_body,
        [
            shape((start, width), F32), face_rows, face_rows, shape((RUN, 16 * bricks)),
            shape((9, bricks, table_rows)), shape((9, bricks, 2 * table_rows)), lists_shape,
        ],
        cot, conv_weight, near, lists, parity,
        scratch=[band, pltpu.VMEM((6, 6, bricks, WIDE), F32)], flops=2 * conv_flops,
    )
    cross_grads = swap_pairs(to_even, to_odd, GX_AXES)
    merged, parents, to_even, to_odd = call(
        merge_body, [rows, shape((8 * bricks, coarse)), faces_and_parents, faces_and_parents],
        received, up_turned, fine, lists,
    )
    sides = swap_pairs(to_even, to_odd, "gy")
    to_even, to_odd = call(cross_body, [face_rows, face_rows], merged, *sides, lists)
    crosses = swap_pairs(to_even, to_odd, GX_AXES)
    half_sums_dims = (count // 2, sums_width)
    fine_part, to_even, to_odd, up_sums = call(
        side_grad_body,
        [shape((bricks, width), F32), face_rows, face_rows, shape((count, sums_width - 14 * C), F32)],
        ext_grad, lists, *cross_grads, *sides, parents,
    )
    side_grads = swap_pairs(to_even, to_odd, "gy")
    given, pad = call(
        given_sums_body, [shape(half_sums_dims), shape((6, 6, bricks, WIDE))],
        *crosses[::-1], merged, *sides, turned, mains, ends, lists, up_sums,
        scratch=[pltpu.VMEM((table_rows, width), BF)], flops=conv_flops,
    )
    (kept,) = call(kept_sums_body, [shape(half_sums_dims, F32)], pad, turned, up_sums, lists, flops=conv_flops)
    given = swap(given, "core", 0)
    (sums,) = call(pair_sum_body, [shape(half_sums_dims)], kept, given)
    sums = trade_rows(sums, ("x", "gy"))
    output, lists = call(
        conv_body, [rows, lists_shape], pad, conv_weight, lists, scratch=[band], flops=conv_flops
    )
    grad_fine, replies = call(
        functools.partial(fine_grad_body, across=across), [rows, shape((count // 2, 2 * item_lanes))],
        fine_part, lists, *side_grads, up_turned,
    )
    (back,) = call(
        functools.partial(share_body, across=across), [shape((count // 2, 2 * item_lanes + sums_width))], sums, replies
    )
    back = trade_rows(back, ("x", "gy"))
    given = swap(back, "core", 0)
    scale = 1.0 / math.sqrt(64 * bricks * devices)
    sizes = dict(item_lanes=item_lanes, across=across, scale=scale)
    half_conv, half_up = ((14, C, C), (8 * C // count, count // 2, coarse))
    own_conv, own_up, part = call(
        functools.partial(own_half_body, **sizes),
        [shape(half_conv, F32), shape(half_up, F32), shape((item_count, item_width), F32)], back, sends, lists,
    )
    grad_conv, grad_up, coarse_grad = call(
        functools.partial(last_body, **sizes),
        [shape((27, C, C), F32), shape((8 * C, coarse), F32), shape((item_count, item_width))],
        given, own_conv, own_up, part, sends, lists,
        scratch=[pltpu.VMEM(half_conv, F32), pltpu.VMEM(half_up, F32)],
    )
    return (
        output.reshape(1, 1, bricks, width),
        grad_fine.reshape(1, 1, bricks, width),
        coarse_grad.reshape(1, 1, item_count, item_width),
        grad_conv,
        grad_up.reshape(8, C, coarse).transpose(0, 2, 1),
    )


def solution(mesh):
    groups, across_x, across_y = mesh.devices.shape
    split_mesh = Mesh(mesh.devices.reshape(groups, across_x // 2, 2, across_y), ("groups", "x", "core", "gy"))
    rows = ("groups", "x", "core")
    split = P(rows, "gy", None, None)
    placed = (split, split, P(), P(), split, split, split, P(rows, "gy", None), split, split)
    return jax.shard_map(
        on_device,
        mesh=split_mesh,
        in_specs=placed,
        out_specs=(split, split, split, P("groups", None, None), P("groups", None, None)),
        check_vma=False,
    )
```

```python
import functools
import math

import jax
import jax.numpy as jnp
from jax import lax
from jax.experimental import pallas as pl
from jax.experimental.pallas import tpu as pltpu
from jax.sharding import Mesh
from jax.sharding import PartitionSpec as P

BF = jnp.bfloat16
F32 = jnp.float32
I32 = jnp.int32

C = 64
RUN = 4 * C
WIDE = RUN + 2 * C


def iota(shape, axis):
    return lax.broadcasted_iota(I32, shape, axis)


def ones_where(mask):
    return jnp.where(mask, 1.0, 0.0).astype(BF)


def dot(a, b):
    return jnp.dot(a, b, preferred_element_type=F32)


def dot_tn(a, b):
    return lax.dot_general(a, b, (((0,), (0,)), ((), ())), preferred_element_type=F32)


def dot_nt(a, b):
    return lax.dot_general(a, b, (((1,), (1,)), ((), ())), preferred_element_type=F32)


def column_of(row):
    size = row.shape[1]
    diagonal = iota((size, size), 0) == iota((size, size), 1)
    spread = jnp.broadcast_to(row.astype(F32), (size, size))
    return jnp.sum(jnp.where(diagonal, spread, 0.0), axis=1, keepdims=True).astype(I32)


def call(body, outs, *args, scratch=(), flops=0, in_hbm=False):
    moved = sum(a.size * a.dtype.itemsize for a in list(args) + list(outs))
    return pl.pallas_call(
        body,
        out_shape=tuple(outs),
        in_specs=[pl.BlockSpec(memory_space=pltpu.HBM) if in_hbm else pl.BlockSpec() for _ in args],
        scratch_shapes=tuple(scratch),
        cost_estimate=pl.CostEstimate(flops=flops, bytes_accessed=moved, transcendentals=0),
        compiler_params=pltpu.CompilerParams(vmem_limit_bytes=None if in_hbm else 28 * 2**20),
    )(*args)


def shape(dims, dtype=BF):
    return jax.ShapeDtypeStruct(dims, dtype)


def items_named(sends_ref, count):
    capacity, devices = sends_ref.shape
    group = 2 * capacity
    lanes = devices * group
    spread = ones_where(iota((lanes, devices), 0) // group == iota((lanes, devices), 1))
    slot = iota((lanes, capacity), 0) % group // 2
    values = dot_nt(spread, sends_ref[...].astype(F32).astype(BF))
    item = jnp.sum(jnp.where(slot == iota((lanes, capacity), 1), values, 0.0), axis=1, keepdims=True).astype(I32)
    place = jnp.where(item < count, item + iota((lanes, 1), 0) % 2 * count, -1)
    return ones_where(iota((lanes, 2 * count), 1) == place)


def merge(received_ref, slots, up_ref, fine_ref, merged_ref, parents_ref):
    bricks = fine_ref.shape[0]
    lanes, half = received_ref.shape
    slot = column_of(slots)
    place = iota((bricks, lanes), 1)
    named = place // 2 == slot
    received = received_ref[...]
    parents = jnp.concatenate(
        [dot(ones_where(named & (place % 2 == h)), received) for h in (0, 1)], axis=1
    ).astype(BF)
    coarse = 2 * half // 8
    stacked = jnp.concatenate([parents[:, v * coarse : (v + 1) * coarse] for v in range(8)], axis=0)
    parents_ref[...] = stacked
    lifted = dot_nt(stacked, up_ref[...])
    for v in range(8):
        cx, cy, cz = (v // 4, v // 2 % 2, v % 2)
        for parity in range(4):
            vx, vy = (2 * cx + parity // 2, 2 * cy + parity % 2)
            at = (vx * 4 + vy) * RUN + cz * 2 * C
            add = lifted[v * bricks : (v + 1) * bricks, parity * 2 * C : (parity + 1) * 2 * C]
            merged_ref[:, at : at + 2 * C] = (fine_ref[:, at : at + 2 * C].astype(F32) + add).astype(BF)
    return parents


def pick_rows(lists, rows):
    return [dot_tn(ones_where(iota((rows.shape[0], one.shape[1]), 0) == one), rows) for one in lists]


GX, GY = (0, 1)
GX_AXES = ("x", "core")


def by_pair(lists_ref, axis, of_next, of_prev):
    odd = jnp.broadcast_to(lists_ref[5:6, axis : axis + 1], of_next.shape) == 1
    return jnp.where(odd, of_prev, of_next), jnp.where(odd, of_next, of_prev)


def from_pairs(lists_ref, axis, even_ref, odd_ref):
    return by_pair(lists_ref, axis, even_ref[...].astype(F32), odd_ref[...].astype(F32))


def stack_rows(*parts):
    return jnp.concatenate([p.astype(F32) for p in parts], axis=0).astype(BF)


def sides_of(lists_ref, face):
    return lists_ref[0:2, :face]


def crosses_of(lists_ref, face):
    return lists_ref[2:4, :face]


def slots_of(lists_ref, bricks):
    return lists_ref[4:5, :bricks]


def cross_body(merged_ref, even_ref, odd_ref, lists_ref, a_ref, b_ref):
    face, width = a_ref.shape
    high, low = from_pairs(lists_ref, GY, even_ref, odd_ref)
    rows = jnp.concatenate([merged_ref[...], stack_rows(low[:, :width], high[:, :width])], axis=0)
    lists = crosses_of(lists_ref, face)
    picked = pick_rows(by_pair(lists_ref, GX, lists[0:1], lists[1:2]), rows)
    a_ref[...] = picked[0].astype(BF)
    b_ref[...] = picked[1].astype(BF)


def build_bands(weight_ref, band_ref):
    zero = jnp.zeros((C, C), BF)
    blank = jnp.zeros((C, 2 * C), BF)

    def pair(a, b):
        return jnp.concatenate([a, b], axis=1)

    for e in range(9):
        low, mid, high = (weight_ref[3 * e + z] for z in range(3))
        first, second = (pair(mid, low), pair(high, mid))
        left, right = (pair(low, zero), pair(zero, high))
        rows = (
            (first, blank),
            (second, left),
            (right, first),
            (blank, second),
            (blank, right),
            (left, blank),
        )
        for z, halves in enumerate(rows):
            for s in range(2):
                band_ref[e, z * C : (z + 1) * C, s * 2 * C : (s + 1) * 2 * C] = halves[s]


def options(at):
    return [(at + 1, 0)] + ([(5, 1)] if at == 0 else []) + ([(0, -1)] if at == 3 else [])


def offset_of(dx, dy, dz):
    return (dx + 1) * 9 + (dy + 1) * 3 + dz + 1


def stack_lanes(value, lanes):
    return jnp.concatenate([value[:, p * lanes : (p + 1) * lanes] for p in range(value.shape[1] // lanes)], axis=0)


def stack_parities(value):
    stacked = []
    for v in range(8):
        cx, cy, cz = (v // 4, v // 2 % 2, v % 2)
        lanes = []
        for parity in range(4):
            at = ((2 * cx + parity // 2) * 4 + 2 * cy + parity % 2) * RUN + cz * 2 * C
            lanes.append(value[:, at : at + 2 * C])
        stacked.append(jnp.concatenate(lanes, axis=1))
    return jnp.concatenate(stacked, axis=0)


def stack_runs(ref):
    return jnp.concatenate([ref[:, p * RUN : (p + 1) * RUN] for p in range(16)], axis=0)


def split_two(value):
    head = value.astype(BF)
    return head, (value - head.astype(F32)).astype(BF)


def table_grad_body(
    cot_ref, weight_ref, near_ref, lists_ref, parity_ref,
    ext_ref, even_ref, odd_ref, turned_ref, mains_ref, ends_ref, again_ref, band_ref, pad_ref,
):
    again_ref[...] = lists_ref[...]
    again_ref[5:6] = parity_ref[...]
    bricks = cot_ref.shape[0]
    face = even_ref.shape[0]
    start = ext_ref.shape[0]
    rows = start + 2 * face
    build_bands(weight_ref, band_ref)
    cot = stack_runs(cot_ref)
    turned_ref[...] = cot.T
    pad_ref[...] = jnp.zeros(pad_ref.shape, F32)
    for e in range(9):
        ex, ey = (e // 3, e % 3)
        part = dot_nt(cot, band_ref[e]).reshape(4, 4, bricks, WIDE)
        pad_ref[ex : ex + 4, ey : ey + 4] += part
    near = [near_ref[o] for o in range(27)]

    def chooser(which):
        index = jnp.concatenate([near[o] for o in which], axis=1)
        return ones_where(iota((rows, index.shape[1]), 0) == index)

    lower_half = iota((rows, 2 * C), 1) < C
    cache = {}
    for x in range(4):
        for y in range(4):
            places = [(X, Y, dx, dy) for X, dx in options(x) for Y, dy in options(y)]
            key = tuple((dx, dy) for _, _, dx, dy in places)
            if key not in cache:
                moved = [d for d in key if d != (0, 0)]
                main = chooser([offset_of(*d, 0) for d in moved] * 2) if moved else None
                up = chooser([offset_of(*d, 1) for d in key] * 2)
                down = chooser([offset_of(*d, -1) for d in key] * 2)
                cache[key] = (main, jnp.concatenate([up, down], axis=0))
            main, ends = cache[key]
            own = pad_ref[x + 1, y + 1, :, :RUN]
            own = jnp.concatenate([own, jnp.zeros((rows - bricks, RUN), F32)], axis=0)
            if main is not None:
                parts = [split_two(pad_ref[X, Y, :, :RUN]) for X, Y, dx, dy in places if (dx, dy) != (0, 0)]
                value = jnp.concatenate([p[0] for p in parts] + [p[1] for p in parts], axis=0)
                own += dot(main, value)
            parts = [split_two(pad_ref[X, Y, :, RUN:]) for X, Y, _, _ in places]
            value = jnp.concatenate([p[0] for p in parts] + [p[1] for p in parts], axis=0)
            halo = dot(ends, value)
            first = own[:, : 2 * C] + jnp.where(lower_half, halo[:rows], 0.0)
            second = own[:, 2 * C :] + jnp.where(lower_half, 0.0, halo[rows:])
            total = jnp.concatenate([first, second], axis=1)
            at = (x * 4 + y) * RUN
            ext_ref[:, at : at + RUN] = total[:start]
            even, odd = by_pair(again_ref, GX, total[start + face :], total[start : start + face])
            even_ref[:, at : at + RUN] = even.astype(BF)
            odd_ref[:, at : at + RUN] = odd.astype(BF)
    make_choosers(near_ref, rows, mains_ref, ends_ref)


def make_choosers(near_ref, rows, mains_ref, ends_ref):
    bricks = mains_ref.shape[1]
    near = jnp.concatenate([near_ref[o] for o in range(27)] + [jnp.zeros((5, bricks), I32)], axis=0)
    near = near.astype(F32).T.astype(I32)
    place = iota((bricks, rows), 1)
    pair_place = iota((bricks, 2 * rows), 1)
    for d in range(9):
        down, straight, up = (near[:, 3 * d + z : 3 * d + z + 1] for z in range(3))
        mains_ref[d] = ones_where(place == straight)
        ends_ref[d] = ones_where(pair_place == jnp.where(pair_place < rows, up, down + rows))


def first_body(
    sends_hbm, items_hbm, sides_hbm, crosses_hbm, slots_hbm, out_ref, lists_ref,
    sends_ref, items_ref, sides_ref, crosses_ref, slots_ref, arrived,
):
    sources = (sends_hbm, items_hbm, sides_hbm, crosses_hbm, slots_hbm)
    places = (sends_ref, items_ref, sides_ref, crosses_ref, slots_ref)
    copies = [pltpu.make_async_copy(s, p, arrived.at[i]) for i, (s, p) in enumerate(zip(sources, places))]
    for copy in copies:
        copy.start()
    copies[0].wait()
    chosen = items_named(sends_ref, items_ref.shape[0])
    copies[1].wait()
    half = out_ref.shape[1]
    items = jnp.concatenate([items_ref[:, :half], items_ref[:, half:]], axis=0)
    out_ref[...] = dot(chosen, items).astype(BF)
    for copy in copies[2:]:
        copy.wait()
    face, bricks = (sides_ref.shape[1], slots_ref.shape[1])
    lists_ref[...] = jnp.zeros(lists_ref.shape, I32)
    lists_ref[0:2, :face] = sides_ref[...]
    lists_ref[2:4, :face] = crosses_ref[...]
    lists_ref[4:5, :bricks] = slots_ref[...]


def side_grad_body(
    ext_ref, lists_ref, even_grad_ref, odd_grad_ref, even_side_ref, odd_side_ref, parents_ref,
    conv_given_ref, part_ref, to_even_ref, to_odd_ref, up_kept_ref, given_ref, up_sums_ref,
):
    bricks, width = part_ref.shape
    face = to_even_ref.shape[0]
    from_next, from_prev = from_pairs(lists_ref, GX, even_grad_ref, odd_grad_ref)
    total = add_rows(ext_ref[...], crosses_of(lists_ref, face), from_next, from_prev)
    part_ref[...] = total[:bricks]
    to_even, to_odd = by_pair(lists_ref, GY, total[bricks + face :], total[bricks : bricks + face])
    to_even_ref[...] = to_even.astype(BF)
    to_odd_ref[...] = to_odd.astype(BF)
    high, low = by_pair(
        lists_ref, GY, even_side_ref[:, width:].astype(F32), odd_side_ref[:, width:].astype(F32)
    )
    side_parents = stack_lanes(stack_rows(low, high), parents_ref.shape[1])
    grads = [stack_parities(total[:bricks].astype(BF)), stack_parities(total[bricks:].astype(BF))]
    up_sum = dot_tn(jnp.concatenate(grads, axis=0), jnp.concatenate([parents_ref[...], side_parents], axis=0))
    coarse = up_sum.shape[1]
    count = up_sums_ref.shape[0]
    for q in range(up_sum.shape[0] // count):
        up_sums_ref[:, q * coarse : (q + 1) * coarse] = up_sum[q * count : (q + 1) * count]
    kept, given = by_pair(lists_ref, GX, up_sums_ref[: count // 2], up_sums_ref[count // 2 :])
    up_kept_ref[...] = kept
    up_lanes = kept.shape[1]
    given_ref[:, :up_lanes] = given.astype(BF)
    given_ref[:, up_lanes:] = conv_given_ref[...]


def given_sums_body(
    odd_cross_ref, even_cross_ref, merged_ref, even_side_ref, odd_side_ref, turned_ref, mains_ref, ends_ref, lists_ref,
    given_ref, pad_ref, table_ref,
):
    bricks, width = merged_ref.shape
    face = even_side_ref.shape[0]
    rows = bricks + 4 * face
    high, low = by_pair(lists_ref, GY, even_side_ref[:, :width].astype(F32), odd_side_ref[:, :width].astype(F32))
    above, below = from_pairs(lists_ref, GX, even_cross_ref, odd_cross_ref)
    table_ref[:bricks] = merged_ref[...]
    table_ref[bricks:] = stack_rows(low, high, below, above)
    lower_half = iota((rows, 2 * C), 1) < C
    zero = jnp.zeros((rows, 2 * C), BF)
    for x in range(4):
        for y in range(4):
            places = [(X, Y, dx, dy) for X, dx in options(x) for Y, dy in options(y)]
            at = (x * 4 + y) * RUN
            columns = table_ref[:, at : at + RUN]
            first = jnp.where(lower_half, columns[:, : 2 * C], zero)
            second = jnp.where(lower_half, zero, columns[:, 2 * C :])
            ends = jnp.concatenate([ends_ref[3 * dx + dy + 4] for _, _, dx, dy in places], axis=0)
            halo = dot(ends, jnp.concatenate([first, second], axis=0)).astype(BF)
            for i, (X, Y, _, _) in enumerate(places):
                pad_ref[X, Y, :, RUN:] = halo[i * bricks : (i + 1) * bricks]
            pad_ref[x + 1, y + 1, :, :RUN] = columns[:bricks]
            moved = [p for p in places if p[2:] != (0, 0)]
            if moved:
                main = jnp.concatenate([mains_ref[3 * dx + dy + 4] for _, _, dx, dy in moved], axis=0)
                got = dot(main, columns).astype(BF)
                for i, (X, Y, _, _) in enumerate(moved):
                    pad_ref[X, Y, :, :RUN] = got[i * bricks : (i + 1) * bricks]

    half_sums(1 - lists_ref[5, GX], pad_ref, turned_ref, given_ref, 0)


def half_sums(group, pad_ref, turned_ref, out_ref, start):
    turned = turned_ref[...]
    bricks = pad_ref.shape[2]
    lanes_low = iota((C, 2 * C), 1) < C
    sums = []
    for i in range(5):
        ex, ey = (jnp.where(group == 0, i // 3, (i + 4) // 3), jnp.where(group == 0, i % 3, (i + 4) % 3))
        wide = dot(turned, pad_ref[pl.ds(ex, 4), pl.ds(ey, 4)].reshape(16 * bricks, WIDE))

        def block(z, s):
            return wide[z * C : (z + 1) * C, s * 2 * C : (s + 1) * 2 * C]

        low = jnp.where(lanes_low, block(1, 0) + block(3, 1), block(0, 2) + block(2, 0))
        mid = jnp.where(lanes_low, block(0, 0) + block(2, 1), block(1, 0) + block(3, 1))
        high = jnp.where(lanes_low, block(1, 1) + block(3, 2), block(0, 0) + block(2, 1))
        for value in (low, mid, high):
            sums.append(value + pltpu.roll(value, C, 1))
    sums.append(jnp.zeros((C, 2 * C), F32))
    pairs = [jnp.where(lanes_low, sums[2 * k], sums[2 * k + 1]) for k in range(8)]
    for p in range(7):
        at = start + p * 2 * C
        out_ref[:, at : at + 2 * C] = jnp.where(group == 0, pairs[p], pairs[p + 1]).astype(out_ref.dtype)


def kept_sums_body(pad_ref, turned_ref, up_kept_ref, lists_ref, kept_ref):
    up_lanes = up_kept_ref.shape[1]
    kept_ref[:, :up_lanes] = up_kept_ref[...]
    half_sums(lists_ref[5, GX], pad_ref, turned_ref, kept_ref, up_lanes)


def pair_sum_body(kept_ref, given_ref, out_ref):
    out_ref[...] = (kept_ref[...] + given_ref[...].astype(F32)).astype(BF)


def inputs_at(pad_ref, e):
    bricks = pad_ref.shape[2]
    ex, ey = (e // 3, e % 3)
    return pad_ref[ex : ex + 4, ey : ey + 4].reshape(16 * bricks, WIDE)


def conv_body(pad_ref, weight_ref, lists_ref, out_ref, again_ref, band_ref):
    again_ref[...] = lists_ref[...]
    bricks = pad_ref.shape[2]
    build_bands(weight_ref, band_ref)
    total = None
    for e in range(9):
        part = dot(inputs_at(pad_ref, e), band_ref[e])
        total = part if total is None else total + part
    for p in range(16):
        out_ref[:, p * RUN : (p + 1) * RUN] = total[p * bricks : (p + 1) * bricks].astype(BF)


def add_rows(base, lists, first, second):
    count, face = (base.shape[0], lists.shape[1])
    index = jnp.concatenate([lists[0:1], lists[1:2]], axis=1)
    chosen = ones_where(iota((count, 2 * face), 0) == index)
    return base + dot(chosen, stack_rows(first, second))


def merge_body(received_ref, up_ref, fine_ref, lists_ref, merged_ref, parents_ref, a_ref, b_ref):
    bricks, width = fine_ref.shape
    face = a_ref.shape[0]
    parents = merge(received_ref, slots_of(lists_ref, bricks), up_ref, fine_ref, merged_ref, parents_ref)
    lists = sides_of(lists_ref, face)
    lists = by_pair(lists_ref, GY, lists[0:1], lists[1:2])
    for out_ref, rows, owners in zip((a_ref, b_ref), pick_rows(lists, merged_ref[...]), pick_rows(lists, parents)):
        out_ref[:, :width] = rows.astype(BF)
        out_ref[:, width:] = owners.astype(BF)


def fine_grad_body(part_ref, lists_ref, even_ref, odd_ref, up_ref, grad_ref, replies_ref, across):
    bricks = part_ref.shape[0]
    face = even_ref.shape[0]
    from_next, from_prev = from_pairs(lists_ref, GY, even_ref, odd_ref)
    total = add_rows(part_ref[...], sides_of(lists_ref, face), from_next, from_prev)
    grad_ref[...] = total.astype(BF)
    items = dot(stack_parities(grad_ref[...]), up_ref[...]).astype(BF)
    items = jnp.concatenate([items[v * bricks : (v + 1) * bricks] for v in range(8)], axis=1)
    half = items.shape[1] // 2
    count, both_lanes = replies_ref.shape
    pieces = both_lanes // 2 // half
    capacity, group = chip_slots(count, pieces, across)
    slots = slots_of(lists_ref, bricks)
    row = iota((count, bricks), 0)
    for other in range(2):
        owner = device_of(row // group, lists_ref, other, across)
        for j in range(pieces):
            piece = row % group * pieces + j
            named = owner * capacity + piece // 2 == slots
            rows = dot(ones_where(named & (piece % 2 == 0)), items[:, :half])
            rows += dot(ones_where(named & (piece % 2 == 1)), items[:, half:])
            at = (other * pieces + j) * half
            replies_ref[:, at : at + half] = rows.astype(BF)


def chip_slots(count, pieces, across):
    group = count // (across[0] * across[1] // 2)
    return group * pieces // 2, group


def device_of(chip, lists_ref, other, across):
    core = jnp.broadcast_to(lists_ref[5:6, GX : GX + 1], chip.shape)
    core = 1 - core if other else core
    return (chip // across[1] * 2 + core) * across[1] + chip % across[1]


def share_body(sums_ref, replies_ref, out_ref, across):
    count, item_lanes = replies_ref.shape
    share = count // (across[0] * across[1] // 2)
    same = iota((count, count), 0) % share == iota((count, count), 1) % share
    out_ref[:, :item_lanes] = replies_ref[...]
    out_ref[:, item_lanes:] = dot(ones_where(same), sums_ref[...]).astype(BF)


def coarse_grad(arrivals, sends_ref, lists_ref, out_ref, across):
    capacity, devices = sends_ref.shape
    count, item_width = out_ref.shape
    half = item_width // 2
    lanes = arrivals[0].shape[0]
    pieces = arrivals[0].shape[1] // half
    _, group = chip_slots(lanes, pieces, across)
    sends = sends_ref[...].astype(F32).astype(BF)
    lane = iota((1, lanes), 1)
    totals = [None, None]
    for other in range(2):
        source = device_of(lane // group, lists_ref, other, across)
        rows = dot(sends, ones_where(source == iota((devices, lanes), 0)))
        for j in range(pieces):
            piece = lane % group * pieces + j
            picked = jnp.where(piece // 2 == iota((capacity, lanes), 0), rows, 0.0)
            index = jnp.sum(picked, axis=0, keepdims=True).astype(I32)
            named = iota((count, lanes), 0) == index
            for h in range(2):
                part = dot(ones_where(named & (piece % 2 == h)), arrivals[other][:, j * half : (j + 1) * half])
                totals[h] = part if totals[h] is None else totals[h] + part
    for h in range(2):
        out_ref[:, h * half : (h + 1) * half] = totals[h].astype(BF)


def last_body(back_ref, given_ref, sends_ref, lists_ref, conv_ref, up_ref, out_ref, item_lanes, across, scale):
    half_count = back_ref.shape[0]
    items = (back_ref[:, :item_lanes], given_ref[:, item_lanes : 2 * item_lanes])
    coarse_grad(items, sends_ref, lists_ref, out_ref, across)
    coarse = up_ref.shape[1]
    count = 2 * half_count
    parts = up_ref.shape[0] // count
    own = back_ref[:, 2 * item_lanes :].astype(F32) * scale
    others = given_ref[:, 2 * item_lanes :].astype(F32) * scale
    first, second = by_pair(lists_ref, GX, own, others)
    at = 0
    for q in range(parts):
        up_ref[q * count : q * count + half_count] = first[:, at : at + coarse]
        up_ref[q * count + half_count : (q + 1) * count] = second[:, at : at + coarse]
        at += coarse
    for pair in range(7):
        turned = jnp.concatenate([first[:, at : at + 2 * C], second[:, at : at + 2 * C]], axis=0).T
        at += 2 * C
        for h in range(2):
            for s in range(2):
                o = 14 * h + 2 * pair + s
                if o < 27:
                    conv_ref[o] = turned[s * C : (s + 1) * C, h * C : (h + 1) * C]


def swap(value, axis, first):
    count = lax.axis_size(axis)
    lower = range(first, count - 1, 2)
    return lax.ppermute(value, axis, [(i, i + 1) for i in lower] + [(i + 1, i) for i in lower])


def swap_pairs(to_even, to_odd, axis):
    return swap(to_even, axis, 0), swap(to_odd, axis, 1)


def trade_rows(values, axes):
    rows, width = values.shape
    devices = math.prod(lax.axis_size(axis) for axis in axes)
    grid_view = values.reshape(devices, rows // devices, width)
    return lax.all_to_all(grid_view, axes, split_axis=0, concat_axis=0, tiled=True).reshape(rows, width)


def on_device(
    fine_features, coarse_items, conv_weight, up_weight, neighbours,
    side_sends, cross_sends, parent_slots, coarse_sends, cotangent,
):
    fine = fine_features[0, 0]
    items = coarse_items[0, 0]
    cot = cotangent[0, 0]
    bricks, width = fine.shape
    face = side_sends.shape[-1]
    across = (lax.axis_size(GX_AXES), lax.axis_size("gy"))
    devices = across[0] * across[1]
    capacity = coarse_sends.shape[-1]
    item_count, item_width = items.shape
    coarse = up_weight.shape[1]
    start = bricks + 2 * face
    sends = coarse_sends.transpose(0, 1, 3, 2)[0, 0]
    slots = parent_slots[0]
    sides = side_sends[0, 0]
    crosses = cross_sends[0, 0]
    near = neighbours.transpose(0, 3, 1, 2)[0]
    up_turned = up_weight.transpose(0, 2, 1).reshape(8 * C, coarse)
    half = item_width // 2
    count = 2 * C
    item_lanes = capacity * devices // 2 * item_width // (count // 2)
    sums_width = 8 * C * coarse // count + 14 * C
    rows = shape((bricks, width))
    face_rows = shape((face, width))
    faces_and_parents = shape((face, width + item_width))
    lists_shape = shape((8, 128), I32)
    band = pltpu.VMEM((9, WIDE, RUN), BF)
    conv_flops = 2 * 9 * 16 * bricks * WIDE * RUN

    listed = (sends, items, sides, crosses, slots)
    outgoing, lists = call(
        first_body, [shape((2 * capacity * devices, half)), lists_shape], *listed,
        scratch=[pltpu.VMEM(a.shape, a.dtype) for a in listed] + [pltpu.SemaphoreType.DMA((len(listed),))],
        in_hbm=True,
    )
    received = trade_rows(outgoing, ("x", "core", "gy"))
    lane = jnp.arange(128, dtype=I32)[None]
    parity = jnp.where(lane == GX, lax.axis_index("core"), lax.axis_index("gy") % 2).astype(I32)
    table_rows = start + 2 * face
    ext_grad, to_even, to_odd, turned, mains, ends, lists = call(
        table_grad_body,
        [
            shape((start, width), F32), face_rows, face_rows, shape((RUN, 16 * bricks)),
            shape((9, bricks, table_rows)), shape((9, bricks, 2 * table_rows)), lists_shape,
        ],
        cot, conv_weight, near, lists, parity,
        scratch=[band, pltpu.VMEM((6, 6, bricks, WIDE), F32)], flops=2 * conv_flops,
    )
    cross_grads = swap_pairs(to_even, to_odd, GX_AXES)
    merged, parents, to_even, to_odd = call(
        merge_body, [rows, shape((8 * bricks, coarse)), faces_and_parents, faces_and_parents],
        received, up_turned, fine, lists,
    )
    sides = swap_pairs(to_even, to_odd, "gy")
    to_even, to_odd = call(cross_body, [face_rows, face_rows], merged, *sides, lists)
    crosses = swap_pairs(to_even, to_odd, GX_AXES)
    half_sums_dims = (count // 2, sums_width)
    conv_given, pad = call(
        given_sums_body, [shape((count // 2, 14 * C)), shape((6, 6, bricks, WIDE))],
        *crosses[::-1], merged, *sides, turned, mains, ends, lists,
        scratch=[pltpu.VMEM((table_rows, width), BF)], flops=conv_flops,
    )
    up_lanes = sums_width - 14 * C
    fine_part, to_even, to_odd, up_kept, given = call(
        side_grad_body,
        [
            shape((bricks, width), F32), face_rows, face_rows, shape((count // 2, up_lanes), F32),
            shape(half_sums_dims),
        ],
        ext_grad, lists, *cross_grads, *sides, parents, conv_given,
        scratch=[pltpu.VMEM((count, up_lanes), F32)],
    )
    side_grads = swap_pairs(to_even, to_odd, "gy")
    (kept,) = call(kept_sums_body, [shape(half_sums_dims, F32)], pad, turned, up_kept, lists, flops=conv_flops)
    given = swap(given, "core", 0)
    (sums,) = call(pair_sum_body, [shape(half_sums_dims)], kept, given)
    sums = trade_rows(sums, ("x", "gy"))
    output, lists = call(
        conv_body, [rows, lists_shape], pad, conv_weight, lists, scratch=[band], flops=conv_flops
    )
    grad_fine, replies = call(
        functools.partial(fine_grad_body, across=across), [rows, shape((count // 2, 2 * item_lanes))],
        fine_part, lists, *side_grads, up_turned,
    )
    (back,) = call(
        functools.partial(share_body, across=across), [shape((count // 2, 2 * item_lanes + sums_width))], sums, replies
    )
    back = trade_rows(back, ("x", "gy"))
    given = swap(back, "core", 0)
    scale = 1.0 / math.sqrt(64 * bricks * devices)
    grad_conv, grad_up, coarse_grad = call(
        functools.partial(last_body, item_lanes=item_lanes, across=across, scale=scale),
        [shape((27, C, C), F32), shape((8 * C, coarse), F32), shape((item_count, item_width))],
        back, given, sends, lists,
    )
    return (
        output.reshape(1, 1, bricks, width),
        grad_fine.reshape(1, 1, bricks, width),
        coarse_grad.reshape(1, 1, item_count, item_width),
        grad_conv,
        grad_up.reshape(8, C, coarse).transpose(0, 2, 1),
    )


def solution(mesh):
    groups, across_x, across_y = mesh.devices.shape
    split_mesh = Mesh(mesh.devices.reshape(groups, across_x // 2, 2, across_y), ("groups", "x", "core", "gy"))
    rows = ("groups", "x", "core")
    split = P(rows, "gy", None, None)
    placed = (split, split, P(), P(), split, split, split, P(rows, "gy", None), split, split)
    return jax.shard_map(
        on_device,
        mesh=split_mesh,
        in_specs=placed,
        out_specs=(split, split, split, P("groups", None, None), P("groups", None, None)),
        check_vma=False,
    )
```

```python
import functools
import math

import jax
import jax.numpy as jnp
from jax import lax
from jax.experimental import pallas as pl
from jax.experimental.pallas import tpu as pltpu
from jax.sharding import Mesh
from jax.sharding import PartitionSpec as P

BF = jnp.bfloat16
F32 = jnp.float32
I32 = jnp.int32

C = 64
RUN = 4 * C
WIDE = RUN + 2 * C


def iota(shape, axis):
    return lax.broadcasted_iota(I32, shape, axis)


def ones_where(mask):
    return jnp.where(mask, 1.0, 0.0).astype(BF)


def dot(a, b):
    return jnp.dot(a, b, preferred_element_type=F32)


def dot_tn(a, b):
    return lax.dot_general(a, b, (((0,), (0,)), ((), ())), preferred_element_type=F32)


def dot_nt(a, b):
    return lax.dot_general(a, b, (((1,), (1,)), ((), ())), preferred_element_type=F32)


def column_of(row):
    size = row.shape[1]
    diagonal = iota((size, size), 0) == iota((size, size), 1)
    spread = jnp.broadcast_to(row.astype(F32), (size, size))
    return jnp.sum(jnp.where(diagonal, spread, 0.0), axis=1, keepdims=True).astype(I32)


def call(body, outs, *args, scratch=(), flops=0, in_hbm=False):
    moved = sum(a.size * a.dtype.itemsize for a in list(args) + list(outs))
    return pl.pallas_call(
        body,
        out_shape=tuple(outs),
        in_specs=[pl.BlockSpec(memory_space=pltpu.HBM) if in_hbm else pl.BlockSpec() for _ in args],
        scratch_shapes=tuple(scratch),
        cost_estimate=pl.CostEstimate(flops=flops, bytes_accessed=moved, transcendentals=0),
        compiler_params=pltpu.CompilerParams(vmem_limit_bytes=None if in_hbm else 28 * 2**20),
    )(*args)


def shape(dims, dtype=BF):
    return jax.ShapeDtypeStruct(dims, dtype)


def items_named(sends_ref, count):
    capacity, devices = sends_ref.shape
    group = 2 * capacity
    lanes = devices * group
    spread = ones_where(iota((lanes, devices), 0) // group == iota((lanes, devices), 1))
    slot = iota((lanes, capacity), 0) % group // 2
    values = dot_nt(spread, sends_ref[...].astype(F32).astype(BF))
    item = jnp.sum(jnp.where(slot == iota((lanes, capacity), 1), values, 0.0), axis=1, keepdims=True).astype(I32)
    place = jnp.where(item < count, item + iota((lanes, 1), 0) % 2 * count, -1)
    return ones_where(iota((lanes, 2 * count), 1) == place)


def merge(received_ref, slots, up_ref, fine_ref, merged_ref, parents_ref):
    bricks = fine_ref.shape[0]
    lanes, half = received_ref.shape
    slot = column_of(slots)
    place = iota((bricks, lanes), 1)
    named = place // 2 == slot
    received = received_ref[...]
    parents = jnp.concatenate(
        [dot(ones_where(named & (place % 2 == h)), received) for h in (0, 1)], axis=1
    ).astype(BF)
    coarse = 2 * half // 8
    stacked = jnp.concatenate([parents[:, v * coarse : (v + 1) * coarse] for v in range(8)], axis=0)
    parents_ref[...] = stacked
    lifted = dot_nt(stacked, up_ref[...])
    for v in range(8):
        cx, cy, cz = (v // 4, v // 2 % 2, v % 2)
        for parity in range(4):
            vx, vy = (2 * cx + parity // 2, 2 * cy + parity % 2)
            at = (vx * 4 + vy) * RUN + cz * 2 * C
            add = lifted[v * bricks : (v + 1) * bricks, parity * 2 * C : (parity + 1) * 2 * C]
            merged_ref[:, at : at + 2 * C] = (fine_ref[:, at : at + 2 * C].astype(F32) + add).astype(BF)
    return parents


def pick_rows(lists, rows):
    return [dot_tn(ones_where(iota((rows.shape[0], one.shape[1]), 0) == one), rows) for one in lists]


GX, GY = (0, 1)
GX_AXES = ("x", "core")


def by_pair(lists_ref, axis, of_next, of_prev):
    odd = jnp.broadcast_to(lists_ref[5:6, axis : axis + 1], of_next.shape) == 1
    return jnp.where(odd, of_prev, of_next), jnp.where(odd, of_next, of_prev)


def from_pairs(lists_ref, axis, even_ref, odd_ref):
    return by_pair(lists_ref, axis, even_ref[...].astype(F32), odd_ref[...].astype(F32))


def stack_rows(*parts):
    return jnp.concatenate([p.astype(F32) for p in parts], axis=0).astype(BF)


def sides_of(lists_ref, face):
    return lists_ref[0:2, :face]


def crosses_of(lists_ref, face):
    return lists_ref[2:4, :face]


def slots_of(lists_ref, bricks):
    return lists_ref[4:5, :bricks]


def cross_body(merged_ref, even_ref, odd_ref, lists_ref, a_ref, b_ref):
    face, width = a_ref.shape
    high, low = from_pairs(lists_ref, GY, even_ref, odd_ref)
    rows = jnp.concatenate([merged_ref[...], stack_rows(low[:, :width], high[:, :width])], axis=0)
    lists = crosses_of(lists_ref, face)
    picked = pick_rows(by_pair(lists_ref, GX, lists[0:1], lists[1:2]), rows)
    a_ref[...] = picked[0].astype(BF)
    b_ref[...] = picked[1].astype(BF)


def build_bands(weight_ref, band_ref):
    zero = jnp.zeros((C, C), BF)
    blank = jnp.zeros((C, 2 * C), BF)

    def pair(a, b):
        return jnp.concatenate([a, b], axis=1)

    for e in range(9):
        low, mid, high = (weight_ref[3 * e + z] for z in range(3))
        first, second = (pair(mid, low), pair(high, mid))
        left, right = (pair(low, zero), pair(zero, high))
        rows = (
            (first, blank),
            (second, left),
            (right, first),
            (blank, second),
            (blank, right),
            (left, blank),
        )
        for z, halves in enumerate(rows):
            for s in range(2):
                band_ref[e, z * C : (z + 1) * C, s * 2 * C : (s + 1) * 2 * C] = halves[s]


def options(at):
    return [(at + 1, 0)] + ([(5, 1)] if at == 0 else []) + ([(0, -1)] if at == 3 else [])


def offset_of(dx, dy, dz):
    return (dx + 1) * 9 + (dy + 1) * 3 + dz + 1


def stack_lanes(value, lanes):
    return jnp.concatenate([value[:, p * lanes : (p + 1) * lanes] for p in range(value.shape[1] // lanes)], axis=0)


def stack_parities(value):
    stacked = []
    for v in range(8):
        cx, cy, cz = (v // 4, v // 2 % 2, v % 2)
        lanes = []
        for parity in range(4):
            at = ((2 * cx + parity // 2) * 4 + 2 * cy + parity % 2) * RUN + cz * 2 * C
            lanes.append(value[:, at : at + 2 * C])
        stacked.append(jnp.concatenate(lanes, axis=1))
    return jnp.concatenate(stacked, axis=0)


def stack_runs(ref):
    return jnp.concatenate([ref[:, p * RUN : (p + 1) * RUN] for p in range(16)], axis=0)


def split_two(value):
    head = value.astype(BF)
    return head, (value - head.astype(F32)).astype(BF)


def table_grad_body(
    cot_ref, weight_ref, near_ref, lists_ref, parity_ref,
    ext_ref, even_ref, odd_ref, turned_ref, mains_ref, ends_ref, again_ref, band_ref, pad_ref,
):
    again_ref[...] = lists_ref[...]
    again_ref[5:6] = parity_ref[...]
    bricks = cot_ref.shape[0]
    face = even_ref.shape[0]
    start = ext_ref.shape[0]
    rows = start + 2 * face
    build_bands(weight_ref, band_ref)
    cot = stack_runs(cot_ref)
    turned_ref[...] = cot.T
    pad_ref[...] = jnp.zeros(pad_ref.shape, F32)
    for e in range(9):
        ex, ey = (e // 3, e % 3)
        part = dot_nt(cot, band_ref[e]).reshape(4, 4, bricks, WIDE)
        pad_ref[ex : ex + 4, ey : ey + 4] += part
    near = [near_ref[o] for o in range(27)]

    def chooser(which):
        index = jnp.concatenate([near[o] for o in which], axis=1)
        return ones_where(iota((rows, index.shape[1]), 0) == index)

    lower_half = iota((rows, 2 * C), 1) < C
    cache = {}
    for x in range(4):
        for y in range(4):
            places = [(X, Y, dx, dy) for X, dx in options(x) for Y, dy in options(y)]
            key = tuple((dx, dy) for _, _, dx, dy in places)
            if key not in cache:
                moved = [d for d in key if d != (0, 0)]
                main = chooser([offset_of(*d, 0) for d in moved] * 2) if moved else None
                up = chooser([offset_of(*d, 1) for d in key] * 2)
                down = chooser([offset_of(*d, -1) for d in key] * 2)
                cache[key] = (main, jnp.concatenate([up, down], axis=0))
            main, ends = cache[key]
            own = pad_ref[x + 1, y + 1, :, :RUN]
            own = jnp.concatenate([own, jnp.zeros((rows - bricks, RUN), F32)], axis=0)
            if main is not None:
                parts = [split_two(pad_ref[X, Y, :, :RUN]) for X, Y, dx, dy in places if (dx, dy) != (0, 0)]
                value = jnp.concatenate([p[0] for p in parts] + [p[1] for p in parts], axis=0)
                own += dot(main, value)
            parts = [split_two(pad_ref[X, Y, :, RUN:]) for X, Y, _, _ in places]
            value = jnp.concatenate([p[0] for p in parts] + [p[1] for p in parts], axis=0)
            halo = dot(ends, value)
            first = own[:, : 2 * C] + jnp.where(lower_half, halo[:rows], 0.0)
            second = own[:, 2 * C :] + jnp.where(lower_half, 0.0, halo[rows:])
            total = jnp.concatenate([first, second], axis=1)
            at = (x * 4 + y) * RUN
            ext_ref[:, at : at + RUN] = total[:start]
            even, odd = by_pair(again_ref, GX, total[start + face :], total[start : start + face])
            even_ref[:, at : at + RUN] = even.astype(BF)
            odd_ref[:, at : at + RUN] = odd.astype(BF)
    make_choosers(near_ref, rows, mains_ref, ends_ref)


def make_choosers(near_ref, rows, mains_ref, ends_ref):
    bricks = mains_ref.shape[1]
    near = jnp.concatenate([near_ref[o] for o in range(27)] + [jnp.zeros((5, bricks), I32)], axis=0)
    near = near.astype(F32).T.astype(I32)
    place = iota((bricks, rows), 1)
    pair_place = iota((bricks, 2 * rows), 1)
    for d in range(9):
        down, straight, up = (near[:, 3 * d + z : 3 * d + z + 1] for z in range(3))
        mains_ref[d] = ones_where(place == straight)
        ends_ref[d] = ones_where(pair_place == jnp.where(pair_place < rows, up, down + rows))


def first_body(
    sends_hbm, items_hbm, sides_hbm, crosses_hbm, slots_hbm, out_ref, lists_ref,
    sends_ref, items_ref, sides_ref, crosses_ref, slots_ref, arrived,
):
    sources = (sends_hbm, items_hbm, sides_hbm, crosses_hbm, slots_hbm)
    places = (sends_ref, items_ref, sides_ref, crosses_ref, slots_ref)
    copies = [pltpu.make_async_copy(s, p, arrived.at[i]) for i, (s, p) in enumerate(zip(sources, places))]
    for copy in copies:
        copy.start()
    copies[0].wait()
    chosen = items_named(sends_ref, items_ref.shape[0])
    copies[1].wait()
    half = out_ref.shape[1]
    items = jnp.concatenate([items_ref[:, :half], items_ref[:, half:]], axis=0)
    out_ref[...] = dot(chosen, items).astype(BF)
    for copy in copies[2:]:
        copy.wait()
    face, bricks = (sides_ref.shape[1], slots_ref.shape[1])
    lists_ref[...] = jnp.zeros(lists_ref.shape, I32)
    lists_ref[0:2, :face] = sides_ref[...]
    lists_ref[2:4, :face] = crosses_ref[...]
    lists_ref[4:5, :bricks] = slots_ref[...]


def side_grad_body(
    ext_ref, lists_ref, even_grad_ref, odd_grad_ref, even_side_ref, odd_side_ref, parents_ref,
    part_ref, to_even_ref, to_odd_ref, up_sums_ref,
):
    bricks, width = part_ref.shape
    face = to_even_ref.shape[0]
    from_next, from_prev = from_pairs(lists_ref, GX, even_grad_ref, odd_grad_ref)
    total = add_rows(ext_ref[...], crosses_of(lists_ref, face), from_next, from_prev)
    part_ref[...] = total[:bricks]
    to_even, to_odd = by_pair(lists_ref, GY, total[bricks + face :], total[bricks : bricks + face])
    to_even_ref[...] = to_even.astype(BF)
    to_odd_ref[...] = to_odd.astype(BF)
    high, low = by_pair(
        lists_ref, GY, even_side_ref[:, width:].astype(F32), odd_side_ref[:, width:].astype(F32)
    )
    side_parents = stack_lanes(stack_rows(low, high), parents_ref.shape[1])
    grads = [stack_parities(total[:bricks].astype(BF)), stack_parities(total[bricks:].astype(BF))]
    up_sum = dot_tn(jnp.concatenate(grads, axis=0), jnp.concatenate([parents_ref[...], side_parents], axis=0))
    coarse = up_sum.shape[1]
    count = up_sums_ref.shape[0]
    for q in range(up_sum.shape[0] // count):
        up_sums_ref[:, q * coarse : (q + 1) * coarse] = up_sum[q * count : (q + 1) * count]


def given_sums_body(
    odd_cross_ref, even_cross_ref, merged_ref, even_side_ref, odd_side_ref, turned_ref, mains_ref, ends_ref, lists_ref,
    up_sums_ref, given_ref, pad_ref, table_ref,
):
    bricks, width = merged_ref.shape
    face = even_side_ref.shape[0]
    rows = bricks + 4 * face
    high, low = by_pair(lists_ref, GY, even_side_ref[:, :width].astype(F32), odd_side_ref[:, :width].astype(F32))
    above, below = from_pairs(lists_ref, GX, even_cross_ref, odd_cross_ref)
    table_ref[:bricks] = merged_ref[...]
    table_ref[bricks:] = stack_rows(low, high, below, above)
    lower_half = iota((rows, 2 * C), 1) < C
    zero = jnp.zeros((rows, 2 * C), BF)
    for x in range(4):
        for y in range(4):
            places = [(X, Y, dx, dy) for X, dx in options(x) for Y, dy in options(y)]
            at = (x * 4 + y) * RUN
            columns = table_ref[:, at : at + RUN]
            first = jnp.where(lower_half, columns[:, : 2 * C], zero)
            second = jnp.where(lower_half, zero, columns[:, 2 * C :])
            ends = jnp.concatenate([ends_ref[3 * dx + dy + 4] for _, _, dx, dy in places], axis=0)
            halo = dot(ends, jnp.concatenate([first, second], axis=0)).astype(BF)
            for i, (X, Y, _, _) in enumerate(places):
                pad_ref[X, Y, :, RUN:] = halo[i * bricks : (i + 1) * bricks]
            pad_ref[x + 1, y + 1, :, :RUN] = columns[:bricks]
            moved = [p for p in places if p[2:] != (0, 0)]
            if moved:
                main = jnp.concatenate([mains_ref[3 * dx + dy + 4] for _, _, dx, dy in moved], axis=0)
                got = dot(main, columns).astype(BF)
                for i, (X, Y, _, _) in enumerate(moved):
                    pad_ref[X, Y, :, :RUN] = got[i * bricks : (i + 1) * bricks]

    half_sums(1 - lists_ref[5, GX], pad_ref, turned_ref, up_sums_ref, given_ref)


def half_sums(group, pad_ref, turned_ref, up_sums_ref, out_ref):
    turned = turned_ref[...]
    half_count = out_ref.shape[0]
    up_lanes = up_sums_ref.shape[1]
    up_half = jnp.where(group == 0, up_sums_ref[:half_count], up_sums_ref[half_count:])
    out_ref[:, :up_lanes] = up_half.astype(out_ref.dtype)
    bricks = pad_ref.shape[2]
    lanes_low = iota((C, 2 * C), 1) < C
    sums = []
    for i in range(5):
        ex, ey = (jnp.where(group == 0, i // 3, (i + 4) // 3), jnp.where(group == 0, i % 3, (i + 4) % 3))
        wide = dot(turned, pad_ref[pl.ds(ex, 4), pl.ds(ey, 4)].reshape(16 * bricks, WIDE))

        def block(z, s):
            return wide[z * C : (z + 1) * C, s * 2 * C : (s + 1) * 2 * C]

        low = jnp.where(lanes_low, block(1, 0) + block(3, 1), block(0, 2) + block(2, 0))
        mid = jnp.where(lanes_low, block(0, 0) + block(2, 1), block(1, 0) + block(3, 1))
        high = jnp.where(lanes_low, block(1, 1) + block(3, 2), block(0, 0) + block(2, 1))
        for value in (low, mid, high):
            sums.append(value + pltpu.roll(value, C, 1))
    sums.append(jnp.zeros((C, 2 * C), F32))
    pairs = [jnp.where(lanes_low, sums[2 * k], sums[2 * k + 1]) for k in range(8)]
    for p in range(7):
        at = up_lanes + p * 2 * C
        out_ref[:, at : at + 2 * C] = jnp.where(group == 0, pairs[p], pairs[p + 1]).astype(out_ref.dtype)


def kept_sums_body(pad_ref, turned_ref, up_sums_ref, lists_ref, kept_ref):
    half_sums(lists_ref[5, GX], pad_ref, turned_ref, up_sums_ref, kept_ref)


def pair_sum_body(kept_ref, given_ref, out_ref):
    out_ref[...] = (kept_ref[...] + given_ref[...].astype(F32)).astype(BF)


def inputs_at(pad_ref, e):
    bricks = pad_ref.shape[2]
    ex, ey = (e // 3, e % 3)
    return pad_ref[ex : ex + 4, ey : ey + 4].reshape(16 * bricks, WIDE)


def conv_body(pad_ref, weight_ref, lists_ref, out_ref, again_ref, band_ref):
    again_ref[...] = lists_ref[...]
    bricks = pad_ref.shape[2]
    build_bands(weight_ref, band_ref)
    total = None
    for e in range(9):
        part = dot(inputs_at(pad_ref, e), band_ref[e])
        total = part if total is None else total + part
    for p in range(16):
        out_ref[:, p * RUN : (p + 1) * RUN] = total[p * bricks : (p + 1) * bricks].astype(BF)


def add_rows(base, lists, first, second):
    count, face = (base.shape[0], lists.shape[1])
    index = jnp.concatenate([lists[0:1], lists[1:2]], axis=1)
    chosen = ones_where(iota((count, 2 * face), 0) == index)
    return base + dot(chosen, stack_rows(first, second))


def merge_body(received_ref, up_ref, fine_ref, lists_ref, merged_ref, parents_ref, a_ref, b_ref):
    bricks, width = fine_ref.shape
    face = a_ref.shape[0]
    parents = merge(received_ref, slots_of(lists_ref, bricks), up_ref, fine_ref, merged_ref, parents_ref)
    lists = sides_of(lists_ref, face)
    lists = by_pair(lists_ref, GY, lists[0:1], lists[1:2])
    for out_ref, rows, owners in zip((a_ref, b_ref), pick_rows(lists, merged_ref[...]), pick_rows(lists, parents)):
        out_ref[:, :width] = rows.astype(BF)
        out_ref[:, width:] = owners.astype(BF)


def fine_grad_body(part_ref, lists_ref, even_ref, odd_ref, up_ref, grad_ref, replies_ref, across):
    bricks = part_ref.shape[0]
    face = even_ref.shape[0]
    from_next, from_prev = from_pairs(lists_ref, GY, even_ref, odd_ref)
    total = add_rows(part_ref[...], sides_of(lists_ref, face), from_next, from_prev)
    grad_ref[...] = total.astype(BF)
    items = dot(stack_parities(grad_ref[...]), up_ref[...]).astype(BF)
    items = jnp.concatenate([items[v * bricks : (v + 1) * bricks] for v in range(8)], axis=1)
    half = items.shape[1] // 2
    count, both_lanes = replies_ref.shape
    pieces = both_lanes // 2 // half
    capacity, group = chip_slots(count, pieces, across)
    slots = slots_of(lists_ref, bricks)
    slots = jnp.concatenate([slots, slots], axis=1)
    stacked = jnp.concatenate([items[:, :half], items[:, half:]], axis=0)
    row = iota((count, 2 * bricks), 0)
    half_of = iota((count, 2 * bricks), 1) // bricks
    for other in range(2):
        owner = device_of(row // group, lists_ref, other, across)
        for j in range(pieces):
            piece = row % group * pieces + j
            named = owner * capacity + piece // 2 == slots
            rows = dot(ones_where(named & (piece % 2 == half_of)), stacked)
            at = (other * pieces + j) * half
            replies_ref[:, at : at + half] = rows.astype(BF)


def chip_slots(count, pieces, across):
    group = count // (across[0] * across[1] // 2)
    return group * pieces // 2, group


def device_of(chip, lists_ref, other, across):
    core = jnp.broadcast_to(lists_ref[5:6, GX : GX + 1], chip.shape)
    core = 1 - core if other else core
    return (chip // across[1] * 2 + core) * across[1] + chip % across[1]


def share_body(sums_ref, replies_ref, out_ref, across):
    count, item_lanes = replies_ref.shape
    share = count // (across[0] * across[1] // 2)
    same = iota((count, count), 0) % share == iota((count, count), 1) % share
    out_ref[:, :item_lanes] = replies_ref[...]
    out_ref[:, item_lanes:] = dot(ones_where(same), sums_ref[...]).astype(BF)


def coarse_grad(arrivals, sends_ref, lists_ref, out_ref, across):
    capacity, devices = sends_ref.shape
    count, item_width = out_ref.shape
    half = item_width // 2
    lanes = arrivals[0].shape[0]
    pieces = arrivals[0].shape[1] // half
    _, group = chip_slots(lanes, pieces, across)
    sends = sends_ref[...].astype(F32).astype(BF)
    lane = iota((1, lanes), 1)
    totals = [None, None]
    for other in range(2):
        source = device_of(lane // group, lists_ref, other, across)
        rows = dot(sends, ones_where(source == iota((devices, lanes), 0)))
        for j in range(pieces):
            piece = lane % group * pieces + j
            picked = jnp.where(piece // 2 == iota((capacity, lanes), 0), rows, 0.0)
            index = jnp.sum(picked, axis=0, keepdims=True).astype(I32)
            named = iota((count, lanes), 0) == index
            for h in range(2):
                part = dot(ones_where(named & (piece % 2 == h)), arrivals[other][:, j * half : (j + 1) * half])
                totals[h] = part if totals[h] is None else totals[h] + part
    for h in range(2):
        out_ref[:, h * half : (h + 1) * half] = totals[h].astype(BF)


def last_body(back_ref, given_ref, sends_ref, lists_ref, conv_ref, up_ref, out_ref, item_lanes, across, scale):
    half_count = back_ref.shape[0]
    items = (back_ref[:, :item_lanes], given_ref[:, item_lanes : 2 * item_lanes])
    coarse_grad(items, sends_ref, lists_ref, out_ref, across)
    coarse = up_ref.shape[1]
    count = 2 * half_count
    parts = up_ref.shape[0] // count
    own = back_ref[:, 2 * item_lanes :].astype(F32) * scale
    others = given_ref[:, 2 * item_lanes :].astype(F32) * scale
    first, second = by_pair(lists_ref, GX, own, others)
    at = 0
    for q in range(parts):
        up_ref[q * count : q * count + half_count] = first[:, at : at + coarse]
        up_ref[q * count + half_count : (q + 1) * count] = second[:, at : at + coarse]
        at += coarse
    for pair in range(7):
        turned = jnp.concatenate([first[:, at : at + 2 * C], second[:, at : at + 2 * C]], axis=0).T
        at += 2 * C
        for h in range(2):
            for s in range(2):
                o = 14 * h + 2 * pair + s
                if o < 27:
                    conv_ref[o] = turned[s * C : (s + 1) * C, h * C : (h + 1) * C]


def swap(value, axis, first):
    count = lax.axis_size(axis)
    lower = range(first, count - 1, 2)
    return lax.ppermute(value, axis, [(i, i + 1) for i in lower] + [(i + 1, i) for i in lower])


def swap_pairs(to_even, to_odd, axis):
    return swap(to_even, axis, 0), swap(to_odd, axis, 1)


def trade_rows(values, axes):
    rows, width = values.shape
    devices = math.prod(lax.axis_size(axis) for axis in axes)
    grid_view = values.reshape(devices, rows // devices, width)
    return lax.all_to_all(grid_view, axes, split_axis=0, concat_axis=0, tiled=True).reshape(rows, width)


def on_device(
    fine_features, coarse_items, conv_weight, up_weight, neighbours,
    side_sends, cross_sends, parent_slots, coarse_sends, cotangent,
):
    fine = fine_features[0, 0]
    items = coarse_items[0, 0]
    cot = cotangent[0, 0]
    bricks, width = fine.shape
    face = side_sends.shape[-1]
    across = (lax.axis_size(GX_AXES), lax.axis_size("gy"))
    devices = across[0] * across[1]
    capacity = coarse_sends.shape[-1]
    item_count, item_width = items.shape
    coarse = up_weight.shape[1]
    start = bricks + 2 * face
    sends = coarse_sends.transpose(0, 1, 3, 2)[0, 0]
    slots = parent_slots[0]
    sides = side_sends[0, 0]
    crosses = cross_sends[0, 0]
    near = neighbours.transpose(0, 3, 1, 2)[0]
    up_turned = up_weight.transpose(0, 2, 1).reshape(8 * C, coarse)
    half = item_width // 2
    count = 2 * C
    item_lanes = capacity * devices // 2 * item_width // (count // 2)
    sums_width = 8 * C * coarse // count + 14 * C
    rows = shape((bricks, width))
    face_rows = shape((face, width))
    faces_and_parents = shape((face, width + item_width))
    lists_shape = shape((8, 128), I32)
    band = pltpu.VMEM((9, WIDE, RUN), BF)
    conv_flops = 2 * 9 * 16 * bricks * WIDE * RUN

    listed = (sends, items, sides, crosses, slots)
    outgoing, lists = call(
        first_body, [shape((2 * capacity * devices, half)), lists_shape], *listed,
        scratch=[pltpu.VMEM(a.shape, a.dtype) for a in listed] + [pltpu.SemaphoreType.DMA((len(listed),))],
        in_hbm=True,
    )
    received = trade_rows(outgoing, ("x", "core", "gy"))
    lane = jnp.arange(128, dtype=I32)[None]
    parity = jnp.where(lane == GX, lax.axis_index("core"), lax.axis_index("gy") % 2).astype(I32)
    table_rows = start + 2 * face
    ext_grad, to_even, to_odd, turned, mains, ends, lists = call(
        table_grad_body,
        [
            shape((start, width), F32), face_rows, face_rows, shape((RUN, 16 * bricks)),
            shape((9, bricks, table_rows)), shape((9, bricks, 2 * table_rows)), lists_shape,
        ],
        cot, conv_weight, near, lists, parity,
        scratch=[band, pltpu.VMEM((6, 6, bricks, WIDE), F32)], flops=2 * conv_flops,
    )
    cross_grads = swap_pairs(to_even, to_odd, GX_AXES)
    merged, parents, to_even, to_odd = call(
        merge_body, [rows, shape((8 * bricks, coarse)), faces_and_parents, faces_and_parents],
        received, up_turned, fine, lists,
    )
    sides = swap_pairs(to_even, to_odd, "gy")
    to_even, to_odd = call(cross_body, [face_rows, face_rows], merged, *sides, lists)
    crosses = swap_pairs(to_even, to_odd, GX_AXES)
    half_sums_dims = (count // 2, sums_width)
    fine_part, to_even, to_odd, up_sums = call(
        side_grad_body,
        [shape((bricks, width), F32), face_rows, face_rows, shape((count, sums_width - 14 * C), F32)],
        ext_grad, lists, *cross_grads, *sides, parents,
    )
    side_grads = swap_pairs(to_even, to_odd, "gy")
    given, pad = call(
        given_sums_body, [shape(half_sums_dims), shape((6, 6, bricks, WIDE))],
        *crosses[::-1], merged, *sides, turned, mains, ends, lists, up_sums,
        scratch=[pltpu.VMEM((table_rows, width), BF)], flops=conv_flops,
    )
    (kept,) = call(kept_sums_body, [shape(half_sums_dims, F32)], pad, turned, up_sums, lists, flops=conv_flops)
    given = swap(given, "core", 0)
    (sums,) = call(pair_sum_body, [shape(half_sums_dims)], kept, given)
    sums = trade_rows(sums, ("x", "gy"))
    output, lists = call(
        conv_body, [rows, lists_shape], pad, conv_weight, lists, scratch=[band], flops=conv_flops
    )
    grad_fine, replies = call(
        functools.partial(fine_grad_body, across=across), [rows, shape((count // 2, 2 * item_lanes))],
        fine_part, lists, *side_grads, up_turned,
    )
    (back,) = call(
        functools.partial(share_body, across=across), [shape((count // 2, 2 * item_lanes + sums_width))], sums, replies
    )
    back = trade_rows(back, ("x", "gy"))
    given = swap(back, "core", 0)
    scale = 1.0 / math.sqrt(64 * bricks * devices)
    grad_conv, grad_up, coarse_grad = call(
        functools.partial(last_body, item_lanes=item_lanes, across=across, scale=scale),
        [shape((27, C, C), F32), shape((8 * C, coarse), F32), shape((item_count, item_width))],
        back, given, sends, lists,
    )
    return (
        output.reshape(1, 1, bricks, width),
        grad_fine.reshape(1, 1, bricks, width),
        coarse_grad.reshape(1, 1, item_count, item_width),
        grad_conv,
        grad_up.reshape(8, C, coarse).transpose(0, 2, 1),
    )


def solution(mesh):
    groups, across_x, across_y = mesh.devices.shape
    split_mesh = Mesh(mesh.devices.reshape(groups, across_x // 2, 2, across_y), ("groups", "x", "core", "gy"))
    rows = ("groups", "x", "core")
    split = P(rows, "gy", None, None)
    placed = (split, split, P(), P(), split, split, split, P(rows, "gy", None), split, split)
    return jax.shard_map(
        on_device,
        mesh=split_mesh,
        in_specs=placed,
        out_specs=(split, split, split, P("groups", None, None), P("groups", None, None)),
        check_vma=False,
    )
```
